32 devices in a mesh: walk: 16 (over z, y, x), tan: 2 (over core).
Axes of the slice: x: 2, y: 2, z: 4, core: 2. Of those that a mesh axis runs over, the one named last changes fastest.
Arguments:
- values: bfloat16 [64, 64, 256], P('walk', 'tan'), may hold values from -6 to 6
- lap_in: bfloat16 [64, 64, 256], P('walk', 'tan'), may hold values from -6 to 6
- tangent: bfloat16 [64, 192, 64, 256], P('walk', None, 'tan'), may hold values from -0.4375 to 0.4375
- slot_electron: int32 [64, 64], P('walk'), may hold values from 0 to 63, each once within a row
- spin_up: int32 [64], P('walk'), may hold values from 16 to 48
- w_self: bfloat16 [256, 256], replicated, may hold values from -0.375 to 0.375
- w_spin: bfloat16 [256, 256], replicated, may hold values from -1.5 to 1.5
- bias: float32 [256], replicated, may hold values from -3 to 3
- readout: float32 [256], replicated, may hold values from -0.046875 to 0.046875
- potential: float32 [64], P('walk'), may hold values from -6 to 6
Outputs:
- laplacian: float32 [64, 64, 256], P('walk', 'tan')
- energy: float32 [64], P('walk')
- grad_self: float32 [256, 256], replicated
- grad_spin: float32 [256, 256], replicated
The draws below stay inside these ranges and needn't reach their ends.
Inputs may be any that keep to these rules, and one draw needn't show every extreme that they name: `slot_electron`: each walker's row names every electron once.
All inputs are finite; a program needn't handle non-finite values.
Results may differ from the reference program's by a relative error of at most 0.004.
Values may be sent and summed in bfloat16 or wider, within the bound.
No kernel may reach another device: no remote copies, remote signals or barrier semaphores. Data moves between devices by JAX's collectives and lax.ppermute only.
A program may use at most 64 MiB of HBM per device.

```python
import jax
import jax.numpy as jnp
from jax import lax

FEAT = 256
ELEC = 64
DIRS = 192
WALKERS = 64


def set_ends(drawn, own_key, smallest, high):
    longest = drawn.shape.index(max(drawn.shape))
    spots = []
    for shift in (0, 1):
        where = [jax.random.randint(jax.random.fold_in(own_key, axis), (), 0, length) for axis, length in enumerate(drawn.shape)]
        where[longest] = (where[longest] + shift) % drawn.shape[longest]
        spots.append(tuple(where))
    return drawn.at[spots[0]].set(smallest).at[spots[1]].set(high)


def levels(stream_key, dims, split, smallest, high):
    loudness, own = 1.0, jax.random.fold_in(stream_key, 6)
    for position, parts in split:
        draws = jnp.exp(jax.random.uniform(jax.random.fold_in(own, position), (parts,), jnp.float32, smallest / len(split), high / len(split)))
        loudness = loudness * jnp.repeat(draws, dims[position] // parts).reshape([-1 if axis == position else 1 for axis in range(len(dims))])
    return loudness


def gaussian(key, shape, scale, bound, pieces=(), kind=jnp.bfloat16):
    drawn = jax.random.normal(key, shape, jnp.float32) * scale
    if len(pieces) > 0:
        drawn = levels(key, shape, pieces, -0.22, 0.18) * drawn
    return jnp.clip(drawn, min=-bound, max=bound).astype(kind)


def setup_inputs(seed: int = 0) -> dict:
    key_list = jax.random.split(jax.random.key(seed), 11)
    values = gaussian(key_list[0], (WALKERS, ELEC, FEAT), 1.0, 6.0, ((0, 16), (1, 2)))
    lap_in = gaussian(key_list[1], (WALKERS, ELEC, FEAT), 1.0, 6.0, ((0, 16), (1, 2)))
    tangent = gaussian(key_list[2], (WALKERS, DIRS, ELEC, FEAT), DIRS ** -0.5, 0.4375, ((0, 16), (2, 2)))
    slot_electron = jax.vmap(lambda own: jax.random.permutation(own, ELEC))(jax.random.split(key_list[3], WALKERS)).reshape((WALKERS, ELEC)).astype(jnp.int32)
    spin_up = set_ends(jax.random.randint(key_list[4], (WALKERS,), ELEC // 4, 3 * ELEC // 4 + 1), jax.random.fold_in(key_list[4], 1), ELEC // 4, (3 * ELEC // 4 + 1) - 1).astype(jnp.int32)
    w_self = gaussian(key_list[5], (FEAT, FEAT), FEAT ** -0.5, 0.375)
    w_spin = gaussian(key_list[6], (FEAT, FEAT), 0.25, 1.5)
    bias = gaussian(key_list[7], (FEAT,), 0.5, 3.0, (), jnp.float32)
    readout = gaussian(key_list[8], (FEAT,), (ELEC * FEAT) ** -0.5, 0.046875, (), jnp.float32)
    potential = gaussian(key_list[9], (WALKERS,), 1.0, 6.0, ((0, 16),), jnp.float32)
    return dict(values=values, lap_in=lap_in, tangent=tangent, slot_electron=slot_electron, spin_up=spin_up, w_self=w_self, w_spin=w_spin, bias=bias, readout=readout, potential=potential)


def pick_spin(upper_spin, mixed_rows):
    return upper_spin[..., :, None] * mixed_rows[..., 0:1, :] + (1.0 - upper_spin[..., :, None]) * mixed_rows[..., 1:2, :]


def one_walker(walker_items, w_self, w_spin, bias, readout):
    feats, lap_feats, tangent_block, mask_rows, count_row, upper_spin, pot_value = walker_items
    mask_bf = mask_rows.astype(jnp.bfloat16)
    mean_values = (jnp.dot(mask_bf, feats, preferred_element_type=jnp.float32) / count_row[:, None]).astype(jnp.bfloat16)
    mean_lap = (jnp.dot(mask_bf, lap_feats, preferred_element_type=jnp.float32) / count_row[:, None]).astype(jnp.bfloat16)
    preact = jnp.dot(feats, w_self, preferred_element_type=jnp.float32) + pick_spin(upper_spin, jnp.dot(mean_values, w_spin, preferred_element_type=jnp.float32)) + bias
    lap_pre = jnp.dot(lap_feats, w_self, preferred_element_type=jnp.float32) + pick_spin(upper_spin, jnp.dot(mean_lap, w_spin, preferred_element_type=jnp.float32))
    squash = jnp.tanh(preact)
    slopes = 1.0 - squash * squash
    curvature = -2.0 * squash * slopes
    spin_sums = jnp.einsum("se,def->dsf", mask_rows.astype(jnp.float32), tangent_block.astype(jnp.float32), precision=lax.Precision.HIGHEST)
    spin_means = (spin_sums / count_row[None, :, None]).astype(jnp.bfloat16)
    dirs_count = tangent_block.shape[0]
    feat_width = tangent_block.shape[2]
    mixed_rows = jnp.dot(spin_means.reshape(-1, feat_width), w_spin, preferred_element_type=jnp.float32).reshape(dirs_count, 2, feat_width)
    change = jnp.dot(tangent_block.reshape(-1, feat_width), w_self, preferred_element_type=jnp.float32).reshape(tangent_block.shape) + pick_spin(upper_spin, mixed_rows)
    squares = jnp.sum(change * change, axis=0)
    weighted_slope = slopes * readout
    gradient = jnp.einsum("def,ef->d", change, weighted_slope, precision=lax.Precision.HIGHEST)
    laplacian = slopes * lap_pre + curvature * squares
    lap_sum = jnp.sum(laplacian * readout)
    energy = -0.5 * (lap_sum + jnp.sum(gradient * gradient)) + pot_value
    slope_bf = weighted_slope.astype(jnp.bfloat16)
    picked = pick_spin(upper_spin, mean_values.astype(jnp.float32)).astype(jnp.bfloat16)
    first_terms = jnp.dot(feats.T, slope_bf, preferred_element_type=jnp.float32)
    spin_terms = jnp.dot(picked.T, slope_bf, preferred_element_type=jnp.float32)
    return laplacian, energy, first_terms, spin_terms


def reference(values, lap_in, tangent, slot_electron, spin_up, w_self, w_spin, bias, readout, potential):
    upper_spin = (slot_electron < spin_up[:, None]).astype(jnp.float32)
    mask_rows = jnp.stack([upper_spin, 1.0 - upper_spin], axis=1)
    up_count = spin_up.astype(jnp.float32)
    count_rows = jnp.stack([up_count, ELEC - up_count], axis=1)
    laplacian, energy, first_terms, spin_terms = lax.map(
        lambda walker_items: one_walker(walker_items, w_self, w_spin, bias, readout),
        (values, lap_in, tangent, mask_rows, count_rows, upper_spin, potential))
    center = jnp.sum(energy) / WALKERS
    spread = energy - center
    grad_self = jnp.einsum("w,wfg->fg", spread, first_terms, precision=lax.Precision.HIGHEST)
    grad_spin = jnp.einsum("w,wfg->fg", spread, spin_terms, precision=lax.Precision.HIGHEST)
    return laplacian, energy, grad_self, grad_spin
```

```python
import functools

import jax
import jax.numpy as jnp
from jax import lax
from jax.experimental import pallas as pl
from jax.experimental.pallas import tpu as pltpu
from jax.sharding import PartitionSpec as P

F32 = jnp.float32
BF16 = jnp.bfloat16
VMEM_LIMIT = 40 * 1024 * 1024
HIGHEST = lax.Precision.HIGHEST


def iota(shape, axis):
    return lax.broadcasted_iota(jnp.int32, shape, axis)


def dot(a, b, dims=((1,), (0,)), precision=None):
    return lax.dot_general(a, b, (dims, ((), ())), precision=precision, preferred_element_type=F32)


def upper_row(slot_ref, w, count):
    return (slot_ref[pl.ds(w, 1), :] < count).astype(F32)


def upper_column(slot_ref, w, count, first, own):
    row = upper_row(slot_ref, w, count)
    place = iota((own, row.shape[1]), 1) == iota((own, row.shape[1]), 0) + first
    return jnp.sum(jnp.where(place, row, 0.0), axis=1, keepdims=True)


def group_rows(slot_ref, w, count, first, own, repeat):
    row = upper_row(slot_ref, w, count).astype(BF16)
    electrons = row.shape[1]
    wide = own * repeat
    place = iota((electrons, wide), 0) == iota((electrons, wide), 1) % own + first
    tiled = dot(jnp.broadcast_to(row, (8, electrons)), place.astype(BF16))[0:1]
    lane_part = iota((2 * repeat, wide), 1) // own
    line = iota((2 * repeat, wide), 0)
    chosen = jnp.where(line < repeat, tiled, 1.0 - tiled)
    return jnp.where(lane_part == line % repeat, chosen, 0.0).astype(BF16)


def value_sums_kernel(info_ref, slot_ref, values_ref, lap_ref, out_ref):
    walkers, own, _ = values_ref.shape
    for w in range(walkers):
        mask = group_rows(slot_ref, w, info_ref[1 + w], info_ref[0], own, 1)
        out_ref[w, 0:2, :] = dot(mask, values_ref[w])
        out_ref[w, 2:4, :] = dot(mask, lap_ref[w])


def tangent_sums_kernel(own, info_ref, slot_ref, tangent_ref, out_ref, mask_ref):
    w, step = pl.program_id(0), pl.program_id(1)
    repeat = mask_ref.shape[0] // 2
    rows = repeat * own

    @pl.when(step == 0)
    def _():
        mask_ref[...] = group_rows(slot_ref, w, info_ref[1 + w], info_ref[0], own, repeat)

    mask = mask_ref[...]
    for part in range(tangent_ref.shape[1] // rows):
        sums = dot(mask, tangent_ref[0, part * rows:(part + 1) * rows, :])
        out_ref[0, 0, part * repeat:(part + 1) * repeat, :] = sums[:repeat]
        out_ref[0, 1, part * repeat:(part + 1) * repeat, :] = sums[repeat:]


def layer_kernel(info_ref, slot_ref, values_ref, lap_ref, own_ref, other_ref, w_self_ref, w_spin_ref,
                 bias_ref, readout_ref, slopes_ref, base_ref, curve_ref, weighted_ref, slope_bf_ref,
                 slope_sums_ref, means_ref):
    walkers, own, feat = values_ref.shape
    electrons = slot_ref.shape[1]
    for w in range(walkers):
        count = info_ref[1 + w]
        column = upper_column(slot_ref, w, count, info_ref[0], own)
        mask = group_rows(slot_ref, w, count, info_ref[0], own, 1)
        ups = count.astype(F32)
        line = iota((4, 1), 0) % 2
        sizes = jnp.where(line == 0, ups, electrons - ups)
        means = ((own_ref[w] + other_ref[w]) / sizes).astype(BF16)
        mixed = dot(means, w_spin_ref[...])
        preact = dot(values_ref[w], w_self_ref[...]) + (
            column * mixed[0:1] + (1.0 - column) * mixed[1:2]) + bias_ref[...]
        lap_pre = dot(lap_ref[w], w_self_ref[...]) + (column * mixed[2:3] + (1.0 - column) * mixed[3:4])
        squash = jnp.tanh(preact)
        slopes = 1.0 - squash * squash
        weighted = slopes * readout_ref[...]
        slope_bf = weighted.astype(BF16)
        slopes_ref[w] = slopes
        base_ref[w] = slopes * lap_pre
        curve_ref[w] = -2.0 * squash * slopes
        weighted_ref[w] = weighted
        slope_bf_ref[w] = slope_bf
        slope_sums_ref[w] = dot(mask, slope_bf)
        means_ref[w] = means[0:2]


def change_kernel(own, info_ref, slot_ref, tangent_ref, own_ref, other_ref, w_self_ref, w_spin_ref,
                  readout_ref, base_ref, curve_ref, weighted_ref, lap_ref, grad_ref,
                  mixed_ref, squares_ref, column_ref, terms_ref):
    w, step = pl.program_id(0), pl.program_id(1)
    feat = w_self_ref.shape[0]
    dirs = own_ref.shape[2]
    block = tangent_ref.shape[1] // own
    electrons = slot_ref.shape[1]

    @pl.when(step == 0)
    def _():
        count = info_ref[1 + w]
        ups = count.astype(F32)
        for g, size in enumerate((ups, electrons - ups)):
            means = ((own_ref[0, g] + other_ref[0, g]) / size).astype(BF16)
            mixed_ref[g] = dot(means, w_spin_ref[...])
        column_ref[...] = jnp.broadcast_to(upper_column(slot_ref, w, count, info_ref[0], own), (own, feat))
        squares_ref[...] = jnp.zeros_like(squares_ref)

    upper = column_ref[...] > 0.5
    weighted = weighted_ref[0]
    part = 8
    squares = squares_ref[...]
    for p in range(block // part):
        plain = dot(tangent_ref[0, p * part * own:(p + 1) * part * own, :], w_self_ref[...])
        for d in range(part):
            at = step * block + p * part + d
            picked = jnp.where(upper, mixed_ref[0, pl.ds(at, 1), :], mixed_ref[1, pl.ds(at, 1), :])
            change = plain[d * own:(d + 1) * own] + picked
            squares = squares + change * change
            terms = (change * weighted).reshape(own // 8, 8, feat).sum(axis=0)
            terms_ref[pl.ds(pl.multiple_of(at * 8, 8), 8), :] = terms[:, :feat // 2] + terms[:, feat // 2:]
    squares_ref[...] = squares

    @pl.when(step == pl.num_programs(1) - 1)
    def _():
        laplacian = base_ref[0] + curve_ref[0] * squares_ref[...]
        lap_ref[0] = laplacian
        summed = terms_ref[...].reshape(dirs, 8, feat // 2).sum(axis=1)
        grad_ref[0, 0:8, 0:dirs] = dot(jnp.ones((8, feat // 2), F32), summed, ((1,), (1,)), HIGHEST)
        grad_ref[0, 0:8, dirs:] = jnp.broadcast_to(jnp.sum(laplacian * readout_ref[...]), (8, 256 - dirs))


def gradients_kernel(info_ref, spread_ref, values_ref, slope_bf_ref, slope_sums_ref, means_ref, out_ref):
    walkers, own, feat = values_ref.shape
    total = jnp.zeros((feat, feat), F32)
    spin = jnp.zeros((feat, feat), F32)
    for w in range(walkers):
        scaled = slope_bf_ref[w].astype(F32) * spread_ref[w]
        high = scaled.astype(BF16)
        low = (scaled - high.astype(F32)).astype(BF16)
        total = total + dot(values_ref[w], high, ((0,), (0,))) + dot(values_ref[w], low, ((0,), (0,)))
        scaled = slope_sums_ref[w] * spread_ref[w]
        high = scaled.astype(BF16)
        low = (scaled - high.astype(F32)).astype(BF16)
        spin = spin + dot(means_ref[w], high, ((0,), (0,))) + dot(means_ref[w], low, ((0,), (0,)))
    out_ref[0:feat] = total
    out_ref[feat:] = spin


def whole(memory=pltpu.VMEM):
    return pl.BlockSpec(memory_space=memory)


def call(kernel, out_shape, in_specs, out_specs=None, grid=(), scratch=(), cost=None):
    return pl.pallas_call(
        kernel,
        out_shape=out_shape,
        grid=grid,
        in_specs=in_specs,
        out_specs=out_specs if out_specs is not None else jax.tree.map(lambda _: whole(), out_shape),
        scratch_shapes=scratch,
        cost_estimate=cost,
        compiler_params=pltpu.CompilerParams(vmem_limit_bytes=VMEM_LIMIT),
    )


def flip(array, axis, bit):
    size = lax.axis_size(axis)
    return lax.ppermute(array, axis, [(i, i ^ bit) for i in range(size)])


def shards(values, lap_in, tangent, slot_electron, spin_up, w_self, w_spin, bias, readout, potential):
    walk_size, tan_size = lax.axis_size("walk"), lax.axis_size("tan")
    tan_rank, walk_rank = lax.axis_index("tan"), lax.axis_index("walk")
    walkers, own, feat = values.shape
    dirs = tangent.shape[1]
    electrons = slot_electron.shape[1]
    shape = jax.ShapeDtypeStruct
    smem = whole(pltpu.SMEM)
    info = jnp.concatenate([(tan_rank * own).reshape(1).astype(jnp.int32), spin_up])
    flat = tangent.reshape(walkers, dirs * own, feat)
    bias_row, readout_row = bias.reshape(1, feat), readout.reshape(1, feat)

    value_sums = call(value_sums_kernel, shape((walkers, 4, feat), F32), [smem, whole(), whole(), whole()])(
        info, slot_electron, values, lap_in)
    other_value_sums = flip(value_sums, "tan", 1)

    block = 48
    steps = dirs // block
    repeat = 8
    sums = call(
        functools.partial(tangent_sums_kernel, own), shape((walkers, 2, dirs, feat), F32),
        [smem, whole(), pl.BlockSpec((1, block * own, feat), lambda w, i: (w, i, 0))],
        pl.BlockSpec((1, 2, block, feat), lambda w, i: (w, 0, i, 0)),
        (walkers, steps), [pltpu.VMEM((2 * repeat, repeat * own), BF16)],
        pl.CostEstimate(flops=2 * walkers * dirs * own * feat * 16, bytes_accessed=walkers * dirs * own * feat * 2, transcendentals=0),
    )(info, slot_electron, flat)
    other_sums = flip(sums, "tan", 1)

    full = shape((walkers, own, feat), F32)
    _, base, curve, weighted, slope_bf, slope_sums, means = call(
        layer_kernel,
        (full, full, full, full, shape((walkers, own, feat), BF16), shape((walkers, 2, feat), F32),
         shape((walkers, 2, feat), BF16)),
        [smem] + [whole()] * 9)(
            info, slot_electron, values, lap_in, value_sums, other_value_sums, w_self, w_spin, bias_row, readout_row)

    per_walker = pl.BlockSpec((1, own, feat), lambda w, i: (w, 0, 0))
    per_sums = pl.BlockSpec((1, 2, dirs, feat), lambda w, i: (w, 0, 0, 0))
    laplacian, partial = call(
        functools.partial(change_kernel, own),
        (full, shape((walkers, 8, 256), F32)),
        [smem, whole(), pl.BlockSpec((1, block * own, feat), lambda w, i: (w, i, 0)), per_sums, per_sums,
         whole(), whole(), whole(), per_walker, per_walker, per_walker],
        (per_walker, pl.BlockSpec((1, 8, 256), lambda w, i: (w, 0, 0))),
        (walkers, steps),
        [pltpu.VMEM((2, dirs, feat), F32), pltpu.VMEM((own, feat), F32), pltpu.VMEM((own, feat), F32),
         pltpu.VMEM((dirs * 8, feat // 2), F32)],
    )(info, slot_electron, flat, sums, other_sums, w_self, w_spin, readout_row, base, curve, weighted)

    partial = partial[:, 0, :dirs + 1]
    both = partial + flip(partial, "tan", 1)
    energy = -0.5 * (both[:, dirs] + jnp.sum(both[:, :dirs] ** 2, axis=1)) + potential
    center = jnp.sum(energy).reshape(1)
    bits = [1 << b for b in range(walk_size.bit_length() - 1)]
    for bit in bits:
        center = center + flip(center, "walk", bit)
    spread = energy - center / (walkers * walk_size)

    grads = call(gradients_kernel, shape((2 * feat, feat), F32), [smem, smem] + [whole()] * 4)(
        info, spread, values, slope_bf, slope_sums, means)
    stages = [("tan", 1, tan_rank)] + [("walk", bit, walk_rank) for bit in bits]
    for axis, bit, rank in stages:
        high = (rank & bit) != 0
        half = grads.shape[0] // 2
        sent = jnp.where(high, grads[:half], grads[half:])
        kept = jnp.where(high, grads[half:], grads[:half])
        grads = kept + flip(sent, axis, bit)
    for axis, bit, rank in reversed(stages):
        high = (rank & bit) != 0
        got = flip(grads, axis, bit)
        grads = jnp.concatenate([jnp.where(high, got, grads), jnp.where(high, grads, got)], axis=0)
    return laplacian, energy, grads[:feat], grads[feat:]


def solution(mesh):
    placed = (
        P("walk", "tan", None),
        P("walk", "tan", None),
        P("walk", None, "tan", None),
        P("walk", None),
        P("walk"),
        P(),
        P(),
        P(),
        P(),
        P("walk"),
    )
    return jax.shard_map(
        shards,
        mesh=mesh,
        in_specs=placed,
        out_specs=(P("walk", "tan", None), P("walk"), P(), P()),
        check_vma=False,
    )
```

```python
import functools

import jax
import jax.numpy as jnp
from jax import lax
from jax.experimental import pallas as pl
from jax.experimental.pallas import tpu as pltpu
from jax.sharding import PartitionSpec as P

F32 = jnp.float32
BF16 = jnp.bfloat16
VMEM_LIMIT = 60 * 1024 * 1024
HIGHEST = lax.Precision.HIGHEST


def iota(shape, axis):
    return lax.broadcasted_iota(jnp.int32, shape, axis)


def dot(a, b, dims=((1,), (0,)), precision=None):
    return lax.dot_general(a, b, (dims, ((), ())), precision=precision, preferred_element_type=F32)


def first_slot(own):
    return lax.axis_index("tan") * own


def upper_row(slot_ref, w, count):
    return (slot_ref[pl.ds(w, 1), :] < count).astype(F32)


def upper_column(slot_ref, w, count, first, own):
    row = upper_row(slot_ref, w, count)
    place = iota((own, row.shape[1]), 1) == iota((own, row.shape[1]), 0) + first
    return jnp.sum(jnp.where(place, row, 0.0), axis=1, keepdims=True)


def group_rows(slot_ref, w, count, first, own, repeat):
    row = upper_row(slot_ref, w, count).astype(BF16)
    electrons = row.shape[1]
    wide = own * repeat
    place = iota((electrons, wide), 0) == iota((electrons, wide), 1) % own + first
    tiled = dot(jnp.broadcast_to(row, (8, electrons)), place.astype(BF16))[0:1]
    lane_part = iota((2 * repeat, wide), 1) // own
    line = iota((2 * repeat, wide), 0)
    chosen = jnp.where(line < repeat, tiled, 1.0 - tiled)
    return jnp.where(lane_part == line % repeat, chosen, 0.0).astype(BF16)


def value_sums_kernel(spin_ref, slot_ref, values_ref, lap_ref, out_ref):
    walkers, own, _ = values_ref.shape
    for w in range(walkers):
        mask = group_rows(slot_ref, w, spin_ref[w], first_slot(own), own, 1)
        out_ref[w, 0:2, :] = dot(mask, values_ref[w])
        out_ref[w, 2:4, :] = dot(mask, lap_ref[w])


def tangent_sums_kernel(own, spin_ref, slot_ref, tangent_ref, out_ref, mask_ref):
    w, step = pl.program_id(0), pl.program_id(1)
    repeat = mask_ref.shape[0] // 2
    rows = repeat * own

    @pl.when(step == 0)
    def _():
        mask_ref[...] = group_rows(slot_ref, w, spin_ref[w], first_slot(own), own, repeat)

    mask = mask_ref[...]
    for part in range(tangent_ref.shape[1] // rows):
        sums = dot(mask, tangent_ref[0, part * rows:(part + 1) * rows, :])
        out_ref[0, 0, part * repeat:(part + 1) * repeat, :] = sums[:repeat]
        out_ref[0, 1, part * repeat:(part + 1) * repeat, :] = sums[repeat:]


def layer_kernel(spin_ref, slot_ref, values_ref, lap_ref, own_ref, other_ref, w_self_ref, w_spin_ref,
                 bias_ref, readout_ref, slopes_ref, base_ref, curve_ref, weighted_ref, slope_bf_ref,
                 slope_sums_ref, means_ref):
    walkers, own, feat = values_ref.shape
    electrons = slot_ref.shape[1]
    for w in range(walkers):
        count = spin_ref[w]
        column = upper_column(slot_ref, w, count, first_slot(own), own)
        mask = group_rows(slot_ref, w, count, first_slot(own), own, 1)
        ups = count.astype(F32)
        line = iota((4, 1), 0) % 2
        sizes = jnp.where(line == 0, ups, electrons - ups)
        means = ((own_ref[w] + other_ref[w]) / sizes).astype(BF16)
        mixed = dot(means, w_spin_ref[...])
        preact = dot(values_ref[w], w_self_ref[...]) + (
            column * mixed[0:1] + (1.0 - column) * mixed[1:2]) + bias_ref[...]
        lap_pre = dot(lap_ref[w], w_self_ref[...]) + (column * mixed[2:3] + (1.0 - column) * mixed[3:4])
        squash = jnp.tanh(preact)
        slopes = 1.0 - squash * squash
        weighted = slopes * readout_ref[...]
        slope_bf = weighted.astype(BF16)
        slopes_ref[w] = slopes
        base_ref[w] = slopes * lap_pre
        curve_ref[w] = -2.0 * squash * slopes
        weighted_ref[w] = weighted
        slope_bf_ref[w] = slope_bf
        slope_sums_ref[w] = dot(mask, slope_bf)
        means_ref[w] = means[0:2]


def change_kernel(own, spin_ref, slot_ref, tangent_ref, own_ref, other_ref, w_self_ref, w_spin_ref,
                  readout_ref, base_ref, curve_ref, weighted_ref, lap_ref, grad_ref,
                  mixed_ref, squares_ref, column_ref, terms_ref):
    w, step = pl.program_id(0), pl.program_id(1)
    feat = w_self_ref.shape[0]
    dirs = own_ref.shape[2]
    block = tangent_ref.shape[1] // own
    electrons = slot_ref.shape[1]

    @pl.when(step == 0)
    def _():
        count = spin_ref[w]
        ups = count.astype(F32)
        for g, size in enumerate((ups, electrons - ups)):
            means = ((own_ref[0, g] + other_ref[0, g]) / size).astype(BF16)
            mixed_ref[g] = dot(means, w_spin_ref[...])
        column_ref[...] = jnp.broadcast_to(upper_column(slot_ref, w, count, first_slot(own), own), (own, feat))
        squares_ref[...] = jnp.zeros_like(squares_ref)

    upper = column_ref[...] > 0.5
    weighted = weighted_ref[0]
    part = 8
    squares = squares_ref[...]
    plain = dot(tangent_ref[0], w_self_ref[...])
    for p in range(block // part):
        at = pl.multiple_of(step * block + p * part, part)
        mixed = mixed_ref[:, pl.ds(at, part), :]
        for d in range(part):
            row = (p * part + d) * own
            picked = jnp.where(upper, mixed[0, d:d + 1], mixed[1, d:d + 1])
            change = plain[row:row + own] + picked
            squares = squares + change * change
            terms = (change * weighted).reshape(own // 8, 8, feat).sum(axis=0)
            terms_ref[pl.ds(pl.multiple_of(at * 8 + d * 8, 8), 8), :] = terms[:, :feat // 2] + terms[:, feat // 2:]
    squares_ref[...] = squares

    @pl.when(step == pl.num_programs(1) - 1)
    def _():
        laplacian = base_ref[0] + curve_ref[0] * squares_ref[...]
        lap_ref[0] = laplacian
        summed = terms_ref[...].reshape(dirs, 8, feat // 2).sum(axis=1)
        grad_ref[0, 0:8, 0:dirs] = dot(jnp.ones((8, feat // 2), F32), summed, ((1,), (1,)), HIGHEST)
        grad_ref[0, 0:8, dirs:] = jnp.broadcast_to(jnp.sum(laplacian * readout_ref[...]), (8, 256 - dirs))


def gradients_kernel(spread_ref, values_ref, slope_bf_ref, slope_sums_ref, means_ref, out_ref):
    walkers, own, feat = values_ref.shape
    total = jnp.zeros((feat, feat), F32)
    spin = jnp.zeros((feat, feat), F32)
    for w in range(walkers):
        scaled = slope_bf_ref[w].astype(F32) * spread_ref[w]
        high = scaled.astype(BF16)
        low = (scaled - high.astype(F32)).astype(BF16)
        total = total + dot(values_ref[w], high, ((0,), (0,))) + dot(values_ref[w], low, ((0,), (0,)))
        scaled = slope_sums_ref[w] * spread_ref[w]
        high = scaled.astype(BF16)
        low = (scaled - high.astype(F32)).astype(BF16)
        spin = spin + dot(means_ref[w], high, ((0,), (0,))) + dot(means_ref[w], low, ((0,), (0,)))
    out_ref[0:feat] = total
    out_ref[feat:] = spin


def whole(memory=pltpu.VMEM):
    return pl.BlockSpec(memory_space=memory)


def call(kernel, out_shape, in_specs, out_specs=None, grid=(), scratch=(), cost=None):
    return pl.pallas_call(
        kernel,
        out_shape=out_shape,
        grid=grid,
        in_specs=in_specs,
        out_specs=out_specs if out_specs is not None else jax.tree.map(lambda _: whole(), out_shape),
        scratch_shapes=scratch,
        cost_estimate=cost,
        compiler_params=pltpu.CompilerParams(vmem_limit_bytes=VMEM_LIMIT),
    )


def flip(array, axis, bit):
    size = lax.axis_size(axis)
    return lax.ppermute(array, axis, [(i, i ^ bit) for i in range(size)])


def shards(values, lap_in, tangent, slot_electron, spin_up, w_self, w_spin, bias, readout, potential):
    walk_size, tan_size = lax.axis_size("walk"), lax.axis_size("tan")
    tan_rank, walk_rank = lax.axis_index("tan"), lax.axis_index("walk")
    walkers, own, feat = values.shape
    dirs = tangent.shape[1]
    electrons = slot_electron.shape[1]
    shape = jax.ShapeDtypeStruct
    smem = whole(pltpu.SMEM)
    flat = tangent.reshape(walkers, dirs * own, feat)
    bias_row, readout_row = bias.reshape(1, feat), readout.reshape(1, feat)

    value_sums = call(value_sums_kernel, shape((walkers, 4, feat), F32), [smem, whole(), whole(), whole()])(
        spin_up, slot_electron, values, lap_in)
    other_value_sums = flip(value_sums, "tan", 1)
    flat, value_sums = lax.optimization_barrier((flat, value_sums))

    block = 48
    steps = dirs // block
    repeat = 8
    sums = call(
        functools.partial(tangent_sums_kernel, own), shape((walkers, 2, dirs, feat), F32),
        [smem, whole(), pl.BlockSpec((1, block * own, feat), lambda w, i: (w, i, 0))],
        pl.BlockSpec((1, 2, block, feat), lambda w, i: (w, 0, i, 0)),
        (walkers, steps), [pltpu.VMEM((2 * repeat, repeat * own), BF16)],
        pl.CostEstimate(flops=2 * walkers * dirs * own * feat * 16, bytes_accessed=walkers * dirs * own * feat * 2, transcendentals=0),
    )(spin_up, slot_electron, flat)
    other_sums = flip(sums, "tan", 1)

    full = shape((walkers, own, feat), F32)
    _, base, curve, weighted, slope_bf, slope_sums, means = call(
        layer_kernel,
        (full, full, full, full, shape((walkers, own, feat), BF16), shape((walkers, 2, feat), F32),
         shape((walkers, 2, feat), BF16)),
        [smem] + [whole()] * 9)(
            spin_up, slot_electron, values, lap_in, value_sums, other_value_sums, w_self, w_spin, bias_row, readout_row)

    per_walker = pl.BlockSpec((1, own, feat), lambda w, i: (w, 0, 0))
    per_sums = pl.BlockSpec((1, 2, dirs, feat), lambda w, i: (w, 0, 0, 0))
    laplacian, partial = call(
        functools.partial(change_kernel, own),
        (full, shape((walkers, 8, 256), F32)),
        [smem, whole(), pl.BlockSpec((1, block * own, feat), lambda w, i: (w, i, 0)), per_sums, per_sums,
         whole(), whole(), whole(), per_walker, per_walker, per_walker],
        (per_walker, pl.BlockSpec((1, 8, 256), lambda w, i: (w, 0, 0))),
        (walkers, steps),
        [pltpu.VMEM((2, dirs, feat), F32), pltpu.VMEM((own, feat), F32), pltpu.VMEM((own, feat), F32),
         pltpu.VMEM((dirs * 8, feat // 2), F32)],
    )(spin_up, slot_electron, flat, sums, other_sums, w_self, w_spin, readout_row, base, curve, weighted)

    partial = partial[:, 0, :dirs + 1]
    both = partial + flip(partial, "tan", 1)
    energy = -0.5 * (both[:, dirs] + jnp.sum(both[:, :dirs] ** 2, axis=1)) + potential
    everyone = ("walk", "tan")
    devices = walk_size * tan_size
    energies = lax.all_to_all(jnp.broadcast_to(energy, (walk_size, walkers)), "walk", 0, 0, tiled=True)
    center = jnp.sum(energies) / (walkers * walk_size)
    grads = call(gradients_kernel, shape((2 * feat, feat), F32), [smem] + [whole()] * 4)(
        energy - center, values, slope_bf, slope_sums, means)
    pieces = lax.all_to_all(grads, everyone, 0, 0, tiled=True)
    piece = jnp.sum(pieces.reshape(devices, 2 * feat // devices, feat), axis=0)
    grads = lax.all_to_all(jnp.broadcast_to(piece, (devices,) + piece.shape), everyone, 0, 0, tiled=True)
    grads = grads.reshape(2 * feat, feat)
    return laplacian, energy, grads[:feat], grads[feat:]


def solution(mesh):
    placed = (
        P("walk", "tan", None),
        P("walk", "tan", None),
        P("walk", None, "tan", None),
        P("walk", None),
        P("walk"),
        P(),
        P(),
        P(),
        P(),
        P("walk"),
    )
    return jax.shard_map(
        shards,
        mesh=mesh,
        in_specs=placed,
        out_specs=(P("walk", "tan", None), P("walk"), P(), P()),
        check_vma=False,
    )
```

```python
import functools

import jax
import jax.numpy as jnp
from jax import lax
from jax.experimental import pallas as pl
from jax.experimental.pallas import tpu as pltpu
from jax.sharding import PartitionSpec as P

F32 = jnp.float32
BF16 = jnp.bfloat16
VMEM_LIMIT = 60 * 1024 * 1024
HIGHEST = lax.Precision.HIGHEST


def iota(shape, axis):
    return lax.broadcasted_iota(jnp.int32, shape, axis)


def dot(a, b, dims=((1,), (0,)), precision=None):
    return lax.dot_general(a, b, (dims, ((), ())), precision=precision, preferred_element_type=F32)


def first_slot(own):
    return lax.axis_index("tan") * own


def upper_row(slot_ref, w, count):
    return (slot_ref[pl.ds(w, 1), :] < count).astype(F32)


def upper_column(slot_ref, w, count, first, own):
    row = upper_row(slot_ref, w, count)
    place = iota((own, row.shape[1]), 1) == iota((own, row.shape[1]), 0) + first
    return jnp.sum(jnp.where(place, row, 0.0), axis=1, keepdims=True)


def group_rows(slot_ref, w, count, first, own, repeat):
    row = upper_row(slot_ref, w, count).astype(BF16)
    electrons = row.shape[1]
    wide = own * repeat
    place = iota((electrons, wide), 0) == iota((electrons, wide), 1) % own + first
    tiled = dot(jnp.broadcast_to(row, (8, electrons)), place.astype(BF16))[0:1]
    lane_part = iota((2 * repeat, wide), 1) // own
    line = iota((2 * repeat, wide), 0)
    chosen = jnp.where(line < repeat, tiled, 1.0 - tiled)
    return jnp.where(lane_part == line % repeat, chosen, 0.0).astype(BF16)


def value_sums_kernel(spin_ref, slot_ref, values_ref, lap_ref, out_ref):
    walkers, own, _ = values_ref.shape
    for w in range(walkers):
        mask = group_rows(slot_ref, w, spin_ref[w], first_slot(own), own, 1)
        out_ref[w, 0:2, :] = dot(mask, values_ref[w])
        out_ref[w, 2:4, :] = dot(mask, lap_ref[w])


def fetch(source_ref, held_ref, sems, chunk):
    return [
        pltpu.make_async_copy(source_ref.at[pl.ds(i * chunk, chunk)], held_ref.at[pl.ds(i * chunk, chunk)], sems.at[i])
        for i in range(source_ref.shape[0] // chunk)
    ]


def await_chunk(source_ref, held_ref, sems, chunk, i):
    at = pl.ds(pl.multiple_of(i * chunk, chunk), chunk)
    pltpu.make_async_copy(source_ref.at[at], held_ref.at[at], sems.at[i]).wait()


def tangent_sums_kernel(own, block, spin_ref, slot_ref, tangent_ref, out_ref, held_ref, sems, mask_ref):
    walkers, _, dirs, _ = out_ref.shape
    repeat = mask_ref.shape[1] // 2
    rows, chunk = repeat * own, block * own
    for copy in fetch(tangent_ref, held_ref, sems, chunk):
        copy.start()
    for w in range(walkers):
        mask_ref[w] = group_rows(slot_ref, w, spin_ref[w], first_slot(own), own, repeat)
    steps = dirs // block

    @pl.loop(0, walkers * steps)
    def _(i):
        w, step = i // steps, i % steps
        await_chunk(tangent_ref, held_ref, sems, chunk, i)
        mask = mask_ref[w]
        for part in range(block // repeat):
            row = pl.multiple_of(i * chunk + part * rows, rows)
            sums = dot(mask, held_ref[pl.ds(row, rows), :])
            at = pl.ds(pl.multiple_of(step * block + part * repeat, repeat), repeat)
            out_ref[w, 0, at, :] = sums[:repeat]
            out_ref[w, 1, at, :] = sums[repeat:]


def layer_kernel(spin_ref, slot_ref, values_ref, lap_ref, own_ref, other_ref, w_self_ref, w_spin_ref,
                 bias_ref, readout_ref, base_ref, curve_ref, weighted_ref, packed_ref):
    walkers, own, feat = values_ref.shape
    electrons = slot_ref.shape[1]
    small = []
    for w in range(walkers):
        count = spin_ref[w]
        column = upper_column(slot_ref, w, count, first_slot(own), own)
        mask = group_rows(slot_ref, w, count, first_slot(own), own, 1)
        ups = count.astype(F32)
        line = iota((4, 1), 0) % 2
        sizes = jnp.where(line == 0, ups, electrons - ups)
        means = ((own_ref[w] + other_ref[w]) / sizes).astype(BF16)
        mixed = dot(means, w_spin_ref[...])
        preact = dot(values_ref[w], w_self_ref[...]) + (
            column * mixed[0:1] + (1.0 - column) * mixed[1:2]) + bias_ref[...]
        lap_pre = dot(lap_ref[w], w_self_ref[...]) + (column * mixed[2:3] + (1.0 - column) * mixed[3:4])
        squash = jnp.tanh(preact)
        slopes = 1.0 - squash * squash
        weighted = slopes * readout_ref[...]
        slope_bf = weighted.astype(BF16)
        base_ref[w] = slopes * lap_pre
        curve_ref[w] = -2.0 * squash * slopes
        weighted_ref[w] = weighted
        packed_ref[w * own:(w + 1) * own, :] = slope_bf
        sums = dot(mask, slope_bf)
        empty = jnp.zeros((6, feat), F32)
        high = sums.astype(BF16).astype(F32)
        small.append((means[0:2].astype(F32), high, sums - high))
    for kind in range(3):
        rows = [piece for w in range(walkers) for piece in (small[w][kind], empty)]
        at = (own + kind * 8) * walkers
        packed_ref[at:at + 8 * walkers, :] = jnp.concatenate(rows, axis=0).astype(BF16)


def change_kernel(own, block, spin_ref, slot_ref, tangent_ref, own_ref, other_ref, w_self_ref, w_spin_ref,
                  readout_ref, base_ref, curve_ref, weighted_ref, lap_ref, grad_ref,
                  held_ref, sems, mixed_ref, squares_ref, column_ref, terms_ref):
    walkers, _, dirs, feat = own_ref.shape
    electrons = slot_ref.shape[1]
    chunk, steps, part = block * own, dirs // block, 8
    for copy in fetch(tangent_ref, held_ref, sems, chunk):
        copy.start()

    @pl.loop(0, walkers)
    def _(w):
        count = spin_ref[w]
        ups = count.astype(F32)
        for g, size in enumerate((ups, electrons - ups)):
            means = ((own_ref[w, g] + other_ref[w, g]) / size).astype(BF16)
            mixed_ref[g] = dot(means, w_spin_ref[...])
        column_ref[...] = jnp.broadcast_to(upper_column(slot_ref, w, count, first_slot(own), own), (own, feat))
        squares_ref[...] = jnp.zeros_like(squares_ref)

        @pl.loop(0, steps)
        def _(step):
            i = w * steps + step
            await_chunk(tangent_ref, held_ref, sems, chunk, i)
            upper = column_ref[...] > 0.5
            weighted = weighted_ref[w]
            squares = squares_ref[...]
            plain = dot(held_ref[pl.ds(pl.multiple_of(i * chunk, chunk), chunk), :], w_self_ref[...])
            for p in range(block // part):
                at = pl.multiple_of(step * block + p * part, part)
                mixed = mixed_ref[:, pl.ds(at, part), :]
                for d in range(part):
                    row = (p * part + d) * own
                    picked = jnp.where(upper, mixed[0, d:d + 1], mixed[1, d:d + 1])
                    change = plain[row:row + own] + picked
                    squares = squares + change * change
                    terms = (change * weighted).reshape(own // 8, 8, feat).sum(axis=0)
                    terms_ref[pl.ds(pl.multiple_of(at * 8 + d * 8, 8), 8), :] = (
                        terms[:, :feat // 2] + terms[:, feat // 2:])
            squares_ref[...] = squares

        laplacian = base_ref[w] + curve_ref[w] * squares_ref[...]
        lap_ref[w] = laplacian
        summed = terms_ref[...].reshape(dirs, 8, feat // 2).sum(axis=1)
        grad_ref[w, 0:8, 0:dirs] = dot(jnp.ones((8, feat // 2), F32), summed, ((1,), (1,)), HIGHEST)
        grad_ref[w, 0:8, dirs:] = jnp.broadcast_to(jnp.sum(laplacian * readout_ref[...]), (8, 256 - dirs))


def two_terms(array):
    high = array.astype(BF16)
    return high, (array - high.astype(F32)).astype(BF16)


def gradients_kernel(walkers, own, energy_ref, values_ref, slopes_ref, out_ref, scaled_ref, groups_ref):
    feat = values_ref.shape[2]
    parts = values_ref.shape[0]
    everyone = parts * walkers
    center = lax.fori_loop(0, everyone, lambda i, total: total + energy_ref[i], jnp.float32(0.0)) / everyone
    out_ref[...] = jnp.zeros_like(out_ref)

    @pl.loop(0, parts)
    def _(r):
        for w in range(walkers):
            spread = energy_ref[r * walkers + w] - center
            rows = slopes_ref[r, w * own:(w + 1) * own, :].astype(F32) * spread
            scaled_ref[0, w * own:(w + 1) * own, :], scaled_ref[1, w * own:(w + 1) * own, :] = two_terms(rows)
            groups_ref[w * 8:(w + 1) * 8, :] = jnp.full((8, feat), spread)
        rows = values_ref[r]
        out_ref[0:feat] += dot(rows, scaled_ref[0], ((0,), (0,))) + dot(rows, scaled_ref[1], ((0,), (0,)))
        small = slopes_ref[r, walkers * own:, :].astype(F32)
        means = small[0:walkers * 8]
        high, low = two_terms((small[walkers * 8:walkers * 16] + small[walkers * 16:]) * groups_ref[...])
        means = means.astype(BF16)
        out_ref[feat:] += dot(means, high, ((0,), (0,))) + dot(means, low, ((0,), (0,)))


def whole(memory=pltpu.VMEM):
    return pl.BlockSpec(memory_space=memory)


def call(kernel, out_shape, in_specs, out_specs=None, grid=(), scratch=(), cost=None):
    return pl.pallas_call(
        kernel,
        out_shape=out_shape,
        grid=grid,
        in_specs=in_specs,
        out_specs=out_specs if out_specs is not None else jax.tree.map(lambda _: whole(), out_shape),
        scratch_shapes=scratch,
        cost_estimate=cost,
        compiler_params=pltpu.CompilerParams(vmem_limit_bytes=VMEM_LIMIT),
    )


def flip(array, axis, bit):
    size = lax.axis_size(axis)
    return lax.ppermute(array, axis, [(i, i ^ bit) for i in range(size)])


def gather_small(row, axis):
    size = lax.axis_size(axis)
    inner = 1 << (size.bit_length() // 2)
    near = [[a * inner + b for b in range(inner)] for a in range(size // inner)]
    far = [[a * inner + b for a in range(size // inner)] for b in range(inner)]
    for groups in (near, far):
        row = row.reshape(-1)
        many = jnp.broadcast_to(row, (len(groups[0]),) + row.shape)
        row = lax.all_to_all(many, axis, 0, 0, tiled=True, axis_index_groups=groups)
    return row.reshape(-1)


def shards(values, lap_in, tangent, slot_electron, spin_up, w_self, w_spin, bias, readout, potential):
    walk_size, tan_size = lax.axis_size("walk"), lax.axis_size("tan")
    tan_rank, walk_rank = lax.axis_index("tan"), lax.axis_index("walk")
    walkers, own, feat = values.shape
    dirs = tangent.shape[1]
    electrons = slot_electron.shape[1]
    shape = jax.ShapeDtypeStruct
    smem = whole(pltpu.SMEM)
    flat = tangent.reshape(walkers * dirs * own, feat)
    bias_row, readout_row = bias.reshape(1, feat), readout.reshape(1, feat)

    value_sums = call(value_sums_kernel, shape((walkers, 4, feat), F32), [smem, whole(), whole(), whole()])(
        spin_up, slot_electron, values, lap_in)
    other_value_sums = flip(value_sums, "tan", 1)
    flat, value_sums = lax.optimization_barrier((flat, value_sums))

    values_all = lax.all_gather(values.reshape(walkers * own, feat), "walk", axis=0)

    block = 48
    chunks = walkers * dirs // block
    repeat = 8
    anywhere = whole(pl.ANY)
    held = [pltpu.VMEM(flat.shape, BF16), pltpu.SemaphoreType.DMA((chunks,))]
    sums = call(
        functools.partial(tangent_sums_kernel, own, block), shape((walkers, 2, dirs, feat), F32),
        [smem, whole(), anywhere], None, (),
        held + [pltpu.VMEM((walkers, 2 * repeat, repeat * own), BF16)],
        pl.CostEstimate(flops=2 * flat.size * 16, bytes_accessed=flat.size * 2, transcendentals=0),
    )(spin_up, slot_electron, flat)
    other_sums = flip(sums, "tan", 1)

    full = shape((walkers, own, feat), F32)
    base, curve, weighted, slopes = call(
        layer_kernel,
        (full, full, full, shape((walkers * (own + 24), feat), BF16)),
        [smem] + [whole()] * 9)(
            spin_up, slot_electron, values, lap_in, value_sums, other_value_sums, w_self, w_spin, bias_row, readout_row)
    slopes_all = lax.all_gather(slopes, "walk", axis=0)

    laplacian, partial = call(
        functools.partial(change_kernel, own, block),
        (full, shape((walkers, 8, 256), F32)),
        [smem, whole(), anywhere] + [whole()] * 8, None, (),
        held + [pltpu.VMEM((2, dirs, feat), F32), pltpu.VMEM((own, feat), F32), pltpu.VMEM((own, feat), F32),
                pltpu.VMEM((dirs * 8, feat // 2), F32)],
        pl.CostEstimate(flops=2 * flat.size * feat, bytes_accessed=flat.size * 2, transcendentals=0),
    )(spin_up, slot_electron, flat, sums, other_sums, w_self, w_spin, readout_row, base, curve, weighted)

    partial = partial[:, 0, :dirs + 1]
    both = partial + flip(partial, "tan", 1)
    energy = -0.5 * (both[:, dirs] + jnp.sum(both[:, :dirs] ** 2, axis=1)) + potential
    energies = gather_small(energy, "walk")
    grads = call(
        functools.partial(gradients_kernel, walkers, own), shape((2 * feat, feat), F32), [smem, whole(), whole()],
        scratch=[pltpu.VMEM((2, walkers * own, feat), BF16), pltpu.VMEM((8 * walkers, feat), F32)],
    )(energies, values_all, slopes_all)
    grads = grads + flip(grads, "tan", 1)
    return laplacian, energy, grads[:feat], grads[feat:]


def solution(mesh):
    placed = (
        P("walk", "tan", None),
        P("walk", "tan", None),
        P("walk", None, "tan", None),
        P("walk", None),
        P("walk"),
        P(),
        P(),
        P(),
        P(),
        P("walk"),
    )
    return jax.shard_map(
        shards,
        mesh=mesh,
        in_specs=placed,
        out_specs=(P("walk", "tan", None), P("walk"), P(), P()),
        check_vma=False,
    )
```

```python
import functools

import jax
import jax.numpy as jnp
from jax import lax
from jax.experimental import pallas as pl
from jax.experimental.pallas import tpu as pltpu
from jax.sharding import PartitionSpec as P

F32 = jnp.float32
BF16 = jnp.bfloat16
VMEM_LIMIT = 60 * 1024 * 1024
HIGHEST = lax.Precision.HIGHEST
FIRST = ((0,), (0,))
LAST = ((1,), (1,))


def iota(shape, axis):
    return lax.broadcasted_iota(jnp.int32, shape, axis)


def dot(a, b, dims=((1,), (0,)), precision=None):
    return lax.dot_general(a, b, (dims, ((), ())), precision=precision, preferred_element_type=F32)


def two_terms(array):
    high = array.astype(BF16)
    return high, (array - high.astype(F32)).astype(BF16)


def three_terms(array):
    high = array.astype(BF16)
    middle, low = two_terms(array - high.astype(F32))
    return jnp.concatenate([high, middle, low], axis=0)


def first_slot(own):
    return lax.axis_index("tan") * own


def upper_row(slot_ref, w, count):
    return (slot_ref[pl.ds(w, 1), :] < count).astype(F32)


def upper_column(slot_ref, w, count, own):
    row = upper_row(slot_ref, w, count)
    place = iota((own, row.shape[1]), 1) == iota((own, row.shape[1]), 0) + first_slot(own)
    return jnp.sum(jnp.where(place, row, 0.0), axis=1, keepdims=True)


def tiled_row(slot_ref, w, count, own, wide):
    row = upper_row(slot_ref, w, count).astype(BF16)
    electrons = row.shape[1]
    place = iota((electrons, wide), 0) == iota((electrons, wide), 1) % own + first_slot(own)
    return dot(jnp.broadcast_to(row, (8, electrons)), place.astype(BF16))[0:1]


def group_rows(slot_ref, w, count, own, repeat):
    wide = own * repeat
    tiled = tiled_row(slot_ref, w, count, own, wide)
    lane_part = iota((2 * repeat, wide), 1) // own
    line = iota((2 * repeat, wide), 0)
    chosen = jnp.where(line < repeat, tiled, 1.0 - tiled)
    return jnp.where(lane_part == line % repeat, chosen, 0.0).astype(BF16)


def pack_kernel(walkers, own, spin_ref, slot_ref, values_ref, lap_ref, sums_ref, packed_ref):
    rows, feat = values_ref.shape
    electrons = slot_ref.shape[1]
    lane = iota((2, feat), 1)
    pieces = []
    for w in range(walkers):
        count = spin_ref[w]
        tiled = tiled_row(slot_ref, w, count, own, feat)
        line = iota((2, feat), 0)
        ups = count.astype(F32)
        chosen = jnp.where(line == 0, tiled, 1.0 - tiled)
        size = jnp.where(line == 0, ups, electrons - ups)
        chosen = jnp.where(lane // own == w, chosen, 0.0)
        pieces.append(jnp.where(lane < rows, chosen, size))
    pieces.append(jnp.zeros((16 - 2 * walkers, feat), F32))
    groups = jnp.concatenate(pieces, axis=0).astype(BF16)
    packed_ref[0:rows, :] = values_ref[...]
    packed_ref[rows:, :] = groups
    sums_ref[0] = dot(groups[:, :rows], values_ref[...])
    sums_ref[1] = dot(groups[:, :rows], lap_ref[...])


def fetch(source_ref, held_ref, sems, base, chunk, i):
    at = pl.multiple_of(i * chunk, chunk)
    return pltpu.make_async_copy(
        source_ref.at[pl.ds(base + at, chunk)], held_ref.at[pl.ds(at, chunk)], sems.at[i])


def tangent_sums_kernel(own, block, window, base, spin_ref, slot_ref, tangent_ref, out_ref, held_ref, sems, mask_ref):
    walkers, _, dirs, _ = out_ref.shape
    repeat = mask_ref.shape[1] // 2
    rows, chunk, steps = repeat * own, block * own, dirs // block
    total = walkers * steps
    start = base * dirs * own
    for i in range(min(window, total)):
        fetch(tangent_ref, held_ref, sems, start, chunk, i).start()
    for w in range(walkers):
        mask_ref[w] = group_rows(slot_ref, base + w, spin_ref[base + w], own, repeat)

    @pl.loop(0, total)
    def _(i):
        w, step = i // steps, i % steps
        fetch(tangent_ref, held_ref, sems, start, chunk, i).wait()

        @pl.when(i + window < total)
        def _():
            fetch(tangent_ref, held_ref, sems, start, chunk, i + window).start()

        mask = mask_ref[w]
        for part in range(block // repeat):
            row = pl.multiple_of(i * chunk + part * rows, rows)
            sums = dot(mask, held_ref[pl.ds(row, rows), :])
            at = pl.ds(pl.multiple_of(step * block + part * repeat, repeat), repeat)
            out_ref[w, 0, at, :] = sums[:repeat]
            out_ref[w, 1, at, :] = sums[repeat:]


def picked_rows(groups, mixed):
    lines = jnp.concatenate([groups, groups, groups], axis=0)
    return dot(lines, three_terms(mixed), FIRST)


def layer_kernel(values_ref, lap_ref, packed_ref, own_ref, other_ref, w_self_ref, w_spin_ref,
                 bias_ref, readout_ref, base_ref, curve_ref, weighted_ref):
    rows, feat = values_ref.shape
    lines = packed_ref[rows:, :]
    groups = lines[:, :rows]
    sizes = jnp.maximum(lines[:, rows:rows + 1].astype(F32), 1.0)
    means = ((own_ref[...] + other_ref[...]) / sizes).astype(BF16)
    preact = dot(values_ref[...], w_self_ref[...]) + picked_rows(groups, dot(means[0], w_spin_ref[...])) + bias_ref[...]
    lap_pre = dot(lap_ref[...], w_self_ref[...]) + picked_rows(groups, dot(means[1], w_spin_ref[...]))
    squash = jnp.tanh(preact)
    slopes = 1.0 - squash * squash
    base_ref[...] = slopes * lap_pre
    curve_ref[...] = -2.0 * squash * slopes
    weighted_ref[...] = slopes * readout_ref[...]


def change_kernel(own, block, window, base, spin_ref, slot_ref, tangent_ref, own_ref, other_ref, w_self_ref,
                  w_spin_ref, readout_ref, base_ref, curve_ref, weighted_ref, lap_ref, grad_ref,
                  held_ref, sems, mixed_ref, squares_ref, column_ref, terms_ref):
    walkers, _, dirs, feat = own_ref.shape
    electrons = slot_ref.shape[1]
    chunk, steps, part = block * own, dirs // block, 8
    total = walkers * steps
    start = base * dirs * own
    for i in range(min(window, total)):
        fetch(tangent_ref, held_ref, sems, start, chunk, i).start()

    @pl.loop(0, walkers)
    def _(w):
        count = spin_ref[base + w]
        ups = count.astype(F32)
        mine = pl.ds(pl.multiple_of((base + w) * own, own), own)
        for g, size in enumerate((ups, electrons - ups)):
            means = ((own_ref[w, g] + other_ref[w, g]) / size).astype(BF16)
            mixed_ref[g] = dot(means, w_spin_ref[...])
        column_ref[...] = jnp.broadcast_to(upper_column(slot_ref, base + w, count, own), (own, feat))
        squares_ref[...] = jnp.zeros_like(squares_ref)

        @pl.loop(0, steps)
        def _(step):
            i = w * steps + step
            fetch(tangent_ref, held_ref, sems, start, chunk, i).wait()

            @pl.when(i + window < total)
            def _():
                fetch(tangent_ref, held_ref, sems, start, chunk, i + window).start()

            upper = column_ref[...] > 0.5
            weighted = weighted_ref[mine, :]
            squares = squares_ref[...]
            plain = dot(held_ref[pl.ds(pl.multiple_of(i * chunk, chunk), chunk), :], w_self_ref[...])
            for p in range(block // part):
                at = pl.multiple_of(step * block + p * part, part)
                mixed = mixed_ref[:, pl.ds(at, part), :]
                for d in range(part):
                    row = (p * part + d) * own
                    picked = jnp.where(upper, mixed[0, d:d + 1], mixed[1, d:d + 1])
                    change = plain[row:row + own] + picked
                    squares = squares + change * change
                    terms = (change * weighted).reshape(own // 8, 8, feat).sum(axis=0)
                    terms_ref[pl.ds(pl.multiple_of(at * 8 + d * 8, 8), 8), :] = (
                        terms[:, :feat // 2] + terms[:, feat // 2:])
            squares_ref[...] = squares

        laplacian = base_ref[mine, :] + curve_ref[mine, :] * squares_ref[...]
        lap_ref[w] = laplacian
        summed = terms_ref[...].reshape(dirs, 8, feat // 2).sum(axis=1)
        wide = grad_ref.shape[2]
        grad_ref[w, 0:1, 0:dirs] = dot(jnp.ones((8, feat // 2), F32), summed, LAST, HIGHEST)[0:1]
        grad_ref[w, 0:1, dirs:] = jnp.broadcast_to(jnp.sum(laplacian * readout_ref[...]), (1, wide - dirs))


def gradients_kernel(walkers, own, offsets, energy_ref, *refs):
    blocks, w_self_ref, w_spin_ref, bias_ref, readout_ref, out_ref, scratch = refs[:4], *refs[4:9], refs[9:]
    means_ref, mixed_ref, sums_ref, spread_ref, total_ref = scratch
    me = lax.axis_index("walk")
    lines, feat = blocks[0].shape[1:]
    rows = walkers * own
    half = blocks[0].shape[0]
    everyone = energy_ref.shape[0]
    center = lax.fori_loop(0, everyone, lambda i, total: total + energy_ref[i], jnp.float32(0.0)) / everyone
    group = lines - rows

    def both(side, r):
        pair = (blocks[side], blocks[side + 2])
        values = jnp.concatenate([block[r, 0:rows, :] for block in pair], axis=0)
        groups = jnp.concatenate([block[r, rows:, 0:rows] for block in pair], axis=1)
        return values, groups

    for side in range(2):
        @pl.loop(0, half)
        def _(r):
            values, groups = both(side, r)
            sizes = jnp.maximum(blocks[side][r, rows:, rows:rows + 1].astype(F32), 1.0)
            means = dot(groups, values) / sizes
            means_ref[pl.ds(pl.multiple_of((side * half + r) * group, group), group), :] = means.astype(BF16)

    mixed_ref[...] = dot(means_ref[...], w_spin_ref[...])
    total_ref[...] = jnp.zeros_like(total_ref)
    for side in range(2):
        @pl.loop(0, half)
        def _(r):
            at = pl.ds(pl.multiple_of((side * half + r) * group, group), group)
            values, groups = both(side, r)
            preact = dot(values, w_self_ref[...]) + picked_rows(groups, mixed_ref[at, :]) + bias_ref[...]
            squash = jnp.tanh(preact)
            slopes = ((1.0 - squash * squash) * readout_ref[...]).astype(BF16)
            sums_ref[at, :] = dot(groups, slopes)
            shift = 0
            for bit, offset in enumerate(offsets):
                shift = shift | (((side * half + r) >> bit) & 1) * offset
            first = (me ^ shift) * walkers
            wide = slopes.astype(F32)
            scaled = []
            line = iota((group, feat), 0) // 2
            spread = jnp.zeros((group, feat), F32)
            for w in range(walkers):
                spread = jnp.where(line == w, energy_ref[first + w] - center, spread)
            spread_ref[at, :] = spread
            for core in range(2):
                for w in range(walkers):
                    place = core * rows + w * own
                    scaled.append(wide[place:place + own] * (energy_ref[first + w] - center))
            high, low = two_terms(jnp.concatenate(scaled, axis=0))
            total_ref[...] += dot(values, high, FIRST) + dot(values, low, FIRST)

    out_ref[0:feat, :] = total_ref[...]
    means = means_ref[...]
    high, low = two_terms(sums_ref[...] * spread_ref[...])
    out_ref[feat:, :] = dot(means, high, FIRST) + dot(means, low, FIRST)


def whole(memory=pltpu.VMEM):
    return pl.BlockSpec(memory_space=memory)


def call(kernel, out_shape, in_specs, scratch=(), cost=None):
    flops, moved = cost if cost is not None else (0, 0)
    return pl.pallas_call(
        kernel,
        out_shape=out_shape,
        in_specs=in_specs,
        out_specs=jax.tree.map(lambda _: whole(), out_shape),
        scratch_shapes=scratch,
        cost_estimate=pl.CostEstimate(flops=flops, bytes_accessed=moved, transcendentals=0) if cost else None,
        compiler_params=pltpu.CompilerParams(vmem_limit_bytes=VMEM_LIMIT),
    )


def flip(array, axis, bit):
    size = lax.axis_size(axis)
    return lax.ppermute(array, axis, [(i, i ^ bit) for i in range(size)])


def tied(*arrays):
    return lax.optimization_barrier(arrays)


def shards(values, lap_in, tangent, slot_electron, spin_up, w_self, w_spin, bias, readout, potential):
    walk_size = lax.axis_size("walk")
    walkers, own, feat = values.shape
    dirs = tangent.shape[1]
    shape = jax.ShapeDtypeStruct
    smem, anywhere = whole(pltpu.SMEM), whole(pl.ANY)
    flat = tangent.reshape(walkers * dirs * own, feat)
    values, lap_in = values.reshape(walkers * own, feat), lap_in.reshape(walkers * own, feat)
    bias, readout = bias.reshape(1, feat), readout.reshape(1, feat)
    bits = [1 << b for b in reversed(range(walk_size.bit_length() - 1))]

    value_sums, packed = call(
        functools.partial(pack_kernel, walkers, own),
        (shape((2, 16, feat), F32), shape((walkers * own + 16, feat), BF16)),
        [smem, whole(), whole(), whole()])(spin_up, slot_electron, values, lap_in)
    other_value_sums = flip(value_sums, "tan", 1)
    gathered = packed.reshape((1,) + packed.shape)

    def doubled(gathered, bit):
        return jnp.concatenate([gathered, flip(gathered, "walk", bit)], axis=0)

    halves = 2
    count = walkers // halves
    part = count * dirs * own
    block, repeat = 24, 8
    chunks = count * dirs // block

    def tangent_sums(base, tangent_rows):
        return call(
            functools.partial(tangent_sums_kernel, own, block, 6, base), shape((count, 2, dirs, feat), F32),
            [smem, whole(), anywhere],
            [pltpu.VMEM((part, feat), BF16), pltpu.SemaphoreType.DMA((chunks,)),
             pltpu.VMEM((count, 2 * repeat, repeat * own), BF16)],
            (part * feat * 64, part * feat * 2),
        )(spin_up, slot_electron, tangent_rows)

    flat, packed = tied(flat, packed)
    early, late = bits[:len(bits) - 2], bits[len(bits) - 2:]
    sums = [tangent_sums(0, flat)]
    flat, other_value_sums, _ = tied(flat, other_value_sums, sums[0])
    sums.append(tangent_sums(count, flat))
    other_sums = [flip(s, "tan", 1) for s in sums]

    gathered = doubled(gathered, bits[0])
    gathered, sums[1] = tied(gathered, sums[1])
    full = shape((walkers * own, feat), F32)
    base, curve, weighted = call(
        layer_kernel, (full, full, full), [whole()] * 9, cost=(2 * feat * feat * walkers * own * 2, 4 << 20))(
            values, lap_in, packed, value_sums, other_value_sums, w_self, w_spin, bias, readout)

    wide = -(-(dirs + 1) // 128) * 128

    def change(h, tangent_rows):
        return call(
            functools.partial(change_kernel, own, 2 * block, 4, h * count),
            (shape((count, own, feat), F32), shape((count, 1, wide), F32)),
            [smem, whole(), anywhere] + [whole()] * 8,
            [pltpu.VMEM((part, feat), BF16), pltpu.SemaphoreType.DMA((chunks // 2,)),
             pltpu.VMEM((2, dirs, feat), F32), pltpu.VMEM((own, feat), F32), pltpu.VMEM((own, feat), F32),
             pltpu.VMEM((dirs * 8, feat // 2), F32)],
            (part * feat * feat * 4, part * feat * 2),
        )(spin_up, slot_electron, tangent_rows, sums[h], other_sums[h], w_self, w_spin, readout, base, curve, weighted)

    for bit in bits[1:-2]:
        gathered = doubled(gathered, bit)
    laplacian, partial = change(0, flat)
    gathered = doubled(gathered, bits[-2])
    flat, gathered, _ = tied(flat, gathered, partial)
    more_laplacian, more_partial = change(1, flat)
    gathered, more_partial = tied(gathered, more_partial)
    side = flip(gathered, "walk", bits[-1])
    partials = [p.reshape(count, wide) for p in (partial, more_partial)]
    both = jnp.concatenate([p + flip(p, "tan", 1) for p in partials], axis=0)
    energy = -0.5 * (both[:, dirs] + jnp.sum(both[:, :dirs] ** 2, axis=1)) + potential
    energies = lax.all_to_all(jnp.broadcast_to(energy, (walk_size, walkers)), "walk", 0, 0, tiled=True).reshape(-1)

    other, other_side = flip(gathered, "tan", 1), flip(side, "tan", 1)
    lines = walk_size * 16
    grads = call(
        functools.partial(gradients_kernel, walkers, own, bits), shape((2 * feat, feat), F32),
        [smem] + [whole()] * 8,
        [pltpu.VMEM((lines, feat), BF16), pltpu.VMEM((lines, feat), F32), pltpu.VMEM((lines, feat), F32),
         pltpu.VMEM((lines, feat), F32), pltpu.VMEM((feat, feat), F32)],
    )(energies, gathered, side, other, other_side, w_self, w_spin, bias, readout)
    return jnp.concatenate([laplacian, more_laplacian], axis=0), energy, grads[:feat], grads[feat:]


def solution(mesh):
    placed = (
        P("walk", "tan", None),
        P("walk", "tan", None),
        P("walk", None, "tan", None),
        P("walk", None),
        P("walk"),
        P(),
        P(),
        P(),
        P(),
        P("walk"),
    )
    return jax.shard_map(
        shards,
        mesh=mesh,
        in_specs=placed,
        out_specs=(P("walk", "tan", None), P("walk"), P(), P()),
        check_vma=False,
    )
```

```python
import functools

import jax
import jax.numpy as jnp
from jax import lax
from jax.experimental import pallas as pl
from jax.experimental.pallas import tpu as pltpu
from jax.sharding import PartitionSpec as P

F32 = jnp.float32
BF16 = jnp.bfloat16
VMEM_LIMIT = 24 * 1024 * 1024
HIGHEST = lax.Precision.HIGHEST
FIRST = ((0,), (0,))
LAST = ((1,), (1,))


def iota(shape, axis):
    return lax.broadcasted_iota(jnp.int32, shape, axis)


def dot(a, b, dims=((1,), (0,)), precision=None):
    return lax.dot_general(a, b, (dims, ((), ())), precision=precision, preferred_element_type=F32)


def two_terms(array):
    high = array.astype(BF16)
    return high, (array - high.astype(F32)).astype(BF16)


def three_terms(array):
    high = array.astype(BF16)
    middle, low = two_terms(array - high.astype(F32))
    return jnp.concatenate([high, middle, low], axis=0)


def first_slot(own):
    return lax.axis_index("tan") * own


def upper_row(slot_ref, w, count):
    return (slot_ref[pl.ds(w, 1), :] < count).astype(F32)


def upper_column(slot_ref, w, count, own):
    row = upper_row(slot_ref, w, count)
    place = iota((own, row.shape[1]), 1) == iota((own, row.shape[1]), 0) + first_slot(own)
    return jnp.sum(jnp.where(place, row, 0.0), axis=1, keepdims=True)


def own_places(electrons, own, wide):
    return (iota((electrons, wide), 0) == iota((electrons, wide), 1) % own + first_slot(own)).astype(BF16)


def group_rows(slot_ref, w, count, own, repeat):
    row = upper_row(slot_ref, w, count).astype(BF16)
    electrons, wide = row.shape[1], own * repeat
    tiled = dot(jnp.broadcast_to(row, (8, electrons)), own_places(electrons, own, wide))[0:1]
    lane_part = iota((2 * repeat, wide), 1) // own
    line = iota((2 * repeat, wide), 0)
    chosen = jnp.where(line < repeat, tiled, 1.0 - tiled)
    return jnp.where(lane_part == line % repeat, chosen, 0.0).astype(BF16)


def pack_kernel(walkers, own, spin_ref, slot_ref, values_ref, lap_ref, sums_ref, packed_ref):
    rows, feat = values_ref.shape
    electrons = slot_ref.shape[1]
    slots = jnp.zeros((2 * walkers, electrons), jnp.int32)
    for w in range(walkers):
        slots = jnp.where(iota(slots.shape, 0) // 2 == w, slot_ref[w:w + 1, :], slots)

    def column(shape):
        line = iota(shape, 0)
        count = jnp.zeros(shape, jnp.int32)
        for w in range(walkers):
            count = jnp.where(line // 2 == w, spin_ref[w], count)
        return line, count

    line, count = column(slots.shape)
    upper = (slots < count).astype(F32)
    chosen = jnp.where(line % 2 == 0, upper, 1.0 - upper).astype(BF16)
    tiled = dot(chosen, own_places(electrons, own, feat))
    line, count = column(tiled.shape)
    lane = iota(tiled.shape, 1)
    size = jnp.where(line % 2 == 0, count, electrons - count).astype(F32)
    groups = jnp.where(lane < rows, jnp.where(lane // own == line // 2, tiled, 0.0), size)
    groups = jnp.concatenate([groups, jnp.zeros((16 - 2 * walkers, feat), F32)], axis=0).astype(BF16)
    packed_ref[0:rows, :] = values_ref[...]
    packed_ref[rows:, :] = groups
    sums_ref[0] = dot(groups[:, :rows], values_ref[...])
    sums_ref[1] = dot(groups[:, :rows], lap_ref[...])


def tangent_sums_kernel(own, block, spin_ref, slot_ref, tangent_ref, out_ref, mask_ref):
    walkers, _, dirs, _ = out_ref.shape
    repeat = mask_ref.shape[1] // 2
    rows, steps = repeat * own, dirs // block
    for w in range(walkers):
        mask_ref[w] = group_rows(slot_ref, w, spin_ref[w], own, repeat)

    @pl.loop(0, walkers * steps)
    def _(i):
        w, step = i // steps, i % steps
        mask = mask_ref[w]
        for part in range(block // repeat):
            row = pl.multiple_of(i * block * own + part * rows, rows)
            sums = dot(mask, tangent_ref[pl.ds(row, rows), :])
            at = pl.ds(pl.multiple_of(step * block + part * repeat, repeat), repeat)
            out_ref[w, 0, at, :] = sums[:repeat]
            out_ref[w, 1, at, :] = sums[repeat:]


def picked_rows(groups, mixed):
    lines = jnp.concatenate([groups, groups, groups], axis=0)
    return dot(lines, three_terms(mixed), FIRST)


def layer_kernel(values_ref, lap_ref, packed_ref, own_ref, other_ref, w_self_ref, w_spin_ref,
                 bias_ref, readout_ref, base_ref, curve_ref, weighted_ref):
    rows, feat = values_ref.shape
    lines = packed_ref[rows:, :]
    groups = lines[:, :rows]
    sizes = jnp.maximum(lines[:, rows:rows + 1].astype(F32), 1.0)
    means = ((own_ref[...] + other_ref[...]) / sizes).astype(BF16)
    preact = dot(values_ref[...], w_self_ref[...]) + picked_rows(groups, dot(means[0], w_spin_ref[...])) + bias_ref[...]
    lap_pre = dot(lap_ref[...], w_self_ref[...]) + picked_rows(groups, dot(means[1], w_spin_ref[...]))
    squash = jnp.tanh(preact)
    slopes = 1.0 - squash * squash
    base_ref[...] = slopes * lap_pre
    curve_ref[...] = -2.0 * squash * slopes
    weighted_ref[...] = slopes * readout_ref[...]


def change_kernel(own, block, piece, base, spin_ref, slot_ref, tangent_ref, own_ref, other_ref, w_self_ref,
                  w_spin_ref, readout_ref, base_ref, curve_ref, weighted_ref, lap_ref, grad_ref,
                  mixed_ref, squares_ref, column_ref, terms_ref):
    walkers, feat = lap_ref.shape[0], w_self_ref.shape[0]
    dirs = own_ref.shape[2]
    electrons = slot_ref.shape[1]
    steps, part = dirs // block, 8
    grad_ref[...] = jnp.zeros_like(grad_ref)

    @pl.loop(0, walkers)
    def _(n):
        w = base + n
        count = spin_ref[w]
        ups = count.astype(F32)
        mine = pl.ds(pl.multiple_of(w * own, own), own)
        for g, size in enumerate((ups, electrons - ups)):
            means = ((own_ref[w, g] + other_ref[w, g]) / size).astype(BF16)
            mixed_ref[g] = dot(means, w_spin_ref[...])
        column_ref[...] = jnp.broadcast_to(upper_column(slot_ref, w, count, own), (own, feat))
        squares_ref[...] = jnp.zeros_like(squares_ref)

        @pl.loop(0, steps)
        def _(step):
            upper = column_ref[...] > 0.5
            weighted = weighted_ref[mine, :]
            squares = squares_ref[...]
            for c in range(block // piece):
                row = pl.multiple_of(((w * steps + step) * block + c * piece) * own, own)
                plain = dot(tangent_ref[pl.ds(row, piece * own), :], w_self_ref[...])
                for p in range(piece // part):
                    at = pl.multiple_of(step * block + c * piece + p * part, part)
                    mixed = mixed_ref[:, pl.ds(at, part), :]
                    for d in range(part):
                        row = (p * part + d) * own
                        picked = jnp.where(upper, mixed[0, d:d + 1], mixed[1, d:d + 1])
                        change = plain[row:row + own] + picked
                        squares = squares + change * change
                        terms = (change * weighted).reshape(own // 8, 8, feat).sum(axis=0)
                        terms_ref[pl.ds(pl.multiple_of(at * 8 + d * 8, 8), 8), :] = (
                            terms[:, :feat // 2] + terms[:, feat // 2:])
            squares_ref[...] = squares

        laplacian = base_ref[mine, :] + curve_ref[mine, :] * squares_ref[...]
        lap_ref[n] = laplacian
        summed = terms_ref[...].reshape(dirs, 8, feat // 2).sum(axis=1)
        spare = jnp.zeros((grad_ref.shape[1] - dirs, feat // 2), F32)
        summed = jnp.concatenate([summed, spare], axis=0)
        row = dot(jnp.ones((8, feat // 2), F32), summed, LAST, HIGHEST)
        row = jnp.where(iota(row.shape, 1) == dirs, jnp.sum(laplacian * readout_ref[...]), row)
        grad_ref[...] = jnp.where(iota(row.shape, 0) == n, row, grad_ref[...])


def energy_kernel(dirs, count, pot_ref, *refs):
    halves, out_ref = refs[:-1], refs[-1]
    lane = iota((1, 128), 1)
    row = jnp.zeros((1, 128), F32)
    for h in range(len(halves) // 2):
        both = halves[2 * h][...] + halves[2 * h + 1][...]
        place = iota(both.shape, 1)
        parts = jnp.where(place < dirs, both * both, jnp.where(place == dirs, both, 0.0))
        energy = -0.5 * jnp.sum(parts, axis=1, keepdims=True)
        for n in range(count):
            w = h * count + n
            row = jnp.where(lane == w, energy[n:n + 1] + pot_ref[w], row)
    out_ref[...] = jnp.broadcast_to(row.reshape(1, 1, 128), out_ref.shape)


def pair(own_ref, other_ref, rows, r):
    values = jnp.concatenate([ref[r, 0:rows, :] for ref in (own_ref, other_ref)], axis=0)
    groups = jnp.concatenate([ref[r, rows:, 0:rows] for ref in (own_ref, other_ref)], axis=1)
    return values, groups


def half_slopes(rows, own_ref, other_ref, w_self_ref, w_spin_ref, bias_ref, readout_ref,
                slopes_ref, sums_ref, means_ref):
    blocks, lines, _ = own_ref.shape
    group = lines - rows
    bunch = min(blocks, 8)

    @pl.loop(0, blocks // bunch)
    def _(i):
        pairs = [pair(own_ref, other_ref, rows, i * bunch + k) for k in range(bunch)]
        means = []
        for k, (values, groups) in enumerate(pairs):
            sizes = jnp.maximum(own_ref[i * bunch + k, rows:, rows:rows + 1].astype(F32), 1.0)
            means.append(dot(groups, values) / sizes)
        means = jnp.concatenate(means, axis=0).astype(BF16)
        at = pl.ds(pl.multiple_of(i * bunch * group, bunch * group), bunch * group)
        means_ref[at, :] = means
        mixed = dot(means, w_spin_ref[...])
        sums = []
        for k, (values, groups) in enumerate(pairs):
            preact = (dot(values, w_self_ref[...]) + picked_rows(groups, mixed[k * group:(k + 1) * group])
                      + bias_ref[...])
            squash = jnp.tanh(preact)
            slopes = ((1.0 - squash * squash) * readout_ref[...]).astype(BF16)
            row = pl.multiple_of((i * bunch + k) * 2 * rows, 2 * rows)
            slopes_ref[pl.ds(row, 2 * rows), :] = slopes
            sums.append(dot(groups, slopes))
        sums_ref[at, :] = jnp.concatenate(sums, axis=0)


def gradients_kernel(walkers, own, offsets, energy_ref, own_ref, other_ref, slopes_ref, sums_ref, means_ref,
                     own_side_ref, other_side_ref, w_self_ref, w_spin_ref, bias_ref, readout_ref,
                     self_ref, spin_ref, side_slopes_ref, side_sums_ref, side_means_ref):
    rows = walkers * own
    me = lax.axis_index("walk")
    half_slopes(rows, own_side_ref, other_side_ref, w_self_ref, w_spin_ref, bias_ref, readout_ref,
                side_slopes_ref, side_sums_ref, side_means_ref)
    blocks, lines, feat = own_ref.shape
    group = lines - rows
    bunch = min(blocks, 8)
    everyone = energy_ref.shape[0] * walkers
    center = jnp.sum(jnp.sum(energy_ref[...], axis=0), axis=1, keepdims=True) / everyone
    self_ref[...] = jnp.zeros_like(self_ref)
    spin_ref[...] = jnp.zeros_like(spin_ref)
    line = iota((group, feat), 0) // 2
    sides = ((own_ref, other_ref, slopes_ref, sums_ref, means_ref),
             (own_side_ref, other_side_ref, side_slopes_ref, side_sums_ref, side_means_ref))
    for side, (first_ref, second_ref, part_slopes, part_sums, part_means) in enumerate(sides):
        @pl.loop(0, blocks // bunch)
        def _(i):
            values, high, low, spreads = [], [], [], []
            for k in range(bunch):
                place = side * blocks + i * bunch + k
                shift = 0
                for bit, offset in enumerate(offsets):
                    shift = shift | ((place >> bit) & 1) * offset
                row = energy_ref[me ^ shift] - center
                row_at = pl.multiple_of((i * bunch + k) * 2 * rows, 2 * rows)
                slopes = part_slopes[pl.ds(row_at, 2 * rows), :].astype(F32)
                spread = jnp.zeros((group, feat), F32)
                for w in range(walkers):
                    spread = jnp.where(line == w, row[:, w:w + 1], spread)
                spreads.append(spread)
                for core in range(2):
                    for w in range(walkers):
                        at = core * rows + w * own
                        top, rest = two_terms(slopes[at:at + own] * row[:, w:w + 1])
                        high.append(top)
                        low.append(rest)
                values.append(pair(first_ref, second_ref, rows, i * bunch + k)[0])
            values = jnp.concatenate(values, axis=0)
            self_ref[...] += dot(values, jnp.concatenate(high, axis=0), FIRST) + dot(
                values, jnp.concatenate(low, axis=0), FIRST)
            at = pl.ds(pl.multiple_of(i * bunch * group, bunch * group), bunch * group)
            top, rest = two_terms(part_sums[at, :] * jnp.concatenate(spreads, axis=0))
            means = part_means[at, :]
            spin_ref[...] += dot(means, top, FIRST) + dot(means, rest, FIRST)


def whole(memory=pltpu.VMEM):
    return pl.BlockSpec(memory_space=memory)


def call(kernel, out_shape, in_specs, scratch=(), cost=None):
    flops, moved = cost if cost is not None else (0, 0)
    return pl.pallas_call(
        kernel,
        out_shape=out_shape,
        in_specs=in_specs,
        out_specs=jax.tree.map(lambda _: whole(), out_shape),
        scratch_shapes=scratch,
        cost_estimate=pl.CostEstimate(flops=flops, bytes_accessed=moved, transcendentals=0) if cost else None,
        compiler_params=pltpu.CompilerParams(vmem_limit_bytes=VMEM_LIMIT),
    )


def flip(array, axis, bit):
    size = lax.axis_size(axis)
    return lax.ppermute(array, axis, [(i, i ^ bit) for i in range(size)])


def tied(*arrays):
    return lax.optimization_barrier(arrays)


def shards(values, lap_in, tangent, slot_electron, spin_up, w_self, w_spin, bias, readout, potential):
    walk_size = lax.axis_size("walk")
    walkers, own, feat = values.shape
    dirs = tangent.shape[1]
    shape = jax.ShapeDtypeStruct
    smem, anywhere = whole(pltpu.SMEM), whole(pl.ANY)
    flat = tangent.reshape(walkers * dirs * own, feat)
    values, lap_in = values.reshape(walkers * own, feat), lap_in.reshape(walkers * own, feat)
    bias, readout = bias.reshape(1, feat), readout.reshape(1, feat)
    bits = [1 << b for b in reversed(range(walk_size.bit_length() - 1))]

    value_sums, packed = call(
        functools.partial(pack_kernel, walkers, own),
        (shape((2, 16, feat), F32), shape((walkers * own + 16, feat), BF16)),
        [smem, whole(), whole(), whole()])(spin_up, slot_electron, values, lap_in)
    other_value_sums = flip(value_sums, "tan", 1)
    gathered = packed.reshape((1,) + packed.shape)

    repeat, block, piece = 8, dirs // 2, dirs // 4
    sums = call(
        functools.partial(tangent_sums_kernel, own, block), shape((walkers, 2, dirs, feat), F32),
        [smem, whole(), whole()], [pltpu.VMEM((walkers, 2 * repeat, repeat * own), BF16)],
        (flat.size * 32, flat.size * 2))(spin_up, slot_electron, flat)
    received, sums, other_value_sums = tied(flip(gathered, "walk", bits[0]), sums, other_value_sums)
    gathered = jnp.concatenate([gathered, received], axis=0)
    other_sums = flip(sums, "tan", 1)
    for bit in bits[1:-3]:
        gathered = jnp.concatenate([gathered, flip(gathered, "walk", bit)], axis=0)
    received = flip(gathered, "walk", bits[-3])

    full = shape((walkers * own, feat), F32)
    base, curve, weighted = call(
        layer_kernel, (full, full, full), [whole()] * 9, cost=(4 * feat * feat * walkers * own, 4 << 20))(
            values, lap_in, packed, value_sums, other_value_sums, w_self, w_spin, bias, readout)

    halves = 2
    count = walkers // halves
    wide = -(-(dirs + 1) // 128) * 128

    def change(h, ups):
        return call(
            functools.partial(change_kernel, own, block, piece, h * count),
            (shape((count, own, feat), F32), shape((8, wide), F32)),
            [smem] + [whole()] * 10,
            [pltpu.VMEM((2, dirs, feat), F32), pltpu.VMEM((own, feat), F32), pltpu.VMEM((own, feat), F32),
             pltpu.VMEM((dirs * 8, feat // 2), F32)],
            (flat.size * feat, flat.size),
        )(ups, slot_electron, flat, sums, other_sums, w_self, w_spin, readout, base, curve, weighted)

    laplacian, partial = change(0, spin_up)
    received, late_spin_up, partial = tied(received, spin_up, partial)
    gathered = jnp.concatenate([gathered, received], axis=0)
    received = flip(gathered, "walk", bits[-2])
    more_laplacian, more_partial = change(1, late_spin_up)
    received, more_partial = tied(received, more_partial)
    gathered = jnp.concatenate([gathered, received], axis=0)
    side, other = flip(gathered, "walk", bits[-1]), flip(gathered, "tan", 1)
    partials = [p for own_part in (partial, more_partial) for p in (own_part, flip(own_part, "tan", 1))]
    rows = call(
        functools.partial(energy_kernel, dirs, count), shape((walk_size, 1, 128), F32), [smem] + [whole()] * 4)(
            potential, *partials)
    energy = rows[0, 0, :walkers]
    energies = lax.all_to_all(rows, "walk", 0, 0, tiled=True)
    other, _ = tied(other, rows)

    blocks = walk_size // 2
    group_shape = (blocks * 16, feat)
    half = [((blocks * 2 * walkers * own, feat), BF16), (group_shape, F32), (group_shape, BF16)]
    weights = (w_self, w_spin, bias, readout)
    slopes = call(
        functools.partial(half_slopes, walkers * own), tuple(shape(*h) for h in half), [whole()] * 6,
        cost=(blocks * 8 * walkers * own * feat * feat, 8 << 20))(gathered, other, *weights)
    side, _ = tied(side, slopes[1])
    other_side = flip(side, "tan", 1)
    square = shape((feat, feat), F32)
    grad_self, grad_spin = call(
        functools.partial(gradients_kernel, walkers, own, bits), (square, square), [whole()] * 12,
        [pltpu.VMEM(*h) for h in half])(energies, gathered, other, *slopes, side, other_side, *weights)
    return jnp.concatenate([laplacian, more_laplacian], axis=0), energy, grad_self, grad_spin


def solution(mesh):
    placed = (
        P("walk", "tan", None),
        P("walk", "tan", None),
        P("walk", None, "tan", None),
        P("walk", None),
        P("walk"),
        P(),
        P(),
        P(),
        P(),
        P("walk"),
    )
    return jax.shard_map(
        shards,
        mesh=mesh,
        in_specs=placed,
        out_specs=(P("walk", "tan", None), P("walk"), P(), P()),
        check_vma=False,
    )
```

```python
import functools

import jax
import jax.numpy as jnp
from jax import lax
from jax.experimental import pallas as pl
from jax.experimental.pallas import tpu as pltpu
from jax.sharding import PartitionSpec as P

F32 = jnp.float32
BF16 = jnp.bfloat16
MIB = 1024 * 1024
VMEM_LIMIT = 24 * MIB
HIGHEST = lax.Precision.HIGHEST
FIRST = ((0,), (0,))
LAST = ((1,), (1,))


def iota(shape, axis):
    return lax.broadcasted_iota(jnp.int32, shape, axis)


def dot(a, b, dims=((1,), (0,)), precision=None):
    return lax.dot_general(a, b, (dims, ((), ())), precision=precision, preferred_element_type=F32)


def two_terms(array):
    high = array.astype(BF16)
    return high, (array - high.astype(F32)).astype(BF16)


def three_terms(array):
    high = array.astype(BF16)
    middle, low = two_terms(array - high.astype(F32))
    return jnp.concatenate([high, middle, low], axis=0)


def first_slot(own):
    return lax.axis_index("tan") * own


def upper_row(slot_ref, w, count):
    return (slot_ref[pl.ds(w, 1), :] < count).astype(F32)


def upper_column(slot_ref, w, count, own):
    row = upper_row(slot_ref, w, count)
    place = iota((own, row.shape[1]), 1) == iota((own, row.shape[1]), 0) + first_slot(own)
    return jnp.sum(jnp.where(place, row, 0.0), axis=1, keepdims=True)


def own_places(electrons, own, wide):
    return (iota((electrons, wide), 0) == iota((electrons, wide), 1) % own + first_slot(own)).astype(BF16)


def group_rows(slot_ref, w, count, own, repeat):
    row = upper_row(slot_ref, w, count).astype(BF16)
    electrons, wide = row.shape[1], own * repeat
    tiled = dot(jnp.broadcast_to(row, (8, electrons)), own_places(electrons, own, wide))[0:1]
    lane_part = iota((2 * repeat, wide), 1) // own
    line = iota((2 * repeat, wide), 0)
    chosen = jnp.where(line < repeat, tiled, 1.0 - tiled)
    return jnp.where(lane_part == line % repeat, chosen, 0.0).astype(BF16)


def pack_kernel(walkers, own, spin_ref, slot_far, values_far, lap_far, sums_ref, packed_ref, slot_ref, lap_ref, sems):
    rows, feat = lap_ref.shape
    electrons = slot_ref.shape[1]
    values_ref = packed_ref.at[pl.ds(0, rows)]
    copies = [pltpu.make_async_copy(far, near, sems.at[i]) for i, (far, near) in enumerate(
        ((slot_far, slot_ref), (values_far, values_ref), (lap_far, lap_ref)))]
    for copy in copies:
        copy.start()
    copies[0].wait()
    slots = jnp.zeros((2 * walkers, electrons), jnp.int32)
    for w in range(walkers):
        slots = jnp.where(iota(slots.shape, 0) // 2 == w, slot_ref[w:w + 1, :], slots)

    def column(shape):
        line = iota(shape, 0)
        count = jnp.zeros(shape, jnp.int32)
        for w in range(walkers):
            count = jnp.where(line // 2 == w, spin_ref[w], count)
        return line, count

    line, count = column(slots.shape)
    upper = (slots < count).astype(F32)
    chosen = jnp.where(line % 2 == 0, upper, 1.0 - upper).astype(BF16)
    tiled = dot(chosen, own_places(electrons, own, feat))
    line, count = column(tiled.shape)
    lane = iota(tiled.shape, 1)
    size = jnp.where(line % 2 == 0, count, electrons - count).astype(F32)
    groups = jnp.where(lane < rows, jnp.where(lane // own == line // 2, tiled, 0.0), size)
    groups = jnp.concatenate([groups, jnp.zeros((16 - 2 * walkers, feat), F32)], axis=0).astype(BF16)
    packed_ref[rows:, :] = groups
    copies[1].wait()
    copies[2].wait()
    sums_ref[0] = dot(groups[:, :rows], values_ref[...])
    sums_ref[1] = dot(groups[:, :rows], lap_ref[...])


def tangent_sums_kernel(own, block, spin_ref, slot_ref, far_ref, out_ref, tangent_ref, mask_ref, sems):
    walkers, _, dirs, _ = out_ref.shape
    repeat = mask_ref.shape[1] // 2
    rows, steps, chunk = repeat * own, dirs // block, block * own

    def fetch(i):
        at = pl.ds(pl.multiple_of(i * chunk, chunk), chunk)
        return pltpu.make_async_copy(far_ref.at[at], tangent_ref.at[at], sems.at[i])

    for i in range(walkers * steps):
        fetch(i).start()
    for w in range(walkers):
        mask_ref[w] = group_rows(slot_ref, w, spin_ref[w], own, repeat)

    @pl.loop(0, walkers * steps)
    def _(i):
        w, step = i // steps, i % steps
        mask = mask_ref[w]
        fetch(i).wait()
        for part in range(block // repeat):
            row = pl.multiple_of(i * chunk + part * rows, rows)
            sums = dot(mask, tangent_ref[pl.ds(row, rows), :])
            at = pl.ds(pl.multiple_of(step * block + part * repeat, repeat), repeat)
            out_ref[w, 0, at, :] = sums[:repeat]
            out_ref[w, 1, at, :] = sums[repeat:]


def picked_rows(groups, mixed):
    lines = jnp.concatenate([groups, groups, groups], axis=0)
    return dot(lines, three_terms(mixed), FIRST)


def layer_kernel(values_ref, lap_ref, packed_ref, own_ref, other_ref, w_self_ref, w_spin_ref,
                 bias_ref, readout_ref, base_ref, curve_ref, weighted_ref):
    rows, feat = values_ref.shape
    lines = packed_ref[rows:, :]
    groups = lines[:, :rows]
    sizes = jnp.maximum(lines[:, rows:rows + 1].astype(F32), 1.0)
    means = ((own_ref[...] + other_ref[...]) / sizes).astype(BF16)
    preact = dot(values_ref[...], w_self_ref[...]) + picked_rows(groups, dot(means[0], w_spin_ref[...])) + bias_ref[...]
    lap_pre = dot(lap_ref[...], w_self_ref[...]) + picked_rows(groups, dot(means[1], w_spin_ref[...]))
    squash = jnp.tanh(preact)
    slopes = 1.0 - squash * squash
    base_ref[...] = slopes * lap_pre
    curve_ref[...] = -2.0 * squash * slopes
    weighted_ref[...] = slopes * readout_ref[...]


def change_kernel(own, piece, base, spin_ref, slot_ref, tangent_ref, own_ref, other_ref, w_self_ref,
                  w_spin_ref, readout_ref, base_ref, curve_ref, weighted_ref, lap_ref, grad_ref,
                  mixed_ref, column_ref, terms_ref, *plain_refs):
    walkers, feat = lap_ref.shape[0], w_self_ref.shape[0]
    dirs = own_ref.shape[2]
    electrons = slot_ref.shape[1]
    steps, part = dirs // piece, 8
    grad_ref[...] = jnp.zeros_like(grad_ref)

    def multiply(i, plain_ref):
        row = pl.multiple_of((base * steps + i) * piece * own, own)
        plain_ref[...] = dot(tangent_ref[pl.ds(row, piece * own), :], w_self_ref[...])

    multiply(0, plain_refs[0])

    @pl.loop(0, walkers)
    def _(n):
        w = base + n
        count = spin_ref[w]
        ups = count.astype(F32)
        mine = pl.ds(pl.multiple_of(w * own, own), own)
        for g, size in enumerate((ups, electrons - ups)):
            means = ((own_ref[w, g] + other_ref[w, g]) / size).astype(BF16)
            mixed_ref[g] = dot(means, w_spin_ref[...])
        column_ref[...] = jnp.broadcast_to(upper_column(slot_ref, w, count, own), (own, feat))
        upper = column_ref[...] > 0.5
        weighted = weighted_ref[mine, :]
        squares = jnp.zeros((own, feat), F32)
        for c in range(steps):
            plain_ref = plain_refs[c % 2]
            multiply(jnp.minimum(n * steps + c + 1, walkers * steps - 1), plain_refs[(c + 1) % 2])
            for p in range(piece // part):
                at = c * piece + p * part
                mixed = mixed_ref[:, at:at + part, :]
                for d in range(part):
                    row = (p * part + d) * own
                    picked = jnp.where(upper, mixed[0, d:d + 1], mixed[1, d:d + 1])
                    change = plain_ref[row:row + own, :] + picked
                    squares = squares + change * change
                    terms = (change * weighted).reshape(own // 8, 8, feat).sum(axis=0)
                    terms_ref[(at + d) * 8:(at + d + 1) * 8, :] = terms[:, :feat // 2] + terms[:, feat // 2:]

        laplacian = base_ref[mine, :] + curve_ref[mine, :] * squares
        lap_ref[n] = laplacian
        summed = terms_ref[...].reshape(dirs, 8, feat // 2).sum(axis=1)
        spare = jnp.zeros((grad_ref.shape[1] - dirs, feat // 2), F32)
        summed = jnp.concatenate([summed, spare], axis=0)
        row = dot(jnp.ones((8, feat // 2), F32), summed, LAST, HIGHEST)
        row = jnp.where(iota(row.shape, 1) == dirs, jnp.sum(laplacian * readout_ref[...]), row)
        grad_ref[...] = jnp.where(iota(row.shape, 0) == n, row, grad_ref[...])


def energy_kernel(dirs, count, pot_ref, *refs):
    halves, out_ref = refs[:-1], refs[-1]
    lane = iota((1, 128), 1)
    row = jnp.zeros((1, 128), F32)
    for h in range(len(halves) // 2):
        both = halves[2 * h][...] + halves[2 * h + 1][...]
        place = iota(both.shape, 1)
        parts = jnp.where(place < dirs, both * both, jnp.where(place == dirs, both, 0.0))
        energy = -0.5 * jnp.sum(parts, axis=1, keepdims=True)
        for n in range(count):
            w = h * count + n
            row = jnp.where(lane == w, energy[n:n + 1] + pot_ref[w], row)
    out_ref[...] = jnp.broadcast_to(row.reshape(1, 1, 128), out_ref.shape)


def pair(own_ref, other_ref, rows, r):
    values = jnp.concatenate([ref[r, 0:rows, :] for ref in (own_ref, other_ref)], axis=0)
    groups = jnp.concatenate([ref[r, rows:, 0:rows] for ref in (own_ref, other_ref)], axis=1)
    return values, groups


def half_slopes(rows, own_ref, other_ref, w_self_ref, w_spin_ref, bias_ref, readout_ref,
                slopes_ref, sums_ref, means_ref):
    blocks, lines, _ = own_ref.shape
    group = lines - rows
    bunch = min(blocks, 8)

    @pl.loop(0, blocks // bunch)
    def _(i):
        pairs = [pair(own_ref, other_ref, rows, i * bunch + k) for k in range(bunch)]
        means = []
        for k, (values, groups) in enumerate(pairs):
            sizes = jnp.maximum(own_ref[i * bunch + k, rows:, rows:rows + 1].astype(F32), 1.0)
            means.append(dot(groups, values) / sizes)
        means = jnp.concatenate(means, axis=0).astype(BF16)
        at = pl.ds(pl.multiple_of(i * bunch * group, bunch * group), bunch * group)
        means_ref[at, :] = means
        mixed = dot(means, w_spin_ref[...])
        sums = []
        for k, (values, groups) in enumerate(pairs):
            preact = (dot(values, w_self_ref[...]) + picked_rows(groups, mixed[k * group:(k + 1) * group])
                      + bias_ref[...])
            squash = jnp.tanh(preact)
            slopes = ((1.0 - squash * squash) * readout_ref[...]).astype(BF16)
            row = pl.multiple_of((i * bunch + k) * 2 * rows, 2 * rows)
            slopes_ref[pl.ds(row, 2 * rows), :] = slopes
            sums.append(dot(groups, slopes))
        sums_ref[at, :] = jnp.concatenate(sums, axis=0)


def add_products(walkers, own, offsets, first, energy_ref, own_ref, other_ref, slopes_ref, sums_ref, means_ref,
                 self_ref, spin_ref):
    rows = walkers * own
    me = lax.axis_index("walk")
    blocks, lines, feat = own_ref.shape
    group = lines - rows
    bunch = min(blocks, 8)
    everyone = energy_ref.shape[0] * walkers
    center = jnp.sum(jnp.sum(energy_ref[...], axis=0), axis=1, keepdims=True) / everyone
    line = iota((group, feat), 0) // 2

    @pl.loop(0, blocks // bunch)
    def _(i):
        values, high, low, spreads = [], [], [], []
        for k in range(bunch):
            place = first + i * bunch + k
            shift = 0
            for bit, offset in enumerate(offsets):
                shift = shift | ((place >> bit) & 1) * offset
            row = energy_ref[me ^ shift] - center
            row_at = pl.multiple_of((i * bunch + k) * 2 * rows, 2 * rows)
            slopes = slopes_ref[pl.ds(row_at, 2 * rows), :].astype(F32)
            spread = jnp.zeros((group, feat), F32)
            for w in range(walkers):
                spread = jnp.where(line == w, row[:, w:w + 1], spread)
            spreads.append(spread)
            for core in range(2):
                for w in range(walkers):
                    at = core * rows + w * own
                    top, rest = two_terms(slopes[at:at + own] * row[:, w:w + 1])
                    high.append(top)
                    low.append(rest)
            values.append(pair(own_ref, other_ref, rows, i * bunch + k)[0])
        values = jnp.concatenate(values, axis=0)
        self_ref[...] += dot(values, jnp.concatenate(high, axis=0), FIRST) + dot(
            values, jnp.concatenate(low, axis=0), FIRST)
        at = pl.ds(pl.multiple_of(i * bunch * group, bunch * group), bunch * group)
        top, rest = two_terms(sums_ref[at, :] * jnp.concatenate(spreads, axis=0))
        means = means_ref[at, :]
        spin_ref[...] += dot(means, top, FIRST) + dot(means, rest, FIRST)


def first_gradients_kernel(walkers, own, offsets, *refs):
    self_ref, spin_ref = refs[-2:]
    self_ref[...] = jnp.zeros_like(self_ref)
    spin_ref[...] = jnp.zeros_like(spin_ref)
    add_products(walkers, own, offsets, 0, *refs)


def last_gradients_kernel(walkers, own, offsets, energy_ref, own_ref, other_ref, w_self_ref, w_spin_ref, bias_ref,
                          readout_ref, first_self_ref, first_spin_ref, self_ref, spin_ref, *scratch):
    half_slopes(walkers * own, own_ref, other_ref, w_self_ref, w_spin_ref, bias_ref, readout_ref, *scratch)
    self_ref[...] = first_self_ref[...]
    spin_ref[...] = first_spin_ref[...]
    add_products(walkers, own, offsets, own_ref.shape[0], energy_ref, own_ref, other_ref, *scratch, self_ref, spin_ref)


def whole(memory=pltpu.VMEM):
    return pl.BlockSpec(memory_space=memory)


def call(kernel, out_shape, in_specs, scratch=(), cost=None, limit=VMEM_LIMIT):
    flops, moved = cost if cost is not None else (0, 0)
    return pl.pallas_call(
        kernel,
        out_shape=out_shape,
        in_specs=in_specs,
        out_specs=jax.tree.map(lambda _: whole(), out_shape),
        scratch_shapes=scratch,
        cost_estimate=pl.CostEstimate(flops=flops, bytes_accessed=moved, transcendentals=0) if cost else None,
        compiler_params=pltpu.CompilerParams(vmem_limit_bytes=limit),
    )


def flip(array, axis, bit):
    size = lax.axis_size(axis)
    return lax.ppermute(array, axis, [(i, i ^ bit) for i in range(size)])


def tied(*arrays):
    return lax.optimization_barrier(arrays)


def shards(values, lap_in, tangent, slot_electron, spin_up, w_self, w_spin, bias, readout, potential):
    walk_size = lax.axis_size("walk")
    walkers, own, feat = values.shape
    dirs = tangent.shape[1]
    shape = jax.ShapeDtypeStruct
    smem = whole(pltpu.SMEM)
    flat = tangent.reshape(walkers * dirs * own, feat)
    values, lap_in = values.reshape(walkers * own, feat), lap_in.reshape(walkers * own, feat)
    bias, readout = bias.reshape(1, feat), readout.reshape(1, feat)
    bits = [1 << b for b in reversed(range(walk_size.bit_length() - 1))]

    value_sums, packed = call(
        functools.partial(pack_kernel, walkers, own),
        (shape((2, 16, feat), F32), shape((walkers * own + 16, feat), BF16)),
        [smem] + [whole(pltpu.HBM)] * 3,
        [pltpu.VMEM(slot_electron.shape, jnp.int32), pltpu.VMEM(lap_in.shape, BF16), pltpu.SemaphoreType.DMA((3,))],
        limit=63 * MIB)(spin_up, slot_electron, values, lap_in)
    other_value_sums = flip(value_sums, "tan", 1)
    gathered = packed.reshape((1,) + packed.shape)

    repeat, block, piece = 8, dirs // 2, dirs // 4
    sums, held = call(
        functools.partial(tangent_sums_kernel, own, block),
        (shape((walkers, 2, dirs, feat), F32), shape(flat.shape, BF16)),
        [smem, whole(), whole(pltpu.HBM)],
        [pltpu.VMEM((walkers, 2 * repeat, repeat * own), BF16), pltpu.SemaphoreType.DMA((walkers * dirs // block,))],
        (flat.size * 32, flat.size * 2), 36 * MIB)(spin_up, slot_electron, flat)
    received, sums, other_value_sums = tied(flip(gathered, "walk", bits[0]), sums, other_value_sums)
    gathered = jnp.concatenate([gathered, received], axis=0)
    other_sums = flip(sums, "tan", 1)
    for bit in bits[1:-3]:
        gathered = jnp.concatenate([gathered, flip(gathered, "walk", bit)], axis=0)
    received = flip(gathered, "walk", bits[-3])

    full = shape((walkers * own, feat), F32)
    base, curve, weighted = call(
        layer_kernel, (full, full, full), [whole()] * 9, cost=(4 * feat * feat * walkers * own, 4 << 20))(
            values, lap_in, packed, value_sums, other_value_sums, w_self, w_spin, bias, readout)

    halves = 2
    count = walkers // halves
    wide = -(-(dirs + 1) // 128) * 128

    def change(h, ups):
        return call(
            functools.partial(change_kernel, own, piece, h * count),
            (shape((count, own, feat), F32), shape((8, wide), F32)),
            [smem] + [whole()] * 10,
            [pltpu.VMEM((2, dirs, feat), F32), pltpu.VMEM((own, feat), F32), pltpu.VMEM((dirs * 8, feat // 2), F32),
             pltpu.VMEM((piece * own, feat), F32), pltpu.VMEM((piece * own, feat), F32)],
            (flat.size * feat, flat.size),
        )(ups, slot_electron, held, sums, other_sums, w_self, w_spin, readout, base, curve, weighted)

    laplacian, partial = change(0, spin_up)
    received, late_spin_up, partial = tied(received, spin_up, partial)
    gathered = jnp.concatenate([gathered, received], axis=0)
    received = flip(gathered, "walk", bits[-2])
    more_laplacian, more_partial = change(1, late_spin_up)
    received, more_partial = tied(received, more_partial)
    gathered = jnp.concatenate([gathered, received], axis=0)
    side, other = flip(gathered, "walk", bits[-1]), flip(gathered, "tan", 1)
    partials = [p for own_part in (partial, more_partial) for p in (own_part, flip(own_part, "tan", 1))]
    rows = call(
        functools.partial(energy_kernel, dirs, count), shape((walk_size, 1, 128), F32), [smem] + [whole()] * 4)(
            potential, *partials)
    energy = rows[0, 0, :walkers]
    energies = lax.all_to_all(rows, "walk", 0, 0, tiled=True)
    other, _ = tied(other, rows)

    blocks = walk_size // 2
    group_shape = (blocks * 16, feat)
    half = [((blocks * 2 * walkers * own, feat), BF16), (group_shape, F32), (group_shape, BF16)]
    weights = (w_self, w_spin, bias, readout)
    slopes = call(
        functools.partial(half_slopes, walkers * own), tuple(shape(*h) for h in half), [whole()] * 6,
        cost=(blocks * 8 * walkers * own * feat * feat, 8 << 20))(gathered, other, *weights)
    energies, side, *slopes = tied(energies, side, *slopes)
    other_side = flip(side, "tan", 1)
    square = shape((feat, feat), F32)
    settings = walkers, own, bits
    first = call(
        functools.partial(first_gradients_kernel, *settings), (square, square), [whole()] * 6,
        cost=(blocks * 16 * walkers * own * feat * feat, 8 << 20))(energies, gathered, other, *slopes)
    grad_self, grad_spin = call(
        functools.partial(last_gradients_kernel, *settings), (square, square), [whole()] * 9,
        [pltpu.VMEM(*h) for h in half])(energies, side, other_side, *weights, *first)
    return jnp.concatenate([laplacian, more_laplacian], axis=0), energy, grad_self, grad_spin


def solution(mesh):
    placed = (
        P("walk", "tan", None),
        P("walk", "tan", None),
        P("walk", None, "tan", None),
        P("walk", None),
        P("walk"),
        P(),
        P(),
        P(),
        P(),
        P("walk"),
    )
    return jax.shard_map(
        shards,
        mesh=mesh,
        in_specs=placed,
        out_specs=(P("walk", "tan", None), P("walk"), P(), P()),
        check_vma=False,
    )
```

```python
import functools

import jax
import jax.numpy as jnp
from jax import lax
from jax.experimental import pallas as pl
from jax.experimental.pallas import tpu as pltpu
from jax.sharding import PartitionSpec as P

F32 = jnp.float32
BF16 = jnp.bfloat16
MIB = 1024 * 1024
VMEM_LIMIT = 24 * MIB
HIGHEST = lax.Precision.HIGHEST
FIRST = ((0,), (0,))
LAST = ((1,), (1,))


def iota(shape, axis):
    return lax.broadcasted_iota(jnp.int32, shape, axis)


def dot(a, b, dims=((1,), (0,)), precision=None):
    return lax.dot_general(a, b, (dims, ((), ())), precision=precision, preferred_element_type=F32)


def two_terms(array):
    high = array.astype(BF16)
    return high, (array - high.astype(F32)).astype(BF16)


def three_terms(array):
    high = array.astype(BF16)
    middle, low = two_terms(array - high.astype(F32))
    return jnp.concatenate([high, middle, low], axis=0)


def first_slot(own):
    return lax.axis_index("tan") * own


def upper_row(slot_ref, w, count):
    return (slot_ref[pl.ds(w, 1), :] < count).astype(F32)


def upper_column(slot_ref, w, count, own):
    row = upper_row(slot_ref, w, count)
    place = iota((own, row.shape[1]), 1) == iota((own, row.shape[1]), 0) + first_slot(own)
    return jnp.sum(jnp.where(place, row, 0.0), axis=1, keepdims=True)


def own_places(electrons, own, wide):
    return (iota((electrons, wide), 0) == iota((electrons, wide), 1) % own + first_slot(own)).astype(BF16)


def head_kernel(walkers, own, block, spin_ref, slot_far, values_far, lap_far, tangent_far,
                packed_far, value_sums_far, sums_far,
                slot_ref, values_ref, lines_ref, value_sums_ref, mask_ref, tangent_ref, sums_ref,
                small_sems, sums_sems, sems):
    _, rows, feat = values_ref.shape
    electrons, dirs = slot_ref.shape[1], sums_ref.shape[2]
    repeat = mask_ref.shape[1] // 2
    steps, chunk = dirs // block, block * own
    total = walkers * steps

    def fetch(i):
        at = pl.ds(pl.multiple_of(i * chunk, chunk), chunk)
        return pltpu.make_async_copy(tangent_far.at[at], tangent_ref.at[at], sems.at[i])

    def leave(w):
        return pltpu.make_async_copy(sums_ref.at[w], sums_far.at[w], sums_sems.at[w])

    near = [pltpu.make_async_copy(*ends, small_sems.at[i]) for i, ends in enumerate(
        ((slot_far, slot_ref), (values_far, values_ref.at[0]), (lap_far, values_ref.at[1]),
         (values_far, packed_far.at[pl.ds(0, rows)])))]
    far = [pltpu.make_async_copy(*ends, small_sems.at[4 + i]) for i, ends in enumerate(
        ((lines_ref, packed_far.at[pl.ds(rows, 16)]), (value_sums_ref, value_sums_far)))]
    for copy in near:
        copy.start()
    for i in range(total):
        fetch(i).start()
    near[0].wait()
    slots = jnp.zeros((2 * walkers, electrons), jnp.int32)
    for w in range(walkers):
        slots = jnp.where(iota(slots.shape, 0) // 2 == w, slot_ref[w:w + 1, :], slots)

    def column(shape):
        line = iota(shape, 0)
        count = jnp.zeros(shape, jnp.int32)
        for w in range(walkers):
            count = jnp.where(line // 2 == w, spin_ref[w], count)
        return line, count

    line, count = column(slots.shape)
    upper = (slots < count).astype(F32)
    chosen = jnp.where(line % 2 == 0, upper, 1.0 - upper).astype(BF16)
    tiled = dot(chosen, own_places(electrons, own, feat))
    line, count = column(tiled.shape)
    lane = iota(tiled.shape, 1)
    size = jnp.where(line % 2 == 0, count, electrons - count).astype(F32)
    groups = jnp.where(lane < rows, jnp.where(lane // own == line // 2, tiled, 0.0), size)
    groups = jnp.concatenate([groups, jnp.zeros((16 - 2 * walkers, feat), F32)], axis=0).astype(BF16)
    lines_ref[...] = groups
    far[0].start()
    place = iota((repeat, feat), 1) // own == iota((repeat, feat), 0)
    for w in range(walkers):
        both = [jnp.where(place, tiled[2 * w + g:2 * w + g + 1], 0.0) for g in range(2)]
        mask_ref[w] = jnp.concatenate(both, axis=0).astype(BF16)
    near[1].wait()
    near[2].wait()
    for kind in range(2):
        value_sums_ref[kind] = dot(groups[:, :rows], values_ref[kind])
    far[1].start()

    @pl.loop(0, total)
    def _(i):
        w, step = i // steps, i % steps
        mask = mask_ref[w]
        fetch(i).wait()
        for part in range(block // repeat):
            row = pl.multiple_of(i * chunk + part * repeat * own, repeat * own)
            sums = dot(mask, tangent_ref[pl.ds(row, repeat * own), :])
            at = pl.ds(pl.multiple_of(step * block + part * repeat, repeat), repeat)
            sums_ref[w, 0, at, :] = sums[:repeat]
            sums_ref[w, 1, at, :] = sums[repeat:]

        @pl.when(step == steps - 1)
        def _():
            leave(w).start()

    for w in range(walkers):
        leave(w).wait()
    near[3].wait()
    far[0].wait()
    far[1].wait()


def picked_rows(groups, mixed):
    lines = jnp.concatenate([groups, groups, groups], axis=0)
    return dot(lines, three_terms(mixed), FIRST)


def layer_kernel(values_ref, lap_ref, packed_ref, own_ref, other_ref, w_self_ref, w_spin_ref,
                 bias_ref, readout_ref, base_ref, curve_ref, weighted_ref):
    rows, feat = values_ref.shape
    lines = packed_ref[rows:, :]
    groups = lines[:, :rows]
    sizes = jnp.maximum(lines[:, rows:rows + 1].astype(F32), 1.0)
    means = ((own_ref[...] + other_ref[...]) / sizes).astype(BF16)
    preact = dot(values_ref[...], w_self_ref[...]) + picked_rows(groups, dot(means[0], w_spin_ref[...])) + bias_ref[...]
    lap_pre = dot(lap_ref[...], w_self_ref[...]) + picked_rows(groups, dot(means[1], w_spin_ref[...]))
    squash = jnp.tanh(preact)
    slopes = 1.0 - squash * squash
    base_ref[...] = slopes * lap_pre
    curve_ref[...] = -2.0 * squash * slopes
    weighted_ref[...] = slopes * readout_ref[...]


def change_kernel(own, piece, base, spin_ref, slot_ref, tangent_ref, own_ref, other_ref, w_self_ref,
                  w_spin_ref, readout_ref, base_ref, curve_ref, weighted_ref, lap_ref, grad_ref,
                  mixed_ref, column_ref, terms_ref, held_ref, both_ref, sums_sems, sems):
    walkers, feat = lap_ref.shape[0], w_self_ref.shape[0]
    dirs = own_ref.shape[2]
    electrons = slot_ref.shape[1]
    steps, part = dirs // piece, 8
    chunk = piece * own
    rows = chunk // 2

    def bring(n, k):
        return pltpu.make_async_copy((own_ref, other_ref)[k].at[base + n], both_ref.at[k, n], sums_sems.at[2 * n + k])

    def fetch(i):
        from_row = pl.ds(pl.multiple_of((base * steps + i) * chunk, chunk), chunk)
        return pltpu.make_async_copy(
            tangent_ref.at[from_row], held_ref.at[pl.ds(pl.multiple_of(i * chunk, chunk), chunk)], sems.at[i])

    for n in range(walkers):
        for k in range(2):
            bring(n, k).start()
        for c in range(steps):
            fetch(n * steps + c).start()
    grad_ref[...] = jnp.zeros_like(grad_ref)

    @pl.loop(0, walkers)
    def _(n):
        w = base + n
        count = spin_ref[w]
        ups = count.astype(F32)
        mine = pl.ds(pl.multiple_of(w * own, own), own)
        for k in range(2):
            bring(n, k).wait()
        for g, size in enumerate((ups, electrons - ups)):
            means = ((both_ref[0, n, g] + both_ref[1, n, g]) / size).astype(BF16)
            mixed_ref[g] = dot(means, w_spin_ref[...])
        column_ref[...] = jnp.broadcast_to(upper_column(slot_ref, w, count, own), (own, feat))
        upper = column_ref[...] > 0.5
        weighted = weighted_ref[mine, :]
        squares = jnp.zeros((own, feat), F32)
        for c in range(steps):
            fetch(n * steps + c).wait()
        for c in range(steps):
            first = pl.multiple_of((n * steps + c) * chunk, chunk)
            plain = [dot(held_ref[pl.ds(first + h * rows, rows), :], w_self_ref[...]) for h in range(2)]
            for p in range(piece // part):
                at = c * piece + p * part
                mixed = mixed_ref[:, at:at + part, :]
                for d in range(part):
                    row = (p * part + d) * own
                    picked = jnp.where(upper, mixed[0, d:d + 1], mixed[1, d:d + 1])
                    change = plain[row // rows][row % rows:row % rows + own] + picked
                    squares = squares + change * change
                    terms = (change * weighted).reshape(own // 8, 8, feat).sum(axis=0)
                    terms_ref[(at + d) * 8:(at + d + 1) * 8, :] = terms[:, :feat // 2] + terms[:, feat // 2:]

        laplacian = base_ref[mine, :] + curve_ref[mine, :] * squares
        lap_ref[n] = laplacian
        summed = terms_ref[...].reshape(dirs, 8, feat // 2).sum(axis=1)
        spare = jnp.zeros((grad_ref.shape[1] - dirs, feat // 2), F32)
        summed = jnp.concatenate([summed, spare], axis=0)
        row = dot(jnp.ones((8, feat // 2), F32), summed, LAST, HIGHEST)
        row = jnp.where(iota(row.shape, 1) == dirs, jnp.sum(laplacian * readout_ref[...]), row)
        grad_ref[...] = jnp.where(iota(row.shape, 0) == n, row, grad_ref[...])


def energy_kernel(dirs, counts, pot_ref, *refs):
    halves, out_ref = refs[:-1], refs[-1]
    lane = iota((1, 128), 1)
    row = jnp.zeros((1, 128), F32)
    for h, count in enumerate(counts):
        both = halves[2 * h][...] + halves[2 * h + 1][...]
        place = iota(both.shape, 1)
        parts = jnp.where(place < dirs, both * both, jnp.where(place == dirs, both, 0.0))
        energy = -0.5 * jnp.sum(parts, axis=1, keepdims=True)
        for n in range(count):
            w = sum(counts[:h]) + n
            row = jnp.where(lane == w, energy[n:n + 1] + pot_ref[w], row)
    out_ref[...] = jnp.broadcast_to(row.reshape(1, 1, 128), out_ref.shape)


def pair(own_ref, other_ref, rows, r):
    values = jnp.concatenate([ref[r, 0:rows, :] for ref in (own_ref, other_ref)], axis=0)
    groups = jnp.concatenate([ref[r, rows:, 0:rows] for ref in (own_ref, other_ref)], axis=1)
    return values, groups


def half_slopes(rows, own_ref, other_ref, w_self_ref, w_spin_ref, bias_ref, readout_ref,
                slopes_ref, sums_ref, means_ref):
    blocks, lines, _ = own_ref.shape
    group = lines - rows
    bunch = min(blocks, 8)

    @pl.loop(0, blocks // bunch)
    def _(i):
        pairs = [pair(own_ref, other_ref, rows, i * bunch + k) for k in range(bunch)]
        means = []
        for k, (values, groups) in enumerate(pairs):
            sizes = jnp.maximum(own_ref[i * bunch + k, rows:, rows:rows + 1].astype(F32), 1.0)
            means.append(dot(groups, values) / sizes)
        means = jnp.concatenate(means, axis=0).astype(BF16)
        at = pl.ds(pl.multiple_of(i * bunch * group, bunch * group), bunch * group)
        means_ref[at, :] = means
        mixed = dot(means, w_spin_ref[...])
        sums = []
        for k, (values, groups) in enumerate(pairs):
            preact = (dot(values, w_self_ref[...]) + picked_rows(groups, mixed[k * group:(k + 1) * group])
                      + bias_ref[...])
            squash = jnp.tanh(preact)
            slopes = ((1.0 - squash * squash) * readout_ref[...]).astype(BF16)
            row = pl.multiple_of((i * bunch + k) * 2 * rows, 2 * rows)
            slopes_ref[pl.ds(row, 2 * rows), :] = slopes
            sums.append(dot(groups, slopes))
        sums_ref[at, :] = jnp.concatenate(sums, axis=0)


def add_products(walkers, own, offsets, first, energy_ref, own_ref, other_ref, slopes_ref, sums_ref, means_ref,
                 self_ref, spin_ref):
    rows = walkers * own
    me = lax.axis_index("walk")
    blocks, lines, feat = own_ref.shape
    group = lines - rows
    bunch = min(blocks, 8)
    everyone = energy_ref.shape[0] * walkers
    center = jnp.sum(jnp.sum(energy_ref[...], axis=0), axis=1, keepdims=True) / everyone
    line = iota((group, feat), 0) // 2

    @pl.loop(0, blocks // bunch)
    def _(i):
        values, high, low, spreads = [], [], [], []
        for k in range(bunch):
            place = first + i * bunch + k
            shift = 0
            for bit, offset in enumerate(offsets):
                shift = shift | ((place >> bit) & 1) * offset
            row = energy_ref[me ^ shift] - center
            row_at = pl.multiple_of((i * bunch + k) * 2 * rows, 2 * rows)
            slopes = slopes_ref[pl.ds(row_at, 2 * rows), :].astype(F32)
            spread = jnp.zeros((group, feat), F32)
            for w in range(walkers):
                spread = jnp.where(line == w, row[:, w:w + 1], spread)
            spreads.append(spread)
            for core in range(2):
                for w in range(walkers):
                    at = core * rows + w * own
                    top, rest = two_terms(slopes[at:at + own] * row[:, w:w + 1])
                    high.append(top)
                    low.append(rest)
            values.append(pair(own_ref, other_ref, rows, i * bunch + k)[0])
        values = jnp.concatenate(values, axis=0)
        self_ref[...] += dot(values, jnp.concatenate(high, axis=0), FIRST) + dot(
            values, jnp.concatenate(low, axis=0), FIRST)
        at = pl.ds(pl.multiple_of(i * bunch * group, bunch * group), bunch * group)
        top, rest = two_terms(sums_ref[at, :] * jnp.concatenate(spreads, axis=0))
        means = means_ref[at, :]
        spin_ref[...] += dot(means, top, FIRST) + dot(means, rest, FIRST)


def first_gradients_kernel(walkers, own, offsets, *refs):
    self_ref, spin_ref = refs[-2:]
    self_ref[...] = jnp.zeros_like(self_ref)
    spin_ref[...] = jnp.zeros_like(spin_ref)
    add_products(walkers, own, offsets, 0, *refs)


def last_gradients_kernel(walkers, own, offsets, energy_ref, own_ref, other_ref, w_self_ref, w_spin_ref, bias_ref,
                          readout_ref, first_self_ref, first_spin_ref, self_ref, spin_ref, *scratch):
    half_slopes(walkers * own, own_ref, other_ref, w_self_ref, w_spin_ref, bias_ref, readout_ref, *scratch)
    self_ref[...] = first_self_ref[...]
    spin_ref[...] = first_spin_ref[...]
    add_products(walkers, own, offsets, own_ref.shape[0], energy_ref, own_ref, other_ref, *scratch, self_ref, spin_ref)


def whole(memory=pltpu.VMEM):
    return pl.BlockSpec(memory_space=memory)


def call(kernel, out_shape, in_specs, scratch=(), cost=None, limit=VMEM_LIMIT, out_specs=None):
    flops, moved = cost if cost is not None else (0, 0)
    return pl.pallas_call(
        kernel,
        out_shape=out_shape,
        in_specs=in_specs,
        out_specs=jax.tree.map(lambda _: whole(), out_shape) if out_specs is None else out_specs,
        scratch_shapes=scratch,
        cost_estimate=pl.CostEstimate(flops=flops, bytes_accessed=moved, transcendentals=0) if cost else None,
        compiler_params=pltpu.CompilerParams(vmem_limit_bytes=limit),
    )


def flip(array, axis, bit):
    size = lax.axis_size(axis)
    return lax.ppermute(array, axis, [(i, i ^ bit) for i in range(size)])


def tied(*arrays):
    return lax.optimization_barrier(arrays)


def shards(values, lap_in, tangent, slot_electron, spin_up, w_self, w_spin, bias, readout, potential):
    walk_size = lax.axis_size("walk")
    walkers, own, feat = values.shape
    dirs = tangent.shape[1]
    shape = jax.ShapeDtypeStruct
    smem = whole(pltpu.SMEM)
    flat = tangent.reshape(walkers * dirs * own, feat)
    values, lap_in = values.reshape(walkers * own, feat), lap_in.reshape(walkers * own, feat)
    bias, readout = bias.reshape(1, feat), readout.reshape(1, feat)
    bits = [1 << b for b in reversed(range(walk_size.bit_length() - 1))]

    repeat, block, piece = feat // own, dirs // 2, dirs // 4
    sums_shape, small = (walkers, 2, dirs, feat), (2, 16, feat)
    packed, value_sums, sums = call(
        functools.partial(head_kernel, walkers, own, block),
        (shape((walkers * own + 16, feat), BF16), shape(small, F32), shape(sums_shape, F32)),
        [smem] + [whole(pltpu.HBM)] * 4,
        [pltpu.VMEM(slot_electron.shape, jnp.int32), pltpu.VMEM((2,) + values.shape, BF16),
         pltpu.VMEM((16, feat), BF16), pltpu.VMEM(small, F32), pltpu.VMEM((walkers, 2 * repeat, feat), BF16),
         pltpu.VMEM(flat.shape, BF16), pltpu.VMEM(sums_shape, F32), pltpu.SemaphoreType.DMA((6,)),
         pltpu.SemaphoreType.DMA((walkers,)), pltpu.SemaphoreType.DMA((walkers * dirs // block,))],
        (flat.size * 32, flat.size * 2), 63 * MIB, (whole(pltpu.HBM),) * 3)(
            spin_up, slot_electron, values, lap_in, flat)
    gathered = packed.reshape((1,) + packed.shape)
    other_value_sums, other_sums = flip(value_sums, "tan", 1), flip(sums, "tan", 1)

    def doubled(gathered, received):
        return jnp.concatenate([gathered, received], axis=0)

    for bit in bits[:-4]:
        gathered = doubled(gathered, flip(gathered, "walk", bit))
    received = flip(gathered, "walk", bits[-4])
    full = shape((walkers * own, feat), F32)
    base, curve, weighted = call(
        layer_kernel, (full, full, full), [whole()] * 9, cost=(4 * feat * feat * walkers * own, 4 << 20), limit=62 * MIB)(
            values, lap_in, packed, value_sums, other_value_sums, w_self, w_spin, bias, readout)

    counts = (1, walkers - 2, 1)
    wide = -(-(dirs + 1) // 128) * 128

    def change(h, ups):
        return call(
            functools.partial(change_kernel, own, piece, sum(counts[:h])),
            (shape((counts[h], own, feat), F32), shape((8, wide), F32)),
            [smem, whole()] + [whole(pltpu.HBM)] * 3 + [whole()] * 6,
            [pltpu.VMEM((2, dirs, feat), F32), pltpu.VMEM((own, feat), F32), pltpu.VMEM((dirs * 8, feat // 2), F32),
             pltpu.VMEM((counts[h] * dirs * own, feat), BF16), pltpu.VMEM((2, counts[h], 2, dirs, feat), F32),
             pltpu.SemaphoreType.DMA((2 * counts[h],)), pltpu.SemaphoreType.DMA((counts[h] * dirs // piece,))],
            (flat.size * feat * counts[h] // 2, flat.size), 62 * MIB,
        )(ups, slot_electron, flat, sums, other_sums, w_self, w_spin, readout, base, curve, weighted)

    laplacians, partials, ups = [], [], spin_up
    for h, bit in enumerate((bits[-3], bits[-2], None)):
        laplacian, partial = change(h, ups)
        received, ups, partial = tied(received, ups, partial)
        gathered = doubled(gathered, received)
        received = flip(gathered, "walk", bit) if bit else None
        laplacians.append(laplacian)
        partials.append(partial)
    side, other = flip(gathered, "walk", bits[-1]), flip(gathered, "tan", 1)
    partials = [p for partial in partials for p in (partial, flip(partial, "tan", 1))]
    rows = call(
        functools.partial(energy_kernel, dirs, counts), shape((walk_size, 1, 128), F32), [smem] + [whole()] * 6)(
            potential, *partials)
    energy = rows[0, 0, :walkers]
    energies = lax.all_to_all(rows, "walk", 0, 0, tiled=True)
    other, _ = tied(other, rows)

    blocks = walk_size // 2
    group_shape = (blocks * 16, feat)
    half = [((blocks * 2 * walkers * own, feat), BF16), (group_shape, F32), (group_shape, BF16)]
    weights = (w_self, w_spin, bias, readout)
    slopes = call(
        functools.partial(half_slopes, walkers * own), tuple(shape(*h) for h in half), [whole()] * 6,
        cost=(blocks * 8 * walkers * own * feat * feat, 8 << 20))(gathered, other, *weights)
    laplacian = jnp.concatenate(laplacians, axis=0)
    energies, side, laplacian, energy, *slopes = tied(energies, side, laplacian, energy, *slopes)
    other_side = flip(side, "tan", 1)
    square = shape((feat, feat), F32)
    settings = walkers, own, bits
    first = call(
        functools.partial(first_gradients_kernel, *settings), (square, square), [whole()] * 6,
        cost=(blocks * 16 * walkers * own * feat * feat, 8 << 20))(energies, gathered, other, *slopes)
    grad_self, grad_spin = call(
        functools.partial(last_gradients_kernel, *settings), (square, square), [whole()] * 9,
        [pltpu.VMEM(*h) for h in half])(energies, side, other_side, *weights, *first)
    return laplacian, energy, grad_self, grad_spin


def solution(mesh):
    placed = (
        P("walk", "tan", None),
        P("walk", "tan", None),
        P("walk", None, "tan", None),
        P("walk", None),
        P("walk"),
        P(),
        P(),
        P(),
        P(),
        P("walk"),
    )
    return jax.shard_map(
        shards,
        mesh=mesh,
        in_specs=placed,
        out_specs=(P("walk", "tan", None), P("walk"), P(), P()),
        check_vma=False,
    )
```

```python
import functools

import jax
import jax.numpy as jnp
from jax import lax
from jax.experimental import pallas as pl
from jax.experimental.pallas import tpu as pltpu
from jax.sharding import PartitionSpec as P

F32 = jnp.float32
BF16 = jnp.bfloat16
MIB = 1024 * 1024
VMEM_LIMIT = 24 * MIB
HIGHEST = lax.Precision.HIGHEST
FIRST = ((0,), (0,))
LAST = ((1,), (1,))


def iota(shape, axis):
    return lax.broadcasted_iota(jnp.int32, shape, axis)


def dot(a, b, dims=((1,), (0,)), precision=None):
    return lax.dot_general(a, b, (dims, ((), ())), precision=precision, preferred_element_type=F32)


def two_terms(array):
    high = array.astype(BF16)
    return high, (array - high.astype(F32)).astype(BF16)


def three_terms(array):
    high = array.astype(BF16)
    middle, low = two_terms(array - high.astype(F32))
    return jnp.concatenate([high, middle, low], axis=0)


def first_slot(own):
    return lax.axis_index("tan") * own


def upper_row(slot_ref, w, count):
    return (slot_ref[pl.ds(w, 1), :] < count).astype(F32)


def upper_column(slot_ref, w, count, own):
    row = upper_row(slot_ref, w, count)
    place = iota((own, row.shape[1]), 1) == iota((own, row.shape[1]), 0) + first_slot(own)
    return jnp.sum(jnp.where(place, row, 0.0), axis=1, keepdims=True)


def own_places(electrons, own, wide):
    return (iota((electrons, wide), 0) == iota((electrons, wide), 1) % own + first_slot(own)).astype(BF16)


def pack_kernel(walkers, own, spin_ref, slot_far, values_far, lap_far, packed_far, value_sums_far,
                slot_ref, values_ref, lines_ref, value_sums_ref, small_sems):
    _, rows, feat = values_ref.shape
    electrons = slot_ref.shape[1]
    near = [pltpu.make_async_copy(*ends, small_sems.at[i]) for i, ends in enumerate(
        ((slot_far, slot_ref), (values_far, values_ref.at[0]), (lap_far, values_ref.at[1]),
         (values_far, packed_far.at[pl.ds(0, rows)])))]
    far = [pltpu.make_async_copy(*ends, small_sems.at[4 + i]) for i, ends in enumerate(
        ((lines_ref, packed_far.at[pl.ds(rows, 16)]), (value_sums_ref, value_sums_far)))]
    for copy in near:
        copy.start()
    near[0].wait()
    slots = jnp.zeros((2 * walkers, electrons), jnp.int32)
    for w in range(walkers):
        slots = jnp.where(iota(slots.shape, 0) // 2 == w, slot_ref[w:w + 1, :], slots)

    def column(shape):
        line = iota(shape, 0)
        count = jnp.zeros(shape, jnp.int32)
        for w in range(walkers):
            count = jnp.where(line // 2 == w, spin_ref[w], count)
        return line, count

    line, count = column(slots.shape)
    upper = (slots < count).astype(F32)
    chosen = jnp.where(line % 2 == 0, upper, 1.0 - upper).astype(BF16)
    tiled = dot(chosen, own_places(electrons, own, feat))
    line, count = column(tiled.shape)
    lane = iota(tiled.shape, 1)
    size = jnp.where(line % 2 == 0, count, electrons - count).astype(F32)
    groups = jnp.where(lane < rows, jnp.where(lane // own == line // 2, tiled, 0.0), size)
    groups = jnp.concatenate([groups, jnp.zeros((16 - 2 * walkers, feat), F32)], axis=0).astype(BF16)
    lines_ref[...] = groups
    far[0].start()
    near[1].wait()
    near[2].wait()
    for kind in range(2):
        value_sums_ref[kind] = dot(groups[:, :rows], values_ref[kind])
    far[1].start()
    near[3].wait()
    far[0].wait()
    far[1].wait()


def sums_kernel(walkers, own, block, packed_ref, far_ref, out_ref, tangent_ref, mask_ref, sems):
    dirs = out_ref.shape[2]
    rows, feat = walkers * own, packed_ref.shape[1]
    repeat = mask_ref.shape[1] // 2
    steps, chunk = dirs // block, block * own

    def fetch(i):
        at = pl.ds(pl.multiple_of(i * chunk, chunk), chunk)
        return pltpu.make_async_copy(far_ref.at[at], tangent_ref.at[at], sems.at[i])

    for i in range(walkers * steps):
        fetch(i).start()
    spots = (iota((rows, feat), 0) % own == iota((rows, feat), 1) % own).astype(F32).astype(BF16)
    tiled = dot(packed_ref[rows:, :rows], spots)
    place = iota((repeat, feat), 1) // own == iota((repeat, feat), 0)
    for w in range(walkers):
        both = [jnp.where(place, tiled[2 * w + g:2 * w + g + 1], 0.0) for g in range(2)]
        mask_ref[w] = jnp.concatenate(both, axis=0).astype(BF16)

    @pl.loop(0, walkers * steps)
    def _(i):
        w, step = i // steps, i % steps
        mask = mask_ref[w]
        fetch(i).wait()
        for part in range(block // repeat):
            row = pl.multiple_of(i * chunk + part * repeat * own, repeat * own)
            sums = dot(mask, tangent_ref[pl.ds(row, repeat * own), :])
            at = pl.ds(pl.multiple_of(step * block + part * repeat, repeat), repeat)
            out_ref[w, 0, at, :] = sums[:repeat]
            out_ref[w, 1, at, :] = sums[repeat:]


def picked_rows(groups, mixed):
    lines = jnp.concatenate([groups, groups, groups], axis=0)
    return dot(lines, three_terms(mixed), FIRST)


def layer_kernel(values_ref, lap_ref, packed_ref, own_ref, other_ref, w_self_ref, w_spin_ref,
                 bias_ref, readout_ref, base_ref, curve_ref, weighted_ref):
    rows, feat = values_ref.shape
    lines = packed_ref[rows:, :]
    groups = lines[:, :rows]
    sizes = jnp.maximum(lines[:, rows:rows + 1].astype(F32), 1.0)
    means = ((own_ref[...] + other_ref[...]) / sizes).astype(BF16)
    preact = dot(values_ref[...], w_self_ref[...]) + picked_rows(groups, dot(means[0], w_spin_ref[...])) + bias_ref[...]
    lap_pre = dot(lap_ref[...], w_self_ref[...]) + picked_rows(groups, dot(means[1], w_spin_ref[...]))
    squash = jnp.tanh(preact)
    slopes = 1.0 - squash * squash
    base_ref[...] = slopes * lap_pre
    curve_ref[...] = -2.0 * squash * slopes
    weighted_ref[...] = slopes * readout_ref[...]


def change_kernel(own, block, piece, base, spin_ref, slot_ref, tangent_ref, own_ref, other_ref, w_self_ref,
                  w_spin_ref, readout_ref, base_ref, curve_ref, weighted_ref, lap_ref, grad_ref,
                  mixed_ref, squares_ref, column_ref, terms_ref):
    walkers, feat = lap_ref.shape[0], w_self_ref.shape[0]
    dirs = own_ref.shape[2]
    electrons = slot_ref.shape[1]
    steps, part = dirs // block, 8
    grad_ref[...] = jnp.zeros_like(grad_ref)

    @pl.loop(0, walkers)
    def _(n):
        w = base + n
        count = spin_ref[w]
        ups = count.astype(F32)
        mine = pl.ds(pl.multiple_of(w * own, own), own)
        for g, size in enumerate((ups, electrons - ups)):
            means = ((own_ref[w, g] + other_ref[w, g]) / size).astype(BF16)
            mixed_ref[g] = dot(means, w_spin_ref[...])
        column_ref[...] = jnp.broadcast_to(upper_column(slot_ref, w, count, own), (own, feat))
        squares_ref[...] = jnp.zeros_like(squares_ref)

        @pl.loop(0, steps)
        def _(step):
            upper = column_ref[...] > 0.5
            weighted = weighted_ref[mine, :]
            squares = squares_ref[...]
            for c in range(block // piece):
                row = pl.multiple_of(((w * steps + step) * block + c * piece) * own, own)
                plain = dot(tangent_ref[pl.ds(row, piece * own), :], w_self_ref[...])
                for p in range(piece // part):
                    at = pl.multiple_of(step * block + c * piece + p * part, part)
                    mixed = mixed_ref[:, pl.ds(at, part), :]
                    for d in range(part):
                        row = (p * part + d) * own
                        picked = jnp.where(upper, mixed[0, d:d + 1], mixed[1, d:d + 1])
                        change = plain[row:row + own] + picked
                        squares = squares + change * change
                        terms = (change * weighted).reshape(own // 8, 8, feat).sum(axis=0)
                        terms_ref[pl.ds(pl.multiple_of(at * 8 + d * 8, 8), 8), :] = (
                            terms[:, :feat // 2] + terms[:, feat // 2:])
            squares_ref[...] = squares

        laplacian = base_ref[mine, :] + curve_ref[mine, :] * squares_ref[...]
        lap_ref[n] = laplacian
        summed = terms_ref[...].reshape(dirs, 8, feat // 2).sum(axis=1)
        spare = jnp.zeros((grad_ref.shape[1] - dirs, feat // 2), F32)
        summed = jnp.concatenate([summed, spare], axis=0)
        row = dot(jnp.ones((8, feat // 2), F32), summed, LAST, HIGHEST)
        row = jnp.where(iota(row.shape, 1) == dirs, jnp.sum(laplacian * readout_ref[...]), row)
        grad_ref[...] = jnp.where(iota(row.shape, 0) == n, row, grad_ref[...])


def energy_kernel(dirs, counts, pot_ref, *refs):
    halves, out_ref = refs[:-1], refs[-1]
    lane = iota((1, 128), 1)
    row = jnp.zeros((1, 128), F32)
    for h, count in enumerate(counts):
        both = halves[2 * h][...] + halves[2 * h + 1][...]
        place = iota(both.shape, 1)
        parts = jnp.where(place < dirs, both * both, jnp.where(place == dirs, both, 0.0))
        energy = -0.5 * jnp.sum(parts, axis=1, keepdims=True)
        for n in range(count):
            w = sum(counts[:h]) + n
            row = jnp.where(lane == w, energy[n:n + 1] + pot_ref[w], row)
    out_ref[...] = jnp.broadcast_to(row.reshape(1, 1, 128), out_ref.shape)


def pair(own_ref, other_ref, rows, r):
    values = jnp.concatenate([ref[r, 0:rows, :] for ref in (own_ref, other_ref)], axis=0)
    groups = jnp.concatenate([ref[r, rows:, 0:rows] for ref in (own_ref, other_ref)], axis=1)
    return values, groups


def half_slopes(rows, own_ref, other_ref, w_self_ref, w_spin_ref, bias_ref, readout_ref,
                slopes_ref, sums_ref, means_ref):
    blocks, lines, _ = own_ref.shape
    group = lines - rows
    bunch = min(blocks, 8)

    @pl.loop(0, blocks // bunch)
    def _(i):
        pairs = [pair(own_ref, other_ref, rows, i * bunch + k) for k in range(bunch)]
        means = []
        for k, (values, groups) in enumerate(pairs):
            sizes = jnp.maximum(own_ref[i * bunch + k, rows:, rows:rows + 1].astype(F32), 1.0)
            means.append(dot(groups, values) / sizes)
        means = jnp.concatenate(means, axis=0).astype(BF16)
        at = pl.ds(pl.multiple_of(i * bunch * group, bunch * group), bunch * group)
        means_ref[at, :] = means
        mixed = dot(means, w_spin_ref[...])
        sums = []
        for k, (values, groups) in enumerate(pairs):
            preact = (dot(values, w_self_ref[...]) + picked_rows(groups, mixed[k * group:(k + 1) * group])
                      + bias_ref[...])
            squash = jnp.tanh(preact)
            slopes = ((1.0 - squash * squash) * readout_ref[...]).astype(BF16)
            row = pl.multiple_of((i * bunch + k) * 2 * rows, 2 * rows)
            slopes_ref[pl.ds(row, 2 * rows), :] = slopes
            sums.append(dot(groups, slopes))
        sums_ref[at, :] = jnp.concatenate(sums, axis=0)


def add_products(walkers, own, offsets, first, energy_ref, own_ref, other_ref, slopes_ref, sums_ref, means_ref,
                 self_ref, spin_ref):
    rows = walkers * own
    me = lax.axis_index("walk")
    blocks, lines, feat = own_ref.shape
    group = lines - rows
    bunch = min(blocks, 8)
    everyone = energy_ref.shape[0] * walkers
    center = jnp.sum(jnp.sum(energy_ref[...], axis=0), axis=1, keepdims=True) / everyone
    line = iota((group, feat), 0) // 2

    @pl.loop(0, blocks // bunch)
    def _(i):
        values, high, low, spreads = [], [], [], []
        for k in range(bunch):
            place = first + i * bunch + k
            shift = 0
            for bit, offset in enumerate(offsets):
                shift = shift | ((place >> bit) & 1) * offset
            row = energy_ref[me ^ shift] - center
            row_at = pl.multiple_of((i * bunch + k) * 2 * rows, 2 * rows)
            slopes = slopes_ref[pl.ds(row_at, 2 * rows), :].astype(F32)
            spread = jnp.zeros((group, feat), F32)
            for w in range(walkers):
                spread = jnp.where(line == w, row[:, w:w + 1], spread)
            spreads.append(spread)
            for core in range(2):
                for w in range(walkers):
                    at = core * rows + w * own
                    top, rest = two_terms(slopes[at:at + own] * row[:, w:w + 1])
                    high.append(top)
                    low.append(rest)
            values.append(pair(own_ref, other_ref, rows, i * bunch + k)[0])
        values = jnp.concatenate(values, axis=0)
        self_ref[...] += dot(values, jnp.concatenate(high, axis=0), FIRST) + dot(
            values, jnp.concatenate(low, axis=0), FIRST)
        at = pl.ds(pl.multiple_of(i * bunch * group, bunch * group), bunch * group)
        top, rest = two_terms(sums_ref[at, :] * jnp.concatenate(spreads, axis=0))
        means = means_ref[at, :]
        spin_ref[...] += dot(means, top, FIRST) + dot(means, rest, FIRST)


def first_gradients_kernel(walkers, own, offsets, *refs):
    self_ref, spin_ref = refs[-2:]
    self_ref[...] = jnp.zeros_like(self_ref)
    spin_ref[...] = jnp.zeros_like(spin_ref)
    add_products(walkers, own, offsets, 0, *refs)


def last_gradients_kernel(walkers, own, offsets, energy_ref, own_ref, other_ref, w_self_ref, w_spin_ref, bias_ref,
                          readout_ref, first_self_ref, first_spin_ref, self_ref, spin_ref, *scratch):
    half_slopes(walkers * own, own_ref, other_ref, w_self_ref, w_spin_ref, bias_ref, readout_ref, *scratch)
    self_ref[...] = first_self_ref[...]
    spin_ref[...] = first_spin_ref[...]
    add_products(walkers, own, offsets, own_ref.shape[0], energy_ref, own_ref, other_ref, *scratch, self_ref, spin_ref)


def whole(memory=pltpu.VMEM):
    return pl.BlockSpec(memory_space=memory)


def call(kernel, out_shape, in_specs, scratch=(), cost=None, limit=VMEM_LIMIT, out_specs=None):
    flops, moved = cost if cost is not None else (0, 0)
    return pl.pallas_call(
        kernel,
        out_shape=out_shape,
        in_specs=in_specs,
        out_specs=jax.tree.map(lambda _: whole(), out_shape) if out_specs is None else out_specs,
        scratch_shapes=scratch,
        cost_estimate=pl.CostEstimate(flops=flops, bytes_accessed=moved, transcendentals=0) if cost else None,
        compiler_params=pltpu.CompilerParams(vmem_limit_bytes=limit),
    )


def flip(array, axis, bit):
    size = lax.axis_size(axis)
    return lax.ppermute(array, axis, [(i, i ^ bit) for i in range(size)])


def tied(*arrays):
    return lax.optimization_barrier(arrays)


def shards(values, lap_in, tangent, slot_electron, spin_up, w_self, w_spin, bias, readout, potential):
    walk_size = lax.axis_size("walk")
    walkers, own, feat = values.shape
    dirs = tangent.shape[1]
    shape = jax.ShapeDtypeStruct
    smem = whole(pltpu.SMEM)
    flat = tangent.reshape(walkers * dirs * own, feat)
    values, lap_in = values.reshape(walkers * own, feat), lap_in.reshape(walkers * own, feat)
    bias, readout = bias.reshape(1, feat), readout.reshape(1, feat)
    bits = [1 << b for b in reversed(range(walk_size.bit_length() - 1))]

    small = (2, 16, feat)
    packed, value_sums = call(
        functools.partial(pack_kernel, walkers, own),
        (shape((walkers * own + 16, feat), BF16), shape(small, F32)),
        [smem] + [whole(pltpu.HBM)] * 3,
        [pltpu.VMEM(slot_electron.shape, jnp.int32), pltpu.VMEM((2,) + values.shape, BF16),
         pltpu.VMEM((16, feat), BF16), pltpu.VMEM(small, F32), pltpu.SemaphoreType.DMA((6,))],
        limit=63 * MIB, out_specs=(whole(pltpu.HBM),) * 2)(spin_up, slot_electron, values, lap_in)
    other_value_sums = flip(value_sums, "tan", 1)
    gathered = packed.reshape((1,) + packed.shape)

    repeat, block, piece = feat // own, dirs // 2, dirs // 4
    sums, held = call(
        functools.partial(sums_kernel, walkers, own, block),
        (shape((walkers, 2, dirs, feat), F32), shape(flat.shape, BF16)),
        [whole(), whole(pltpu.HBM)],
        [pltpu.VMEM((walkers, 2 * repeat, feat), BF16), pltpu.SemaphoreType.DMA((walkers * dirs // block,))],
        (flat.size * 32, flat.size * 2), 36 * MIB)(packed, flat)
    received, sums, other_value_sums = tied(flip(gathered, "walk", bits[0]), sums, other_value_sums)
    gathered = jnp.concatenate([gathered, received], axis=0)
    other_sums = flip(sums, "tan", 1)
    for bit in bits[1:-3]:
        gathered = jnp.concatenate([gathered, flip(gathered, "walk", bit)], axis=0)
    received = flip(gathered, "walk", bits[-3])

    full = shape((walkers * own, feat), F32)
    base, curve, weighted = call(
        layer_kernel, (full, full, full), [whole()] * 9, cost=(4 * feat * feat * walkers * own, 4 << 20))(
            values, lap_in, packed, value_sums, other_value_sums, w_self, w_spin, bias, readout)

    counts = (1, walkers - 1)
    wide = -(-(dirs + 1) // 128) * 128

    def change(h, ups):
        return call(
            functools.partial(change_kernel, own, block, piece, sum(counts[:h])),
            (shape((counts[h], own, feat), F32), shape((8, wide), F32)),
            [smem] + [whole()] * 10,
            [pltpu.VMEM((2, dirs, feat), F32), pltpu.VMEM((own, feat), F32), pltpu.VMEM((own, feat), F32),
             pltpu.VMEM((dirs * 8, feat // 2), F32)],
            (flat.size * feat * counts[h] // 2, flat.size),
        )(ups, slot_electron, held, sums, other_sums, w_self, w_spin, readout, base, curve, weighted)

    laplacian, partial = change(0, spin_up)
    received, late_spin_up, partial = tied(received, spin_up, partial)
    gathered = jnp.concatenate([gathered, received], axis=0)
    received = flip(gathered, "walk", bits[-2])
    more_laplacian, more_partial = change(1, late_spin_up)
    received, more_partial = tied(received, more_partial)
    gathered = jnp.concatenate([gathered, received], axis=0)
    side, other = flip(gathered, "walk", bits[-1]), flip(gathered, "tan", 1)
    partials = [p for own_part in (partial, more_partial) for p in (own_part, flip(own_part, "tan", 1))]
    rows = call(
        functools.partial(energy_kernel, dirs, counts), shape((walk_size, 1, 128), F32), [smem] + [whole()] * 4)(
            potential, *partials)
    energy = rows[0, 0, :walkers]
    energies = lax.all_to_all(rows, "walk", 0, 0, tiled=True)
    other, more_laplacian, _ = tied(other, more_laplacian, rows)

    blocks = walk_size // 2
    group_shape = (blocks * 16, feat)
    half = [((blocks * 2 * walkers * own, feat), BF16), (group_shape, F32), (group_shape, BF16)]
    weights = (w_self, w_spin, bias, readout)
    slopes = call(
        functools.partial(half_slopes, walkers * own), tuple(shape(*h) for h in half), [whole()] * 6,
        cost=(blocks * 8 * walkers * own * feat * feat, 8 << 20))(gathered, other, *weights)
    laplacian = jnp.concatenate([laplacian, more_laplacian], axis=0)
    energies, side, laplacian, energy, *slopes = tied(energies, side, laplacian, energy, *slopes)
    other_side = flip(side, "tan", 1)
    square = shape((feat, feat), F32)
    settings = walkers, own, bits
    first = call(
        functools.partial(first_gradients_kernel, *settings), (square, square), [whole()] * 6,
        cost=(blocks * 16 * walkers * own * feat * feat, 8 << 20))(energies, gathered, other, *slopes)
    grad_self, grad_spin = call(
        functools.partial(last_gradients_kernel, *settings), (square, square), [whole()] * 9,
        [pltpu.VMEM(*h) for h in half])(energies, side, other_side, *weights, *first)
    return laplacian, energy, grad_self, grad_spin


def solution(mesh):
    placed = (
        P("walk", "tan", None),
        P("walk", "tan", None),
        P("walk", None, "tan", None),
        P("walk", None),
        P("walk"),
        P(),
        P(),
        P(),
        P(),
        P("walk"),
    )
    return jax.shard_map(
        shards,
        mesh=mesh,
        in_specs=placed,
        out_specs=(P("walk", "tan", None), P("walk"), P(), P()),
        check_vma=False,
    )
```

```python
import functools

import jax
import jax.numpy as jnp
from jax import lax
from jax.experimental import pallas as pl
from jax.experimental.pallas import tpu as pltpu
from jax.sharding import PartitionSpec as P

F32 = jnp.float32
BF16 = jnp.bfloat16
MIB = 1024 * 1024
VMEM_LIMIT = 24 * MIB
HIGHEST = lax.Precision.HIGHEST
FIRST = ((0,), (0,))
LAST = ((1,), (1,))


def iota(shape, axis):
    return lax.broadcasted_iota(jnp.int32, shape, axis)


def dot(a, b, dims=((1,), (0,)), precision=None):
    return lax.dot_general(a, b, (dims, ((), ())), precision=precision, preferred_element_type=F32)


def two_terms(array):
    high = array.astype(BF16)
    return high, (array - high.astype(F32)).astype(BF16)


def three_terms(array):
    high = array.astype(BF16)
    middle, low = two_terms(array - high.astype(F32))
    return jnp.concatenate([high, middle, low], axis=0)


def first_slot(own):
    return lax.axis_index("tan") * own


def upper_row(slot_ref, w, count):
    return (slot_ref[pl.ds(w, 1), :] < count).astype(F32)


def upper_column(slot_ref, w, count, own):
    row = upper_row(slot_ref, w, count)
    place = iota((own, row.shape[1]), 1) == iota((own, row.shape[1]), 0) + first_slot(own)
    return jnp.sum(jnp.where(place, row, 0.0), axis=1, keepdims=True)


def own_places(electrons, own, wide):
    return (iota((electrons, wide), 0) == iota((electrons, wide), 1) % own + first_slot(own)).astype(BF16)


def pack_kernel(walkers, own, spin_ref, slot_far, values_far, lap_far, packed_ref, value_sums_ref,
                slot_ref, lap_ref, small_sems):
    rows, feat = lap_ref.shape
    electrons = slot_ref.shape[1]
    values_ref = packed_ref.at[pl.ds(0, rows)]
    near = [pltpu.make_async_copy(*ends, small_sems.at[i]) for i, ends in enumerate(
        ((slot_far, slot_ref), (values_far, values_ref), (lap_far, lap_ref)))]
    for copy in near:
        copy.start()
    near[0].wait()
    slots = jnp.zeros((2 * walkers, electrons), jnp.int32)
    for w in range(walkers):
        slots = jnp.where(iota(slots.shape, 0) // 2 == w, slot_ref[w:w + 1, :], slots)

    def column(shape):
        line = iota(shape, 0)
        count = jnp.zeros(shape, jnp.int32)
        for w in range(walkers):
            count = jnp.where(line // 2 == w, spin_ref[w], count)
        return line, count

    line, count = column(slots.shape)
    upper = (slots < count).astype(F32)
    chosen = jnp.where(line % 2 == 0, upper, 1.0 - upper).astype(BF16)
    tiled = dot(chosen, own_places(electrons, own, feat))
    line, count = column(tiled.shape)
    lane = iota(tiled.shape, 1)
    size = jnp.where(line % 2 == 0, count, electrons - count).astype(F32)
    groups = jnp.where(lane < rows, jnp.where(lane // own == line // 2, tiled, 0.0), size)
    groups = jnp.concatenate([groups, jnp.zeros((16 - 2 * walkers, feat), F32)], axis=0).astype(BF16)
    packed_ref[rows:, :] = groups
    near[1].wait()
    near[2].wait()
    value_sums_ref[0] = dot(groups[:, :rows], values_ref[...])
    value_sums_ref[1] = dot(groups[:, :rows], lap_ref[...])


def sums_kernel(walkers, own, block, packed_ref, far_ref, out_ref, tangent_ref, mask_ref, sems):
    dirs = out_ref.shape[2]
    rows, feat = walkers * own, packed_ref.shape[1]
    repeat = mask_ref.shape[1] // 2
    steps, chunk = dirs // block, block * own

    def fetch(i):
        at = pl.ds(pl.multiple_of(i * chunk, chunk), chunk)
        return pltpu.make_async_copy(far_ref.at[at], tangent_ref.at[at], sems.at[i])

    for i in range(walkers * steps):
        fetch(i).start()
    spots = (iota((rows, feat), 0) % own == iota((rows, feat), 1) % own).astype(F32).astype(BF16)
    tiled = dot(packed_ref[rows:, :rows], spots)
    place = iota((repeat, feat), 1) // own == iota((repeat, feat), 0)
    for w in range(walkers):
        both = [jnp.where(place, tiled[2 * w + g:2 * w + g + 1], 0.0) for g in range(2)]
        mask_ref[w] = jnp.concatenate(both, axis=0).astype(BF16)

    @pl.loop(0, walkers * steps)
    def _(i):
        w, step = i // steps, i % steps
        mask = mask_ref[w]
        fetch(i).wait()
        for part in range(block // repeat):
            row = pl.multiple_of(i * chunk + part * repeat * own, repeat * own)
            sums = dot(mask, tangent_ref[pl.ds(row, repeat * own), :])
            at = pl.ds(pl.multiple_of(step * block + part * repeat, repeat), repeat)
            out_ref[w, 0, at, :] = sums[:repeat]
            out_ref[w, 1, at, :] = sums[repeat:]


def picked_rows(groups, mixed):
    lines = jnp.concatenate([groups, groups, groups], axis=0)
    return dot(lines, three_terms(mixed), FIRST)


def layer_kernel(values_ref, lap_ref, packed_ref, own_ref, other_ref, w_self_ref, w_spin_ref,
                 bias_ref, readout_ref, base_ref, curve_ref, weighted_ref):
    rows, feat = values_ref.shape
    lines = packed_ref[rows:, :]
    groups = lines[:, :rows]
    sizes = jnp.maximum(lines[:, rows:rows + 1].astype(F32), 1.0)
    means = ((own_ref[...] + other_ref[...]) / sizes).astype(BF16)
    preact = dot(values_ref[...], w_self_ref[...]) + picked_rows(groups, dot(means[0], w_spin_ref[...])) + bias_ref[...]
    lap_pre = dot(lap_ref[...], w_self_ref[...]) + picked_rows(groups, dot(means[1], w_spin_ref[...]))
    squash = jnp.tanh(preact)
    slopes = 1.0 - squash * squash
    base_ref[...] = slopes * lap_pre
    curve_ref[...] = -2.0 * squash * slopes
    weighted_ref[...] = slopes * readout_ref[...]


def change_kernel(own, block, piece, base, spin_ref, pot_ref, slot_ref, tangent_ref, own_ref, other_ref, w_self_ref,
                  w_spin_ref, readout_ref, base_ref, curve_ref, weighted_ref, lap_ref, grad_ref,
                  mixed_ref, squares_ref, column_ref, terms_ref):
    walkers, feat = lap_ref.shape[0], w_self_ref.shape[0]
    dirs = own_ref.shape[2]
    electrons = slot_ref.shape[1]
    steps, part = dirs // block, 8
    grad_ref[...] = jnp.zeros_like(grad_ref)

    @pl.loop(0, walkers)
    def _(n):
        w = base + n
        count = spin_ref[w]
        ups = count.astype(F32)
        mine = pl.ds(pl.multiple_of(w * own, own), own)
        for g, size in enumerate((ups, electrons - ups)):
            means = ((own_ref[w, g] + other_ref[w, g]) / size).astype(BF16)
            mixed_ref[g] = dot(means, w_spin_ref[...])
        column_ref[...] = jnp.broadcast_to(upper_column(slot_ref, w, count, own), (own, feat))
        squares_ref[...] = jnp.zeros_like(squares_ref)

        @pl.loop(0, steps)
        def _(step):
            upper = column_ref[...] > 0.5
            weighted = weighted_ref[mine, :]
            squares = squares_ref[...]
            for c in range(block // piece):
                row = pl.multiple_of(((w * steps + step) * block + c * piece) * own, own)
                plain = dot(tangent_ref[pl.ds(row, piece * own), :], w_self_ref[...])
                for p in range(piece // part):
                    at = pl.multiple_of(step * block + c * piece + p * part, part)
                    mixed = mixed_ref[:, pl.ds(at, part), :]
                    for d in range(part):
                        row = (p * part + d) * own
                        picked = jnp.where(upper, mixed[0, d:d + 1], mixed[1, d:d + 1])
                        change = plain[row:row + own] + picked
                        squares = squares + change * change
                        terms = (change * weighted).reshape(own // 8, 8, feat).sum(axis=0)
                        terms_ref[pl.ds(pl.multiple_of(at * 8 + d * 8, 8), 8), :] = (
                            terms[:, :feat // 2] + terms[:, feat // 2:])
            squares_ref[...] = squares

        laplacian = base_ref[mine, :] + curve_ref[mine, :] * squares_ref[...]
        lap_ref[n] = laplacian
        summed = terms_ref[...].reshape(dirs, 8, feat // 2).sum(axis=1)
        spare = jnp.zeros((grad_ref.shape[1] - dirs, feat // 2), F32)
        summed = jnp.concatenate([summed, spare], axis=0)
        row = dot(jnp.ones((8, feat // 2), F32), summed, LAST, HIGHEST)
        share = jnp.sum(laplacian * readout_ref[...]) - jnp.where(lax.axis_index("tan") == 0, 2.0 * pot_ref[w], 0.0)
        row = jnp.where(iota(row.shape, 1) == dirs, share, row)
        grad_ref[...] = jnp.where(iota(row.shape, 0) == n, row, grad_ref[...])


def energy_kernel(dirs, counts, *refs):
    halves, out_ref = refs[:-1], refs[-1]
    lane = iota((1, 128), 1)
    row = jnp.zeros((1, 128), F32)
    for h, count in enumerate(counts):
        both = halves[2 * h][...] + halves[2 * h + 1][...]
        place = iota(both.shape, 1)
        parts = jnp.where(place < dirs, both * both, jnp.where(place == dirs, both, 0.0))
        energy = -0.5 * jnp.sum(parts, axis=1, keepdims=True)
        for n in range(count):
            w = sum(counts[:h]) + n
            row = jnp.where(lane == w, energy[n:n + 1], row)
    out_ref[...] = jnp.broadcast_to(row.reshape(1, 1, 128), out_ref.shape)


def pair(own_ref, other_ref, rows, r):
    values = jnp.concatenate([ref[r, 0:rows, :] for ref in (own_ref, other_ref)], axis=0)
    groups = jnp.concatenate([ref[r, rows:, 0:rows] for ref in (own_ref, other_ref)], axis=1)
    return values, groups


def half_slopes(rows, own_ref, other_ref, w_self_ref, w_spin_ref, bias_ref, readout_ref,
                slopes_ref, sums_ref, means_ref):
    blocks, lines, _ = own_ref.shape
    group = lines - rows
    bunch = min(blocks, 8)

    @pl.loop(0, blocks // bunch)
    def _(i):
        pairs = [pair(own_ref, other_ref, rows, i * bunch + k) for k in range(bunch)]
        means = []
        for k, (values, groups) in enumerate(pairs):
            sizes = jnp.maximum(own_ref[i * bunch + k, rows:, rows:rows + 1].astype(F32), 1.0)
            means.append(dot(groups, values) / sizes)
        means = jnp.concatenate(means, axis=0).astype(BF16)
        at = pl.ds(pl.multiple_of(i * bunch * group, bunch * group), bunch * group)
        means_ref[at, :] = means
        mixed = dot(means, w_spin_ref[...])
        sums = []
        for k, (values, groups) in enumerate(pairs):
            preact = (dot(values, w_self_ref[...]) + picked_rows(groups, mixed[k * group:(k + 1) * group])
                      + bias_ref[...])
            squash = jnp.tanh(preact)
            slopes = ((1.0 - squash * squash) * readout_ref[...]).astype(BF16)
            row = pl.multiple_of((i * bunch + k) * 2 * rows, 2 * rows)
            slopes_ref[pl.ds(row, 2 * rows), :] = slopes
            sums.append(dot(groups, slopes))
        sums_ref[at, :] = jnp.concatenate(sums, axis=0)


def add_products(walkers, own, offsets, first, energy_ref, own_ref, other_ref, slopes_ref, sums_ref, means_ref,
                 self_ref, spin_ref):
    rows = walkers * own
    me = lax.axis_index("walk")
    blocks, lines, feat = own_ref.shape
    group = lines - rows
    bunch = min(blocks, 8)
    everyone = energy_ref.shape[0] * walkers
    center = jnp.sum(jnp.sum(energy_ref[...], axis=0), axis=1, keepdims=True) / everyone
    line = iota((group, feat), 0) // 2

    @pl.loop(0, blocks // bunch)
    def _(i):
        values, high, low, spreads = [], [], [], []
        for k in range(bunch):
            place = first + i * bunch + k
            shift = 0
            for bit, offset in enumerate(offsets):
                shift = shift | ((place >> bit) & 1) * offset
            row = energy_ref[me ^ shift] - center
            row_at = pl.multiple_of((i * bunch + k) * 2 * rows, 2 * rows)
            slopes = slopes_ref[pl.ds(row_at, 2 * rows), :].astype(F32)
            spread = jnp.zeros((group, feat), F32)
            for w in range(walkers):
                spread = jnp.where(line == w, row[:, w:w + 1], spread)
            spreads.append(spread)
            for core in range(2):
                for w in range(walkers):
                    at = core * rows + w * own
                    top, rest = two_terms(slopes[at:at + own] * row[:, w:w + 1])
                    high.append(top)
                    low.append(rest)
            values.append(pair(own_ref, other_ref, rows, i * bunch + k)[0])
        values = jnp.concatenate(values, axis=0)
        self_ref[...] += dot(values, jnp.concatenate(high, axis=0), FIRST) + dot(
            values, jnp.concatenate(low, axis=0), FIRST)
        at = pl.ds(pl.multiple_of(i * bunch * group, bunch * group), bunch * group)
        top, rest = two_terms(sums_ref[at, :] * jnp.concatenate(spreads, axis=0))
        means = means_ref[at, :]
        spin_ref[...] += dot(means, top, FIRST) + dot(means, rest, FIRST)


def first_gradients_kernel(walkers, own, offsets, *refs):
    self_ref, spin_ref = refs[-2:]
    self_ref[...] = jnp.zeros_like(self_ref)
    spin_ref[...] = jnp.zeros_like(spin_ref)
    add_products(walkers, own, offsets, 0, *refs)


def last_gradients_kernel(walkers, own, offsets, energy_ref, own_ref, other_ref, w_self_ref, w_spin_ref, bias_ref,
                          readout_ref, first_self_ref, first_spin_ref, self_ref, spin_ref, *scratch):
    half_slopes(walkers * own, own_ref, other_ref, w_self_ref, w_spin_ref, bias_ref, readout_ref, *scratch)
    self_ref[...] = first_self_ref[...]
    spin_ref[...] = first_spin_ref[...]
    add_products(walkers, own, offsets, own_ref.shape[0], energy_ref, own_ref, other_ref, *scratch, self_ref, spin_ref)


def whole(memory=pltpu.VMEM):
    return pl.BlockSpec(memory_space=memory)


def call(kernel, out_shape, in_specs, scratch=(), cost=None, limit=VMEM_LIMIT, out_specs=None):
    flops, moved = cost if cost is not None else (0, 0)
    return pl.pallas_call(
        kernel,
        out_shape=out_shape,
        in_specs=in_specs,
        out_specs=jax.tree.map(lambda _: whole(), out_shape) if out_specs is None else out_specs,
        scratch_shapes=scratch,
        cost_estimate=pl.CostEstimate(flops=flops, bytes_accessed=moved, transcendentals=0) if cost else None,
        compiler_params=pltpu.CompilerParams(vmem_limit_bytes=limit),
    )


def flip(array, axis, bit):
    size = lax.axis_size(axis)
    return lax.ppermute(array, axis, [(i, i ^ bit) for i in range(size)])


def tied(*arrays):
    return lax.optimization_barrier(arrays)


def shards(values, lap_in, tangent, slot_electron, spin_up, w_self, w_spin, bias, readout, potential):
    walk_size = lax.axis_size("walk")
    walkers, own, feat = values.shape
    dirs = tangent.shape[1]
    shape = jax.ShapeDtypeStruct
    smem = whole(pltpu.SMEM)
    flat = tangent.reshape(walkers * dirs * own, feat)
    values, lap_in = values.reshape(walkers * own, feat), lap_in.reshape(walkers * own, feat)
    bias, readout = bias.reshape(1, feat), readout.reshape(1, feat)
    bits = [1 << b for b in reversed(range(walk_size.bit_length() - 1))]

    small = (2, 16, feat)
    packed, value_sums = call(
        functools.partial(pack_kernel, walkers, own),
        (shape((walkers * own + 16, feat), BF16), shape(small, F32)),
        [smem] + [whole(pltpu.HBM)] * 3,
        [pltpu.VMEM(slot_electron.shape, jnp.int32), pltpu.VMEM(lap_in.shape, BF16), pltpu.SemaphoreType.DMA((3,))],
        limit=63 * MIB)(spin_up, slot_electron, values, lap_in)
    other_value_sums = flip(value_sums, "tan", 1)
    gathered = packed.reshape((1,) + packed.shape)

    repeat, block, piece = feat // own, dirs // 2, dirs // 2
    sums, held = call(
        functools.partial(sums_kernel, walkers, own, block),
        (shape((walkers, 2, dirs, feat), F32), shape(flat.shape, BF16)),
        [whole(), whole(pltpu.HBM)],
        [pltpu.VMEM((walkers, 2 * repeat, feat), BF16), pltpu.SemaphoreType.DMA((walkers * dirs // block,))],
        (flat.size * 32, flat.size * 2), 36 * MIB)(packed, flat)
    received, sums, other_value_sums = tied(flip(gathered, "walk", bits[0]), sums, other_value_sums)
    gathered = jnp.concatenate([gathered, received], axis=0)
    other_sums = flip(sums, "tan", 1)
    for bit in bits[1:-3]:
        gathered = jnp.concatenate([gathered, flip(gathered, "walk", bit)], axis=0)
    received = flip(gathered, "walk", bits[-3])

    full = shape((walkers * own, feat), F32)
    base, curve, weighted = call(
        layer_kernel, (full, full, full), [whole()] * 9, cost=(4 * feat * feat * walkers * own, 4 << 20))(
            values, lap_in, packed, value_sums, other_value_sums, w_self, w_spin, bias, readout)

    counts = (1, walkers - 1)
    wide = -(-(dirs + 1) // 128) * 128

    def change(h, ups):
        return call(
            functools.partial(change_kernel, own, block, piece, sum(counts[:h])),
            (shape((counts[h], own, feat), F32), shape((8, wide), F32)),
            [smem, smem] + [whole()] * 10,
            [pltpu.VMEM((2, dirs, feat), F32), pltpu.VMEM((own, feat), F32), pltpu.VMEM((own, feat), F32),
             pltpu.VMEM((dirs * 8, feat // 2), F32)],
            (flat.size * feat * counts[h] // 2, flat.size),
        )(ups, potential, slot_electron, held, sums, other_sums, w_self, w_spin, readout, base, curve, weighted)

    laplacian, partial = change(0, spin_up)
    received, late_spin_up, partial = tied(received, spin_up, partial)
    gathered = jnp.concatenate([gathered, received], axis=0)
    received = flip(gathered, "walk", bits[-2])
    more_laplacian, more_partial = change(1, late_spin_up)
    received, more_partial = tied(received, more_partial)
    gathered = jnp.concatenate([gathered, received], axis=0)
    side, other = flip(gathered, "walk", bits[-1]), flip(gathered, "tan", 1)
    partials = [p for own_part in (partial, more_partial) for p in (own_part, flip(own_part, "tan", 1))]
    rows = call(
        functools.partial(energy_kernel, dirs, counts), shape((walk_size, 1, 128), F32), [whole()] * 4)(
            *partials)
    energy = rows[0, 0, :walkers]
    energies = lax.all_to_all(rows, "walk", 0, 0, tiled=True)
    other, more_laplacian, _ = tied(other, more_laplacian, rows)

    blocks = walk_size // 2
    group_shape = (blocks * 16, feat)
    half = [((blocks * 2 * walkers * own, feat), BF16), (group_shape, F32), (group_shape, BF16)]
    weights = (w_self, w_spin, bias, readout)
    slopes = call(
        functools.partial(half_slopes, walkers * own), tuple(shape(*h) for h in half), [whole()] * 6,
        cost=(blocks * 8 * walkers * own * feat * feat, 8 << 20))(gathered, other, *weights)
    laplacian = jnp.concatenate([laplacian, more_laplacian], axis=0)
    energies, side, laplacian, energy, last = tied(energies, side, laplacian, energy, slopes[2])
    slopes = slopes[0], slopes[1], last
    other_side = flip(side, "tan", 1)
    square = shape((feat, feat), F32)
    settings = walkers, own, bits
    first = call(
        functools.partial(first_gradients_kernel, *settings), (square, square), [whole()] * 6,
        cost=(blocks * 16 * walkers * own * feat * feat, 8 << 20))(energies, gathered, other, *slopes)
    grad_self, grad_spin = call(
        functools.partial(last_gradients_kernel, *settings), (square, square), [whole()] * 9,
        [pltpu.VMEM(*h) for h in half])(energies, side, other_side, *weights, *first)
    return laplacian, energy, grad_self, grad_spin


def solution(mesh):
    placed = (
        P("walk", "tan", None),
        P("walk", "tan", None),
        P("walk", None, "tan", None),
        P("walk", None),
        P("walk"),
        P(),
        P(),
        P(),
        P(),
        P("walk"),
    )
    return jax.shard_map(
        shards,
        mesh=mesh,
        in_specs=placed,
        out_specs=(P("walk", "tan", None), P("walk"), P(), P()),
        check_vma=False,
    )
```

```python
import functools

import jax
import jax.numpy as jnp
from jax import lax
from jax.experimental import pallas as pl
from jax.experimental.pallas import tpu as pltpu
from jax.sharding import PartitionSpec as P

F32 = jnp.float32
BF16 = jnp.bfloat16
MIB = 1024 * 1024
VMEM_LIMIT = 24 * MIB
HIGHEST = lax.Precision.HIGHEST
FIRST = ((0,), (0,))
LAST = ((1,), (1,))


def iota(shape, axis):
    return lax.broadcasted_iota(jnp.int32, shape, axis)


def dot(a, b, dims=((1,), (0,)), precision=None):
    return lax.dot_general(a, b, (dims, ((), ())), precision=precision, preferred_element_type=F32)


def two_terms(array):
    high = array.astype(BF16)
    return high, (array - high.astype(F32)).astype(BF16)


def three_terms(array):
    high = array.astype(BF16)
    middle, low = two_terms(array - high.astype(F32))
    return jnp.concatenate([high, middle, low], axis=0)


def first_slot(own):
    return lax.axis_index("tan") * own


def upper_row(slot_ref, w, count):
    return (slot_ref[pl.ds(w, 1), :] < count).astype(F32)


def upper_column(slot_ref, w, count, own):
    row = upper_row(slot_ref, w, count)
    place = iota((own, row.shape[1]), 1) == iota((own, row.shape[1]), 0) + first_slot(own)
    return jnp.sum(jnp.where(place, row, 0.0), axis=1, keepdims=True)


def own_places(electrons, own, wide):
    return (iota((electrons, wide), 0) == iota((electrons, wide), 1) % own + first_slot(own)).astype(BF16)


def pack_kernel(walkers, own, spin_ref, slot_far, values_far, lap_far, packed_ref, value_sums_ref, lines_ref,
                slot_ref, lap_ref, small_sems):
    rows, feat = lap_ref.shape
    electrons = slot_ref.shape[1]
    values_ref = packed_ref.at[pl.ds(0, rows)]
    near = [pltpu.make_async_copy(*ends, small_sems.at[i]) for i, ends in enumerate(
        ((slot_far, slot_ref), (values_far, values_ref), (lap_far, lap_ref)))]
    for copy in near:
        copy.start()
    near[0].wait()
    slots = jnp.zeros((2 * walkers, electrons), jnp.int32)
    for w in range(walkers):
        slots = jnp.where(iota(slots.shape, 0) // 2 == w, slot_ref[w:w + 1, :], slots)

    def column(shape):
        line = iota(shape, 0)
        count = jnp.zeros(shape, jnp.int32)
        for w in range(walkers):
            count = jnp.where(line // 2 == w, spin_ref[w], count)
        return line, count

    line, count = column(slots.shape)
    upper = (slots < count).astype(F32)
    chosen = jnp.where(line % 2 == 0, upper, 1.0 - upper).astype(BF16)
    tiled = dot(chosen, own_places(electrons, own, feat))
    line, count = column(tiled.shape)
    lane = iota(tiled.shape, 1)
    size = jnp.where(line % 2 == 0, count, electrons - count).astype(F32)
    groups = jnp.where(lane < rows, jnp.where(lane // own == line // 2, tiled, 0.0), size)
    groups = jnp.concatenate([groups, jnp.zeros((16 - 2 * walkers, feat), F32)], axis=0).astype(BF16)
    packed_ref[rows:, :] = groups
    lines_ref[...] = groups
    near[1].wait()
    near[2].wait()
    value_sums_ref[0] = dot(groups[:, :rows], values_ref[...])
    value_sums_ref[1] = dot(groups[:, :rows], lap_ref[...])


def sums_kernel(walkers, own, block, lines_ref, far_ref, out_ref, sent_ref, tangent_ref, mask_ref, sems):
    dirs = out_ref.shape[2]
    rows, feat = walkers * own, lines_ref.shape[1]
    repeat = mask_ref.shape[1] // 2
    steps, chunk = dirs // block, block * own

    def fetch(i):
        at = pl.ds(pl.multiple_of(i * chunk, chunk), chunk)
        return pltpu.make_async_copy(far_ref.at[at], tangent_ref.at[at], sems.at[i])

    for i in range(walkers * steps):
        fetch(i).start()
    spots = (iota((rows, feat), 0) % own == iota((rows, feat), 1) % own).astype(F32).astype(BF16)
    tiled = dot(lines_ref[:, :rows], spots)
    place = iota((repeat, feat), 1) // own == iota((repeat, feat), 0)
    for w in range(walkers):
        both = [jnp.where(place, tiled[2 * w + g:2 * w + g + 1], 0.0) for g in range(2)]
        mask_ref[w] = jnp.concatenate(both, axis=0).astype(BF16)

    @pl.loop(0, walkers * steps)
    def _(i):
        w, step = i // steps, i % steps
        mask = mask_ref[w]
        fetch(i).wait()
        for part in range(block // repeat):
            row = pl.multiple_of(i * chunk + part * repeat * own, repeat * own)
            sums = dot(mask, tangent_ref[pl.ds(row, repeat * own), :])
            at = pl.ds(pl.multiple_of(step * block + part * repeat, repeat), repeat)
            out_ref[w, 0, at, :] = sums[:repeat]
            out_ref[w, 1, at, :] = sums[repeat:]
        at = pl.ds(pl.multiple_of(step * block, block), block)
        sent_ref[w, :, at, :] = out_ref[w, :, at, :].astype(BF16)


def picked_rows(groups, mixed):
    lines = jnp.concatenate([groups, groups, groups], axis=0)
    return dot(lines, three_terms(mixed), FIRST)


def layer_kernel(values_ref, lap_ref, packed_ref, own_ref, other_ref, w_self_ref, w_spin_ref,
                 bias_ref, readout_ref, base_ref, curve_ref, weighted_ref):
    rows, feat = values_ref.shape
    lines = packed_ref[rows:, :]
    groups = lines[:, :rows]
    sizes = jnp.maximum(lines[:, rows:rows + 1].astype(F32), 1.0)
    means = ((own_ref[...] + other_ref[...]) / sizes).astype(BF16)
    preact = dot(values_ref[...], w_self_ref[...]) + picked_rows(groups, dot(means[0], w_spin_ref[...])) + bias_ref[...]
    lap_pre = dot(lap_ref[...], w_self_ref[...]) + picked_rows(groups, dot(means[1], w_spin_ref[...]))
    squash = jnp.tanh(preact)
    slopes = 1.0 - squash * squash
    base_ref[...] = slopes * lap_pre
    curve_ref[...] = -2.0 * squash * slopes
    weighted_ref[...] = slopes * readout_ref[...]


def change_kernel(own, block, piece, base, spin_ref, pot_ref, slot_ref, tangent_ref, own_ref, other_ref, w_self_ref,
                  w_spin_ref, readout_ref, base_ref, curve_ref, weighted_ref, before_ref, lap_ref, grad_ref,
                  mixed_ref, squares_ref, column_ref, terms_ref):
    walkers, feat = lap_ref.shape[0], w_self_ref.shape[0]
    dirs = own_ref.shape[2]
    electrons = slot_ref.shape[1]
    steps, part = dirs // block, 8
    grad_ref[...] = before_ref[...]

    @pl.loop(0, walkers)
    def _(n):
        w = base + n
        count = spin_ref[w]
        ups = count.astype(F32)
        mine = pl.ds(pl.multiple_of(w * own, own), own)
        for g, size in enumerate((ups, electrons - ups)):
            means = ((own_ref[w, g] + other_ref[w, g].astype(F32)) / size).astype(BF16)
            mixed_ref[g] = dot(means, w_spin_ref[...])
        column_ref[...] = jnp.broadcast_to(upper_column(slot_ref, w, count, own), (own, feat))
        squares_ref[...] = jnp.zeros_like(squares_ref)

        @pl.loop(0, steps)
        def _(step):
            upper = column_ref[...] > 0.5
            weighted = weighted_ref[mine, :]
            squares = squares_ref[...]
            for c in range(block // piece):
                row = pl.multiple_of(((w * steps + step) * block + c * piece) * own, own)
                plain = dot(tangent_ref[pl.ds(row, piece * own), :], w_self_ref[...])
                for p in range(piece // part):
                    at = pl.multiple_of(step * block + c * piece + p * part, part)
                    mixed = mixed_ref[:, pl.ds(at, part), :]
                    for d in range(part):
                        row = (p * part + d) * own
                        picked = jnp.where(upper, mixed[0, d:d + 1], mixed[1, d:d + 1])
                        change = plain[row:row + own] + picked
                        squares = squares + change * change
                        terms = (change * weighted).reshape(own // 8, 8, feat).sum(axis=0)
                        terms_ref[pl.ds(pl.multiple_of(at * 8 + d * 8, 8), 8), :] = (
                            terms[:, :feat // 2] + terms[:, feat // 2:])
            squares_ref[...] = squares

        laplacian = base_ref[mine, :] + curve_ref[mine, :] * squares_ref[...]
        lap_ref[n] = laplacian
        summed = terms_ref[...].reshape(dirs, 8, feat // 2).sum(axis=1)
        spare = jnp.zeros((grad_ref.shape[1] - dirs, feat // 2), F32)
        summed = jnp.concatenate([summed, spare], axis=0)
        row = dot(jnp.ones((8, feat // 2), F32), summed, LAST, HIGHEST)
        share = jnp.sum(laplacian * readout_ref[...]) - jnp.where(lax.axis_index("tan") == 0, 2.0 * pot_ref[w], 0.0)
        row = jnp.where(iota(row.shape, 1) == dirs, share, row)
        grad_ref[...] = jnp.where(iota(row.shape, 0) == w, row, grad_ref[...])


def energy_kernel(dirs, walkers, own_ref, other_ref, out_ref):
    both = own_ref[...] + other_ref[...]
    place = iota(both.shape, 1)
    parts = jnp.where(place < dirs, both * both, jnp.where(place == dirs, both, 0.0))
    energy = -0.5 * jnp.sum(parts, axis=1, keepdims=True)
    lane = iota((1, 128), 1)
    row = jnp.zeros((1, 128), F32)
    for w in range(walkers):
        row = jnp.where(lane == w, energy[w:w + 1], row)
    out_ref[...] = jnp.broadcast_to(row.reshape(1, 1, 128), out_ref.shape)


def pair(own_ref, other_ref, rows, r):
    values = jnp.concatenate([ref[r, 0:rows, :] for ref in (own_ref, other_ref)], axis=0)
    groups = jnp.concatenate([ref[r, rows:, 0:rows] for ref in (own_ref, other_ref)], axis=1)
    return values, groups


def half_slopes(rows, own_ref, other_ref, w_self_ref, w_spin_ref, bias_ref, readout_ref,
                slopes_ref, sums_ref, means_ref):
    blocks, lines, _ = own_ref.shape
    group = lines - rows
    bunch = min(blocks, 8)

    @pl.loop(0, blocks // bunch)
    def _(i):
        pairs = [pair(own_ref, other_ref, rows, i * bunch + k) for k in range(bunch)]
        means = []
        for k, (values, groups) in enumerate(pairs):
            sizes = jnp.maximum(own_ref[i * bunch + k, rows:, rows:rows + 1].astype(F32), 1.0)
            means.append(dot(groups, values) / sizes)
        means = jnp.concatenate(means, axis=0).astype(BF16)
        at = pl.ds(pl.multiple_of(i * bunch * group, bunch * group), bunch * group)
        means_ref[at, :] = means
        mixed = dot(means, w_spin_ref[...])
        sums = []
        for k, (values, groups) in enumerate(pairs):
            preact = (dot(values, w_self_ref[...]) + picked_rows(groups, mixed[k * group:(k + 1) * group])
                      + bias_ref[...])
            squash = jnp.tanh(preact)
            slopes = ((1.0 - squash * squash) * readout_ref[...]).astype(BF16)
            row = pl.multiple_of((i * bunch + k) * 2 * rows, 2 * rows)
            slopes_ref[pl.ds(row, 2 * rows), :] = slopes
            sums.append(dot(groups, slopes))
        sums_ref[at, :] = jnp.concatenate(sums, axis=0)


def add_products(walkers, own, offsets, first, energy_ref, own_ref, other_ref, slopes_ref, sums_ref, means_ref,
                 self_ref, spin_ref):
    rows = walkers * own
    me = lax.axis_index("walk")
    blocks, lines, feat = own_ref.shape
    group = lines - rows
    bunch = min(blocks, 8)
    everyone = energy_ref.shape[0] * walkers
    center = jnp.sum(jnp.sum(energy_ref[...], axis=0), axis=1, keepdims=True) / everyone
    line = iota((group, feat), 0) // 2

    @pl.loop(0, blocks // bunch)
    def _(i):
        values, high, low, spreads = [], [], [], []
        for k in range(bunch):
            place = first + i * bunch + k
            shift = 0
            for bit, offset in enumerate(offsets):
                shift = shift | ((place >> bit) & 1) * offset
            row = energy_ref[me ^ shift] - center
            row_at = pl.multiple_of((i * bunch + k) * 2 * rows, 2 * rows)
            slopes = slopes_ref[pl.ds(row_at, 2 * rows), :].astype(F32)
            spread = jnp.zeros((group, feat), F32)
            for w in range(walkers):
                spread = jnp.where(line == w, row[:, w:w + 1], spread)
            spreads.append(spread)
            for core in range(2):
                for w in range(walkers):
                    at = core * rows + w * own
                    top, rest = two_terms(slopes[at:at + own] * row[:, w:w + 1])
                    high.append(top)
                    low.append(rest)
            values.append(pair(own_ref, other_ref, rows, i * bunch + k)[0])
        values = jnp.concatenate(values, axis=0)
        self_ref[...] += dot(values, jnp.concatenate(high, axis=0), FIRST) + dot(
            values, jnp.concatenate(low, axis=0), FIRST)
        at = pl.ds(pl.multiple_of(i * bunch * group, bunch * group), bunch * group)
        top, rest = two_terms(sums_ref[at, :] * jnp.concatenate(spreads, axis=0))
        means = means_ref[at, :]
        spin_ref[...] += dot(means, top, FIRST) + dot(means, rest, FIRST)


def first_gradients_kernel(walkers, own, offsets, *refs):
    self_ref, spin_ref = refs[-2:]
    self_ref[...] = jnp.zeros_like(self_ref)
    spin_ref[...] = jnp.zeros_like(spin_ref)
    add_products(walkers, own, offsets, 0, *refs)


def last_gradients_kernel(walkers, own, offsets, energy_ref, own_ref, other_ref, w_self_ref, w_spin_ref, bias_ref,
                          readout_ref, first_self_ref, first_spin_ref, self_ref, spin_ref, *scratch):
    half_slopes(walkers * own, own_ref, other_ref, w_self_ref, w_spin_ref, bias_ref, readout_ref, *scratch)
    self_ref[...] = first_self_ref[...]
    spin_ref[...] = first_spin_ref[...]
    add_products(walkers, own, offsets, own_ref.shape[0], energy_ref, own_ref, other_ref, *scratch, self_ref, spin_ref)


def whole(memory=pltpu.VMEM):
    return pl.BlockSpec(memory_space=memory)


def call(kernel, out_shape, in_specs, scratch=(), cost=None, limit=VMEM_LIMIT, out_specs=None):
    flops, moved = cost if cost is not None else (0, 0)
    return pl.pallas_call(
        kernel,
        out_shape=out_shape,
        in_specs=in_specs,
        out_specs=jax.tree.map(lambda _: whole(), out_shape) if out_specs is None else out_specs,
        scratch_shapes=scratch,
        cost_estimate=pl.CostEstimate(flops=flops, bytes_accessed=moved, transcendentals=0) if cost else None,
        compiler_params=pltpu.CompilerParams(vmem_limit_bytes=limit),
    )


def flip(array, axis, bit):
    size = lax.axis_size(axis)
    return lax.ppermute(array, axis, [(i, i ^ bit) for i in range(size)])


def tied(*arrays):
    return lax.optimization_barrier(arrays)


def shards(values, lap_in, tangent, slot_electron, spin_up, w_self, w_spin, bias, readout, potential):
    walk_size = lax.axis_size("walk")
    walkers, own, feat = values.shape
    dirs = tangent.shape[1]
    shape = jax.ShapeDtypeStruct
    smem = whole(pltpu.SMEM)
    flat = tangent.reshape(walkers * dirs * own, feat)
    values, lap_in = values.reshape(walkers * own, feat), lap_in.reshape(walkers * own, feat)
    bias, readout = bias.reshape(1, feat), readout.reshape(1, feat)
    bits = [1 << b for b in reversed(range(walk_size.bit_length() - 1))]

    small = (2, 16, feat)
    packed, value_sums, lines = call(
        functools.partial(pack_kernel, walkers, own),
        (shape((walkers * own + 16, feat), BF16), shape(small, F32), shape((16, feat), BF16)),
        [smem] + [whole(pltpu.HBM)] * 3,
        [pltpu.VMEM(slot_electron.shape, jnp.int32), pltpu.VMEM(lap_in.shape, BF16), pltpu.SemaphoreType.DMA((3,))],
        limit=63 * MIB)(spin_up, slot_electron, values, lap_in)
    other_value_sums = flip(value_sums, "tan", 1)
    gathered = packed.reshape((1,) + packed.shape)

    repeat, block, piece = feat // own, dirs // 2, dirs // 2
    sums, sent, held = call(
        functools.partial(sums_kernel, walkers, own, block),
        (shape((walkers, 2, dirs, feat), F32), shape((walkers, 2, dirs, feat), BF16), shape(flat.shape, BF16)),
        [whole(), whole(pltpu.HBM)],
        [pltpu.VMEM((walkers, 2 * repeat, feat), BF16), pltpu.SemaphoreType.DMA((walkers * dirs // block,))],
        (flat.size * 32, flat.size * 2), 36 * MIB)(lines, flat)
    received, sent, other_value_sums = tied(flip(gathered, "walk", bits[0]), sent, other_value_sums)
    gathered = jnp.concatenate([gathered, received], axis=0)
    other_sums = flip(sent, "tan", 1)
    for bit in bits[1:-3]:
        gathered = jnp.concatenate([gathered, flip(gathered, "walk", bit)], axis=0)
    received = flip(gathered, "walk", bits[-3])

    full = shape((walkers * own, feat), F32)
    base, curve, weighted = call(
        layer_kernel, (full, full, full), [whole()] * 9, cost=(4 * feat * feat * walkers * own, 4 << 20))(
            values, lap_in, packed, value_sums, other_value_sums, w_self, w_spin, bias, readout)

    counts = (1, walkers - 1)
    wide = -(-(dirs + 1) // 128) * 128

    def change(h, ups, before):
        return call(
            functools.partial(change_kernel, own, block, piece, sum(counts[:h])),
            (shape((counts[h], own, feat), F32), shape((8, wide), F32)),
            [smem, smem] + [whole()] * 11,
            [pltpu.VMEM((2, dirs, feat), F32), pltpu.VMEM((own, feat), F32), pltpu.VMEM((own, feat), F32),
             pltpu.VMEM((dirs * 8, feat // 2), F32)],
            (flat.size * feat * counts[h] // 2, flat.size),
        )(ups, potential, slot_electron, held, sums, other_sums, w_self, w_spin, readout, base, curve, weighted, before)

    laplacian, partial = change(0, spin_up, jnp.zeros((8, wide), F32))
    received, late_spin_up, partial = tied(received, spin_up, partial)
    gathered = jnp.concatenate([gathered, received], axis=0)
    received = flip(gathered, "walk", bits[-2])
    more_laplacian, more_partial = change(1, late_spin_up, partial)
    received, more_partial = tied(received, more_partial)
    gathered = jnp.concatenate([gathered, received], axis=0)
    side, other = flip(gathered, "walk", bits[-1]), flip(gathered, "tan", 1)
    rows = call(
        functools.partial(energy_kernel, dirs, walkers), shape((walk_size, 1, 128), F32), [whole()] * 2)(
            more_partial, flip(more_partial, "tan", 1))
    energy = rows[0, 0, :walkers]
    energies = lax.all_to_all(rows, "walk", 0, 0, tiled=True)
    other, more_laplacian, _ = tied(other, more_laplacian, rows)

    blocks = walk_size // 2
    group_shape = (blocks * 16, feat)
    half = [((blocks * 2 * walkers * own, feat), BF16), (group_shape, F32), (group_shape, BF16)]
    weights = (w_self, w_spin, bias, readout)
    slopes = call(
        functools.partial(half_slopes, walkers * own), tuple(shape(*h) for h in half), [whole()] * 6,
        cost=(blocks * 8 * walkers * own * feat * feat, 8 << 20), limit=63 * MIB)(gathered, other, *weights)
    laplacian = jnp.concatenate([laplacian, more_laplacian], axis=0)
    side, last = tied(side, slopes[2])
    other_side = flip(side, "tan", 1)
    energies, laplacian, energy, last = tied(energies, laplacian, energy, last)
    slopes = slopes[0], slopes[1], last
    square = shape((feat, feat), F32)
    settings = walkers, own, bits
    first = call(
        functools.partial(first_gradients_kernel, *settings), (square, square), [whole()] * 6,
        cost=(blocks * 16 * walkers * own * feat * feat, 64 << 20), limit=63 * MIB)(energies, gathered, other, *slopes)
    grad_self, grad_spin = call(
        functools.partial(last_gradients_kernel, *settings), (square, square), [whole()] * 9,
        [pltpu.VMEM(*h) for h in half], limit=63 * MIB)(energies, side, other_side, *weights, *first)
    return laplacian, energy, grad_self, grad_spin


def solution(mesh):
    placed = (
        P("walk", "tan", None),
        P("walk", "tan", None),
        P("walk", None, "tan", None),
        P("walk", None),
        P("walk"),
        P(),
        P(),
        P(),
        P(),
        P("walk"),
    )
    return jax.shard_map(
        shards,
        mesh=mesh,
        in_specs=placed,
        out_specs=(P("walk", "tan", None), P("walk"), P(), P()),
        check_vma=False,
    )
```

```python
import functools

import jax
import jax.numpy as jnp
from jax import lax
from jax.experimental import pallas as pl
from jax.experimental.pallas import tpu as pltpu
from jax.sharding import PartitionSpec as P

F32 = jnp.float32
BF16 = jnp.bfloat16
MIB = 1024 * 1024
VMEM_LIMIT = 24 * MIB
HIGHEST = lax.Precision.HIGHEST
FIRST = ((0,), (0,))
LAST = ((1,), (1,))


def iota(shape, axis):
    return lax.broadcasted_iota(jnp.int32, shape, axis)


def dot(a, b, dims=((1,), (0,)), precision=None):
    return lax.dot_general(a, b, (dims, ((), ())), precision=precision, preferred_element_type=F32)


def two_terms(array):
    high = array.astype(BF16)
    return high, (array - high.astype(F32)).astype(BF16)


def three_terms(array):
    high = array.astype(BF16)
    middle, low = two_terms(array - high.astype(F32))
    return jnp.concatenate([high, middle, low], axis=0)


def first_slot(own):
    return lax.axis_index("tan") * own


def upper_row(slot_ref, w, count):
    return (slot_ref[pl.ds(w, 1), :] < count).astype(F32)


def upper_column(slot_ref, w, count, own):
    row = upper_row(slot_ref, w, count)
    place = iota((own, row.shape[1]), 1) == iota((own, row.shape[1]), 0) + first_slot(own)
    return jnp.sum(jnp.where(place, row, 0.0), axis=1, keepdims=True)


def own_places(electrons, own, wide):
    return (iota((electrons, wide), 0) == iota((electrons, wide), 1) % own + first_slot(own)).astype(BF16)


def pack_kernel(walkers, own, spin_ref, slot_far, values_far, lap_far, packed_ref, value_sums_ref, lines_ref,
                slot_ref, lap_ref, small_sems):
    rows, feat = lap_ref.shape
    electrons = slot_ref.shape[1]
    values_ref = packed_ref.at[pl.ds(0, rows)]
    near = [pltpu.make_async_copy(*ends, small_sems.at[i]) for i, ends in enumerate(
        ((slot_far, slot_ref), (values_far, values_ref), (lap_far, lap_ref)))]
    for copy in near:
        copy.start()
    near[0].wait()
    slots = jnp.zeros((2 * walkers, electrons), jnp.int32)
    for w in range(walkers):
        slots = jnp.where(iota(slots.shape, 0) // 2 == w, slot_ref[w:w + 1, :], slots)

    def column(shape):
        line = iota(shape, 0)
        count = jnp.zeros(shape, jnp.int32)
        for w in range(walkers):
            count = jnp.where(line // 2 == w, spin_ref[w], count)
        return line, count

    line, count = column(slots.shape)
    upper = (slots < count).astype(F32)
    chosen = jnp.where(line % 2 == 0, upper, 1.0 - upper).astype(BF16)
    tiled = dot(chosen, own_places(electrons, own, feat))
    line, count = column(tiled.shape)
    lane = iota(tiled.shape, 1)
    size = jnp.where(line % 2 == 0, count, electrons - count).astype(F32)
    groups = jnp.where(lane < rows, jnp.where(lane // own == line // 2, tiled, 0.0), size)
    groups = jnp.concatenate([groups, jnp.zeros((16 - 2 * walkers, feat), F32)], axis=0).astype(BF16)
    packed_ref[rows:, :] = groups
    lines_ref[...] = groups
    near[1].wait()
    near[2].wait()
    value_sums_ref[0] = dot(groups[:, :rows], values_ref[...])
    value_sums_ref[1] = dot(groups[:, :rows], lap_ref[...])


def sums_kernel(walkers, own, block, lines_ref, far_ref, out_ref, sent_ref, tangent_ref, mask_ref, sems):
    dirs = out_ref.shape[2]
    rows, feat = walkers * own, lines_ref.shape[1]
    repeat = mask_ref.shape[1] // 2
    steps, chunk = dirs // block, block * own

    def fetch(i):
        at = pl.ds(pl.multiple_of(i * chunk, chunk), chunk)
        return pltpu.make_async_copy(far_ref.at[at], tangent_ref.at[at], sems.at[i])

    for i in range(walkers * steps):
        fetch(i).start()
    spots = (iota((rows, feat), 0) % own == iota((rows, feat), 1) % own).astype(F32).astype(BF16)
    tiled = dot(lines_ref[:, :rows], spots)
    place = iota((repeat, feat), 1) // own == iota((repeat, feat), 0)
    for w in range(walkers):
        both = [jnp.where(place, tiled[2 * w + g:2 * w + g + 1], 0.0) for g in range(2)]
        mask_ref[w] = jnp.concatenate(both, axis=0).astype(BF16)

    @pl.loop(0, walkers * steps)
    def _(i):
        w, step = i // steps, i % steps
        mask = mask_ref[w]
        fetch(i).wait()
        for part in range(block // repeat):
            row = pl.multiple_of(i * chunk + part * repeat * own, repeat * own)
            sums = dot(mask, tangent_ref[pl.ds(row, repeat * own), :])
            at = pl.ds(pl.multiple_of(step * block + part * repeat, repeat), repeat)
            out_ref[w, 0, at, :] = sums[:repeat]
            out_ref[w, 1, at, :] = sums[repeat:]
        at = pl.ds(pl.multiple_of(step * block, block), block)
        sent_ref[w, :, at, :] = out_ref[w, :, at, :].astype(BF16)


def picked_rows(groups, mixed):
    lines = jnp.concatenate([groups, groups, groups], axis=0)
    return dot(lines, three_terms(mixed), FIRST)


def layer_kernel(values_ref, lap_ref, packed_ref, own_ref, other_ref, w_self_ref, w_spin_ref,
                 bias_ref, readout_ref, base_ref, curve_ref, weighted_ref):
    rows, feat = values_ref.shape
    lines = packed_ref[rows:, :]
    groups = lines[:, :rows]
    sizes = jnp.maximum(lines[:, rows:rows + 1].astype(F32), 1.0)
    means = ((own_ref[...] + other_ref[...]) / sizes).astype(BF16)
    preact = dot(values_ref[...], w_self_ref[...]) + picked_rows(groups, dot(means[0], w_spin_ref[...])) + bias_ref[...]
    lap_pre = dot(lap_ref[...], w_self_ref[...]) + picked_rows(groups, dot(means[1], w_spin_ref[...]))
    squash = jnp.tanh(preact)
    slopes = 1.0 - squash * squash
    base_ref[...] = slopes * lap_pre
    curve_ref[...] = -2.0 * squash * slopes
    weighted_ref[...] = slopes * readout_ref[...]


def change_kernel(own, block, piece, base, spin_ref, pot_ref, slot_ref, tangent_ref, own_ref, other_ref, w_self_ref,
                  w_spin_ref, readout_ref, base_ref, curve_ref, weighted_ref, before_ref, lap_ref, grad_ref,
                  mixed_ref, places_ref, squares_ref, terms_ref):
    walkers, feat = lap_ref.shape[0], w_self_ref.shape[0]
    dirs = own_ref.shape[2]
    electrons = slot_ref.shape[1]
    steps, pieces = dirs // block, block // piece
    grad_ref[...] = before_ref[...]

    @pl.loop(0, walkers)
    def _(n):
        w = base + n
        count = spin_ref[w]
        ups = count.astype(F32)
        mine = pl.ds(pl.multiple_of(w * own, own), own)
        for g, size in enumerate((ups, electrons - ups)):
            means = ((own_ref[w, g] + other_ref[w, g].astype(F32)) / size).astype(BF16)
            for t, term in enumerate(two_terms(dot(means, w_spin_ref[...]))):
                for c in range(dirs // piece):
                    at = (2 * t + g) * piece
                    mixed_ref[c, at:at + piece, :] = term[c * piece:(c + 1) * piece]
        column = upper_column(slot_ref, w, count, own)
        place = iota((own, 4 * piece), 1)
        chosen = jnp.where(place // piece % 2 == 0, column, 1.0 - column)
        for d in range(piece):
            places_ref[d * own:(d + 1) * own, :] = jnp.where(place % piece == d, chosen, 0.0).astype(BF16)
        squares_ref[...] = jnp.zeros_like(squares_ref)

        @pl.loop(0, steps)
        def _(step):
            weighted = weighted_ref[mine, :]
            squares = squares_ref[...]
            for c in range(pieces):
                row = pl.multiple_of(((w * steps + step) * block + c * piece) * own, own)
                change = dot(places_ref[...], mixed_ref[step * pieces + c]) + dot(
                    tangent_ref[pl.ds(row, piece * own), :], w_self_ref[...])
                for d in range(piece):
                    part = change[d * own:(d + 1) * own]
                    squares = squares + part * part
                    terms = (part * weighted).reshape(own // 8, 8, feat).sum(axis=0)
                    at = (step * block + c * piece + d) * 8
                    terms_ref[pl.ds(pl.multiple_of(at, 8), 8), :] = terms[:, :feat // 2] + terms[:, feat // 2:]
            squares_ref[...] = squares

        laplacian = base_ref[mine, :] + curve_ref[mine, :] * squares_ref[...]
        lap_ref[n] = laplacian
        summed = terms_ref[...].reshape(dirs, 8, feat // 2).sum(axis=1)
        spare = jnp.zeros((grad_ref.shape[1] - dirs, feat // 2), F32)
        summed = jnp.concatenate([summed, spare], axis=0)
        row = dot(jnp.ones((8, feat // 2), F32), summed, LAST, HIGHEST)
        share = jnp.sum(laplacian * readout_ref[...]) - jnp.where(lax.axis_index("tan") == 0, 2.0 * pot_ref[w], 0.0)
        row = jnp.where(iota(row.shape, 1) == dirs, share, row)
        grad_ref[...] = jnp.where(iota(row.shape, 0) == w, row, grad_ref[...])


def energy_kernel(dirs, walkers, own_ref, other_ref, out_ref):
    both = own_ref[...] + other_ref[...]
    place = iota(both.shape, 1)
    parts = jnp.where(place < dirs, both * both, jnp.where(place == dirs, both, 0.0))
    energy = -0.5 * jnp.sum(parts, axis=1, keepdims=True)
    lane = iota((1, 128), 1)
    row = jnp.zeros((1, 128), F32)
    for w in range(walkers):
        row = jnp.where(lane == w, energy[w:w + 1], row)
    out_ref[...] = jnp.broadcast_to(row.reshape(1, 1, 128), out_ref.shape)


def pair(own_ref, other_ref, rows, r):
    values = jnp.concatenate([ref[r, 0:rows, :] for ref in (own_ref, other_ref)], axis=0)
    groups = jnp.concatenate([ref[r, rows:, 0:rows] for ref in (own_ref, other_ref)], axis=1)
    return values, groups


def half_slopes(rows, own_ref, other_ref, w_self_ref, w_spin_ref, bias_ref, readout_ref,
                slopes_ref, sums_ref, means_ref):
    blocks, lines, _ = own_ref.shape
    group = lines - rows
    bunch = min(blocks, 8)

    @pl.loop(0, blocks // bunch)
    def _(i):
        pairs = [pair(own_ref, other_ref, rows, i * bunch + k) for k in range(bunch)]
        means = []
        for k, (values, groups) in enumerate(pairs):
            sizes = jnp.maximum(own_ref[i * bunch + k, rows:, rows:rows + 1].astype(F32), 1.0)
            means.append(dot(groups, values) / sizes)
        means = jnp.concatenate(means, axis=0).astype(BF16)
        at = pl.ds(pl.multiple_of(i * bunch * group, bunch * group), bunch * group)
        means_ref[at, :] = means
        mixed = dot(means, w_spin_ref[...])
        sums = []
        for k, (values, groups) in enumerate(pairs):
            preact = (dot(values, w_self_ref[...]) + picked_rows(groups, mixed[k * group:(k + 1) * group])
                      + bias_ref[...])
            squash = jnp.tanh(preact)
            slopes = ((1.0 - squash * squash) * readout_ref[...]).astype(BF16)
            row = pl.multiple_of((i * bunch + k) * 2 * rows, 2 * rows)
            slopes_ref[pl.ds(row, 2 * rows), :] = slopes
            sums.append(dot(groups, slopes))
        sums_ref[at, :] = jnp.concatenate(sums, axis=0)


def add_products(walkers, own, offsets, first, energy_ref, own_ref, other_ref, slopes_ref, sums_ref, means_ref,
                 self_ref, spin_ref):
    rows = walkers * own
    me = lax.axis_index("walk")
    blocks, lines, feat = own_ref.shape
    group = lines - rows
    bunch = min(blocks, 8)
    everyone = energy_ref.shape[0] * walkers
    center = jnp.sum(jnp.sum(energy_ref[...], axis=0), axis=1, keepdims=True) / everyone
    line = iota((group, feat), 0) // 2

    @pl.loop(0, blocks // bunch)
    def _(i):
        values, high, low, spreads = [], [], [], []
        for k in range(bunch):
            place = first + i * bunch + k
            shift = 0
            for bit, offset in enumerate(offsets):
                shift = shift | ((place >> bit) & 1) * offset
            row = energy_ref[me ^ shift] - center
            row_at = pl.multiple_of((i * bunch + k) * 2 * rows, 2 * rows)
            slopes = slopes_ref[pl.ds(row_at, 2 * rows), :].astype(F32)
            spread = jnp.zeros((group, feat), F32)
            for w in range(walkers):
                spread = jnp.where(line == w, row[:, w:w + 1], spread)
            spreads.append(spread)
            for core in range(2):
                for w in range(walkers):
                    at = core * rows + w * own
                    top, rest = two_terms(slopes[at:at + own] * row[:, w:w + 1])
                    high.append(top)
                    low.append(rest)
            values.append(pair(own_ref, other_ref, rows, i * bunch + k)[0])
        values = jnp.concatenate(values, axis=0)
        self_ref[...] += dot(values, jnp.concatenate(high, axis=0), FIRST) + dot(
            values, jnp.concatenate(low, axis=0), FIRST)
        at = pl.ds(pl.multiple_of(i * bunch * group, bunch * group), bunch * group)
        top, rest = two_terms(sums_ref[at, :] * jnp.concatenate(spreads, axis=0))
        means = means_ref[at, :]
        spin_ref[...] += dot(means, top, FIRST) + dot(means, rest, FIRST)


def first_gradients_kernel(walkers, own, offsets, *refs):
    self_ref, spin_ref = refs[-2:]
    self_ref[...] = jnp.zeros_like(self_ref)
    spin_ref[...] = jnp.zeros_like(spin_ref)
    add_products(walkers, own, offsets, 0, *refs)


def last_gradients_kernel(walkers, own, offsets, energy_ref, own_ref, other_ref, w_self_ref, w_spin_ref, bias_ref,
                          readout_ref, first_self_ref, first_spin_ref, self_ref, spin_ref, *scratch):
    half_slopes(walkers * own, own_ref, other_ref, w_self_ref, w_spin_ref, bias_ref, readout_ref, *scratch)
    self_ref[...] = first_self_ref[...]
    spin_ref[...] = first_spin_ref[...]
    add_products(walkers, own, offsets, own_ref.shape[0], energy_ref, own_ref, other_ref, *scratch, self_ref, spin_ref)


def whole(memory=pltpu.VMEM):
    return pl.BlockSpec(memory_space=memory)


def call(kernel, out_shape, in_specs, scratch=(), cost=None, limit=VMEM_LIMIT, out_specs=None):
    flops, moved = cost if cost is not None else (0, 0)
    return pl.pallas_call(
        kernel,
        out_shape=out_shape,
        in_specs=in_specs,
        out_specs=jax.tree.map(lambda _: whole(), out_shape) if out_specs is None else out_specs,
        scratch_shapes=scratch,
        cost_estimate=pl.CostEstimate(flops=flops, bytes_accessed=moved, transcendentals=0) if cost else None,
        compiler_params=pltpu.CompilerParams(vmem_limit_bytes=limit),
    )


def flip(array, axis, bit):
    size = lax.axis_size(axis)
    return lax.ppermute(array, axis, [(i, i ^ bit) for i in range(size)])


def tied(*arrays):
    return lax.optimization_barrier(arrays)


def shards(values, lap_in, tangent, slot_electron, spin_up, w_self, w_spin, bias, readout, potential):
    walk_size = lax.axis_size("walk")
    walkers, own, feat = values.shape
    dirs = tangent.shape[1]
    shape = jax.ShapeDtypeStruct
    smem = whole(pltpu.SMEM)
    flat = tangent.reshape(walkers * dirs * own, feat)
    values, lap_in = values.reshape(walkers * own, feat), lap_in.reshape(walkers * own, feat)
    bias, readout = bias.reshape(1, feat), readout.reshape(1, feat)
    bits = [1 << b for b in reversed(range(walk_size.bit_length() - 1))]

    small = (2, 16, feat)
    packed, value_sums, lines = call(
        functools.partial(pack_kernel, walkers, own),
        (shape((walkers * own + 16, feat), BF16), shape(small, F32), shape((16, feat), BF16)),
        [smem] + [whole(pltpu.HBM)] * 3,
        [pltpu.VMEM(slot_electron.shape, jnp.int32), pltpu.VMEM(lap_in.shape, BF16), pltpu.SemaphoreType.DMA((3,))],
        limit=63 * MIB)(spin_up, slot_electron, values, lap_in)
    other_value_sums = flip(value_sums, "tan", 1)
    gathered = packed.reshape((1,) + packed.shape)

    repeat, block, piece = feat // own, dirs // 2, dirs // 4
    sums, sent, held = call(
        functools.partial(sums_kernel, walkers, own, block),
        (shape((walkers, 2, dirs, feat), F32), shape((walkers, 2, dirs, feat), BF16), shape(flat.shape, BF16)),
        [whole(), whole(pltpu.HBM)],
        [pltpu.VMEM((walkers, 2 * repeat, feat), BF16), pltpu.SemaphoreType.DMA((walkers * dirs // block,))],
        (flat.size * 32, flat.size * 2), 36 * MIB)(lines, flat)
    received, sent, other_value_sums = tied(flip(gathered, "walk", bits[0]), sent, other_value_sums)
    gathered = jnp.concatenate([gathered, received], axis=0)
    other_sums = flip(sent, "tan", 1)
    for bit in bits[1:-3]:
        gathered = jnp.concatenate([gathered, flip(gathered, "walk", bit)], axis=0)
    received = flip(gathered, "walk", bits[-3])

    full = shape((walkers * own, feat), F32)
    base, curve, weighted = call(
        layer_kernel, (full, full, full), [whole()] * 9, cost=(4 * feat * feat * walkers * own, 4 << 20))(
            values, lap_in, packed, value_sums, other_value_sums, w_self, w_spin, bias, readout)

    counts = (1, walkers - 1)
    wide = -(-(dirs + 1) // 128) * 128

    def change(h, ups, before):
        return call(
            functools.partial(change_kernel, own, block, piece, sum(counts[:h])),
            (shape((counts[h], own, feat), F32), shape((8, wide), F32)),
            [smem, smem] + [whole()] * 11,
            [pltpu.VMEM((dirs // piece, 4 * piece, feat), BF16), pltpu.VMEM((piece * own, 4 * piece), BF16),
             pltpu.VMEM((own, feat), F32), pltpu.VMEM((dirs * 8, feat // 2), F32)],
            (flat.size * feat * counts[h] // 2, flat.size),
        )(ups, potential, slot_electron, held, sums, other_sums, w_self, w_spin, readout, base, curve, weighted, before)

    laplacian, partial = change(0, spin_up, jnp.zeros((8, wide), F32))
    received, late_spin_up, partial = tied(received, spin_up, partial)
    gathered = jnp.concatenate([gathered, received], axis=0)
    received = flip(gathered, "walk", bits[-2])
    more_laplacian, more_partial = change(1, late_spin_up, partial)
    received, more_partial = tied(received, more_partial)
    gathered = jnp.concatenate([gathered, received], axis=0)
    side, other = flip(gathered, "walk", bits[-1]), flip(gathered, "tan", 1)
    rows = call(
        functools.partial(energy_kernel, dirs, walkers), shape((walk_size, 1, 128), F32), [whole()] * 2)(
            more_partial, flip(more_partial, "tan", 1))
    energy = rows[0, 0, :walkers]
    energies = lax.all_to_all(rows, "walk", 0, 0, tiled=True)
    other, more_laplacian, _ = tied(other, more_laplacian, rows)

    blocks = walk_size // 2
    group_shape = (blocks * 16, feat)
    half = [((blocks * 2 * walkers * own, feat), BF16), (group_shape, F32), (group_shape, BF16)]
    weights = (w_self, w_spin, bias, readout)
    slopes = call(
        functools.partial(half_slopes, walkers * own), tuple(shape(*h) for h in half), [whole()] * 6,
        cost=(blocks * 8 * walkers * own * feat * feat, 8 << 20))(gathered, other, *weights)
    laplacian = jnp.concatenate([laplacian, more_laplacian], axis=0)
    energies, side, laplacian, energy, last = tied(energies, side, laplacian, energy, slopes[2])
    slopes = slopes[0], slopes[1], last
    other_side = flip(side, "tan", 1)
    square = shape((feat, feat), F32)
    settings = walkers, own, bits
    first = call(
        functools.partial(first_gradients_kernel, *settings), (square, square), [whole()] * 6,
        cost=(blocks * 16 * walkers * own * feat * feat, 8 << 20))(energies, gathered, other, *slopes)
    grad_self, grad_spin = call(
        functools.partial(last_gradients_kernel, *settings), (square, square), [whole()] * 9,
        [pltpu.VMEM(*h) for h in half])(energies, side, other_side, *weights, *first)
    return laplacian, energy, grad_self, grad_spin


def solution(mesh):
    placed = (
        P("walk", "tan", None),
        P("walk", "tan", None),
        P("walk", None, "tan", None),
        P("walk", None),
        P("walk"),
        P(),
        P(),
        P(),
        P(),
        P("walk"),
    )
    return jax.shard_map(
        shards,
        mesh=mesh,
        in_specs=placed,
        out_specs=(P("walk", "tan", None), P("walk"), P(), P()),
        check_vma=False,
    )
```

```python
import functools

import jax
import jax.numpy as jnp
from jax import lax
from jax.experimental import pallas as pl
from jax.experimental.pallas import tpu as pltpu
from jax.sharding import PartitionSpec as P

F32 = jnp.float32
BF16 = jnp.bfloat16
MIB = 1024 * 1024
VMEM_LIMIT = 24 * MIB
HIGHEST = lax.Precision.HIGHEST
FIRST = ((0,), (0,))
LAST = ((1,), (1,))


def iota(shape, axis):
    return lax.broadcasted_iota(jnp.int32, shape, axis)


def dot(a, b, dims=((1,), (0,)), precision=None):
    return lax.dot_general(a, b, (dims, ((), ())), precision=precision, preferred_element_type=F32)


def two_terms(array):
    high = array.astype(BF16)
    return high, (array - high.astype(F32)).astype(BF16)


def three_terms(array):
    high = array.astype(BF16)
    middle, low = two_terms(array - high.astype(F32))
    return jnp.concatenate([high, middle, low], axis=0)


def first_slot(own):
    return lax.axis_index("tan") * own


def upper_row(slot_ref, w, count):
    return (slot_ref[pl.ds(w, 1), :] < count).astype(F32)


def upper_column(slot_ref, w, count, own):
    row = upper_row(slot_ref, w, count)
    place = iota((own, row.shape[1]), 1) == iota((own, row.shape[1]), 0) + first_slot(own)
    return jnp.sum(jnp.where(place, row, 0.0), axis=1, keepdims=True)


def own_places(electrons, own, wide):
    return (iota((electrons, wide), 0) == iota((electrons, wide), 1) % own + first_slot(own)).astype(BF16)


def pack_kernel(walkers, own, spin_ref, slot_far, values_far, lap_far, packed_ref, value_sums_ref, lines_ref,
                slot_ref, lap_ref, small_sems):
    rows, feat = lap_ref.shape
    electrons = slot_ref.shape[1]
    values_ref = packed_ref.at[pl.ds(0, rows)]
    near = [pltpu.make_async_copy(*ends, small_sems.at[i]) for i, ends in enumerate(
        ((slot_far, slot_ref), (values_far, values_ref), (lap_far, lap_ref)))]
    for copy in near:
        copy.start()
    near[0].wait()
    slots = jnp.zeros((2 * walkers, electrons), jnp.int32)
    for w in range(walkers):
        slots = jnp.where(iota(slots.shape, 0) // 2 == w, slot_ref[w:w + 1, :], slots)

    def column(shape):
        line = iota(shape, 0)
        count = jnp.zeros(shape, jnp.int32)
        for w in range(walkers):
            count = jnp.where(line // 2 == w, spin_ref[w], count)
        return line, count

    line, count = column(slots.shape)
    upper = (slots < count).astype(F32)
    chosen = jnp.where(line % 2 == 0, upper, 1.0 - upper).astype(BF16)
    tiled = dot(chosen, own_places(electrons, own, feat))
    line, count = column(tiled.shape)
    lane = iota(tiled.shape, 1)
    size = jnp.where(line % 2 == 0, count, electrons - count).astype(F32)
    groups = jnp.where(lane < rows, jnp.where(lane // own == line // 2, tiled, 0.0), size)
    groups = jnp.concatenate([groups, jnp.zeros((16 - 2 * walkers, feat), F32)], axis=0).astype(BF16)
    packed_ref[rows:, :] = groups
    lines_ref[...] = groups
    near[1].wait()
    near[2].wait()
    value_sums_ref[0] = dot(groups[:, :rows], values_ref[...])
    value_sums_ref[1] = dot(groups[:, :rows], lap_ref[...])


def sums_kernel(walkers, own, block, lines_ref, far_ref, out_ref, sent_ref, tangent_ref, mask_ref, sems):
    dirs = out_ref.shape[2]
    rows, feat = walkers * own, lines_ref.shape[1]
    repeat = mask_ref.shape[1] // 2
    steps, chunk = dirs // block, block * own

    def fetch(i):
        at = pl.ds(pl.multiple_of(i * chunk, chunk), chunk)
        return pltpu.make_async_copy(far_ref.at[at], tangent_ref.at[at], sems.at[i])

    for i in range(walkers * steps):
        fetch(i).start()
    spots = (iota((rows, feat), 0) % own == iota((rows, feat), 1) % own).astype(F32).astype(BF16)
    tiled = dot(lines_ref[:, :rows], spots)
    place = iota((repeat, feat), 1) // own == iota((repeat, feat), 0)
    for w in range(walkers):
        both = [jnp.where(place, tiled[2 * w + g:2 * w + g + 1], 0.0) for g in range(2)]
        mask_ref[w] = jnp.concatenate(both, axis=0).astype(BF16)

    @pl.loop(0, walkers * steps)
    def _(i):
        w, step = i // steps, i % steps
        mask = mask_ref[w]
        fetch(i).wait()
        for part in range(block // repeat):
            row = pl.multiple_of(i * chunk + part * repeat * own, repeat * own)
            sums = dot(mask, tangent_ref[pl.ds(row, repeat * own), :])
            at = pl.ds(pl.multiple_of(step * block + part * repeat, repeat), repeat)
            out_ref[w, 0, at, :] = sums[:repeat]
            out_ref[w, 1, at, :] = sums[repeat:]
        at = pl.ds(pl.multiple_of(step * block, block), block)
        sent_ref[w, :, at, :] = out_ref[w, :, at, :].astype(BF16)


def picked_rows(groups, mixed):
    lines = jnp.concatenate([groups, groups, groups], axis=0)
    return dot(lines, three_terms(mixed), FIRST)


def layer_kernel(values_ref, lap_ref, packed_ref, own_ref, other_ref, w_self_ref, w_spin_ref,
                 bias_ref, readout_ref, base_ref, curve_ref, weighted_ref):
    rows, feat = values_ref.shape
    lines = packed_ref[rows:, :]
    groups = lines[:, :rows]
    sizes = jnp.maximum(lines[:, rows:rows + 1].astype(F32), 1.0)
    means = ((own_ref[...] + other_ref[...]) / sizes).astype(BF16)
    preact = dot(values_ref[...], w_self_ref[...]) + picked_rows(groups, dot(means[0], w_spin_ref[...])) + bias_ref[...]
    lap_pre = dot(lap_ref[...], w_self_ref[...]) + picked_rows(groups, dot(means[1], w_spin_ref[...]))
    squash = jnp.tanh(preact)
    slopes = 1.0 - squash * squash
    base_ref[...] = slopes * lap_pre
    curve_ref[...] = -2.0 * squash * slopes
    weighted_ref[...] = slopes * readout_ref[...]


def change_kernel(own, block, piece, base, spin_ref, pot_ref, slot_ref, tangent_ref, own_ref, other_ref, w_self_ref,
                  w_spin_ref, readout_ref, base_ref, curve_ref, weighted_ref, before_ref, lap_ref, grad_ref,
                  mixed_ref, squares_ref, column_ref, terms_ref):
    walkers, feat = lap_ref.shape[0], w_self_ref.shape[0]
    dirs = own_ref.shape[2]
    electrons = slot_ref.shape[1]
    steps, part = dirs // block, 8
    halves = [slice(0, feat // 2), slice(feat // 2, feat)]
    grad_ref[...] = before_ref[...]

    @pl.loop(0, walkers)
    def _(n):
        w = base + n
        count = spin_ref[w]
        ups = count.astype(F32)
        mine = pl.ds(pl.multiple_of(w * own, own), own)
        for g, size in enumerate((ups, electrons - ups)):
            means = ((own_ref[w, g] + other_ref[w, g].astype(F32)) / size).astype(BF16)
            mixed_ref[g] = dot(means, w_spin_ref[...])
        column_ref[...] = jnp.broadcast_to(upper_column(slot_ref, w, count, own), (own, feat // 2))
        squares_ref[...] = jnp.zeros_like(squares_ref)

        @pl.loop(0, steps)
        def _(step):
            upper = column_ref[...] > 0.5
            weighted = [weighted_ref[mine, lanes] for lanes in halves]
            squares = [squares_ref[:, lanes] for lanes in halves]
            for c in range(block // piece):
                row = pl.multiple_of(((w * steps + step) * block + c * piece) * own, own)
                plain = dot(tangent_ref[pl.ds(row, piece * own), :], w_self_ref[...])
                for p in range(piece // part):
                    at = pl.multiple_of(step * block + c * piece + p * part, part)
                    mixed = mixed_ref[:, pl.ds(at, part), :]
                    for d in range(part):
                        row = (p * part + d) * own
                        terms = jnp.zeros((8, feat // 2), F32)
                        for h, lanes in enumerate(halves):
                            picked = jnp.where(upper, mixed[0, d:d + 1, lanes], mixed[1, d:d + 1, lanes])
                            change = plain[row:row + own, lanes] + picked
                            squares[h] = squares[h] + change * change
                            terms = terms + (change * weighted[h]).reshape(own // 8, 8, feat // 2).sum(axis=0)
                        terms_ref[pl.ds(pl.multiple_of(at * 8 + d * 8, 8), 8), :] = terms
            for lanes, total in zip(halves, squares):
                squares_ref[:, lanes] = total

        laplacian = base_ref[mine, :] + curve_ref[mine, :] * squares_ref[...]
        lap_ref[n] = laplacian
        summed = terms_ref[...].reshape(dirs, 8, feat // 2).sum(axis=1)
        spare = jnp.zeros((grad_ref.shape[1] - dirs, feat // 2), F32)
        summed = jnp.concatenate([summed, spare], axis=0)
        row = dot(jnp.ones((8, feat // 2), F32), summed, LAST, HIGHEST)
        share = jnp.sum(laplacian * readout_ref[...]) - jnp.where(lax.axis_index("tan") == 0, 2.0 * pot_ref[w], 0.0)
        row = jnp.where(iota(row.shape, 1) == dirs, share, row)
        grad_ref[...] = jnp.where(iota(row.shape, 0) == w, row, grad_ref[...])


def energy_kernel(dirs, walkers, own_ref, other_ref, out_ref):
    both = own_ref[...] + other_ref[...]
    place = iota(both.shape, 1)
    parts = jnp.where(place < dirs, both * both, jnp.where(place == dirs, both, 0.0))
    energy = -0.5 * jnp.sum(parts, axis=1, keepdims=True)
    lane = iota((1, 128), 1)
    row = jnp.zeros((1, 128), F32)
    for w in range(walkers):
        row = jnp.where(lane == w, energy[w:w + 1], row)
    out_ref[...] = jnp.broadcast_to(row.reshape(1, 1, 128), out_ref.shape)


def pair(own_ref, other_ref, rows, r):
    values = jnp.concatenate([ref[r, 0:rows, :] for ref in (own_ref, other_ref)], axis=0)
    groups = jnp.concatenate([ref[r, rows:, 0:rows] for ref in (own_ref, other_ref)], axis=1)
    return values, groups


def half_slopes(rows, own_ref, other_ref, w_self_ref, w_spin_ref, bias_ref, readout_ref,
                slopes_ref, sums_ref, means_ref):
    blocks, lines, _ = own_ref.shape
    group = lines - rows
    bunch = min(blocks, 8)

    @pl.loop(0, blocks // bunch)
    def _(i):
        pairs = [pair(own_ref, other_ref, rows, i * bunch + k) for k in range(bunch)]
        means = []
        for k, (values, groups) in enumerate(pairs):
            sizes = jnp.maximum(own_ref[i * bunch + k, rows:, rows:rows + 1].astype(F32), 1.0)
            means.append(dot(groups, values) / sizes)
        means = jnp.concatenate(means, axis=0).astype(BF16)
        at = pl.ds(pl.multiple_of(i * bunch * group, bunch * group), bunch * group)
        means_ref[at, :] = means
        mixed = dot(means, w_spin_ref[...])
        sums = []
        for k, (values, groups) in enumerate(pairs):
            preact = (dot(values, w_self_ref[...]) + picked_rows(groups, mixed[k * group:(k + 1) * group])
                      + bias_ref[...])
            squash = jnp.tanh(preact)
            slopes = ((1.0 - squash * squash) * readout_ref[...]).astype(BF16)
            row = pl.multiple_of((i * bunch + k) * 2 * rows, 2 * rows)
            slopes_ref[pl.ds(row, 2 * rows), :] = slopes
            sums.append(dot(groups, slopes))
        sums_ref[at, :] = jnp.concatenate(sums, axis=0)


def add_products(walkers, own, offsets, first, energy_ref, own_ref, other_ref, slopes_ref, sums_ref, means_ref,
                 self_ref, spin_ref):
    rows = walkers * own
    me = lax.axis_index("walk")
    blocks, lines, feat = own_ref.shape
    group = lines - rows
    bunch = min(blocks, 8)
    everyone = energy_ref.shape[0] * walkers
    center = jnp.sum(jnp.sum(energy_ref[...], axis=0), axis=1, keepdims=True) / everyone
    line = iota((group, feat), 0) // 2

    @pl.loop(0, blocks // bunch)
    def _(i):
        values, high, low, spreads = [], [], [], []
        for k in range(bunch):
            place = first + i * bunch + k
            shift = 0
            for bit, offset in enumerate(offsets):
                shift = shift | ((place >> bit) & 1) * offset
            row = energy_ref[me ^ shift] - center
            row_at = pl.multiple_of((i * bunch + k) * 2 * rows, 2 * rows)
            slopes = slopes_ref[pl.ds(row_at, 2 * rows), :].astype(F32)
            spread = jnp.zeros((group, feat), F32)
            for w in range(walkers):
                spread = jnp.where(line == w, row[:, w:w + 1], spread)
            spreads.append(spread)
            for core in range(2):
                for w in range(walkers):
                    at = core * rows + w * own
                    top, rest = two_terms(slopes[at:at + own] * row[:, w:w + 1])
                    high.append(top)
                    low.append(rest)
            values.append(pair(own_ref, other_ref, rows, i * bunch + k)[0])
        values = jnp.concatenate(values, axis=0)
        self_ref[...] += dot(values, jnp.concatenate(high, axis=0), FIRST) + dot(
            values, jnp.concatenate(low, axis=0), FIRST)
        at = pl.ds(pl.multiple_of(i * bunch * group, bunch * group), bunch * group)
        top, rest = two_terms(sums_ref[at, :] * jnp.concatenate(spreads, axis=0))
        means = means_ref[at, :]
        spin_ref[...] += dot(means, top, FIRST) + dot(means, rest, FIRST)


def first_gradients_kernel(walkers, own, offsets, *refs):
    self_ref, spin_ref = refs[-2:]
    self_ref[...] = jnp.zeros_like(self_ref)
    spin_ref[...] = jnp.zeros_like(spin_ref)
    add_products(walkers, own, offsets, 0, *refs)


def last_gradients_kernel(walkers, own, offsets, energy_ref, own_ref, other_ref, w_self_ref, w_spin_ref, bias_ref,
                          readout_ref, first_self_ref, first_spin_ref, self_ref, spin_ref, *scratch):
    half_slopes(walkers * own, own_ref, other_ref, w_self_ref, w_spin_ref, bias_ref, readout_ref, *scratch)
    self_ref[...] = first_self_ref[...]
    spin_ref[...] = first_spin_ref[...]
    add_products(walkers, own, offsets, own_ref.shape[0], energy_ref, own_ref, other_ref, *scratch, self_ref, spin_ref)


def whole(memory=pltpu.VMEM):
    return pl.BlockSpec(memory_space=memory)


def call(kernel, out_shape, in_specs, scratch=(), cost=None, limit=VMEM_LIMIT, out_specs=None):
    flops, moved = cost if cost is not None else (0, 0)
    return pl.pallas_call(
        kernel,
        out_shape=out_shape,
        in_specs=in_specs,
        out_specs=jax.tree.map(lambda _: whole(), out_shape) if out_specs is None else out_specs,
        scratch_shapes=scratch,
        cost_estimate=pl.CostEstimate(flops=flops, bytes_accessed=moved, transcendentals=0) if cost else None,
        compiler_params=pltpu.CompilerParams(vmem_limit_bytes=limit),
    )


def flip(array, axis, bit):
    size = lax.axis_size(axis)
    return lax.ppermute(array, axis, [(i, i ^ bit) for i in range(size)])


def tied(*arrays):
    return lax.optimization_barrier(arrays)


def shards(values, lap_in, tangent, slot_electron, spin_up, w_self, w_spin, bias, readout, potential):
    walk_size = lax.axis_size("walk")
    walkers, own, feat = values.shape
    dirs = tangent.shape[1]
    shape = jax.ShapeDtypeStruct
    smem = whole(pltpu.SMEM)
    flat = tangent.reshape(walkers * dirs * own, feat)
    values, lap_in = values.reshape(walkers * own, feat), lap_in.reshape(walkers * own, feat)
    bias, readout = bias.reshape(1, feat), readout.reshape(1, feat)
    bits = [1 << b for b in reversed(range(walk_size.bit_length() - 1))]

    small = (2, 16, feat)
    packed, value_sums, lines = call(
        functools.partial(pack_kernel, walkers, own),
        (shape((walkers * own + 16, feat), BF16), shape(small, F32), shape((16, feat), BF16)),
        [smem] + [whole(pltpu.HBM)] * 3,
        [pltpu.VMEM(slot_electron.shape, jnp.int32), pltpu.VMEM(lap_in.shape, BF16), pltpu.SemaphoreType.DMA((3,))],
        limit=63 * MIB)(spin_up, slot_electron, values, lap_in)
    other_value_sums = flip(value_sums, "tan", 1)
    gathered = packed.reshape((1,) + packed.shape)

    repeat, block, piece = feat // own, dirs // 2, dirs // 4
    sums, sent, held = call(
        functools.partial(sums_kernel, walkers, own, block),
        (shape((walkers, 2, dirs, feat), F32), shape((walkers, 2, dirs, feat), BF16), shape(flat.shape, BF16)),
        [whole(), whole(pltpu.HBM)],
        [pltpu.VMEM((walkers, 2 * repeat, feat), BF16), pltpu.SemaphoreType.DMA((walkers * dirs // block,))],
        (flat.size * 32, flat.size * 2), 36 * MIB)(lines, flat)
    received, sent, other_value_sums = tied(flip(gathered, "walk", bits[0]), sent, other_value_sums)
    gathered = jnp.concatenate([gathered, received], axis=0)
    other_sums = flip(sent, "tan", 1)
    for bit in bits[1:-3]:
        gathered = jnp.concatenate([gathered, flip(gathered, "walk", bit)], axis=0)
    received = flip(gathered, "walk", bits[-3])

    full = shape((walkers * own, feat), F32)
    base, curve, weighted = call(
        layer_kernel, (full, full, full), [whole()] * 9, cost=(4 * feat * feat * walkers * own, 4 << 20))(
            values, lap_in, packed, value_sums, other_value_sums, w_self, w_spin, bias, readout)

    counts = (1, walkers - 1)
    wide = -(-(dirs + 1) // 128) * 128

    def change(h, ups, before):
        return call(
            functools.partial(change_kernel, own, block, piece, sum(counts[:h])),
            (shape((counts[h], own, feat), F32), shape((8, wide), F32)),
            [smem, smem] + [whole()] * 11,
            [pltpu.VMEM((2, dirs, feat), F32), pltpu.VMEM((own, feat), F32), pltpu.VMEM((own, feat // 2), F32),
             pltpu.VMEM((dirs * 8, feat // 2), F32)],
            (flat.size * feat * counts[h] // 2, flat.size),
        )(ups, potential, slot_electron, held, sums, other_sums, w_self, w_spin, readout, base, curve, weighted, before)

    laplacian, partial = change(0, spin_up, jnp.zeros((8, wide), F32))
    received, late_spin_up, partial = tied(received, spin_up, partial)
    gathered = jnp.concatenate([gathered, received], axis=0)
    received = flip(gathered, "walk", bits[-2])
    more_laplacian, more_partial = change(1, late_spin_up, partial)
    received, more_partial = tied(received, more_partial)
    gathered = jnp.concatenate([gathered, received], axis=0)
    side, other = flip(gathered, "walk", bits[-1]), flip(gathered, "tan", 1)
    rows = call(
        functools.partial(energy_kernel, dirs, walkers), shape((walk_size, 1, 128), F32), [whole()] * 2)(
            more_partial, flip(more_partial, "tan", 1))
    energy = rows[0, 0, :walkers]
    energies = lax.all_to_all(rows, "walk", 0, 0, tiled=True)
    other, more_laplacian, _ = tied(other, more_laplacian, rows)

    blocks = walk_size // 2
    group_shape = (blocks * 16, feat)
    half = [((blocks * 2 * walkers * own, feat), BF16), (group_shape, F32), (group_shape, BF16)]
    weights = (w_self, w_spin, bias, readout)
    slopes = call(
        functools.partial(half_slopes, walkers * own), tuple(shape(*h) for h in half), [whole()] * 6,
        cost=(blocks * 8 * walkers * own * feat * feat, 8 << 20))(gathered, other, *weights)
    laplacian = jnp.concatenate([laplacian, more_laplacian], axis=0)
    energies, side, laplacian, energy, last = tied(energies, side, laplacian, energy, slopes[2])
    slopes = slopes[0], slopes[1], last
    other_side = flip(side, "tan", 1)
    square = shape((feat, feat), F32)
    settings = walkers, own, bits
    first = call(
        functools.partial(first_gradients_kernel, *settings), (square, square), [whole()] * 6,
        cost=(blocks * 16 * walkers * own * feat * feat, 8 << 20))(energies, gathered, other, *slopes)
    grad_self, grad_spin = call(
        functools.partial(last_gradients_kernel, *settings), (square, square), [whole()] * 9,
        [pltpu.VMEM(*h) for h in half])(energies, side, other_side, *weights, *first)
    return laplacian, energy, grad_self, grad_spin


def solution(mesh):
    placed = (
        P("walk", "tan", None),
        P("walk", "tan", None),
        P("walk", None, "tan", None),
        P("walk", None),
        P("walk"),
        P(),
        P(),
        P(),
        P(),
        P("walk"),
    )
    return jax.shard_map(
        shards,
        mesh=mesh,
        in_specs=placed,
        out_specs=(P("walk", "tan", None), P("walk"), P(), P()),
        check_vma=False,
    )
```

```python
import functools

import jax
import jax.numpy as jnp
from jax import lax
from jax.experimental import pallas as pl
from jax.experimental.pallas import tpu as pltpu
from jax.sharding import PartitionSpec as P

F32 = jnp.float32
BF16 = jnp.bfloat16
MIB = 1024 * 1024
VMEM_LIMIT = 24 * MIB
HIGHEST = lax.Precision.HIGHEST
FIRST = ((0,), (0,))
LAST = ((1,), (1,))


def iota(shape, axis):
    return lax.broadcasted_iota(jnp.int32, shape, axis)


def dot(a, b, dims=((1,), (0,)), precision=None):
    return lax.dot_general(a, b, (dims, ((), ())), precision=precision, preferred_element_type=F32)


def two_terms(array):
    high = array.astype(BF16)
    return high, (array - high.astype(F32)).astype(BF16)


def three_terms(array):
    high = array.astype(BF16)
    middle, low = two_terms(array - high.astype(F32))
    return jnp.concatenate([high, middle, low], axis=0)


def first_slot(own):
    return lax.axis_index("tan") * own


def upper_row(slot_ref, w, count):
    return (slot_ref[pl.ds(w, 1), :] < count).astype(F32)


def upper_column(slot_ref, w, count, own):
    row = upper_row(slot_ref, w, count)
    place = iota((own, row.shape[1]), 1) == iota((own, row.shape[1]), 0) + first_slot(own)
    return jnp.sum(jnp.where(place, row, 0.0), axis=1, keepdims=True)


def own_places(electrons, own, wide):
    return (iota((electrons, wide), 0) == iota((electrons, wide), 1) % own + first_slot(own)).astype(BF16)


def pack_kernel(walkers, own, spin_ref, slot_far, values_far, lap_far, packed_ref, value_sums_ref, lines_ref,
                slot_ref, lap_ref, small_sems):
    rows, feat = lap_ref.shape
    electrons = slot_ref.shape[1]
    values_ref = packed_ref.at[pl.ds(0, rows)]
    near = [pltpu.make_async_copy(*ends, small_sems.at[i]) for i, ends in enumerate(
        ((slot_far, slot_ref), (values_far, values_ref), (lap_far, lap_ref)))]
    for copy in near:
        copy.start()
    near[0].wait()
    slots = jnp.zeros((2 * walkers, electrons), jnp.int32)
    for w in range(walkers):
        slots = jnp.where(iota(slots.shape, 0) // 2 == w, slot_ref[w:w + 1, :], slots)

    def column(shape):
        line = iota(shape, 0)
        count = jnp.zeros(shape, jnp.int32)
        for w in range(walkers):
            count = jnp.where(line // 2 == w, spin_ref[w], count)
        return line, count

    line, count = column(slots.shape)
    upper = (slots < count).astype(F32)
    chosen = jnp.where(line % 2 == 0, upper, 1.0 - upper).astype(BF16)
    tiled = dot(chosen, own_places(electrons, own, feat))
    line, count = column(tiled.shape)
    lane = iota(tiled.shape, 1)
    size = jnp.where(line % 2 == 0, count, electrons - count).astype(F32)
    groups = jnp.where(lane < rows, jnp.where(lane // own == line // 2, tiled, 0.0), size)
    groups = jnp.concatenate([groups, jnp.zeros((16 - 2 * walkers, feat), F32)], axis=0).astype(BF16)
    packed_ref[rows:, :] = groups
    lines_ref[...] = groups
    near[1].wait()
    near[2].wait()
    value_sums_ref[0] = dot(groups[:, :rows], values_ref[...])
    value_sums_ref[1] = dot(groups[:, :rows], lap_ref[...])


def sums_kernel(walkers, own, block, lines_ref, far_ref, out_ref, sent_ref, tangent_ref, mask_ref, sems):
    dirs = out_ref.shape[2]
    rows, feat = walkers * own, lines_ref.shape[1]
    repeat = mask_ref.shape[1] // 2
    steps, chunk = dirs // block, block * own

    def fetch(i):
        at = pl.ds(pl.multiple_of(i * chunk, chunk), chunk)
        return pltpu.make_async_copy(far_ref.at[at], tangent_ref.at[at], sems.at[i])

    for i in range(walkers * steps):
        fetch(i).start()
    spots = (iota((rows, feat), 0) % own == iota((rows, feat), 1) % own).astype(F32).astype(BF16)
    tiled = dot(lines_ref[:, :rows], spots)
    place = iota((repeat, feat), 1) // own == iota((repeat, feat), 0)
    for w in range(walkers):
        both = [jnp.where(place, tiled[2 * w + g:2 * w + g + 1], 0.0) for g in range(2)]
        mask_ref[w] = jnp.concatenate(both, axis=0).astype(BF16)

    @pl.loop(0, walkers * steps)
    def _(i):
        w, step = i // steps, i % steps
        mask = mask_ref[w]
        fetch(i).wait()
        for part in range(block // repeat):
            row = pl.multiple_of(i * chunk + part * repeat * own, repeat * own)
            sums = dot(mask, tangent_ref[pl.ds(row, repeat * own), :])
            at = pl.ds(pl.multiple_of(step * block + part * repeat, repeat), repeat)
            out_ref[w, 0, at, :] = sums[:repeat]
            out_ref[w, 1, at, :] = sums[repeat:]
        at = pl.ds(pl.multiple_of(step * block, block), block)
        sent_ref[w, :, at, :] = out_ref[w, :, at, :].astype(BF16)


def picked_rows(groups, mixed):
    lines = jnp.concatenate([groups, groups, groups], axis=0)
    return dot(lines, three_terms(mixed), FIRST)


def layer_kernel(values_ref, lap_ref, packed_ref, own_ref, other_ref, w_self_ref, w_spin_ref,
                 bias_ref, readout_ref, base_ref, curve_ref, weighted_ref):
    rows, feat = values_ref.shape
    lines = packed_ref[rows:, :]
    groups = lines[:, :rows]
    sizes = jnp.maximum(lines[:, rows:rows + 1].astype(F32), 1.0)
    means = ((own_ref[...] + other_ref[...]) / sizes).astype(BF16)
    preact = dot(values_ref[...], w_self_ref[...]) + picked_rows(groups, dot(means[0], w_spin_ref[...])) + bias_ref[...]
    lap_pre = dot(lap_ref[...], w_self_ref[...]) + picked_rows(groups, dot(means[1], w_spin_ref[...]))
    squash = jnp.tanh(preact)
    slopes = 1.0 - squash * squash
    base_ref[...] = slopes * lap_pre
    curve_ref[...] = -2.0 * squash * slopes
    weighted_ref[...] = slopes * readout_ref[...]


def change_kernel(own, block, piece, base, spin_ref, pot_ref, slot_ref, tangent_ref, own_ref, other_ref, w_self_ref,
                  w_spin_ref, readout_ref, base_ref, curve_ref, weighted_ref, before_ref, lap_ref, grad_ref,
                  mixed_ref, squares_ref, column_ref, terms_ref):
    walkers, feat = lap_ref.shape[0], w_self_ref.shape[0]
    dirs = own_ref.shape[2]
    electrons = slot_ref.shape[1]
    steps, part = dirs // block, 8
    halves = [slice(0, feat // 2), slice(feat // 2, feat)]
    grad_ref[...] = before_ref[...]

    @pl.loop(0, walkers)
    def _(n):
        w = base + n
        count = spin_ref[w]
        ups = count.astype(F32)
        mine = pl.ds(pl.multiple_of(w * own, own), own)
        for g, size in enumerate((ups, electrons - ups)):
            means = ((own_ref[w, g] + other_ref[w, g].astype(F32)) / size).astype(BF16)
            mixed_ref[g] = dot(means, w_spin_ref[...])
        column_ref[...] = jnp.broadcast_to(upper_column(slot_ref, w, count, own), (own, feat // 2))
        squares_ref[...] = jnp.zeros_like(squares_ref)

        @pl.loop(0, steps)
        def _(step):
            upper = column_ref[...] > 0.5
            weighted = [weighted_ref[mine, lanes] for lanes in halves]
            squares = [squares_ref[:, lanes] for lanes in halves]
            def multiply(c):
                row = pl.multiple_of(((w * steps + step) * block + c * piece) * own, own)
                return dot(tangent_ref[pl.ds(row, piece * own), :], w_self_ref[...])

            later = multiply(0)
            for c in range(block // piece):
                plain, later = later, multiply(c + 1) if c + 1 < block // piece else None
                for p in range(piece // part):
                    at = pl.multiple_of(step * block + c * piece + p * part, part)
                    mixed = mixed_ref[:, pl.ds(at, part), :]
                    for d in range(part):
                        row = (p * part + d) * own
                        terms = jnp.zeros((8, feat // 2), F32)
                        for h, lanes in enumerate(halves):
                            picked = jnp.where(upper, mixed[0, d:d + 1, lanes], mixed[1, d:d + 1, lanes])
                            change = plain[row:row + own, lanes] + picked
                            squares[h] = squares[h] + change * change
                            terms = terms + (change * weighted[h]).reshape(own // 8, 8, feat // 2).sum(axis=0)
                        terms_ref[pl.ds(pl.multiple_of(at * 8 + d * 8, 8), 8), :] = terms
            for lanes, total in zip(halves, squares):
                squares_ref[:, lanes] = total

        laplacian = base_ref[mine, :] + curve_ref[mine, :] * squares_ref[...]
        lap_ref[n] = laplacian
        summed = terms_ref[...].reshape(dirs, 8, feat // 2).sum(axis=1)
        spare = jnp.zeros((grad_ref.shape[1] - dirs, feat // 2), F32)
        summed = jnp.concatenate([summed, spare], axis=0)
        row = dot(jnp.ones((8, feat // 2), F32), summed, LAST, HIGHEST)
        share = jnp.sum(laplacian * readout_ref[...]) - jnp.where(lax.axis_index("tan") == 0, 2.0 * pot_ref[w], 0.0)
        row = jnp.where(iota(row.shape, 1) == dirs, share, row)
        grad_ref[...] = jnp.where(iota(row.shape, 0) == w, row, grad_ref[...])


def energy_kernel(dirs, walkers, own_ref, other_ref, out_ref):
    both = own_ref[...] + other_ref[...]
    place = iota(both.shape, 1)
    parts = jnp.where(place < dirs, both * both, jnp.where(place == dirs, both, 0.0))
    energy = -0.5 * jnp.sum(parts, axis=1, keepdims=True)
    lane = iota((1, 128), 1)
    row = jnp.zeros((1, 128), F32)
    for w in range(walkers):
        row = jnp.where(lane == w, energy[w:w + 1], row)
    out_ref[...] = jnp.broadcast_to(row.reshape(1, 1, 128), out_ref.shape)


def pair(own_ref, other_ref, rows, r):
    values = jnp.concatenate([ref[r, 0:rows, :] for ref in (own_ref, other_ref)], axis=0)
    groups = jnp.concatenate([ref[r, rows:, 0:rows] for ref in (own_ref, other_ref)], axis=1)
    return values, groups


def half_slopes(rows, own_ref, other_ref, w_self_ref, w_spin_ref, bias_ref, readout_ref,
                slopes_ref, sums_ref, means_ref):
    blocks, lines, _ = own_ref.shape
    group = lines - rows
    bunch = min(blocks, 8)

    @pl.loop(0, blocks // bunch)
    def _(i):
        pairs = [pair(own_ref, other_ref, rows, i * bunch + k) for k in range(bunch)]
        means = []
        for k, (values, groups) in enumerate(pairs):
            sizes = jnp.maximum(own_ref[i * bunch + k, rows:, rows:rows + 1].astype(F32), 1.0)
            means.append(dot(groups, values) / sizes)
        means = jnp.concatenate(means, axis=0).astype(BF16)
        at = pl.ds(pl.multiple_of(i * bunch * group, bunch * group), bunch * group)
        means_ref[at, :] = means
        mixed = dot(means, w_spin_ref[...])
        sums = []
        for k, (values, groups) in enumerate(pairs):
            preact = (dot(values, w_self_ref[...]) + picked_rows(groups, mixed[k * group:(k + 1) * group])
                      + bias_ref[...])
            squash = jnp.tanh(preact)
            slopes = ((1.0 - squash * squash) * readout_ref[...]).astype(BF16)
            row = pl.multiple_of((i * bunch + k) * 2 * rows, 2 * rows)
            slopes_ref[pl.ds(row, 2 * rows), :] = slopes
            sums.append(dot(groups, slopes))
        sums_ref[at, :] = jnp.concatenate(sums, axis=0)


def add_products(walkers, own, offsets, first, energy_ref, own_ref, other_ref, slopes_ref, sums_ref, means_ref,
                 self_ref, spin_ref):
    rows = walkers * own
    me = lax.axis_index("walk")
    blocks, lines, feat = own_ref.shape
    group = lines - rows
    bunch = min(blocks, 8)
    everyone = energy_ref.shape[0] * walkers
    center = jnp.sum(jnp.sum(energy_ref[...], axis=0), axis=1, keepdims=True) / everyone
    line = iota((group, feat), 0) // 2

    @pl.loop(0, blocks // bunch)
    def _(i):
        values, high, low, spreads = [], [], [], []
        for k in range(bunch):
            place = first + i * bunch + k
            shift = 0
            for bit, offset in enumerate(offsets):
                shift = shift | ((place >> bit) & 1) * offset
            row = energy_ref[me ^ shift] - center
            row_at = pl.multiple_of((i * bunch + k) * 2 * rows, 2 * rows)
            slopes = slopes_ref[pl.ds(row_at, 2 * rows), :].astype(F32)
            spread = jnp.zeros((group, feat), F32)
            for w in range(walkers):
                spread = jnp.where(line == w, row[:, w:w + 1], spread)
            spreads.append(spread)
            for core in range(2):
                for w in range(walkers):
                    at = core * rows + w * own
                    top, rest = two_terms(slopes[at:at + own] * row[:, w:w + 1])
                    high.append(top)
                    low.append(rest)
            values.append(pair(own_ref, other_ref, rows, i * bunch + k)[0])
        values = jnp.concatenate(values, axis=0)
        self_ref[...] += dot(values, jnp.concatenate(high, axis=0), FIRST) + dot(
            values, jnp.concatenate(low, axis=0), FIRST)
        at = pl.ds(pl.multiple_of(i * bunch * group, bunch * group), bunch * group)
        top, rest = two_terms(sums_ref[at, :] * jnp.concatenate(spreads, axis=0))
        means = means_ref[at, :]
        spin_ref[...] += dot(means, top, FIRST) + dot(means, rest, FIRST)


def first_gradients_kernel(walkers, own, offsets, *refs):
    self_ref, spin_ref = refs[-2:]
    self_ref[...] = jnp.zeros_like(self_ref)
    spin_ref[...] = jnp.zeros_like(spin_ref)
    add_products(walkers, own, offsets, 0, *refs)


def last_gradients_kernel(walkers, own, offsets, energy_ref, own_ref, other_ref, w_self_ref, w_spin_ref, bias_ref,
                          readout_ref, first_self_ref, first_spin_ref, self_ref, spin_ref, *scratch):
    half_slopes(walkers * own, own_ref, other_ref, w_self_ref, w_spin_ref, bias_ref, readout_ref, *scratch)
    self_ref[...] = first_self_ref[...]
    spin_ref[...] = first_spin_ref[...]
    add_products(walkers, own, offsets, own_ref.shape[0], energy_ref, own_ref, other_ref, *scratch, self_ref, spin_ref)


def whole(memory=pltpu.VMEM):
    return pl.BlockSpec(memory_space=memory)


def call(kernel, out_shape, in_specs, scratch=(), cost=None, limit=VMEM_LIMIT, out_specs=None):
    flops, moved = cost if cost is not None else (0, 0)
    return pl.pallas_call(
        kernel,
        out_shape=out_shape,
        in_specs=in_specs,
        out_specs=jax.tree.map(lambda _: whole(), out_shape) if out_specs is None else out_specs,
        scratch_shapes=scratch,
        cost_estimate=pl.CostEstimate(flops=flops, bytes_accessed=moved, transcendentals=0) if cost else None,
        compiler_params=pltpu.CompilerParams(vmem_limit_bytes=limit),
    )


def flip(array, axis, bit):
    size = lax.axis_size(axis)
    return lax.ppermute(array, axis, [(i, i ^ bit) for i in range(size)])


def tied(*arrays):
    return lax.optimization_barrier(arrays)


def shards(values, lap_in, tangent, slot_electron, spin_up, w_self, w_spin, bias, readout, potential):
    walk_size = lax.axis_size("walk")
    walkers, own, feat = values.shape
    dirs = tangent.shape[1]
    shape = jax.ShapeDtypeStruct
    smem = whole(pltpu.SMEM)
    flat = tangent.reshape(walkers * dirs * own, feat)
    values, lap_in = values.reshape(walkers * own, feat), lap_in.reshape(walkers * own, feat)
    bias, readout = bias.reshape(1, feat), readout.reshape(1, feat)
    bits = [1 << b for b in reversed(range(walk_size.bit_length() - 1))]

    small = (2, 16, feat)
    packed, value_sums, lines = call(
        functools.partial(pack_kernel, walkers, own),
        (shape((walkers * own + 16, feat), BF16), shape(small, F32), shape((16, feat), BF16)),
        [smem] + [whole(pltpu.HBM)] * 3,
        [pltpu.VMEM(slot_electron.shape, jnp.int32), pltpu.VMEM(lap_in.shape, BF16), pltpu.SemaphoreType.DMA((3,))],
        limit=63 * MIB)(spin_up, slot_electron, values, lap_in)
    other_value_sums = flip(value_sums, "tan", 1)
    gathered = packed.reshape((1,) + packed.shape)

    repeat, block = feat // own, dirs // 2
    sums, sent, held = call(
        functools.partial(sums_kernel, walkers, own, block),
        (shape((walkers, 2, dirs, feat), F32), shape((walkers, 2, dirs, feat), BF16), shape(flat.shape, BF16)),
        [whole(), whole(pltpu.HBM)],
        [pltpu.VMEM((walkers, 2 * repeat, feat), BF16), pltpu.SemaphoreType.DMA((walkers * dirs // block,))],
        (flat.size * 32, flat.size * 2), 36 * MIB)(lines, flat)
    received, sent, other_value_sums = tied(flip(gathered, "walk", bits[0]), sent, other_value_sums)
    gathered = jnp.concatenate([gathered, received], axis=0)
    other_sums = flip(sent, "tan", 1)
    for bit in bits[1:-3]:
        gathered = jnp.concatenate([gathered, flip(gathered, "walk", bit)], axis=0)
    received = flip(gathered, "walk", bits[-3])

    full = shape((walkers * own, feat), F32)
    base, curve, weighted = call(
        layer_kernel, (full, full, full), [whole()] * 9, cost=(4 * feat * feat * walkers * own, 4 << 20))(
            values, lap_in, packed, value_sums, other_value_sums, w_self, w_spin, bias, readout)

    counts, pieces = (1, walkers - 1), (16, 8)
    wide = -(-(dirs + 1) // 128) * 128

    def change(h, ups, before):
        return call(
            functools.partial(change_kernel, own, block, pieces[h], sum(counts[:h])),
            (shape((counts[h], own, feat), F32), shape((8, wide), F32)),
            [smem, smem] + [whole()] * 11,
            [pltpu.VMEM((2, dirs, feat), F32), pltpu.VMEM((own, feat), F32), pltpu.VMEM((own, feat // 2), F32),
             pltpu.VMEM((dirs * 8, feat // 2), F32)],
            (flat.size * feat * counts[h] // 2, flat.size),
        )(ups, potential, slot_electron, held, sums, other_sums, w_self, w_spin, readout, base, curve, weighted, before)

    laplacian, partial = change(0, spin_up, jnp.zeros((8, wide), F32))
    received, late_spin_up, partial = tied(received, spin_up, partial)
    gathered = jnp.concatenate([gathered, received], axis=0)
    received = flip(gathered, "walk", bits[-2])
    more_laplacian, more_partial = change(1, late_spin_up, partial)
    received, more_partial = tied(received, more_partial)
    gathered = jnp.concatenate([gathered, received], axis=0)
    side, other = flip(gathered, "walk", bits[-1]), flip(gathered, "tan", 1)
    rows = call(
        functools.partial(energy_kernel, dirs, walkers), shape((walk_size, 1, 128), F32), [whole()] * 2)(
            more_partial, flip(more_partial, "tan", 1))
    energy = rows[0, 0, :walkers]
    energies = lax.all_to_all(rows, "walk", 0, 0, tiled=True)
    other, more_laplacian, _ = tied(other, more_laplacian, rows)

    blocks = walk_size // 2
    group_shape = (blocks * 16, feat)
    half = [((blocks * 2 * walkers * own, feat), BF16), (group_shape, F32), (group_shape, BF16)]
    weights = (w_self, w_spin, bias, readout)
    slopes = call(
        functools.partial(half_slopes, walkers * own), tuple(shape(*h) for h in half), [whole()] * 6,
        cost=(blocks * 8 * walkers * own * feat * feat, 8 << 20))(gathered, other, *weights)
    laplacian = jnp.concatenate([laplacian, more_laplacian], axis=0)
    energies, side, laplacian, energy, last = tied(energies, side, laplacian, energy, slopes[2])
    slopes = slopes[0], slopes[1], last
    other_side = flip(side, "tan", 1)
    square = shape((feat, feat), F32)
    settings = walkers, own, bits
    first = call(
        functools.partial(first_gradients_kernel, *settings), (square, square), [whole()] * 6,
        cost=(blocks * 16 * walkers * own * feat * feat, 8 << 20))(energies, gathered, other, *slopes)
    grad_self, grad_spin = call(
        functools.partial(last_gradients_kernel, *settings), (square, square), [whole()] * 9,
        [pltpu.VMEM(*h) for h in half])(energies, side, other_side, *weights, *first)
    return laplacian, energy, grad_self, grad_spin


def solution(mesh):
    placed = (
        P("walk", "tan", None),
        P("walk", "tan", None),
        P("walk", None, "tan", None),
        P("walk", None),
        P("walk"),
        P(),
        P(),
        P(),
        P(),
        P("walk"),
    )
    return jax.shard_map(
        shards,
        mesh=mesh,
        in_specs=placed,
        out_specs=(P("walk", "tan", None), P("walk"), P(), P()),
        check_vma=False,
    )
```

```python
import functools

import jax
import jax.numpy as jnp
from jax import lax
from jax.experimental import pallas as pl
from jax.experimental.pallas import tpu as pltpu
from jax.sharding import PartitionSpec as P

F32 = jnp.float32
BF16 = jnp.bfloat16
MIB = 1024 * 1024
VMEM_LIMIT = 24 * MIB
HIGHEST = lax.Precision.HIGHEST
FIRST = ((0,), (0,))
LAST = ((1,), (1,))


def iota(shape, axis):
    return lax.broadcasted_iota(jnp.int32, shape, axis)


def dot(a, b, dims=((1,), (0,)), precision=None):
    return lax.dot_general(a, b, (dims, ((), ())), precision=precision, preferred_element_type=F32)


def two_terms(array):
    high = array.astype(BF16)
    return high, (array - high.astype(F32)).astype(BF16)


def three_terms(array):
    high = array.astype(BF16)
    middle, low = two_terms(array - high.astype(F32))
    return jnp.concatenate([high, middle, low], axis=0)


def first_slot(own):
    return lax.axis_index("tan") * own


def upper_row(slot_ref, w, count):
    return (slot_ref[pl.ds(w, 1), :] < count).astype(F32)


def upper_column(slot_ref, w, count, own):
    row = upper_row(slot_ref, w, count)
    place = iota((own, row.shape[1]), 1) == iota((own, row.shape[1]), 0) + first_slot(own)
    return jnp.sum(jnp.where(place, row, 0.0), axis=1, keepdims=True)


def own_places(electrons, own, wide):
    return (iota((electrons, wide), 0) == iota((electrons, wide), 1) % own + first_slot(own)).astype(BF16)


def pack_kernel(walkers, own, spin_ref, slot_far, values_far, lap_far, packed_ref, value_sums_ref, lines_ref,
                slot_ref, lap_ref, small_sems):
    rows, feat = lap_ref.shape
    electrons = slot_ref.shape[1]
    values_ref = packed_ref.at[pl.ds(0, rows)]
    near = [pltpu.make_async_copy(*ends, small_sems.at[i]) for i, ends in enumerate(
        ((slot_far, slot_ref), (values_far, values_ref), (lap_far, lap_ref)))]
    for copy in near:
        copy.start()
    near[0].wait()
    slots = jnp.zeros((2 * walkers, electrons), jnp.int32)
    for w in range(walkers):
        slots = jnp.where(iota(slots.shape, 0) // 2 == w, slot_ref[w:w + 1, :], slots)

    def column(shape):
        line = iota(shape, 0)
        count = jnp.zeros(shape, jnp.int32)
        for w in range(walkers):
            count = jnp.where(line // 2 == w, spin_ref[w], count)
        return line, count

    line, count = column(slots.shape)
    upper = (slots < count).astype(F32)
    chosen = jnp.where(line % 2 == 0, upper, 1.0 - upper).astype(BF16)
    tiled = dot(chosen, own_places(electrons, own, feat))
    line, count = column(tiled.shape)
    lane = iota(tiled.shape, 1)
    size = jnp.where(line % 2 == 0, count, electrons - count).astype(F32)
    groups = jnp.where(lane < rows, jnp.where(lane // own == line // 2, tiled, 0.0), size)
    groups = jnp.concatenate([groups, jnp.zeros((16 - 2 * walkers, feat), F32)], axis=0).astype(BF16)
    packed_ref[rows:, :] = groups
    lines_ref[...] = groups
    near[1].wait()
    near[2].wait()
    value_sums_ref[0] = dot(groups[:, :rows], values_ref[...])
    value_sums_ref[1] = dot(groups[:, :rows], lap_ref[...])


def sums_kernel(walkers, own, block, lines_ref, far_ref, out_ref, sent_ref, tangent_ref, mask_ref, sems):
    dirs = out_ref.shape[2]
    rows, feat = walkers * own, lines_ref.shape[1]
    repeat = mask_ref.shape[1] // 2
    steps, chunk = dirs // block, block * own

    def fetch(i):
        at = pl.ds(pl.multiple_of(i * chunk, chunk), chunk)
        return pltpu.make_async_copy(far_ref.at[at], tangent_ref.at[at], sems.at[i])

    for i in range(walkers * steps):
        fetch(i).start()
    spots = (iota((rows, feat), 0) % own == iota((rows, feat), 1) % own).astype(F32).astype(BF16)
    tiled = dot(lines_ref[:, :rows], spots)
    place = iota((repeat, feat), 1) // own == iota((repeat, feat), 0)
    for w in range(walkers):
        both = [jnp.where(place, tiled[2 * w + g:2 * w + g + 1], 0.0) for g in range(2)]
        mask_ref[w] = jnp.concatenate(both, axis=0).astype(BF16)

    @pl.loop(0, walkers * steps)
    def _(i):
        w, step = i // steps, i % steps
        mask = mask_ref[w]
        fetch(i).wait()
        for part in range(block // repeat):
            row = pl.multiple_of(i * chunk + part * repeat * own, repeat * own)
            sums = dot(mask, tangent_ref[pl.ds(row, repeat * own), :])
            at = pl.ds(pl.multiple_of(step * block + part * repeat, repeat), repeat)
            out_ref[w, 0, at, :] = sums[:repeat]
            out_ref[w, 1, at, :] = sums[repeat:]
        at = pl.ds(pl.multiple_of(step * block, block), block)
        sent_ref[w, :, at, :] = out_ref[w, :, at, :].astype(BF16)


def picked_rows(groups, mixed):
    lines = jnp.concatenate([groups, groups, groups], axis=0)
    return dot(lines, three_terms(mixed), FIRST)


def layer_kernel(values_ref, lap_ref, packed_ref, own_ref, other_ref, w_self_ref, w_spin_ref,
                 bias_ref, readout_ref, base_ref, curve_ref, weighted_ref):
    rows, feat = values_ref.shape
    lines = packed_ref[rows:, :]
    groups = lines[:, :rows]
    sizes = jnp.maximum(lines[:, rows:rows + 1].astype(F32), 1.0)
    means = ((own_ref[...] + other_ref[...]) / sizes).astype(BF16)
    preact = dot(values_ref[...], w_self_ref[...]) + picked_rows(groups, dot(means[0], w_spin_ref[...])) + bias_ref[...]
    lap_pre = dot(lap_ref[...], w_self_ref[...]) + picked_rows(groups, dot(means[1], w_spin_ref[...]))
    squash = jnp.tanh(preact)
    slopes = 1.0 - squash * squash
    base_ref[...] = slopes * lap_pre
    curve_ref[...] = -2.0 * squash * slopes
    weighted_ref[...] = slopes * readout_ref[...]


def change_kernel(own, block, piece, base, spin_ref, pot_ref, slot_ref, tangent_ref, own_ref, other_ref, w_self_ref,
                  w_spin_ref, readout_ref, base_ref, curve_ref, weighted_ref, before_ref, lap_ref, grad_ref,
                  mixed_ref, squares_ref, column_ref, terms_ref):
    walkers, feat = lap_ref.shape[0], w_self_ref.shape[0]
    dirs = own_ref.shape[2]
    electrons = slot_ref.shape[1]
    steps, part = dirs // block, 8
    halves = [slice(0, feat // 2), slice(feat // 2, feat)]
    grad_ref[...] = before_ref[...]

    @pl.loop(0, walkers)
    def _(n):
        w = base + n
        count = spin_ref[w]
        ups = count.astype(F32)
        mine = pl.ds(pl.multiple_of(w * own, own), own)
        for g, size in enumerate((ups, electrons - ups)):
            means = ((own_ref[w, g] + other_ref[w, g].astype(F32)) / size).astype(BF16)
            mixed_ref[g] = dot(means, w_spin_ref[...])
        column_ref[...] = jnp.broadcast_to(upper_column(slot_ref, w, count, own), (own, feat // 2))
        squares_ref[...] = jnp.zeros_like(squares_ref)

        @pl.loop(0, steps)
        def _(step):
            upper = column_ref[...] > 0.5
            weighted = [weighted_ref[mine, lanes] for lanes in halves]
            squares = [squares_ref[:, lanes] for lanes in halves]
            for c in range(block // piece):
                row = pl.multiple_of(((w * steps + step) * block + c * piece) * own, own)
                plain = dot(tangent_ref[pl.ds(row, piece * own), :], w_self_ref[...])
                for p in range(piece // part):
                    at = pl.multiple_of(step * block + c * piece + p * part, part)
                    mixed = mixed_ref[:, pl.ds(at, part), :]
                    for d in range(part):
                        row = (p * part + d) * own
                        terms = jnp.zeros((8, feat // 2), F32)
                        for h, lanes in enumerate(halves):
                            picked = jnp.where(upper, mixed[0, d:d + 1, lanes], mixed[1, d:d + 1, lanes])
                            change = plain[row:row + own, lanes] + picked
                            squares[h] = squares[h] + change * change
                            terms = terms + (change * weighted[h]).reshape(own // 8, 8, feat // 2).sum(axis=0)
                        terms_ref[pl.ds(pl.multiple_of(at * 8 + d * 8, 8), 8), :] = terms
            for lanes, total in zip(halves, squares):
                squares_ref[:, lanes] = total

        laplacian = base_ref[mine, :] + curve_ref[mine, :] * squares_ref[...]
        lap_ref[n] = laplacian
        summed = terms_ref[...].reshape(dirs, 8, feat // 2).sum(axis=1)
        spare = jnp.zeros((grad_ref.shape[1] - dirs, feat // 2), F32)
        summed = jnp.concatenate([summed, spare], axis=0)
        row = dot(jnp.ones((8, feat // 2), F32), summed, LAST, HIGHEST)
        share = jnp.sum(laplacian * readout_ref[...]) - jnp.where(lax.axis_index("tan") == 0, 2.0 * pot_ref[w], 0.0)
        row = jnp.where(iota(row.shape, 1) == dirs, share, row)
        grad_ref[...] = jnp.where(iota(row.shape, 0) == w, row, grad_ref[...])


def energy_kernel(dirs, walkers, own_ref, other_ref, out_ref):
    both = own_ref[...] + other_ref[...]
    place = iota(both.shape, 1)
    parts = jnp.where(place < dirs, both * both, jnp.where(place == dirs, both, 0.0))
    energy = -0.5 * jnp.sum(parts, axis=1, keepdims=True)
    lane = iota((1, 128), 1)
    row = jnp.zeros((1, 128), F32)
    for w in range(walkers):
        row = jnp.where(lane == w, energy[w:w + 1], row)
    out_ref[...] = row.reshape(1, 1, 128)


def pair(own_ref, other_ref, rows, r):
    values = jnp.concatenate([ref[r, 0:rows, :] for ref in (own_ref, other_ref)], axis=0)
    groups = jnp.concatenate([ref[r, rows:, 0:rows] for ref in (own_ref, other_ref)], axis=1)
    return values, groups


def half_slopes(rows, own_ref, other_ref, w_self_ref, w_spin_ref, bias_ref, readout_ref,
                slopes_ref, sums_ref, means_ref):
    blocks, lines, _ = own_ref.shape
    group = lines - rows
    bunch = min(blocks, 8)

    @pl.loop(0, blocks // bunch)
    def _(i):
        pairs = [pair(own_ref, other_ref, rows, i * bunch + k) for k in range(bunch)]
        means = []
        for k, (values, groups) in enumerate(pairs):
            sizes = jnp.maximum(own_ref[i * bunch + k, rows:, rows:rows + 1].astype(F32), 1.0)
            means.append(dot(groups, values) / sizes)
        means = jnp.concatenate(means, axis=0).astype(BF16)
        at = pl.ds(pl.multiple_of(i * bunch * group, bunch * group), bunch * group)
        means_ref[at, :] = means
        mixed = dot(means, w_spin_ref[...])
        sums = []
        for k, (values, groups) in enumerate(pairs):
            preact = (dot(values, w_self_ref[...]) + picked_rows(groups, mixed[k * group:(k + 1) * group])
                      + bias_ref[...])
            squash = jnp.tanh(preact)
            slopes = ((1.0 - squash * squash) * readout_ref[...]).astype(BF16)
            row = pl.multiple_of((i * bunch + k) * 2 * rows, 2 * rows)
            slopes_ref[pl.ds(row, 2 * rows), :] = slopes
            sums.append(dot(groups, slopes))
        sums_ref[at, :] = jnp.concatenate(sums, axis=0)


def add_products(walkers, own, first, energy_ref, own_ref, other_ref, slopes_ref, sums_ref, means_ref,
                 self_ref, spin_ref):
    rows = walkers * own
    blocks, lines, feat = own_ref.shape
    group = lines - rows
    bunch = min(blocks, 8)
    everyone = energy_ref.shape[0] * walkers
    center = jnp.sum(jnp.sum(energy_ref[...], axis=0), axis=1, keepdims=True) / everyone
    line = iota((group, feat), 0) // 2

    @pl.loop(0, blocks // bunch)
    def _(i):
        values, high, low, spreads = [], [], [], []
        for k in range(bunch):
            row = energy_ref[first + i * bunch + k] - center
            row_at = pl.multiple_of((i * bunch + k) * 2 * rows, 2 * rows)
            slopes = slopes_ref[pl.ds(row_at, 2 * rows), :].astype(F32)
            spread = jnp.zeros((group, feat), F32)
            for w in range(walkers):
                spread = jnp.where(line == w, row[:, w:w + 1], spread)
            spreads.append(spread)
            for core in range(2):
                for w in range(walkers):
                    at = core * rows + w * own
                    top, rest = two_terms(slopes[at:at + own] * row[:, w:w + 1])
                    high.append(top)
                    low.append(rest)
            values.append(pair(own_ref, other_ref, rows, i * bunch + k)[0])
        values = jnp.concatenate(values, axis=0)
        self_ref[...] += dot(values, jnp.concatenate(high, axis=0), FIRST) + dot(
            values, jnp.concatenate(low, axis=0), FIRST)
        at = pl.ds(pl.multiple_of(i * bunch * group, bunch * group), bunch * group)
        top, rest = two_terms(sums_ref[at, :] * jnp.concatenate(spreads, axis=0))
        means = means_ref[at, :]
        spin_ref[...] += dot(means, top, FIRST) + dot(means, rest, FIRST)


def gradients_kernel(walkers, own, energy_ref, *refs):
    self_ref, spin_ref = refs[-2:]
    self_ref[...] = jnp.zeros_like(self_ref)
    spin_ref[...] = jnp.zeros_like(spin_ref)
    for side in range(2):
        part = refs[5 * side:5 * side + 5]
        add_products(walkers, own, side * part[0].shape[0], energy_ref, *part, self_ref, spin_ref)


def whole(memory=pltpu.VMEM):
    return pl.BlockSpec(memory_space=memory)


def call(kernel, out_shape, in_specs, scratch=(), cost=None, limit=VMEM_LIMIT, out_specs=None):
    flops, moved = cost if cost is not None else (0, 0)
    return pl.pallas_call(
        kernel,
        out_shape=out_shape,
        in_specs=in_specs,
        out_specs=jax.tree.map(lambda _: whole(), out_shape) if out_specs is None else out_specs,
        scratch_shapes=scratch,
        cost_estimate=pl.CostEstimate(flops=flops, bytes_accessed=moved, transcendentals=0) if cost else None,
        compiler_params=pltpu.CompilerParams(vmem_limit_bytes=limit),
    )


def flip(array, axis, bit):
    size = lax.axis_size(axis)
    return lax.ppermute(array, axis, [(i, i ^ bit) for i in range(size)])


def tied(*arrays):
    return lax.optimization_barrier(arrays)


def shards(values, lap_in, tangent, slot_electron, spin_up, w_self, w_spin, bias, readout, potential):
    walk_size = lax.axis_size("walk")
    walkers, own, feat = values.shape
    dirs = tangent.shape[1]
    shape = jax.ShapeDtypeStruct
    smem = whole(pltpu.SMEM)
    flat = tangent.reshape(walkers * dirs * own, feat)
    values, lap_in = values.reshape(walkers * own, feat), lap_in.reshape(walkers * own, feat)
    bias, readout = bias.reshape(1, feat), readout.reshape(1, feat)
    bits = [1 << b for b in reversed(range(walk_size.bit_length() - 1))]

    small = (2, 16, feat)
    packed, value_sums, lines = call(
        functools.partial(pack_kernel, walkers, own),
        (shape((walkers * own + 16, feat), BF16), shape(small, F32), shape((16, feat), BF16)),
        [smem] + [whole(pltpu.HBM)] * 3,
        [pltpu.VMEM(slot_electron.shape, jnp.int32), pltpu.VMEM(lap_in.shape, BF16), pltpu.SemaphoreType.DMA((3,))],
        limit=63 * MIB)(spin_up, slot_electron, values, lap_in)
    other_value_sums = flip(value_sums, "tan", 1)
    gathered = packed.reshape((1,) + packed.shape)

    repeat, block, piece = feat // own, dirs // 2, dirs // 4
    sums, sent, held = call(
        functools.partial(sums_kernel, walkers, own, block),
        (shape((walkers, 2, dirs, feat), F32), shape((walkers, 2, dirs, feat), BF16), shape(flat.shape, BF16)),
        [whole(), whole(pltpu.HBM)],
        [pltpu.VMEM((walkers, 2 * repeat, feat), BF16), pltpu.SemaphoreType.DMA((walkers * dirs // block,))],
        (flat.size * 32, flat.size * 2), 36 * MIB)(lines, flat)
    received, sent, other_value_sums = tied(flip(gathered, "walk", bits[0]), sent, other_value_sums)
    gathered = jnp.concatenate([gathered, received], axis=0)
    other_sums = flip(sent, "tan", 1)
    for bit in bits[1:-3]:
        gathered = jnp.concatenate([gathered, flip(gathered, "walk", bit)], axis=0)
    received = flip(gathered, "walk", bits[-3])

    full = shape((walkers * own, feat), F32)
    base, curve, weighted = call(
        layer_kernel, (full, full, full), [whole()] * 9, cost=(4 * feat * feat * walkers * own, 4 << 20))(
            values, lap_in, packed, value_sums, other_value_sums, w_self, w_spin, bias, readout)

    counts = (1, walkers - 1)
    wide = -(-(dirs + 1) // 128) * 128

    def change(h, ups, before):
        return call(
            functools.partial(change_kernel, own, block, piece, sum(counts[:h])),
            (shape((counts[h], own, feat), F32), shape((8, wide), F32)),
            [smem, smem] + [whole()] * 11,
            [pltpu.VMEM((2, dirs, feat), F32), pltpu.VMEM((own, feat), F32), pltpu.VMEM((own, feat // 2), F32),
             pltpu.VMEM((dirs * 8, feat // 2), F32)],
            (flat.size * feat * counts[h] // 2, flat.size),
        )(ups, potential, slot_electron, held, sums, other_sums, w_self, w_spin, readout, base, curve, weighted, before)

    laplacian, partial = change(0, spin_up, jnp.zeros((8, wide), F32))
    received, late_spin_up, partial = tied(received, spin_up, partial)
    gathered = jnp.concatenate([gathered, received], axis=0)
    received = flip(gathered, "walk", bits[-2])
    more_laplacian, more_partial = change(1, late_spin_up, partial)
    received, more_partial = tied(received, more_partial)
    gathered = jnp.concatenate([gathered, received], axis=0)
    side, other = flip(gathered, "walk", bits[-1]), flip(gathered, "tan", 1)
    rows = call(
        functools.partial(energy_kernel, dirs, walkers), shape((1, 1, 128), F32), [whole()] * 2)(
            more_partial, flip(more_partial, "tan", 1))
    energy = rows[0, 0, :walkers]
    blocks = walk_size // 2
    group_shape = (blocks * 16, feat)
    half = [((blocks * 2 * walkers * own, feat), BF16), (group_shape, F32), (group_shape, BF16)]
    weights = (w_self, w_spin, bias, readout)

    def slopes(*both):
        return call(
            functools.partial(half_slopes, walkers * own), tuple(shape(*h) for h in half), [whole()] * 6,
            cost=(blocks * 8 * walkers * own * feat * feat, 8 << 20))(*both, *weights)

    other, more_laplacian, _ = tied(other, more_laplacian, rows)
    near = gathered, other
    near_slopes = slopes(*near)
    energies = rows
    for stage, bit in enumerate(bits):
        received = flip(energies, "walk", bit)
        if stage == 0:
            received, last = tied(received, near_slopes[2])
        if stage == len(bits) - 2:
            received, side = tied(received, side)
        energies = jnp.concatenate([energies, received], axis=0)
    near_slopes = near_slopes[0], near_slopes[1], last
    far = side, flip(side, "tan", 1)
    laplacian = jnp.concatenate([laplacian, more_laplacian], axis=0)
    square = shape((feat, feat), F32)
    grad_self, grad_spin = call(
        functools.partial(gradients_kernel, walkers, own), (square, square), [whole()] * 11)(
            energies, *near, *near_slopes, *far, *slopes(*far))
    return laplacian, energy, grad_self, grad_spin


def solution(mesh):
    placed = (
        P("walk", "tan", None),
        P("walk", "tan", None),
        P("walk", None, "tan", None),
        P("walk", None),
        P("walk"),
        P(),
        P(),
        P(),
        P(),
        P("walk"),
    )
    return jax.shard_map(
        shards,
        mesh=mesh,
        in_specs=placed,
        out_specs=(P("walk", "tan", None), P("walk"), P(), P()),
        check_vma=False,
    )
```

```python
import functools

import jax
import jax.numpy as jnp
from jax import lax
from jax.experimental import pallas as pl
from jax.experimental.pallas import tpu as pltpu
from jax.sharding import PartitionSpec as P

F32 = jnp.float32
BF16 = jnp.bfloat16
MIB = 1024 * 1024
VMEM_LIMIT = 24 * MIB
HIGHEST = lax.Precision.HIGHEST
FIRST = ((0,), (0,))
LAST = ((1,), (1,))


def iota(shape, axis):
    return lax.broadcasted_iota(jnp.int32, shape, axis)


def dot(a, b, dims=((1,), (0,)), precision=None):
    return lax.dot_general(a, b, (dims, ((), ())), precision=precision, preferred_element_type=F32)


def two_terms(array):
    high = array.astype(BF16)
    return high, (array - high.astype(F32)).astype(BF16)


def three_terms(array):
    high = array.astype(BF16)
    middle, low = two_terms(array - high.astype(F32))
    return jnp.concatenate([high, middle, low], axis=0)


def first_slot(own):
    return lax.axis_index("tan") * own


def upper_row(slot_ref, w, count):
    return (slot_ref[pl.ds(w, 1), :] < count).astype(F32)


def upper_column(slot_ref, w, count, own):
    row = upper_row(slot_ref, w, count)
    place = iota((own, row.shape[1]), 1) == iota((own, row.shape[1]), 0) + first_slot(own)
    return jnp.sum(jnp.where(place, row, 0.0), axis=1, keepdims=True)


def own_places(electrons, own, wide):
    return (iota((electrons, wide), 0) == iota((electrons, wide), 1) % own + first_slot(own)).astype(BF16)


def pack_kernel(walkers, own, spin_ref, slot_far, values_far, lap_far, packed_ref, value_sums_ref, lines_ref,
                slot_ref, lap_ref, small_sems):
    rows, feat = lap_ref.shape
    electrons = slot_ref.shape[1]
    values_ref = packed_ref.at[pl.ds(0, rows)]
    near = [pltpu.make_async_copy(*ends, small_sems.at[i]) for i, ends in enumerate(
        ((slot_far, slot_ref), (values_far, values_ref), (lap_far, lap_ref)))]
    for copy in near:
        copy.start()
    near[0].wait()
    slots = jnp.zeros((2 * walkers, electrons), jnp.int32)
    for w in range(walkers):
        slots = jnp.where(iota(slots.shape, 0) // 2 == w, slot_ref[w:w + 1, :], slots)

    def column(shape):
        line = iota(shape, 0)
        count = jnp.zeros(shape, jnp.int32)
        for w in range(walkers):
            count = jnp.where(line // 2 == w, spin_ref[w], count)
        return line, count

    line, count = column(slots.shape)
    upper = (slots < count).astype(F32)
    chosen = jnp.where(line % 2 == 0, upper, 1.0 - upper).astype(BF16)
    tiled = dot(chosen, own_places(electrons, own, feat))
    line, count = column(tiled.shape)
    lane = iota(tiled.shape, 1)
    size = jnp.where(line % 2 == 0, count, electrons - count).astype(F32)
    groups = jnp.where(lane < rows, jnp.where(lane // own == line // 2, tiled, 0.0), size)
    groups = jnp.concatenate([groups, jnp.zeros((16 - 2 * walkers, feat), F32)], axis=0).astype(BF16)
    packed_ref[rows:, :] = groups
    lines_ref[...] = groups
    near[1].wait()
    near[2].wait()
    value_sums_ref[0] = dot(groups[:, :rows], values_ref[...])
    value_sums_ref[1] = dot(groups[:, :rows], lap_ref[...])


def sums_kernel(walkers, own, block, lines_ref, far_ref, out_ref, sent_ref, tangent_ref, mask_ref, sems):
    dirs = out_ref.shape[2]
    rows, feat = walkers * own, lines_ref.shape[1]
    repeat = mask_ref.shape[1] // 2
    steps, chunk = dirs // block, block * own

    def fetch(i):
        at = pl.ds(pl.multiple_of(i * chunk, chunk), chunk)
        return pltpu.make_async_copy(far_ref.at[at], tangent_ref.at[at], sems.at[i])

    for i in range(walkers * steps):
        fetch(i).start()
    spots = (iota((rows, feat), 0) % own == iota((rows, feat), 1) % own).astype(F32).astype(BF16)
    tiled = dot(lines_ref[:, :rows], spots)
    place = iota((repeat, feat), 1) // own == iota((repeat, feat), 0)
    for w in range(walkers):
        both = [jnp.where(place, tiled[2 * w + g:2 * w + g + 1], 0.0) for g in range(2)]
        mask_ref[w] = jnp.concatenate(both, axis=0).astype(BF16)

    @pl.loop(0, walkers * steps)
    def _(i):
        w, step = i // steps, i % steps
        mask = mask_ref[w]
        fetch(i).wait()
        for part in range(block // repeat):
            row = pl.multiple_of(i * chunk + part * repeat * own, repeat * own)
            sums = dot(mask, tangent_ref[pl.ds(row, repeat * own), :])
            at = pl.ds(pl.multiple_of(step * block + part * repeat, repeat), repeat)
            out_ref[w, 0, at, :] = sums[:repeat]
            out_ref[w, 1, at, :] = sums[repeat:]
        at = pl.ds(pl.multiple_of(step * block, block), block)
        sent_ref[w, :, at, :] = out_ref[w, :, at, :].astype(BF16)


def picked_rows(groups, mixed):
    lines = jnp.concatenate([groups, groups, groups], axis=0)
    return dot(lines, three_terms(mixed), FIRST)


def layer_kernel(values_ref, lap_ref, packed_ref, own_ref, other_ref, w_self_ref, w_spin_ref,
                 bias_ref, readout_ref, base_ref, curve_ref, weighted_ref):
    rows, feat = values_ref.shape
    lines = packed_ref[rows:, :]
    groups = lines[:, :rows]
    sizes = jnp.maximum(lines[:, rows:rows + 1].astype(F32), 1.0)
    means = ((own_ref[...] + other_ref[...]) / sizes).astype(BF16)
    preact = dot(values_ref[...], w_self_ref[...]) + picked_rows(groups, dot(means[0], w_spin_ref[...])) + bias_ref[...]
    lap_pre = dot(lap_ref[...], w_self_ref[...]) + picked_rows(groups, dot(means[1], w_spin_ref[...]))
    squash = jnp.tanh(preact)
    slopes = 1.0 - squash * squash
    base_ref[...] = slopes * lap_pre
    curve_ref[...] = -2.0 * squash * slopes
    weighted_ref[...] = slopes * readout_ref[...]


def change_kernel(own, block, piece, base, spin_ref, pot_ref, slot_ref, tangent_ref, own_ref, other_ref, w_self_ref,
                  w_spin_ref, readout_ref, base_ref, curve_ref, weighted_ref, before_ref, lap_ref, grad_ref,
                  mixed_ref, squares_ref, column_ref, terms_ref):
    walkers, feat = lap_ref.shape[0], w_self_ref.shape[0]
    dirs = own_ref.shape[2]
    electrons = slot_ref.shape[1]
    steps, part = dirs // block, 8
    halves = [slice(0, feat // 2), slice(feat // 2, feat)]
    grad_ref[...] = before_ref[...]

    @pl.loop(0, walkers)
    def _(n):
        w = base + n
        count = spin_ref[w]
        ups = count.astype(F32)
        mine = pl.ds(pl.multiple_of(w * own, own), own)
        for g, size in enumerate((ups, electrons - ups)):
            means = ((own_ref[w, g] + other_ref[w, g].astype(F32)) / size).astype(BF16)
            mixed_ref[g] = dot(means, w_spin_ref[...])
        column_ref[...] = jnp.broadcast_to(upper_column(slot_ref, w, count, own), (own, feat // 2))
        squares_ref[...] = jnp.zeros_like(squares_ref)

        @pl.loop(0, steps)
        def _(step):
            upper = column_ref[...] > 0.5
            weighted = [weighted_ref[mine, lanes] for lanes in halves]
            squares = [squares_ref[:, lanes] for lanes in halves]
            for c in range(block // piece):
                row = pl.multiple_of(((w * steps + step) * block + c * piece) * own, own)
                plain = dot(tangent_ref[pl.ds(row, piece * own), :], w_self_ref[...])
                for p in range(piece // part):
                    at = pl.multiple_of(step * block + c * piece + p * part, part)
                    mixed = mixed_ref[:, pl.ds(at, part), :]
                    for d in range(part):
                        row = (p * part + d) * own
                        terms = jnp.zeros((8, feat // 2), F32)
                        for h, lanes in enumerate(halves):
                            picked = jnp.where(upper, mixed[0, d:d + 1, lanes], mixed[1, d:d + 1, lanes])
                            change = plain[row:row + own, lanes] + picked
                            squares[h] = squares[h] + change * change
                            terms = terms + (change * weighted[h]).reshape(own // 8, 8, feat // 2).sum(axis=0)
                        terms_ref[pl.ds(pl.multiple_of(at * 8 + d * 8, 8), 8), :] = terms
            for lanes, total in zip(halves, squares):
                squares_ref[:, lanes] = total

        laplacian = base_ref[mine, :] + curve_ref[mine, :] * squares_ref[...]
        lap_ref[n] = laplacian
        summed = terms_ref[...].reshape(dirs, 8, feat // 2).sum(axis=1)
        spare = jnp.zeros((grad_ref.shape[1] - dirs, feat // 2), F32)
        summed = jnp.concatenate([summed, spare], axis=0)
        row = dot(jnp.ones((8, feat // 2), F32), summed, LAST, HIGHEST)
        share = jnp.sum(laplacian * readout_ref[...]) - jnp.where(lax.axis_index("tan") == 0, 2.0 * pot_ref[w], 0.0)
        row = jnp.where(iota(row.shape, 1) == dirs, share, row)
        grad_ref[...] = jnp.where(iota(row.shape, 0) == w, row, grad_ref[...])


def energy_kernel(dirs, walkers, own_ref, other_ref, out_ref):
    both = own_ref[...] + other_ref[...]
    place = iota(both.shape, 1)
    parts = jnp.where(place < dirs, both * both, jnp.where(place == dirs, both, 0.0))
    energy = -0.5 * jnp.sum(parts, axis=1, keepdims=True)
    lane = iota((1, 128), 1)
    row = jnp.zeros((1, 128), F32)
    for w in range(walkers):
        row = jnp.where(lane == w, energy[w:w + 1], row)
    out_ref[...] = row.reshape(1, 1, 128)


def pair(own_ref, other_ref, rows, r):
    values = jnp.concatenate([ref[r, 0:rows, :] for ref in (own_ref, other_ref)], axis=0)
    groups = jnp.concatenate([ref[r, rows:, 0:rows] for ref in (own_ref, other_ref)], axis=1)
    return values, groups


def slopes_kernel(rows, *refs):
    owns, others, weights, (slopes_ref, sums_ref, means_ref) = refs[0:2], refs[2:4], refs[4:8], refs[8:]
    w_self_ref, w_spin_ref, bias_ref, readout_ref = weights
    blocks, lines, _ = owns[0].shape
    group = lines - rows
    bunch = min(blocks, 8)

    for part, (own_ref, other_ref) in enumerate(zip(owns, others)):
        @pl.loop(0, blocks // bunch)
        def _(i):
            pairs = [pair(own_ref, other_ref, rows, i * bunch + k) for k in range(bunch)]
            means = []
            for k, (values, groups) in enumerate(pairs):
                sizes = jnp.maximum(own_ref[i * bunch + k, rows:, rows:rows + 1].astype(F32), 1.0)
                means.append(dot(groups, values) / sizes)
            means = jnp.concatenate(means, axis=0).astype(BF16)
            first = part * blocks + i * bunch
            at = pl.ds(pl.multiple_of(first * group, bunch * group), bunch * group)
            means_ref[at, :] = means
            mixed = dot(means, w_spin_ref[...])
            sums = []
            for k, (values, groups) in enumerate(pairs):
                preact = (dot(values, w_self_ref[...]) + picked_rows(groups, mixed[k * group:(k + 1) * group])
                          + bias_ref[...])
                squash = jnp.tanh(preact)
                slopes = ((1.0 - squash * squash) * readout_ref[...]).astype(BF16)
                slopes_ref[pl.ds(pl.multiple_of((first + k) * 2 * rows, 2 * rows), 2 * rows), :] = slopes
                sums.append(dot(groups, slopes))
            sums_ref[at, :] = jnp.concatenate(sums, axis=0)


def gradients_kernel(walkers, own, tables, energy_ref, *refs):
    self_ref, spin_ref = refs[-2:]
    rows = walkers * own
    blocks, lines, feat = refs[0].shape
    group, half = lines - rows, blocks // 2
    bunch = min(blocks, 8)
    everyone = energy_ref.shape[0] * walkers
    center = jnp.sum(jnp.sum(energy_ref[...], axis=0), axis=1, keepdims=True) / everyone
    line = iota((group, feat), 0) // 2
    self_ref[...] = jnp.zeros_like(self_ref)
    spin_ref[...] = jnp.zeros_like(spin_ref)
    for side, part in ((side, part) for side in range(2) for part in range(2)):
        owns, others, (slopes_ref, sums_ref, means_ref) = (
            refs[7 * side:7 * side + 2], refs[7 * side + 2:7 * side + 4], refs[7 * side + 4:7 * side + 7])
        own_ref, other_ref, (low_place, high_place) = owns[part], others[part], tables[side][part]

        @pl.loop(0, blocks // bunch)
        def _(i):
            first = part * blocks + i * bunch
            values, high, low, spreads = [], [], [], []
            for k in range(bunch):
                block = i * bunch + k
                row = energy_ref[block % half + jnp.where(block < half, low_place, high_place)] - center
                row_at = pl.multiple_of((first + k) * 2 * rows, 2 * rows)
                slopes = slopes_ref[pl.ds(row_at, 2 * rows), :].astype(F32)
                spread = jnp.zeros((group, feat), F32)
                for w in range(walkers):
                    spread = jnp.where(line == w, row[:, w:w + 1], spread)
                spreads.append(spread)
                for core in range(2):
                    for w in range(walkers):
                        at = core * rows + w * own
                        top, rest = two_terms(slopes[at:at + own] * row[:, w:w + 1])
                        high.append(top)
                        low.append(rest)
                values.append(pair(own_ref, other_ref, rows, block)[0])
            values = jnp.concatenate(values, axis=0)
            self_ref[...] += dot(values, jnp.concatenate(high, axis=0), FIRST) + dot(
                values, jnp.concatenate(low, axis=0), FIRST)
            at = pl.ds(pl.multiple_of(first * group, bunch * group), bunch * group)
            top, rest = two_terms(sums_ref[at, :] * jnp.concatenate(spreads, axis=0))
            means = means_ref[at, :]
            spin_ref[...] += dot(means, top, FIRST) + dot(means, rest, FIRST)


def whole(memory=pltpu.VMEM):
    return pl.BlockSpec(memory_space=memory)


def call(kernel, out_shape, in_specs, scratch=(), cost=None, limit=VMEM_LIMIT, out_specs=None):
    flops, moved = cost if cost is not None else (0, 0)
    return pl.pallas_call(
        kernel,
        out_shape=out_shape,
        in_specs=in_specs,
        out_specs=jax.tree.map(lambda _: whole(), out_shape) if out_specs is None else out_specs,
        scratch_shapes=scratch,
        cost_estimate=pl.CostEstimate(flops=flops, bytes_accessed=moved, transcendentals=0) if cost else None,
        compiler_params=pltpu.CompilerParams(vmem_limit_bytes=limit),
    )


def flip(array, axis, bit):
    size = lax.axis_size(axis)
    return lax.ppermute(array, axis, [(i, i ^ bit) for i in range(size)])


def tied(*arrays):
    return lax.optimization_barrier(arrays)


def shards(values, lap_in, tangent, slot_electron, spin_up, w_self, w_spin, bias, readout, potential):
    walk_size = lax.axis_size("walk")
    walkers, own, feat = values.shape
    dirs = tangent.shape[1]
    shape = jax.ShapeDtypeStruct
    smem = whole(pltpu.SMEM)
    flat = tangent.reshape(walkers * dirs * own, feat)
    values, lap_in = values.reshape(walkers * own, feat), lap_in.reshape(walkers * own, feat)
    bias, readout = bias.reshape(1, feat), readout.reshape(1, feat)
    bits = [1 << b for b in reversed(range(walk_size.bit_length() - 1))]

    small = (2, 16, feat)
    packed, value_sums, lines = call(
        functools.partial(pack_kernel, walkers, own),
        (shape((walkers * own + 16, feat), BF16), shape(small, F32), shape((16, feat), BF16)),
        [smem] + [whole(pltpu.HBM)] * 3,
        [pltpu.VMEM(slot_electron.shape, jnp.int32), pltpu.VMEM(lap_in.shape, BF16), pltpu.SemaphoreType.DMA((3,))],
        limit=63 * MIB)(spin_up, slot_electron, values, lap_in)
    other_value_sums = flip(value_sums, "tan", 1)
    gathered = packed.reshape((1,) + packed.shape)

    repeat, block, piece = feat // own, dirs // 2, dirs // 4
    sums, sent, held = call(
        functools.partial(sums_kernel, walkers, own, block),
        (shape((walkers, 2, dirs, feat), F32), shape((walkers, 2, dirs, feat), BF16), shape(flat.shape, BF16)),
        [whole(), whole(pltpu.HBM)],
        [pltpu.VMEM((walkers, 2 * repeat, feat), BF16), pltpu.SemaphoreType.DMA((walkers * dirs // block,))],
        (flat.size * 32, flat.size * 2), 36 * MIB)(lines, flat)
    received, sent, other_value_sums = tied(flip(gathered, "walk", bits[0]), sent, other_value_sums)
    gathered = jnp.concatenate([gathered, received], axis=0)
    other_sums = flip(sent, "tan", 1)
    for bit in bits[1:-3]:
        gathered = jnp.concatenate([gathered, flip(gathered, "walk", bit)], axis=0)
    received = flip(gathered, "walk", bits[-3])

    full = shape((walkers * own, feat), F32)
    base, curve, weighted = call(
        layer_kernel, (full, full, full), [whole()] * 9, cost=(4 * feat * feat * walkers * own, 4 << 20))(
            values, lap_in, packed, value_sums, other_value_sums, w_self, w_spin, bias, readout)

    counts = (1, walkers - 1)
    wide = -(-(dirs + 1) // 128) * 128

    def change(h, ups, before):
        return call(
            functools.partial(change_kernel, own, block, piece, sum(counts[:h])),
            (shape((counts[h], own, feat), F32), shape((8, wide), F32)),
            [smem, smem] + [whole()] * 11,
            [pltpu.VMEM((2, dirs, feat), F32), pltpu.VMEM((own, feat), F32), pltpu.VMEM((own, feat // 2), F32),
             pltpu.VMEM((dirs * 8, feat // 2), F32)],
            (flat.size * feat * counts[h] // 2, flat.size),
        )(ups, potential, slot_electron, held, sums, other_sums, w_self, w_spin, readout, base, curve, weighted, before)

    def joined(*arrays):
        return jnp.concatenate(arrays, axis=0)

    def across(arrays):
        return [flip(array, "tan", 1) for array in arrays]

    far_bits = bits[-2:]
    laplacian, partial = change(0, spin_up, jnp.zeros((8, wide), F32))
    received, late_spin_up, partial = tied(received, spin_up, partial)
    gathered = joined(gathered, received)
    middle = gathered.shape[0] // 2
    near = [gathered[:middle], gathered[middle:]]
    received = [flip(part, "walk", bit) for part, bit in zip(near, far_bits)]
    more_laplacian, more_partial = change(1, late_spin_up, partial)
    *received, more_partial = tied(*received, more_partial)
    near = [joined(*both) for both in zip(near, received)]
    far = [flip(part, "walk", bit) for part, bit in zip(near, reversed(far_bits))]
    near_others = across(near)
    rows = call(
        functools.partial(energy_kernel, dirs, walkers), shape((1, 1, 128), F32), [whole()] * 2)(
            more_partial, flip(more_partial, "tan", 1))
    energy = rows[0, 0, :walkers]
    *near_others, more_laplacian, _ = tied(*near_others, more_laplacian, rows)

    blocks = walk_size // 2
    group_shape = (blocks * 16, feat)
    half = [((blocks * 2 * walkers * own, feat), BF16), (group_shape, F32), (group_shape, BF16)]
    weights = (w_self, w_spin, bias, readout)

    def slopes(*parts):
        return call(
            functools.partial(slopes_kernel, walkers * own), tuple(shape(*h) for h in half), [whole()] * 8,
            cost=(blocks * 8 * walkers * own * feat * feat, 8 << 20))(*parts, *weights)

    *near_slopes, last = slopes(*near, *near_others)
    energies = rows
    for stage in range(0, len(bits), 2):
        offsets = [bits[stage]] if stage + 1 == len(bits) else [bits[stage], bits[stage + 1], bits[stage] | bits[stage + 1]]
        received = [flip(energies, "walk", offset) for offset in offsets]
        if stage == 0:
            *received, last, far[0], far[1] = tied(*received, last, *far)
            far_others = across(far)
            *far_slopes, far_last = slopes(*far, *far_others)
        if stage + 2 >= len(bits):
            *received, far_last = tied(*received, far_last)
        energies = joined(energies, *received)
    laplacian = joined(laplacian, more_laplacian)
    square = shape((feat, feat), F32)
    step = walk_size // 4
    tables = (((0, step), (step // 2, step // 2 + 2 * step)),
              ((2 * step, 3 * step), (step // 2 + step, step // 2 + 3 * step)))
    grad_self, grad_spin = call(
        functools.partial(gradients_kernel, walkers, own, tables), (square, square), [whole()] * 15)(
            energies, *near, *near_others, *near_slopes, last, *far, *far_others, *far_slopes, far_last)
    return laplacian, energy, grad_self, grad_spin


def solution(mesh):
    placed = (
        P("walk", "tan", None),
        P("walk", "tan", None),
        P("walk", None, "tan", None),
        P("walk", None),
        P("walk"),
        P(),
        P(),
        P(),
        P(),
        P("walk"),
    )
    return jax.shard_map(
        shards,
        mesh=mesh,
        in_specs=placed,
        out_specs=(P("walk", "tan", None), P("walk"), P(), P()),
        check_vma=False,
    )
```

```python
import functools

import jax
import jax.numpy as jnp
from jax import lax
from jax.experimental import pallas as pl
from jax.experimental.pallas import tpu as pltpu
from jax.sharding import PartitionSpec as P

F32 = jnp.float32
BF16 = jnp.bfloat16
MIB = 1024 * 1024
VMEM_LIMIT = 24 * MIB
HIGHEST = lax.Precision.HIGHEST
FIRST = ((0,), (0,))
LAST = ((1,), (1,))


def iota(shape, axis):
    return lax.broadcasted_iota(jnp.int32, shape, axis)


def dot(a, b, dims=((1,), (0,)), precision=None):
    return lax.dot_general(a, b, (dims, ((), ())), precision=precision, preferred_element_type=F32)


def two_terms(array):
    high = array.astype(BF16)
    return high, (array - high.astype(F32)).astype(BF16)


def three_terms(array):
    high = array.astype(BF16)
    middle, low = two_terms(array - high.astype(F32))
    return jnp.concatenate([high, middle, low], axis=0)


def first_slot(own):
    return lax.axis_index("tan") * own


def upper_row(slot_ref, w, count):
    return (slot_ref[pl.ds(w, 1), :] < count).astype(F32)


def upper_column(slot_ref, w, count, own):
    row = upper_row(slot_ref, w, count)
    place = iota((own, row.shape[1]), 1) == iota((own, row.shape[1]), 0) + first_slot(own)
    return jnp.sum(jnp.where(place, row, 0.0), axis=1, keepdims=True)


def own_places(electrons, own, wide):
    return (iota((electrons, wide), 0) == iota((electrons, wide), 1) % own + first_slot(own)).astype(BF16)


def pack_kernel(walkers, own, spin_ref, slot_far, values_far, lap_far, packed_ref, value_sums_ref, lines_ref,
                slot_ref, lap_ref, small_sems):
    rows, feat = lap_ref.shape
    electrons = slot_ref.shape[1]
    values_ref = packed_ref.at[pl.ds(0, rows)]
    near = [pltpu.make_async_copy(*ends, small_sems.at[i]) for i, ends in enumerate(
        ((slot_far, slot_ref), (values_far, values_ref), (lap_far, lap_ref)))]
    for copy in near:
        copy.start()
    near[0].wait()
    slots = jnp.zeros((2 * walkers, electrons), jnp.int32)
    for w in range(walkers):
        slots = jnp.where(iota(slots.shape, 0) // 2 == w, slot_ref[w:w + 1, :], slots)

    def column(shape):
        line = iota(shape, 0)
        count = jnp.zeros(shape, jnp.int32)
        for w in range(walkers):
            count = jnp.where(line // 2 == w, spin_ref[w], count)
        return line, count

    line, count = column(slots.shape)
    upper = (slots < count).astype(F32)
    chosen = jnp.where(line % 2 == 0, upper, 1.0 - upper).astype(BF16)
    tiled = dot(chosen, own_places(electrons, own, feat))
    line, count = column(tiled.shape)
    lane = iota(tiled.shape, 1)
    size = jnp.where(line % 2 == 0, count, electrons - count).astype(F32)
    groups = jnp.where(lane < rows, jnp.where(lane // own == line // 2, tiled, 0.0), size)
    groups = jnp.concatenate([groups, jnp.zeros((16 - 2 * walkers, feat), F32)], axis=0).astype(BF16)
    packed_ref[rows:, :] = groups
    lines_ref[...] = groups
    near[1].wait()
    near[2].wait()
    value_sums_ref[0] = dot(groups[:, :rows], values_ref[...])
    value_sums_ref[1] = dot(groups[:, :rows], lap_ref[...])


def sums_kernel(walkers, own, block, lines_ref, far_ref, out_ref, sent_ref, tangent_ref, mask_ref, sems):
    dirs = out_ref.shape[2]
    rows, feat = walkers * own, lines_ref.shape[1]
    repeat = mask_ref.shape[1] // 2
    steps, chunk = dirs // block, block * own

    def fetch(i):
        at = pl.ds(pl.multiple_of(i * chunk, chunk), chunk)
        return pltpu.make_async_copy(far_ref.at[at], tangent_ref.at[at], sems.at[i])

    for i in range(walkers * steps):
        fetch(i).start()
    spots = (iota((rows, feat), 0) % own == iota((rows, feat), 1) % own).astype(F32).astype(BF16)
    tiled = dot(lines_ref[:, :rows], spots)
    place = iota((repeat, feat), 1) // own == iota((repeat, feat), 0)
    for w in range(walkers):
        both = [jnp.where(place, tiled[2 * w + g:2 * w + g + 1], 0.0) for g in range(2)]
        mask_ref[w] = jnp.concatenate(both, axis=0).astype(BF16)

    @pl.loop(0, walkers * steps)
    def _(i):
        w, step = i // steps, i % steps
        mask = mask_ref[w]
        fetch(i).wait()
        for part in range(block // repeat):
            row = pl.multiple_of(i * chunk + part * repeat * own, repeat * own)
            sums = dot(mask, tangent_ref[pl.ds(row, repeat * own), :])
            at = pl.ds(pl.multiple_of(step * block + part * repeat, repeat), repeat)
            out_ref[w, 0, at, :] = sums[:repeat]
            out_ref[w, 1, at, :] = sums[repeat:]
        at = pl.ds(pl.multiple_of(step * block, block), block)
        sent_ref[w, :, at, :] = out_ref[w, :, at, :].astype(BF16)


def picked_rows(groups, mixed):
    lines = jnp.concatenate([groups, groups, groups], axis=0)
    return dot(lines, three_terms(mixed), FIRST)


def layer_kernel(values_ref, lap_ref, packed_ref, own_ref, other_ref, w_self_ref, w_spin_ref,
                 bias_ref, readout_ref, base_ref, curve_ref, weighted_ref):
    rows, feat = values_ref.shape
    lines = packed_ref[rows:, :]
    groups = lines[:, :rows]
    sizes = jnp.maximum(lines[:, rows:rows + 1].astype(F32), 1.0)
    means = ((own_ref[...] + other_ref[...]) / sizes).astype(BF16)
    preact = dot(values_ref[...], w_self_ref[...]) + picked_rows(groups, dot(means[0], w_spin_ref[...])) + bias_ref[...]
    lap_pre = dot(lap_ref[...], w_self_ref[...]) + picked_rows(groups, dot(means[1], w_spin_ref[...]))
    squash = jnp.tanh(preact)
    slopes = 1.0 - squash * squash
    base_ref[...] = slopes * lap_pre
    curve_ref[...] = -2.0 * squash * slopes
    weighted_ref[...] = slopes * readout_ref[...]


def change_kernel(own, block, piece, base, spin_ref, pot_ref, slot_ref, tangent_ref, own_ref, other_ref, w_self_ref,
                  w_spin_ref, readout_ref, base_ref, curve_ref, weighted_ref, before_ref, lap_ref, grad_ref,
                  mixed_ref, squares_ref, column_ref, terms_ref):
    walkers, feat = lap_ref.shape[0], w_self_ref.shape[0]
    dirs = own_ref.shape[2]
    electrons = slot_ref.shape[1]
    steps, part = dirs // block, 8
    halves = [slice(0, feat // 2), slice(feat // 2, feat)]
    grad_ref[...] = before_ref[...]

    @pl.loop(0, walkers)
    def _(n):
        w = base + n
        count = spin_ref[w]
        ups = count.astype(F32)
        mine = pl.ds(pl.multiple_of(w * own, own), own)
        for g, size in enumerate((ups, electrons - ups)):
            means = ((own_ref[w, g] + other_ref[w, g].astype(F32)) / size).astype(BF16)
            mixed_ref[g] = dot(means, w_spin_ref[...])
        column_ref[...] = jnp.broadcast_to(upper_column(slot_ref, w, count, own), (own, feat // 2))
        squares_ref[...] = jnp.zeros_like(squares_ref)

        @pl.loop(0, steps)
        def _(step):
            upper = column_ref[...] > 0.5
            weighted = [weighted_ref[mine, lanes] for lanes in halves]
            squares = [squares_ref[:, lanes] for lanes in halves]
            for c in range(block // piece):
                row = pl.multiple_of(((w * steps + step) * block + c * piece) * own, own)
                plain = dot(tangent_ref[pl.ds(row, piece * own), :], w_self_ref[...])
                for p in range(piece // part):
                    at = pl.multiple_of(step * block + c * piece + p * part, part)
                    mixed = mixed_ref[:, pl.ds(at, part), :]
                    for d in range(part):
                        row = (p * part + d) * own
                        terms = jnp.zeros((8, feat // 2), F32)
                        for h, lanes in enumerate(halves):
                            picked = jnp.where(upper, mixed[0, d:d + 1, lanes], mixed[1, d:d + 1, lanes])
                            change = plain[row:row + own, lanes] + picked
                            squares[h] = squares[h] + change * change
                            terms = terms + (change * weighted[h]).reshape(own // 8, 8, feat // 2).sum(axis=0)
                        terms_ref[pl.ds(pl.multiple_of(at * 8 + d * 8, 8), 8), :] = terms
            for lanes, total in zip(halves, squares):
                squares_ref[:, lanes] = total

        laplacian = base_ref[mine, :] + curve_ref[mine, :] * squares_ref[...]
        lap_ref[n] = laplacian
        summed = terms_ref[...].reshape(dirs, 8, feat // 2).sum(axis=1)
        spare = jnp.zeros((grad_ref.shape[1] - dirs, feat // 2), F32)
        summed = jnp.concatenate([summed, spare], axis=0)
        row = dot(jnp.ones((8, feat // 2), F32), summed, LAST, HIGHEST)
        share = jnp.sum(laplacian * readout_ref[...]) - jnp.where(lax.axis_index("tan") == 0, 2.0 * pot_ref[w], 0.0)
        row = jnp.where(iota(row.shape, 1) == dirs, share, row)
        grad_ref[...] = jnp.where(iota(row.shape, 0) == w, row, grad_ref[...])


def energy_kernel(dirs, walkers, own_ref, other_ref, out_ref):
    both = own_ref[...] + other_ref[...]
    place = iota(both.shape, 1)
    parts = jnp.where(place < dirs, both * both, jnp.where(place == dirs, both, 0.0))
    energy = -0.5 * jnp.sum(parts, axis=1, keepdims=True)
    lane = iota((1, 128), 1)
    row = jnp.zeros((1, 128), F32)
    for w in range(walkers):
        row = jnp.where(lane == w, energy[w:w + 1], row)
    out_ref[...] = row.reshape(1, 1, 128)


def pair(own_ref, other_ref, rows, r):
    values = jnp.concatenate([ref[r, 0:rows, :] for ref in (own_ref, other_ref)], axis=0)
    groups = jnp.concatenate([ref[r, rows:, 0:rows] for ref in (own_ref, other_ref)], axis=1)
    return values, groups


def slopes_kernel(rows, *refs):
    owns, others, weights, (slopes_ref, sums_ref, means_ref) = refs[0:2], refs[2:4], refs[4:8], refs[8:]
    w_self_ref, w_spin_ref, bias_ref, readout_ref = weights
    blocks, lines, _ = owns[0].shape
    group = lines - rows
    bunch = min(blocks, 8)

    for part, (own_ref, other_ref) in enumerate(zip(owns, others)):
        @pl.loop(0, blocks // bunch)
        def _(i):
            pairs = [pair(own_ref, other_ref, rows, i * bunch + k) for k in range(bunch)]
            means = []
            for k, (values, groups) in enumerate(pairs):
                sizes = jnp.maximum(own_ref[i * bunch + k, rows:, rows:rows + 1].astype(F32), 1.0)
                means.append(dot(groups, values) / sizes)
            means = jnp.concatenate(means, axis=0).astype(BF16)
            first = part * blocks + i * bunch
            at = pl.ds(pl.multiple_of(first * group, bunch * group), bunch * group)
            means_ref[at, :] = means
            mixed = dot(means, w_spin_ref[...])
            sums = []
            for k, (values, groups) in enumerate(pairs):
                preact = (dot(values, w_self_ref[...]) + picked_rows(groups, mixed[k * group:(k + 1) * group])
                          + bias_ref[...])
                squash = jnp.tanh(preact)
                slopes = ((1.0 - squash * squash) * readout_ref[...]).astype(BF16)
                slopes_ref[pl.ds(pl.multiple_of((first + k) * 2 * rows, 2 * rows), 2 * rows), :] = slopes
                sums.append(dot(groups, slopes))
            sums_ref[at, :] = jnp.concatenate(sums, axis=0)


def gradients_kernel(walkers, own, tables, energy_ref, *refs):
    self_ref, spin_ref = refs[-2:]
    rows = walkers * own
    blocks, lines, feat = refs[0].shape
    group, half = lines - rows, blocks // 2
    bunch = min(blocks, 8)
    everyone = energy_ref.shape[0] * walkers
    center = jnp.sum(jnp.sum(energy_ref[...], axis=0), axis=1, keepdims=True) / everyone
    line = iota((group, feat), 0) // 2
    self_ref[...] = jnp.zeros_like(self_ref)
    spin_ref[...] = jnp.zeros_like(spin_ref)
    for side, part in ((side, part) for side in range(2) for part in range(2)):
        owns, others, (slopes_ref, sums_ref, means_ref) = (
            refs[7 * side:7 * side + 2], refs[7 * side + 2:7 * side + 4], refs[7 * side + 4:7 * side + 7])
        own_ref, other_ref, (low_place, high_place) = owns[part], others[part], tables[side][part]

        @pl.loop(0, blocks // bunch)
        def _(i):
            first = part * blocks + i * bunch
            values, high, low, spreads = [], [], [], []
            for k in range(bunch):
                block = i * bunch + k
                row = energy_ref[block % half + jnp.where(block < half, low_place, high_place)] - center
                row_at = pl.multiple_of((first + k) * 2 * rows, 2 * rows)
                slopes = slopes_ref[pl.ds(row_at, 2 * rows), :].astype(F32)
                spread = jnp.zeros((group, feat), F32)
                for w in range(walkers):
                    spread = jnp.where(line == w, row[:, w:w + 1], spread)
                spreads.append(spread)
                for core in range(2):
                    for w in range(walkers):
                        at = core * rows + w * own
                        top, rest = two_terms(slopes[at:at + own] * row[:, w:w + 1])
                        high.append(top)
                        low.append(rest)
                values.append(pair(own_ref, other_ref, rows, block)[0])
            values = jnp.concatenate(values, axis=0)
            self_ref[...] += dot(values, jnp.concatenate(high, axis=0), FIRST) + dot(
                values, jnp.concatenate(low, axis=0), FIRST)
            at = pl.ds(pl.multiple_of(first * group, bunch * group), bunch * group)
            top, rest = two_terms(sums_ref[at, :] * jnp.concatenate(spreads, axis=0))
            means = means_ref[at, :]
            spin_ref[...] += dot(means, top, FIRST) + dot(means, rest, FIRST)


def whole(memory=pltpu.VMEM):
    return pl.BlockSpec(memory_space=memory)


def call(kernel, out_shape, in_specs, scratch=(), cost=None, limit=VMEM_LIMIT, out_specs=None):
    flops, moved = cost if cost is not None else (0, 0)
    return pl.pallas_call(
        kernel,
        out_shape=out_shape,
        in_specs=in_specs,
        out_specs=jax.tree.map(lambda _: whole(), out_shape) if out_specs is None else out_specs,
        scratch_shapes=scratch,
        cost_estimate=pl.CostEstimate(flops=flops, bytes_accessed=moved, transcendentals=0) if cost else None,
        compiler_params=pltpu.CompilerParams(vmem_limit_bytes=limit),
    )


def flip(array, axis, bit):
    size = lax.axis_size(axis)
    return lax.ppermute(array, axis, [(i, i ^ bit) for i in range(size)])


def tied(*arrays):
    return lax.optimization_barrier(arrays)


def shards(values, lap_in, tangent, slot_electron, spin_up, w_self, w_spin, bias, readout, potential):
    walk_size = lax.axis_size("walk")
    walkers, own, feat = values.shape
    dirs = tangent.shape[1]
    shape = jax.ShapeDtypeStruct
    smem = whole(pltpu.SMEM)
    flat = tangent.reshape(walkers * dirs * own, feat)
    values, lap_in = values.reshape(walkers * own, feat), lap_in.reshape(walkers * own, feat)
    bias, readout = bias.reshape(1, feat), readout.reshape(1, feat)
    bits = [1 << b for b in reversed(range(walk_size.bit_length() - 1))]

    small = (2, 16, feat)
    packed, value_sums, lines = call(
        functools.partial(pack_kernel, walkers, own),
        (shape((walkers * own + 16, feat), BF16), shape(small, F32), shape((16, feat), BF16)),
        [smem] + [whole(pltpu.HBM)] * 3,
        [pltpu.VMEM(slot_electron.shape, jnp.int32), pltpu.VMEM(lap_in.shape, BF16), pltpu.SemaphoreType.DMA((3,))],
        limit=63 * MIB)(spin_up, slot_electron, values, lap_in)
    other_value_sums = flip(value_sums, "tan", 1)
    gathered = packed.reshape((1,) + packed.shape)

    repeat, block, piece = feat // own, dirs // 2, dirs // 4
    sums, sent, held = call(
        functools.partial(sums_kernel, walkers, own, block),
        (shape((walkers, 2, dirs, feat), F32), shape((walkers, 2, dirs, feat), BF16), shape(flat.shape, BF16)),
        [whole(), whole(pltpu.HBM)],
        [pltpu.VMEM((walkers, 2 * repeat, feat), BF16), pltpu.SemaphoreType.DMA((walkers * dirs // block,))],
        (flat.size * 32, flat.size * 2), 36 * MIB)(lines, flat)
    received, sent, other_value_sums = tied(flip(gathered, "walk", bits[0]), sent, other_value_sums)
    gathered = jnp.concatenate([gathered, received], axis=0)
    other_sums = flip(sent, "tan", 1)
    for bit in bits[1:-3]:
        gathered = jnp.concatenate([gathered, flip(gathered, "walk", bit)], axis=0)
    received = flip(gathered, "walk", bits[-3])

    full = shape((walkers * own, feat), F32)
    base, curve, weighted = call(
        layer_kernel, (full, full, full), [whole()] * 9, cost=(4 * feat * feat * walkers * own, 4 << 20))(
            values, lap_in, packed, value_sums, other_value_sums, w_self, w_spin, bias, readout)

    counts = (1, walkers - 1)
    wide = -(-(dirs + 1) // 128) * 128

    def change(h, ups, before):
        return call(
            functools.partial(change_kernel, own, block, piece, sum(counts[:h])),
            (shape((counts[h], own, feat), F32), shape((8, wide), F32)),
            [smem, smem] + [whole()] * 11,
            [pltpu.VMEM((2, dirs, feat), F32), pltpu.VMEM((own, feat), F32), pltpu.VMEM((own, feat // 2), F32),
             pltpu.VMEM((dirs * 8, feat // 2), F32)],
            (flat.size * feat * counts[h] // 2, flat.size),
        )(ups, potential, slot_electron, held, sums, other_sums, w_self, w_spin, readout, base, curve, weighted, before)

    def joined(*arrays):
        return jnp.concatenate(arrays, axis=0)

    def across(arrays):
        return [flip(array, "tan", 1) for array in arrays]

    far_bits = bits[-2:]
    laplacian, partial = change(0, spin_up, jnp.zeros((8, wide), F32))
    received, late_spin_up, partial = tied(received, spin_up, partial)
    gathered = joined(gathered, received)
    middle = gathered.shape[0] // 2
    near = [gathered[:middle], gathered[middle:]]
    received = [flip(part, "walk", bit) for part, bit in zip(near, far_bits)]
    more_laplacian, more_partial = change(1, late_spin_up, partial)
    *received, more_partial = tied(*received, more_partial)
    near = [joined(*both) for both in zip(near, received)]
    far = [flip(part, "walk", bit) for part, bit in zip(near, reversed(far_bits))]
    near_others = across(near)
    rows = call(
        functools.partial(energy_kernel, dirs, walkers), shape((1, 1, 128), F32), [whole()] * 2)(
            more_partial, flip(more_partial, "tan", 1))
    energy = rows[0, 0, :walkers]
    *near_others, more_laplacian, _ = tied(*near_others, more_laplacian, rows)

    blocks = walk_size // 2
    group_shape = (blocks * 16, feat)
    half = [((blocks * 2 * walkers * own, feat), BF16), (group_shape, F32), (group_shape, BF16)]
    weights = (w_self, w_spin, bias, readout)

    def slopes(*parts):
        return call(
            functools.partial(slopes_kernel, walkers * own), tuple(shape(*h) for h in half), [whole()] * 8,
            cost=(blocks * 8 * walkers * own * feat * feat, 8 << 20))(*parts, *weights)

    *near_slopes, last = slopes(*near, *near_others)
    energies = rows
    for stage, bit in enumerate(bits):
        received = flip(energies, "walk", bit)
        if stage == 0:
            received, last = tied(received, last)
        if stage == len(bits) - 3:
            received, *far = tied(received, *far)
            far_others = across(far)
            *far_slopes, far_last = slopes(*far, *far_others)
        if stage == len(bits) - 1:
            received, far_last = tied(received, far_last)
        energies = joined(energies, received)
    laplacian = joined(laplacian, more_laplacian)
    square = shape((feat, feat), F32)
    step = walk_size // 4
    tables = (((0, step), (step // 2, step // 2 + 2 * step)),
              ((2 * step, 3 * step), (step // 2 + step, step // 2 + 3 * step)))
    grad_self, grad_spin = call(
        functools.partial(gradients_kernel, walkers, own, tables), (square, square), [whole()] * 15)(
            energies, *near, *near_others, *near_slopes, last, *far, *far_others, *far_slopes, far_last)
    return laplacian, energy, grad_self, grad_spin


def solution(mesh):
    placed = (
        P("walk", "tan", None),
        P("walk", "tan", None),
        P("walk", None, "tan", None),
        P("walk", None),
        P("walk"),
        P(),
        P(),
        P(),
        P(),
        P("walk"),
    )
    return jax.shard_map(
        shards,
        mesh=mesh,
        in_specs=placed,
        out_specs=(P("walk", "tan", None), P("walk"), P(), P()),
        check_vma=False,
    )
```

```python
import functools

import jax
import jax.numpy as jnp
from jax import lax
from jax.experimental import pallas as pl
from jax.experimental.pallas import tpu as pltpu
from jax.sharding import PartitionSpec as P

F32 = jnp.float32
BF16 = jnp.bfloat16
MIB = 1024 * 1024
VMEM_LIMIT = 24 * MIB
HIGHEST = lax.Precision.HIGHEST
FIRST = ((0,), (0,))
LAST = ((1,), (1,))


def iota(shape, axis):
    return lax.broadcasted_iota(jnp.int32, shape, axis)


def dot(a, b, dims=((1,), (0,)), precision=None):
    return lax.dot_general(a, b, (dims, ((), ())), precision=precision, preferred_element_type=F32)


def two_terms(array):
    high = array.astype(BF16)
    return high, (array - high.astype(F32)).astype(BF16)


def three_terms(array):
    high = array.astype(BF16)
    middle, low = two_terms(array - high.astype(F32))
    return jnp.concatenate([high, middle, low], axis=0)


def first_slot(own):
    return lax.axis_index("tan") * own


def upper_row(slot_ref, w, count):
    return (slot_ref[pl.ds(w, 1), :] < count).astype(F32)


def upper_column(slot_ref, w, count, own):
    row = upper_row(slot_ref, w, count)
    place = iota((own, row.shape[1]), 1) == iota((own, row.shape[1]), 0) + first_slot(own)
    return jnp.sum(jnp.where(place, row, 0.0), axis=1, keepdims=True)


def own_places(electrons, own, wide):
    return (iota((electrons, wide), 0) == iota((electrons, wide), 1) % own + first_slot(own)).astype(BF16)


def pack_kernel(walkers, own, spin_ref, slot_far, values_far, lap_far, packed_ref, value_sums_ref, lines_ref,
                slot_ref, lap_ref, small_sems):
    rows, feat = lap_ref.shape
    electrons = slot_ref.shape[1]
    values_ref = packed_ref.at[pl.ds(0, rows)]
    near = [pltpu.make_async_copy(*ends, small_sems.at[i]) for i, ends in enumerate(
        ((slot_far, slot_ref), (values_far, values_ref), (lap_far, lap_ref)))]
    for copy in near:
        copy.start()
    near[0].wait()
    slots = jnp.zeros((2 * walkers, electrons), jnp.int32)
    for w in range(walkers):
        slots = jnp.where(iota(slots.shape, 0) // 2 == w, slot_ref[w:w + 1, :], slots)

    def column(shape):
        line = iota(shape, 0)
        count = jnp.zeros(shape, jnp.int32)
        for w in range(walkers):
            count = jnp.where(line // 2 == w, spin_ref[w], count)
        return line, count

    line, count = column(slots.shape)
    upper = (slots < count).astype(F32)
    chosen = jnp.where(line % 2 == 0, upper, 1.0 - upper).astype(BF16)
    tiled = dot(chosen, own_places(electrons, own, feat))
    line, count = column(tiled.shape)
    lane = iota(tiled.shape, 1)
    size = jnp.where(line % 2 == 0, count, electrons - count).astype(F32)
    groups = jnp.where(lane < rows, jnp.where(lane // own == line // 2, tiled, 0.0), size)
    groups = jnp.concatenate([groups, jnp.zeros((16 - 2 * walkers, feat), F32)], axis=0).astype(BF16)
    packed_ref[rows:, :] = groups
    lines_ref[...] = groups
    near[1].wait()
    near[2].wait()
    value_sums_ref[0] = dot(groups[:, :rows], values_ref[...])
    value_sums_ref[1] = dot(groups[:, :rows], lap_ref[...])


def sums_kernel(walkers, own, block, lines_ref, far_ref, out_ref, sent_ref, tangent_ref, mask_ref, sems):
    dirs = out_ref.shape[2]
    rows, feat = walkers * own, lines_ref.shape[1]
    repeat = mask_ref.shape[1] // 2
    steps, chunk = dirs // block, block * own

    def fetch(i):
        at = pl.ds(pl.multiple_of(i * chunk, chunk), chunk)
        return pltpu.make_async_copy(far_ref.at[at], tangent_ref.at[at], sems.at[i])

    for i in range(walkers * steps):
        fetch(i).start()
    spots = (iota((rows, feat), 0) % own == iota((rows, feat), 1) % own).astype(F32).astype(BF16)
    tiled = dot(lines_ref[:, :rows], spots)
    place = iota((repeat, feat), 1) // own == iota((repeat, feat), 0)
    for w in range(walkers):
        both = [jnp.where(place, tiled[2 * w + g:2 * w + g + 1], 0.0) for g in range(2)]
        mask_ref[w] = jnp.concatenate(both, axis=0).astype(BF16)

    @pl.loop(0, walkers * steps)
    def _(i):
        w, step = i // steps, i % steps
        mask = mask_ref[w]
        fetch(i).wait()
        for part in range(block // repeat):
            row = pl.multiple_of(i * chunk + part * repeat * own, repeat * own)
            sums = dot(mask, tangent_ref[pl.ds(row, repeat * own), :])
            at = pl.ds(pl.multiple_of(step * block + part * repeat, repeat), repeat)
            out_ref[w, 0, at, :] = sums[:repeat]
            out_ref[w, 1, at, :] = sums[repeat:]
        at = pl.ds(pl.multiple_of(step * block, block), block)
        sent_ref[w, :, at, :] = out_ref[w, :, at, :].astype(BF16)


def picked_rows(groups, mixed):
    lines = jnp.concatenate([groups, groups, groups], axis=0)
    return dot(lines, three_terms(mixed), FIRST)


def layer_kernel(values_ref, lap_ref, packed_ref, own_ref, other_ref, w_self_ref, w_spin_ref,
                 bias_ref, readout_ref, base_ref, curve_ref, weighted_ref):
    rows, feat = values_ref.shape
    lines = packed_ref[rows:, :]
    groups = lines[:, :rows]
    sizes = jnp.maximum(lines[:, rows:rows + 1].astype(F32), 1.0)
    means = ((own_ref[...] + other_ref[...]) / sizes).astype(BF16)
    preact = dot(values_ref[...], w_self_ref[...]) + picked_rows(groups, dot(means[0], w_spin_ref[...])) + bias_ref[...]
    lap_pre = dot(lap_ref[...], w_self_ref[...]) + picked_rows(groups, dot(means[1], w_spin_ref[...]))
    squash = jnp.tanh(preact)
    slopes = 1.0 - squash * squash
    base_ref[...] = slopes * lap_pre
    curve_ref[...] = -2.0 * squash * slopes
    weighted_ref[...] = slopes * readout_ref[...]


def change_kernel(own, block, piece, base, spin_ref, pot_ref, slot_ref, tangent_ref, own_ref, other_ref, w_self_ref,
                  w_spin_ref, readout_ref, base_ref, curve_ref, weighted_ref, before_ref, lap_ref, grad_ref,
                  mixed_ref, squares_ref, column_ref, terms_ref):
    walkers, feat = lap_ref.shape[0], w_self_ref.shape[0]
    dirs = own_ref.shape[2]
    electrons = slot_ref.shape[1]
    steps, part, apart = dirs // block, 8, len(mixed_ref.shape) == 4
    halves = [slice(0, feat // 2), slice(feat // 2, feat)]
    grad_ref[...] = before_ref[...]

    @pl.loop(0, walkers)
    def _(n):
        w = base + n
        count = spin_ref[w]
        ups = count.astype(F32)
        mine = pl.ds(pl.multiple_of(w * own, own), own)
        for g, size in enumerate((ups, electrons - ups)):
            means = ((own_ref[w, g] + other_ref[w, g].astype(F32)) / size).astype(BF16)
            mixed_ref[g] = dot(means, w_spin_ref[...]).reshape(mixed_ref.shape[1:])
        column_ref[...] = jnp.broadcast_to(upper_column(slot_ref, w, count, own), (own, feat // 2))
        squares_ref[...] = jnp.zeros_like(squares_ref)

        @pl.loop(0, steps)
        def _(step):
            upper = column_ref[...] > 0.5
            weighted = [weighted_ref[mine, lanes] for lanes in halves]
            squares = [squares_ref[:, lanes] for lanes in halves]
            for c in range(block // piece):
                row = pl.multiple_of(((w * steps + step) * block + c * piece) * own, own)
                plain = dot(tangent_ref[pl.ds(row, piece * own), :], w_self_ref[...])
                for p in range(piece // part):
                    at = pl.multiple_of(step * block + c * piece + p * part, part)
                    for d in range(part):
                        rows = [mixed_ref[g, at + d] if apart else mixed_ref[g, pl.ds(at + d, 1), :] for g in range(2)]
                        row = (p * part + d) * own
                        terms = jnp.zeros((8, feat // 2), F32)
                        for h, lanes in enumerate(halves):
                            picked = jnp.where(upper, rows[0][:, lanes], rows[1][:, lanes])
                            change = plain[row:row + own, lanes] + picked
                            squares[h] = squares[h] + change * change
                            terms = terms + (change * weighted[h]).reshape(own // 8, 8, feat // 2).sum(axis=0)
                        terms_ref[pl.ds(pl.multiple_of(at * 8 + d * 8, 8), 8), :] = terms
            for lanes, total in zip(halves, squares):
                squares_ref[:, lanes] = total

        laplacian = base_ref[mine, :] + curve_ref[mine, :] * squares_ref[...]
        lap_ref[n] = laplacian
        summed = terms_ref[...].reshape(dirs, 8, feat // 2).sum(axis=1)
        spare = jnp.zeros((grad_ref.shape[1] - dirs, feat // 2), F32)
        summed = jnp.concatenate([summed, spare], axis=0)
        row = dot(jnp.ones((8, feat // 2), F32), summed, LAST, HIGHEST)
        share = jnp.sum(laplacian * readout_ref[...]) - jnp.where(lax.axis_index("tan") == 0, 2.0 * pot_ref[w], 0.0)
        row = jnp.where(iota(row.shape, 1) == dirs, share, row)
        grad_ref[...] = jnp.where(iota(row.shape, 0) == w, row, grad_ref[...])


def energy_kernel(dirs, walkers, own_ref, other_ref, out_ref):
    both = own_ref[...] + other_ref[...]
    place = iota(both.shape, 1)
    parts = jnp.where(place < dirs, both * both, jnp.where(place == dirs, both, 0.0))
    energy = -0.5 * jnp.sum(parts, axis=1, keepdims=True)
    lane = iota((1, 128), 1)
    row = jnp.zeros((1, 128), F32)
    for w in range(walkers):
        row = jnp.where(lane == w, energy[w:w + 1], row)
    out_ref[...] = row.reshape(1, 1, 128)


def pair(own_ref, other_ref, rows, r):
    values = jnp.concatenate([ref[r, 0:rows, :] for ref in (own_ref, other_ref)], axis=0)
    groups = jnp.concatenate([ref[r, rows:, 0:rows] for ref in (own_ref, other_ref)], axis=1)
    return values, groups


def slopes_kernel(rows, *refs):
    owns, others, weights, (slopes_ref, sums_ref, means_ref) = refs[0:2], refs[2:4], refs[4:8], refs[8:]
    w_self_ref, w_spin_ref, bias_ref, readout_ref = weights
    blocks, lines, _ = owns[0].shape
    group = lines - rows
    bunch = min(blocks, 8)

    for part, (own_ref, other_ref) in enumerate(zip(owns, others)):
        @pl.loop(0, blocks // bunch)
        def _(i):
            pairs = [pair(own_ref, other_ref, rows, i * bunch + k) for k in range(bunch)]
            means = []
            for k, (values, groups) in enumerate(pairs):
                sizes = jnp.maximum(own_ref[i * bunch + k, rows:, rows:rows + 1].astype(F32), 1.0)
                means.append(dot(groups, values) / sizes)
            means = jnp.concatenate(means, axis=0).astype(BF16)
            first = part * blocks + i * bunch
            at = pl.ds(pl.multiple_of(first * group, bunch * group), bunch * group)
            means_ref[at, :] = means
            mixed = dot(means, w_spin_ref[...])
            sums = []
            for k, (values, groups) in enumerate(pairs):
                preact = (dot(values, w_self_ref[...]) + picked_rows(groups, mixed[k * group:(k + 1) * group])
                          + bias_ref[...])
                squash = jnp.tanh(preact)
                slopes = ((1.0 - squash * squash) * readout_ref[...]).astype(BF16)
                slopes_ref[pl.ds(pl.multiple_of((first + k) * 2 * rows, 2 * rows), 2 * rows), :] = slopes
                sums.append(dot(groups, slopes))
            sums_ref[at, :] = jnp.concatenate(sums, axis=0)


def gradients_kernel(walkers, own, tables, energy_ref, *refs):
    self_ref, spin_ref = refs[-2:]
    rows = walkers * own
    blocks, lines, feat = refs[0].shape
    group, half = lines - rows, blocks // 2
    bunch = min(blocks, 8)
    everyone = energy_ref.shape[0] * walkers
    center = jnp.sum(jnp.sum(energy_ref[...], axis=0), axis=1, keepdims=True) / everyone
    line = iota((group, feat), 0) // 2
    self_ref[...] = jnp.zeros_like(self_ref)
    spin_ref[...] = jnp.zeros_like(spin_ref)
    for side, part in ((side, part) for side in range(2) for part in range(2)):
        owns, others, (slopes_ref, sums_ref, means_ref) = (
            refs[7 * side:7 * side + 2], refs[7 * side + 2:7 * side + 4], refs[7 * side + 4:7 * side + 7])
        own_ref, other_ref, (low_place, high_place) = owns[part], others[part], tables[side][part]

        @pl.loop(0, blocks // bunch)
        def _(i):
            first = part * blocks + i * bunch
            values, high, low, spreads = [], [], [], []
            for k in range(bunch):
                block = i * bunch + k
                row = energy_ref[block % half + jnp.where(block < half, low_place, high_place)] - center
                row_at = pl.multiple_of((first + k) * 2 * rows, 2 * rows)
                slopes = slopes_ref[pl.ds(row_at, 2 * rows), :].astype(F32)
                spread = jnp.zeros((group, feat), F32)
                for w in range(walkers):
                    spread = jnp.where(line == w, row[:, w:w + 1], spread)
                spreads.append(spread)
                for core in range(2):
                    for w in range(walkers):
                        at = core * rows + w * own
                        top, rest = two_terms(slopes[at:at + own] * row[:, w:w + 1])
                        high.append(top)
                        low.append(rest)
                values.append(pair(own_ref, other_ref, rows, block)[0])
            values = jnp.concatenate(values, axis=0)
            self_ref[...] += dot(values, jnp.concatenate(high, axis=0), FIRST) + dot(
                values, jnp.concatenate(low, axis=0), FIRST)
            at = pl.ds(pl.multiple_of(first * group, bunch * group), bunch * group)
            top, rest = two_terms(sums_ref[at, :] * jnp.concatenate(spreads, axis=0))
            means = means_ref[at, :]
            spin_ref[...] += dot(means, top, FIRST) + dot(means, rest, FIRST)


def whole(memory=pltpu.VMEM):
    return pl.BlockSpec(memory_space=memory)


def call(kernel, out_shape, in_specs, scratch=(), cost=None, limit=VMEM_LIMIT, out_specs=None):
    flops, moved = cost if cost is not None else (0, 0)
    return pl.pallas_call(
        kernel,
        out_shape=out_shape,
        in_specs=in_specs,
        out_specs=jax.tree.map(lambda _: whole(), out_shape) if out_specs is None else out_specs,
        scratch_shapes=scratch,
        cost_estimate=pl.CostEstimate(flops=flops, bytes_accessed=moved, transcendentals=0) if cost else None,
        compiler_params=pltpu.CompilerParams(vmem_limit_bytes=limit),
    )


def flip(array, axis, bit):
    size = lax.axis_size(axis)
    return lax.ppermute(array, axis, [(i, i ^ bit) for i in range(size)])


def tied(*arrays):
    return lax.optimization_barrier(arrays)


def shards(values, lap_in, tangent, slot_electron, spin_up, w_self, w_spin, bias, readout, potential):
    walk_size = lax.axis_size("walk")
    walkers, own, feat = values.shape
    dirs = tangent.shape[1]
    shape = jax.ShapeDtypeStruct
    smem = whole(pltpu.SMEM)
    flat = tangent.reshape(walkers * dirs * own, feat)
    values, lap_in = values.reshape(walkers * own, feat), lap_in.reshape(walkers * own, feat)
    bias, readout = bias.reshape(1, feat), readout.reshape(1, feat)
    bits = [1 << b for b in reversed(range(walk_size.bit_length() - 1))]

    small = (2, 16, feat)
    packed, value_sums, lines = call(
        functools.partial(pack_kernel, walkers, own),
        (shape((walkers * own + 16, feat), BF16), shape(small, F32), shape((16, feat), BF16)),
        [smem] + [whole(pltpu.HBM)] * 3,
        [pltpu.VMEM(slot_electron.shape, jnp.int32), pltpu.VMEM(lap_in.shape, BF16), pltpu.SemaphoreType.DMA((3,))],
        limit=63 * MIB)(spin_up, slot_electron, values, lap_in)
    other_value_sums = flip(value_sums, "tan", 1)
    gathered = packed.reshape((1,) + packed.shape)

    repeat, block, piece = feat // own, dirs // 2, dirs // 4
    sums, sent, held = call(
        functools.partial(sums_kernel, walkers, own, block),
        (shape((walkers, 2, dirs, feat), F32), shape((walkers, 2, dirs, feat), BF16), shape(flat.shape, BF16)),
        [whole(), whole(pltpu.HBM)],
        [pltpu.VMEM((walkers, 2 * repeat, feat), BF16), pltpu.SemaphoreType.DMA((walkers * dirs // block,))],
        (flat.size * 32, flat.size * 2), 36 * MIB)(lines, flat)
    received, sent, other_value_sums = tied(flip(gathered, "walk", bits[0]), sent, other_value_sums)
    gathered = jnp.concatenate([gathered, received], axis=0)
    other_sums = flip(sent, "tan", 1)
    for bit in bits[1:-3]:
        gathered = jnp.concatenate([gathered, flip(gathered, "walk", bit)], axis=0)
    received = flip(gathered, "walk", bits[-3])

    full = shape((walkers * own, feat), F32)
    base, curve, weighted = call(
        layer_kernel, (full, full, full), [whole()] * 9, cost=(4 * feat * feat * walkers * own, 4 << 20))(
            values, lap_in, packed, value_sums, other_value_sums, w_self, w_spin, bias, readout)

    counts = (1, walkers - 1)
    wide = -(-(dirs + 1) // 128) * 128

    def change(h, ups, before):
        return call(
            functools.partial(change_kernel, own, block, piece, sum(counts[:h])),
            (shape((counts[h], own, feat), F32), shape((8, wide), F32)),
            [smem, smem] + [whole()] * 11,
            [pltpu.VMEM((2, dirs, feat) if h else (2, dirs, 1, feat), F32), pltpu.VMEM((own, feat), F32),
             pltpu.VMEM((own, feat // 2), F32),
             pltpu.VMEM((dirs * 8, feat // 2), F32)],
            (flat.size * feat * counts[h] // 2, flat.size),
        )(ups, potential, slot_electron, held, sums, other_sums, w_self, w_spin, readout, base, curve, weighted, before)

    def joined(*arrays):
        return jnp.concatenate(arrays, axis=0)

    def across(arrays):
        return [flip(array, "tan", 1) for array in arrays]

    far_bits = bits[-2:]
    laplacian, partial = change(0, spin_up, jnp.zeros((8, wide), F32))
    received, late_spin_up, partial = tied(received, spin_up, partial)
    gathered = joined(gathered, received)
    middle = gathered.shape[0] // 2
    near = [gathered[:middle], gathered[middle:]]
    received = [flip(part, "walk", bit) for part, bit in zip(near, far_bits)]
    more_laplacian, more_partial = change(1, late_spin_up, partial)
    *received, more_partial = tied(*received, more_partial)
    near = [joined(*both) for both in zip(near, received)]
    far = [flip(part, "walk", bit) for part, bit in zip(near, reversed(far_bits))]
    near_others = across(near)
    rows = call(
        functools.partial(energy_kernel, dirs, walkers), shape((1, 1, 128), F32), [whole()] * 2)(
            more_partial, flip(more_partial, "tan", 1))
    energy = rows[0, 0, :walkers]
    *near_others, more_laplacian, _ = tied(*near_others, more_laplacian, rows)

    blocks = walk_size // 2
    group_shape = (blocks * 16, feat)
    half = [((blocks * 2 * walkers * own, feat), BF16), (group_shape, F32), (group_shape, BF16)]
    weights = (w_self, w_spin, bias, readout)

    def slopes(*parts):
        return call(
            functools.partial(slopes_kernel, walkers * own), tuple(shape(*h) for h in half), [whole()] * 8,
            cost=(blocks * 8 * walkers * own * feat * feat, 8 << 20))(*parts, *weights)

    *near_slopes, last = slopes(*near, *near_others)
    energies = rows
    for stage, bit in enumerate(bits):
        received = flip(energies, "walk", bit)
        if stage == 0:
            received, last = tied(received, last)
        if stage == len(bits) - 3:
            received, *far = tied(received, *far)
            far_others = across(far)
            *far_slopes, far_last = slopes(*far, *far_others)
        if stage == len(bits) - 1:
            received, far_last = tied(received, far_last)
        energies = joined(energies, received)
    laplacian = joined(laplacian, more_laplacian)
    square = shape((feat, feat), F32)
    step = walk_size // 4
    tables = (((0, step), (step // 2, step // 2 + 2 * step)),
              ((2 * step, 3 * step), (step // 2 + step, step // 2 + 3 * step)))
    grad_self, grad_spin = call(
        functools.partial(gradients_kernel, walkers, own, tables), (square, square), [whole()] * 15)(
            energies, *near, *near_others, *near_slopes, last, *far, *far_others, *far_slopes, far_last)
    return laplacian, energy, grad_self, grad_spin


def solution(mesh):
    placed = (
        P("walk", "tan", None),
        P("walk", "tan", None),
        P("walk", None, "tan", None),
        P("walk", None),
        P("walk"),
        P(),
        P(),
        P(),
        P(),
        P("walk"),
    )
    return jax.shard_map(
        shards,
        mesh=mesh,
        in_specs=placed,
        out_specs=(P("walk", "tan", None), P("walk"), P(), P()),
        check_vma=False,
    )
```

```python
import functools

import jax
import jax.numpy as jnp
from jax import lax
from jax.experimental import pallas as pl
from jax.experimental.pallas import tpu as pltpu
from jax.sharding import PartitionSpec as P

F32 = jnp.float32
BF16 = jnp.bfloat16
MIB = 1024 * 1024
VMEM_LIMIT = 24 * MIB
HIGHEST = lax.Precision.HIGHEST
FIRST = ((0,), (0,))
LAST = ((1,), (1,))


def iota(shape, axis):
    return lax.broadcasted_iota(jnp.int32, shape, axis)


def dot(a, b, dims=((1,), (0,)), precision=None):
    return lax.dot_general(a, b, (dims, ((), ())), precision=precision, preferred_element_type=F32)


def two_terms(array):
    high = array.astype(BF16)
    return high, (array - high.astype(F32)).astype(BF16)


def three_terms(array):
    high = array.astype(BF16)
    middle, low = two_terms(array - high.astype(F32))
    return jnp.concatenate([high, middle, low], axis=0)


def first_slot(own):
    return lax.axis_index("tan") * own


def upper_row(slot_ref, w, count):
    return (slot_ref[pl.ds(w, 1), :] < count).astype(F32)


def upper_column(slot_ref, w, count, own):
    row = upper_row(slot_ref, w, count)
    place = iota((own, row.shape[1]), 1) == iota((own, row.shape[1]), 0) + first_slot(own)
    return jnp.sum(jnp.where(place, row, 0.0), axis=1, keepdims=True)


def own_places(electrons, own, wide):
    return (iota((electrons, wide), 0) == iota((electrons, wide), 1) % own + first_slot(own)).astype(BF16)


def pack_kernel(walkers, own, spin_ref, slot_far, values_far, lap_far, packed_ref, value_sums_ref, lines_ref,
                slot_ref, lap_ref, small_sems):
    rows, feat = lap_ref.shape
    electrons = slot_ref.shape[1]
    values_ref = packed_ref.at[pl.ds(0, rows)]
    near = [pltpu.make_async_copy(*ends, small_sems.at[i]) for i, ends in enumerate(
        ((slot_far, slot_ref), (values_far, values_ref), (lap_far, lap_ref)))]
    for copy in near:
        copy.start()
    near[0].wait()
    slots = jnp.zeros((2 * walkers, electrons), jnp.int32)
    for w in range(walkers):
        slots = jnp.where(iota(slots.shape, 0) // 2 == w, slot_ref[w:w + 1, :], slots)

    def column(shape):
        line = iota(shape, 0)
        count = jnp.zeros(shape, jnp.int32)
        for w in range(walkers):
            count = jnp.where(line // 2 == w, spin_ref[w], count)
        return line, count

    line, count = column(slots.shape)
    upper = (slots < count).astype(F32)
    chosen = jnp.where(line % 2 == 0, upper, 1.0 - upper).astype(BF16)
    tiled = dot(chosen, own_places(electrons, own, feat))
    line, count = column(tiled.shape)
    lane = iota(tiled.shape, 1)
    size = jnp.where(line % 2 == 0, count, electrons - count).astype(F32)
    groups = jnp.where(lane < rows, jnp.where(lane // own == line // 2, tiled, 0.0), size)
    groups = jnp.concatenate([groups, jnp.zeros((16 - 2 * walkers, feat), F32)], axis=0).astype(BF16)
    packed_ref[rows:, :] = groups
    lines_ref[...] = groups
    near[1].wait()
    near[2].wait()
    value_sums_ref[0] = dot(groups[:, :rows], values_ref[...])
    value_sums_ref[1] = dot(groups[:, :rows], lap_ref[...])


def sums_kernel(walkers, own, block, lines_ref, far_ref, out_ref, sent_ref, tangent_ref, mask_ref, sems):
    dirs = out_ref.shape[2]
    rows, feat = walkers * own, lines_ref.shape[1]
    repeat = mask_ref.shape[1] // 2
    steps, chunk = dirs // block, block * own

    def fetch(i):
        at = pl.ds(pl.multiple_of(i * chunk, chunk), chunk)
        return pltpu.make_async_copy(far_ref.at[at], tangent_ref.at[at], sems.at[i])

    for i in range(walkers * steps):
        fetch(i).start()
    spots = (iota((rows, feat), 0) % own == iota((rows, feat), 1) % own).astype(F32).astype(BF16)
    tiled = dot(lines_ref[:, :rows], spots)
    place = iota((repeat, feat), 1) // own == iota((repeat, feat), 0)
    for w in range(walkers):
        both = [jnp.where(place, tiled[2 * w + g:2 * w + g + 1], 0.0) for g in range(2)]
        mask_ref[w] = jnp.concatenate(both, axis=0).astype(BF16)

    @pl.loop(0, walkers * steps)
    def _(i):
        w, step = i // steps, i % steps
        mask = mask_ref[w]
        fetch(i).wait()
        for part in range(block // repeat):
            row = pl.multiple_of(i * chunk + part * repeat * own, repeat * own)
            sums = dot(mask, tangent_ref[pl.ds(row, repeat * own), :])
            at = pl.ds(pl.multiple_of(step * block + part * repeat, repeat), repeat)
            out_ref[w, 0, at, :] = sums[:repeat]
            out_ref[w, 1, at, :] = sums[repeat:]
        at = pl.ds(pl.multiple_of(step * block, block), block)
        sent_ref[w, :, at, :] = out_ref[w, :, at, :].astype(BF16)


def picked_rows(groups, mixed):
    lines = jnp.concatenate([groups, groups, groups], axis=0)
    return dot(lines, three_terms(mixed), FIRST)


def layer_kernel(values_ref, lap_ref, packed_ref, own_ref, other_ref, w_self_ref, w_spin_ref,
                 bias_ref, readout_ref, base_ref, curve_ref, weighted_ref):
    rows, feat = values_ref.shape
    lines = packed_ref[rows:, :]
    groups = lines[:, :rows]
    sizes = jnp.maximum(lines[:, rows:rows + 1].astype(F32), 1.0)
    means = ((own_ref[...] + other_ref[...]) / sizes).astype(BF16)
    preact = dot(values_ref[...], w_self_ref[...]) + picked_rows(groups, dot(means[0], w_spin_ref[...])) + bias_ref[...]
    lap_pre = dot(lap_ref[...], w_self_ref[...]) + picked_rows(groups, dot(means[1], w_spin_ref[...]))
    squash = jnp.tanh(preact)
    slopes = 1.0 - squash * squash
    base_ref[...] = slopes * lap_pre
    curve_ref[...] = -2.0 * squash * slopes
    weighted_ref[...] = slopes * readout_ref[...]


def change_kernel(own, block, piece, base, spin_ref, pot_ref, slot_ref, tangent_ref, own_ref, other_ref, w_self_ref,
                  w_spin_ref, readout_ref, base_ref, curve_ref, weighted_ref, before_ref, lap_ref, grad_ref,
                  mixed_ref, squares_ref, column_ref, terms_ref):
    walkers, feat = lap_ref.shape[0], w_self_ref.shape[0]
    dirs = own_ref.shape[2]
    electrons = slot_ref.shape[1]
    steps, part = dirs // block, 8
    halves = [slice(0, feat // 2), slice(feat // 2, feat)]
    grad_ref[...] = before_ref[...]

    @pl.loop(0, walkers)
    def _(n):
        w = base + n
        count = spin_ref[w]
        ups = count.astype(F32)
        mine = pl.ds(pl.multiple_of(w * own, own), own)
        for g, size in enumerate((ups, electrons - ups)):
            means = ((own_ref[w, g] + other_ref[w, g].astype(F32)) / size).astype(BF16)
            mixed_ref[g] = dot(means, w_spin_ref[...])
        column_ref[...] = jnp.broadcast_to(upper_column(slot_ref, w, count, own), (own, feat // 2))
        squares_ref[...] = jnp.zeros_like(squares_ref)

        @pl.loop(0, steps)
        def _(step):
            upper = column_ref[...] > 0.5
            weighted = [weighted_ref[mine, lanes] for lanes in halves]
            squares = [squares_ref[:, lanes] for lanes in halves]
            for c in range(block // piece):
                row = pl.multiple_of(((w * steps + step) * block + c * piece) * own, own)
                plain = dot(tangent_ref[pl.ds(row, piece * own), :], w_self_ref[...])
                for p in range(piece // part):
                    at = pl.multiple_of(step * block + c * piece + p * part, part)
                    mixed = mixed_ref[:, pl.ds(at, part), :]
                    for d in range(part):
                        row = (p * part + d) * own
                        terms = jnp.zeros((8, feat // 2), F32)
                        for h, lanes in enumerate(halves):
                            picked = jnp.where(upper, mixed[0, d:d + 1, lanes], mixed[1, d:d + 1, lanes])
                            change = plain[row:row + own, lanes] + picked
                            squares[h] = squares[h] + change * change
                            terms = terms + (change * weighted[h]).reshape(own // 8, 8, feat // 2).sum(axis=0)
                        terms_ref[pl.ds(pl.multiple_of(at * 8 + d * 8, 8), 8), :] = terms
            for lanes, total in zip(halves, squares):
                squares_ref[:, lanes] = total

        laplacian = base_ref[mine, :] + curve_ref[mine, :] * squares_ref[...]
        lap_ref[n] = laplacian
        summed = terms_ref[...].reshape(dirs, 8, feat // 2).sum(axis=1)
        spare = jnp.zeros((grad_ref.shape[1] - dirs, feat // 2), F32)
        summed = jnp.concatenate([summed, spare], axis=0)
        row = dot(jnp.ones((8, feat // 2), F32), summed, LAST, HIGHEST)
        share = jnp.sum(laplacian * readout_ref[...]) - jnp.where(lax.axis_index("tan") == 0, 2.0 * pot_ref[w], 0.0)
        row = jnp.where(iota(row.shape, 1) == dirs, share, row)
        grad_ref[...] = jnp.where(iota(row.shape, 0) == w, row, grad_ref[...])


def energy_kernel(dirs, walkers, own_ref, other_ref, out_ref):
    both = own_ref[...] + other_ref[...]
    place = iota(both.shape, 1)
    parts = jnp.where(place < dirs, both * both, jnp.where(place == dirs, both, 0.0))
    energy = -0.5 * jnp.sum(parts, axis=1, keepdims=True)
    lane = iota((1, 128), 1)
    row = jnp.zeros((1, 128), F32)
    for w in range(walkers):
        row = jnp.where(lane == w, energy[w:w + 1], row)
    out_ref[...] = row.reshape(1, 1, 128)


def pair(own_ref, other_ref, rows, r):
    values = jnp.concatenate([ref[r, 0:rows, :] for ref in (own_ref, other_ref)], axis=0)
    groups = jnp.concatenate([ref[r, rows:, 0:rows] for ref in (own_ref, other_ref)], axis=1)
    return values, groups


def slopes_kernel(rows, *refs):
    owns, others, weights, (slopes_ref, sums_ref, means_ref) = refs[0:2], refs[2:4], refs[4:8], refs[8:]
    w_self_ref, w_spin_ref, bias_ref, readout_ref = weights
    blocks, lines, _ = owns[0].shape
    group = lines - rows
    bunch = min(blocks, 8)

    for part, (own_ref, other_ref) in enumerate(zip(owns, others)):
        @pl.loop(0, blocks // bunch)
        def _(i):
            pairs = [pair(own_ref, other_ref, rows, i * bunch + k) for k in range(bunch)]
            means = []
            for k, (values, groups) in enumerate(pairs):
                sizes = jnp.maximum(own_ref[i * bunch + k, rows:, rows:rows + 1].astype(F32), 1.0)
                means.append(dot(groups, values) / sizes)
            means = jnp.concatenate(means, axis=0).astype(BF16)
            first = part * blocks + i * bunch
            at = pl.ds(pl.multiple_of(first * group, bunch * group), bunch * group)
            means_ref[at, :] = means
            mixed = dot(means, w_spin_ref[...])
            sums = []
            for k, (values, groups) in enumerate(pairs):
                preact = (dot(values, w_self_ref[...]) + picked_rows(groups, mixed[k * group:(k + 1) * group])
                          + bias_ref[...])
                squash = jnp.tanh(preact)
                slopes = ((1.0 - squash * squash) * readout_ref[...]).astype(BF16)
                slopes_ref[pl.ds(pl.multiple_of((first + k) * 2 * rows, 2 * rows), 2 * rows), :] = slopes
                sums.append(dot(groups, slopes))
            sums_ref[at, :] = jnp.concatenate(sums, axis=0)


def gradients_kernel(walkers, own, tables, energy_ref, *refs):
    self_ref, spin_ref = refs[-2:]
    rows = walkers * own
    blocks, lines, feat = refs[0].shape
    group, half = lines - rows, blocks // 2
    bunch = min(blocks, 8)
    everyone = energy_ref.shape[0] * walkers
    center = jnp.sum(jnp.sum(energy_ref[...], axis=0), axis=1, keepdims=True) / everyone
    line = iota((group, feat), 0) // 2
    self_ref[...] = jnp.zeros_like(self_ref)
    spin_ref[...] = jnp.zeros_like(spin_ref)
    for side, part in ((side, part) for side in range(2) for part in range(2)):
        owns, others, (slopes_ref, sums_ref, means_ref) = (
            refs[7 * side:7 * side + 2], refs[7 * side + 2:7 * side + 4], refs[7 * side + 4:7 * side + 7])
        own_ref, other_ref, (low_place, high_place) = owns[part], others[part], tables[side][part]

        @pl.loop(0, blocks // bunch)
        def _(i):
            first = part * blocks + i * bunch
            values, high, low, spreads = [], [], [], []
            for k in range(bunch):
                block = i * bunch + k
                row = energy_ref[block % half + jnp.where(block < half, low_place, high_place)] - center
                row_at = pl.multiple_of((first + k) * 2 * rows, 2 * rows)
                slopes = slopes_ref[pl.ds(row_at, 2 * rows), :].astype(F32)
                spread = jnp.zeros((group, feat), F32)
                for w in range(walkers):
                    spread = jnp.where(line == w, row[:, w:w + 1], spread)
                spreads.append(spread)
                for core in range(2):
                    for w in range(walkers):
                        at = core * rows + w * own
                        top, rest = two_terms(slopes[at:at + own] * row[:, w:w + 1])
                        high.append(top)
                        low.append(rest)
                values.append(pair(own_ref, other_ref, rows, block)[0])
            values = jnp.concatenate(values, axis=0)
            self_ref[...] += dot(values, jnp.concatenate(high, axis=0), FIRST) + dot(
                values, jnp.concatenate(low, axis=0), FIRST)
            at = pl.ds(pl.multiple_of(first * group, bunch * group), bunch * group)
            top, rest = two_terms(sums_ref[at, :] * jnp.concatenate(spreads, axis=0))
            means = means_ref[at, :]
            spin_ref[...] += dot(means, top, FIRST) + dot(means, rest, FIRST)


def whole(memory=pltpu.VMEM):
    return pl.BlockSpec(memory_space=memory)


def call(kernel, out_shape, in_specs, scratch=(), cost=None, limit=VMEM_LIMIT, out_specs=None):
    flops, moved = cost if cost is not None else (0, 0)
    return pl.pallas_call(
        kernel,
        out_shape=out_shape,
        in_specs=in_specs,
        out_specs=jax.tree.map(lambda _: whole(), out_shape) if out_specs is None else out_specs,
        scratch_shapes=scratch,
        cost_estimate=pl.CostEstimate(flops=flops, bytes_accessed=moved, transcendentals=0) if cost else None,
        compiler_params=pltpu.CompilerParams(vmem_limit_bytes=limit),
    )


def flip(array, axis, bit):
    size = lax.axis_size(axis)
    return lax.ppermute(array, axis, [(i, i ^ bit) for i in range(size)])


def tied(*arrays):
    return lax.optimization_barrier(arrays)


def shards(values, lap_in, tangent, slot_electron, spin_up, w_self, w_spin, bias, readout, potential):
    walk_size = lax.axis_size("walk")
    walkers, own, feat = values.shape
    dirs = tangent.shape[1]
    shape = jax.ShapeDtypeStruct
    smem = whole(pltpu.SMEM)
    flat = tangent.reshape(walkers * dirs * own, feat)
    values, lap_in = values.reshape(walkers * own, feat), lap_in.reshape(walkers * own, feat)
    bias, readout = bias.reshape(1, feat), readout.reshape(1, feat)
    bits = [1 << b for b in reversed(range(walk_size.bit_length() - 1))]

    small = (2, 16, feat)
    packed, value_sums, lines = call(
        functools.partial(pack_kernel, walkers, own),
        (shape((walkers * own + 16, feat), BF16), shape(small, F32), shape((16, feat), BF16)),
        [smem] + [whole(pltpu.HBM)] * 3,
        [pltpu.VMEM(slot_electron.shape, jnp.int32), pltpu.VMEM(lap_in.shape, BF16), pltpu.SemaphoreType.DMA((3,))],
        limit=63 * MIB)(spin_up, slot_electron, values, lap_in)
    other_value_sums = flip(value_sums, "tan", 1)
    gathered = packed.reshape((1,) + packed.shape)

    repeat, block, piece = feat // own, dirs // 2, dirs // 4
    sums, sent, held = call(
        functools.partial(sums_kernel, walkers, own, block),
        (shape((walkers, 2, dirs, feat), F32), shape((walkers, 2, dirs, feat), BF16), shape(flat.shape, BF16)),
        [whole(), whole(pltpu.HBM)],
        [pltpu.VMEM((walkers, 2 * repeat, feat), BF16), pltpu.SemaphoreType.DMA((walkers * dirs // block,))],
        (flat.size * 32, flat.size * 2), 36 * MIB)(lines, flat)
    received, sent, other_value_sums = tied(flip(gathered, "walk", bits[0]), sent, other_value_sums)
    gathered = jnp.concatenate([gathered, received], axis=0)
    other_sums = flip(sent, "tan", 1)
    for bit in bits[1:-3]:
        gathered = jnp.concatenate([gathered, flip(gathered, "walk", bit)], axis=0)
    received = flip(gathered, "walk", bits[-3])

    full = shape((walkers * own, feat), F32)
    base, curve, weighted = call(
        layer_kernel, (full, full, full), [whole()] * 9, cost=(4 * feat * feat * walkers * own, 4 << 20))(
            values, lap_in, packed, value_sums, other_value_sums, w_self, w_spin, bias, readout)

    counts = (1, walkers - 1)
    wide = -(-(dirs + 1) // 128) * 128

    def change(h, ups, before):
        return call(
            functools.partial(change_kernel, own, block, piece, sum(counts[:h])),
            (shape((counts[h], own, feat), F32), shape((8, wide), F32)),
            [smem, smem] + [whole()] * 11,
            [pltpu.VMEM((2, dirs, feat), F32), pltpu.VMEM((own, feat), F32), pltpu.VMEM((own, feat // 2), F32),
             pltpu.VMEM((dirs * 8, feat // 2), F32)],
            (flat.size * feat * counts[h] // 2, flat.size),
        )(ups, potential, slot_electron, held, sums, other_sums, w_self, w_spin, readout, base, curve, weighted, before)

    def joined(*arrays):
        return jnp.concatenate(arrays, axis=0)

    def across(arrays):
        return [flip(array, "tan", 1) for array in arrays]

    far_bits = bits[-2:]
    laplacian, partial = change(0, spin_up, jnp.zeros((8, wide), F32))
    received, late_spin_up, partial = tied(received, spin_up, partial)
    gathered = joined(gathered, received)
    middle = gathered.shape[0] // 2
    received = [flip(gathered, "walk", bit) for bit in far_bits]
    more_laplacian, more_partial = change(1, late_spin_up, partial)
    *received, more_partial = tied(*received, more_partial)
    near = [gathered, received[0]]
    diagonal = [flip(received[0][:middle], "walk", far_bits[1]), flip(received[1][middle:], "walk", far_bits[0])]
    near_others, side_other = across(near), flip(received[1], "tan", 1)
    rows = call(
        functools.partial(energy_kernel, dirs, walkers), shape((1, 1, 128), F32), [whole()] * 2)(
            more_partial, flip(more_partial, "tan", 1))
    energy = rows[0, 0, :walkers]
    *near_others, side_other, more_laplacian, _ = tied(*near_others, side_other, more_laplacian, rows)

    blocks = walk_size // 2
    group_shape = (blocks * 16, feat)
    half = [((blocks * 2 * walkers * own, feat), BF16), (group_shape, F32), (group_shape, BF16)]
    weights = (w_self, w_spin, bias, readout)

    def slopes(*parts):
        return call(
            functools.partial(slopes_kernel, walkers * own), tuple(shape(*h) for h in half), [whole()] * 8,
            cost=(blocks * 8 * walkers * own * feat * feat, 8 << 20))(*parts, *weights)

    *near_slopes, last = slopes(*near, *near_others)
    energies = rows
    for stage, bit in enumerate(bits):
        arrived = flip(energies, "walk", bit)
        if stage == 0:
            arrived, last, *diagonal = tied(arrived, last, *diagonal)
            far = [received[1], joined(*diagonal)]
            far_others = [side_other, flip(far[1], "tan", 1)]
            *far_slopes, far_last = slopes(*far, *far_others)
        if stage == len(bits) - 2:
            arrived, far_last = tied(arrived, far_last)
        energies = joined(energies, arrived)
    laplacian = joined(laplacian, more_laplacian)
    square = shape((feat, feat), F32)
    step = walk_size // 4
    tables = [[(place * step, place * step + step // 2) for place in (side, side + 1)] for side in (0, 2)]
    grad_self, grad_spin = call(
        functools.partial(gradients_kernel, walkers, own, tables), (square, square), [whole()] * 15)(
            energies, *near, *near_others, *near_slopes, last, *far, *far_others, *far_slopes, far_last)
    return laplacian, energy, grad_self, grad_spin


def solution(mesh):
    placed = (
        P("walk", "tan", None),
        P("walk", "tan", None),
        P("walk", None, "tan", None),
        P("walk", None),
        P("walk"),
        P(),
        P(),
        P(),
        P(),
        P("walk"),
    )
    return jax.shard_map(
        shards,
        mesh=mesh,
        in_specs=placed,
        out_specs=(P("walk", "tan", None), P("walk"), P(), P()),
        check_vma=False,
    )
```

```python
import functools

import jax
import jax.numpy as jnp
from jax import lax
from jax.experimental import pallas as pl
from jax.experimental.pallas import tpu as pltpu
from jax.sharding import PartitionSpec as P

F32 = jnp.float32
BF16 = jnp.bfloat16
MIB = 1024 * 1024
VMEM_LIMIT = 24 * MIB
HIGHEST = lax.Precision.HIGHEST
FIRST = ((0,), (0,))
LAST = ((1,), (1,))


def iota(shape, axis):
    return lax.broadcasted_iota(jnp.int32, shape, axis)


def dot(a, b, dims=((1,), (0,)), precision=None):
    return lax.dot_general(a, b, (dims, ((), ())), precision=precision, preferred_element_type=F32)


def two_terms(array):
    high = array.astype(BF16)
    return high, (array - high.astype(F32)).astype(BF16)


def three_terms(array):
    high = array.astype(BF16)
    middle, low = two_terms(array - high.astype(F32))
    return jnp.concatenate([high, middle, low], axis=0)


def first_slot(own):
    return lax.axis_index("tan") * own


def upper_row(slot_ref, w, count):
    return (slot_ref[pl.ds(w, 1), :] < count).astype(F32)


def upper_column(slot_ref, w, count, own):
    row = upper_row(slot_ref, w, count)
    place = iota((own, row.shape[1]), 1) == iota((own, row.shape[1]), 0) + first_slot(own)
    return jnp.sum(jnp.where(place, row, 0.0), axis=1, keepdims=True)


def own_places(electrons, own, wide):
    return (iota((electrons, wide), 0) == iota((electrons, wide), 1) % own + first_slot(own)).astype(BF16)


def pack_kernel(walkers, own, spin_ref, slot_far, values_far, lap_far, packed_ref, value_sums_ref, lines_ref,
                slot_ref, lap_ref, small_sems):
    rows, feat = lap_ref.shape
    electrons = slot_ref.shape[1]
    values_ref = packed_ref.at[pl.ds(0, rows)]
    near = [pltpu.make_async_copy(*ends, small_sems.at[i]) for i, ends in enumerate(
        ((slot_far, slot_ref), (values_far, values_ref), (lap_far, lap_ref)))]
    for copy in near:
        copy.start()
    near[0].wait()
    slots = jnp.zeros((2 * walkers, electrons), jnp.int32)
    for w in range(walkers):
        slots = jnp.where(iota(slots.shape, 0) // 2 == w, slot_ref[w:w + 1, :], slots)

    def column(shape):
        line = iota(shape, 0)
        count = jnp.zeros(shape, jnp.int32)
        for w in range(walkers):
            count = jnp.where(line // 2 == w, spin_ref[w], count)
        return line, count

    line, count = column(slots.shape)
    upper = (slots < count).astype(F32)
    chosen = jnp.where(line % 2 == 0, upper, 1.0 - upper).astype(BF16)
    tiled = dot(chosen, own_places(electrons, own, feat))
    line, count = column(tiled.shape)
    lane = iota(tiled.shape, 1)
    size = jnp.where(line % 2 == 0, count, electrons - count).astype(F32)
    groups = jnp.where(lane < rows, jnp.where(lane // own == line // 2, tiled, 0.0), size)
    groups = jnp.concatenate([groups, jnp.zeros((16 - 2 * walkers, feat), F32)], axis=0).astype(BF16)
    packed_ref[rows:, :] = groups
    lines_ref[...] = groups
    near[1].wait()
    near[2].wait()
    value_sums_ref[0] = dot(groups[:, :rows], values_ref[...])
    value_sums_ref[1] = dot(groups[:, :rows], lap_ref[...])


def sums_kernel(walkers, own, block, lines_ref, far_ref, out_ref, sent_ref, tangent_ref, mask_ref, sems):
    dirs = out_ref.shape[2]
    rows, feat = walkers * own, lines_ref.shape[1]
    repeat = mask_ref.shape[1] // 2
    steps, chunk = dirs // block, block * own

    def fetch(i):
        at = pl.ds(pl.multiple_of(i * chunk, chunk), chunk)
        return pltpu.make_async_copy(far_ref.at[at], tangent_ref.at[at], sems.at[i])

    for i in range(walkers * steps):
        fetch(i).start()
    spots = (iota((rows, feat), 0) % own == iota((rows, feat), 1) % own).astype(F32).astype(BF16)
    tiled = dot(lines_ref[:, :rows], spots)
    place = iota((repeat, feat), 1) // own == iota((repeat, feat), 0)
    for w in range(walkers):
        both = [jnp.where(place, tiled[2 * w + g:2 * w + g + 1], 0.0) for g in range(2)]
        mask_ref[w] = jnp.concatenate(both, axis=0).astype(BF16)

    @pl.loop(0, walkers * steps)
    def _(i):
        w, step = i // steps, i % steps
        mask = mask_ref[w]
        fetch(i).wait()
        for part in range(block // repeat):
            row = pl.multiple_of(i * chunk + part * repeat * own, repeat * own)
            sums = dot(mask, tangent_ref[pl.ds(row, repeat * own), :])
            at = pl.ds(pl.multiple_of(step * block + part * repeat, repeat), repeat)
            out_ref[w, 0, at, :] = sums[:repeat]
            out_ref[w, 1, at, :] = sums[repeat:]
        at = pl.ds(pl.multiple_of(step * block, block), block)
        sent_ref[w, :, at, :] = out_ref[w, :, at, :].astype(BF16)


def picked_rows(groups, mixed):
    lines = jnp.concatenate([groups, groups, groups], axis=0)
    return dot(lines, three_terms(mixed), FIRST)


def layer_kernel(values_ref, lap_ref, packed_ref, own_ref, other_ref, w_self_ref, w_spin_ref,
                 bias_ref, readout_ref, base_ref, curve_ref, weighted_ref):
    rows, feat = values_ref.shape
    lines = packed_ref[rows:, :]
    groups = lines[:, :rows]
    sizes = jnp.maximum(lines[:, rows:rows + 1].astype(F32), 1.0)
    means = ((own_ref[...] + other_ref[...]) / sizes).astype(BF16)
    preact = dot(values_ref[...], w_self_ref[...]) + picked_rows(groups, dot(means[0], w_spin_ref[...])) + bias_ref[...]
    lap_pre = dot(lap_ref[...], w_self_ref[...]) + picked_rows(groups, dot(means[1], w_spin_ref[...]))
    squash = jnp.tanh(preact)
    slopes = 1.0 - squash * squash
    base_ref[...] = slopes * lap_pre
    curve_ref[...] = -2.0 * squash * slopes
    weighted_ref[...] = slopes * readout_ref[...]


def change_kernel(own, block, piece, base, spin_ref, pot_ref, slot_ref, tangent_ref, own_ref, other_ref, w_self_ref,
                  w_spin_ref, readout_ref, base_ref, curve_ref, weighted_ref, before_ref, lap_ref, grad_ref,
                  mixed_ref, squares_ref, column_ref, terms_ref):
    walkers, feat = lap_ref.shape[0], w_self_ref.shape[0]
    dirs = own_ref.shape[2]
    electrons = slot_ref.shape[1]
    steps, part = dirs // block, 8
    halves = [slice(0, feat // 2), slice(feat // 2, feat)]
    grad_ref[...] = before_ref[...]

    @pl.loop(0, walkers)
    def _(n):
        w = base + n
        count = spin_ref[w]
        ups = count.astype(F32)
        mine = pl.ds(pl.multiple_of(w * own, own), own)
        for g, size in enumerate((ups, electrons - ups)):
            means = ((own_ref[w, g] + other_ref[w, g].astype(F32)) / size).astype(BF16)
            mixed_ref[g] = dot(means, w_spin_ref[...])
        column_ref[...] = jnp.broadcast_to(upper_column(slot_ref, w, count, own), (own, feat // 2))
        squares_ref[...] = jnp.zeros_like(squares_ref)

        @pl.loop(0, steps)
        def _(step):
            upper = column_ref[...] > 0.5
            weighted = [weighted_ref[mine, lanes] for lanes in halves]
            squares = [squares_ref[:, lanes] for lanes in halves]
            for c in range(block // piece):
                row = pl.multiple_of(((w * steps + step) * block + c * piece) * own, own)
                plain = dot(tangent_ref[pl.ds(row, piece * own), :], w_self_ref[...])
                for p in range(piece // part):
                    at = pl.multiple_of(step * block + c * piece + p * part, part)
                    mixed = mixed_ref[:, pl.ds(at, part), :]
                    for d in range(part):
                        row = (p * part + d) * own
                        terms = jnp.zeros((8, feat // 2), F32)
                        for h, lanes in enumerate(halves):
                            picked = jnp.where(upper, mixed[0, d:d + 1, lanes], mixed[1, d:d + 1, lanes])
                            change = plain[row:row + own, lanes] + picked
                            squares[h] = squares[h] + change * change
                            terms = terms + (change * weighted[h]).reshape(own // 8, 8, feat // 2).sum(axis=0)
                        terms_ref[pl.ds(pl.multiple_of(at * 8 + d * 8, 8), 8), :] = terms
            for lanes, total in zip(halves, squares):
                squares_ref[:, lanes] = total

        laplacian = base_ref[mine, :] + curve_ref[mine, :] * squares_ref[...]
        lap_ref[n] = laplacian
        summed = terms_ref[...].reshape(dirs, 8, feat // 2).sum(axis=1)
        spare = jnp.zeros((grad_ref.shape[1] - dirs, feat // 2), F32)
        summed = jnp.concatenate([summed, spare], axis=0)
        row = dot(jnp.ones((8, feat // 2), F32), summed, LAST, HIGHEST)
        share = jnp.sum(laplacian * readout_ref[...]) - jnp.where(lax.axis_index("tan") == 0, 2.0 * pot_ref[w], 0.0)
        row = jnp.where(iota(row.shape, 1) == dirs, share, row)
        grad_ref[...] = jnp.where(iota(row.shape, 0) == w, row, grad_ref[...])


def energy_kernel(dirs, walkers, own_ref, other_ref, out_ref):
    both = own_ref[...] + other_ref[...]
    place = iota(both.shape, 1)
    parts = jnp.where(place < dirs, both * both, jnp.where(place == dirs, both, 0.0))
    energy = -0.5 * jnp.sum(parts, axis=1, keepdims=True)
    lane = iota((1, 128), 1)
    row = jnp.zeros((1, 128), F32)
    for w in range(walkers):
        row = jnp.where(lane == w, energy[w:w + 1], row)
    out_ref[...] = row.reshape(1, 1, 128)


def pair(own_ref, other_ref, rows, r):
    values = jnp.concatenate([ref[r, 0:rows, :] for ref in (own_ref, other_ref)], axis=0)
    groups = jnp.concatenate([ref[r, rows:, 0:rows] for ref in (own_ref, other_ref)], axis=1)
    return values, groups


def slopes_kernel(rows, *refs):
    count = (len(refs) - 7) // 2
    owns, others, weights = refs[:count], refs[count:2 * count], refs[2 * count:2 * count + 4]
    slopes_ref, sums_ref, means_ref = refs[2 * count + 4:]
    w_self_ref, w_spin_ref, bias_ref, readout_ref = weights
    blocks, lines, _ = owns[0].shape
    group = lines - rows
    bunch = min(blocks, 8)

    for part, (own_ref, other_ref) in enumerate(zip(owns, others)):
        @pl.loop(0, blocks // bunch)
        def _(i):
            pairs = [pair(own_ref, other_ref, rows, i * bunch + k) for k in range(bunch)]
            means = []
            for k, (values, groups) in enumerate(pairs):
                sizes = jnp.maximum(own_ref[i * bunch + k, rows:, rows:rows + 1].astype(F32), 1.0)
                means.append(dot(groups, values) / sizes)
            means = jnp.concatenate(means, axis=0).astype(BF16)
            first = part * blocks + i * bunch
            at = pl.ds(pl.multiple_of(first * group, bunch * group), bunch * group)
            means_ref[at, :] = means
            mixed = dot(means, w_spin_ref[...])
            sums = []
            for k, (values, groups) in enumerate(pairs):
                preact = (dot(values, w_self_ref[...]) + picked_rows(groups, mixed[k * group:(k + 1) * group])
                          + bias_ref[...])
                squash = jnp.tanh(preact)
                slopes = ((1.0 - squash * squash) * readout_ref[...]).astype(BF16)
                slopes_ref[pl.ds(pl.multiple_of((first + k) * 2 * rows, 2 * rows), 2 * rows), :] = slopes
                sums.append(dot(groups, slopes))
            sums_ref[at, :] = jnp.concatenate(sums, axis=0)


def gradients_kernel(walkers, own, tables, energy_ref, *refs):
    self_ref, spin_ref = refs[-2:]
    rows = walkers * own
    blocks, lines, feat = refs[0].shape
    group, half = lines - rows, blocks // 2
    bunch = min(blocks, 8)
    everyone = energy_ref.shape[0] * walkers
    center = jnp.sum(jnp.sum(energy_ref[...], axis=0), axis=1, keepdims=True) / everyone
    line = iota((group, feat), 0) // 2
    self_ref[...] = jnp.zeros_like(self_ref)
    spin_ref[...] = jnp.zeros_like(spin_ref)
    near, far = refs[:7], (refs[7:12], refs[12:17])
    sets = [(part, near[part], near[2 + part]) + tuple(near[4:]) for part in range(2)] + [(0,) + tuple(f) for f in far]
    for (part, own_ref, other_ref, slopes_ref, sums_ref, means_ref), (low_place, high_place) in zip(sets, tables):
        @pl.loop(0, blocks // bunch)
        def _(i):
            first = part * blocks + i * bunch
            values, high, low, spreads = [], [], [], []
            for k in range(bunch):
                block = i * bunch + k
                row = energy_ref[block % half + jnp.where(block < half, low_place, high_place)] - center
                row_at = pl.multiple_of((first + k) * 2 * rows, 2 * rows)
                slopes = slopes_ref[pl.ds(row_at, 2 * rows), :].astype(F32)
                spread = jnp.zeros((group, feat), F32)
                for w in range(walkers):
                    spread = jnp.where(line == w, row[:, w:w + 1], spread)
                spreads.append(spread)
                for core in range(2):
                    for w in range(walkers):
                        at = core * rows + w * own
                        top, rest = two_terms(slopes[at:at + own] * row[:, w:w + 1])
                        high.append(top)
                        low.append(rest)
                values.append(pair(own_ref, other_ref, rows, block)[0])
            values = jnp.concatenate(values, axis=0)
            self_ref[...] += dot(values, jnp.concatenate(high, axis=0), FIRST) + dot(
                values, jnp.concatenate(low, axis=0), FIRST)
            at = pl.ds(pl.multiple_of(first * group, bunch * group), bunch * group)
            top, rest = two_terms(sums_ref[at, :] * jnp.concatenate(spreads, axis=0))
            means = means_ref[at, :]
            spin_ref[...] += dot(means, top, FIRST) + dot(means, rest, FIRST)


def whole(memory=pltpu.VMEM):
    return pl.BlockSpec(memory_space=memory)


def call(kernel, out_shape, in_specs, scratch=(), cost=None, limit=VMEM_LIMIT, out_specs=None):
    flops, moved = cost if cost is not None else (0, 0)
    return pl.pallas_call(
        kernel,
        out_shape=out_shape,
        in_specs=in_specs,
        out_specs=jax.tree.map(lambda _: whole(), out_shape) if out_specs is None else out_specs,
        scratch_shapes=scratch,
        cost_estimate=pl.CostEstimate(flops=flops, bytes_accessed=moved, transcendentals=0) if cost else None,
        compiler_params=pltpu.CompilerParams(vmem_limit_bytes=limit),
    )


def flip(array, axis, bit):
    size = lax.axis_size(axis)
    return lax.ppermute(array, axis, [(i, i ^ bit) for i in range(size)])


def tied(*arrays):
    return lax.optimization_barrier(arrays)


def shards(values, lap_in, tangent, slot_electron, spin_up, w_self, w_spin, bias, readout, potential):
    walk_size = lax.axis_size("walk")
    walkers, own, feat = values.shape
    dirs = tangent.shape[1]
    shape = jax.ShapeDtypeStruct
    smem = whole(pltpu.SMEM)
    flat = tangent.reshape(walkers * dirs * own, feat)
    values, lap_in = values.reshape(walkers * own, feat), lap_in.reshape(walkers * own, feat)
    bias, readout = bias.reshape(1, feat), readout.reshape(1, feat)
    bits = [1 << b for b in reversed(range(walk_size.bit_length() - 1))]

    small = (2, 16, feat)
    packed, value_sums, lines = call(
        functools.partial(pack_kernel, walkers, own),
        (shape((walkers * own + 16, feat), BF16), shape(small, F32), shape((16, feat), BF16)),
        [smem] + [whole(pltpu.HBM)] * 3,
        [pltpu.VMEM(slot_electron.shape, jnp.int32), pltpu.VMEM(lap_in.shape, BF16), pltpu.SemaphoreType.DMA((3,))],
        limit=63 * MIB)(spin_up, slot_electron, values, lap_in)
    other_value_sums = flip(value_sums, "tan", 1)
    gathered = packed.reshape((1,) + packed.shape)

    repeat, block, piece = feat // own, dirs // 2, dirs // 4
    sums, sent, held = call(
        functools.partial(sums_kernel, walkers, own, block),
        (shape((walkers, 2, dirs, feat), F32), shape((walkers, 2, dirs, feat), BF16), shape(flat.shape, BF16)),
        [whole(), whole(pltpu.HBM)],
        [pltpu.VMEM((walkers, 2 * repeat, feat), BF16), pltpu.SemaphoreType.DMA((walkers * dirs // block,))],
        (flat.size * 32, flat.size * 2), 36 * MIB)(lines, flat)
    received, sent, other_value_sums = tied(flip(gathered, "walk", bits[0]), sent, other_value_sums)
    gathered = jnp.concatenate([gathered, received], axis=0)
    other_sums = flip(sent, "tan", 1)
    for bit in bits[1:-3]:
        gathered = jnp.concatenate([gathered, flip(gathered, "walk", bit)], axis=0)
    received = flip(gathered, "walk", bits[-3])

    full = shape((walkers * own, feat), F32)
    base, curve, weighted = call(
        layer_kernel, (full, full, full), [whole()] * 9, cost=(4 * feat * feat * walkers * own, 4 << 20))(
            values, lap_in, packed, value_sums, other_value_sums, w_self, w_spin, bias, readout)

    counts = (1, walkers - 1)
    wide = -(-(dirs + 1) // 128) * 128

    def change(h, ups, before):
        return call(
            functools.partial(change_kernel, own, block, piece, sum(counts[:h])),
            (shape((counts[h], own, feat), F32), shape((8, wide), F32)),
            [smem, smem] + [whole()] * 11,
            [pltpu.VMEM((2, dirs, feat), F32), pltpu.VMEM((own, feat), F32), pltpu.VMEM((own, feat // 2), F32),
             pltpu.VMEM((dirs * 8, feat // 2), F32)],
            (flat.size * feat * counts[h] // 2, flat.size),
        )(ups, potential, slot_electron, held, sums, other_sums, w_self, w_spin, readout, base, curve, weighted, before)

    def joined(*arrays):
        return jnp.concatenate(arrays, axis=0)

    def across(arrays):
        return [flip(array, "tan", 1) for array in arrays]

    far_bits = bits[-2:]
    laplacian, partial = change(0, spin_up, jnp.zeros((8, wide), F32))
    received, late_spin_up, partial = tied(received, spin_up, partial)
    gathered = joined(gathered, received)
    middle = gathered.shape[0] // 2
    near = [gathered[:middle], gathered[middle:]]
    received = [flip(part, "walk", bit) for part, bit in zip(near, far_bits)]
    received[0], late_spin_up = tied(received[0], late_spin_up)
    more_laplacian, more_partial = change(1, late_spin_up, partial)
    received[1], more_partial = tied(received[1], more_partial)
    near = [joined(*both) for both in zip(near, received)]
    far = [flip(part, "walk", bit) for part, bit in zip(near, reversed(far_bits))]
    near_others = across(near)
    rows = call(
        functools.partial(energy_kernel, dirs, walkers), shape((1, 1, 128), F32), [whole()] * 2)(
            more_partial, flip(more_partial, "tan", 1))
    energy = rows[0, 0, :walkers]
    *near_others, more_laplacian, _ = tied(*near_others, more_laplacian, rows)

    blocks = walk_size // 2
    group_shape = (blocks * 16, feat)
    half = [((blocks * 2 * walkers * own, feat), BF16), (group_shape, F32), (group_shape, BF16)]
    weights = (w_self, w_spin, bias, readout)

    def slopes(*parts):
        count = len(parts) // 2
        return call(
            functools.partial(slopes_kernel, walkers * own),
            tuple(shape((size[0] * count // 2,) + size[1:], kind) for size, kind in half), [whole()] * (2 * count + 4),
            cost=(blocks * 4 * count * walkers * own * feat * feat, count << 22))(*parts, *weights)

    *near_slopes, last = slopes(*near, *near_others)
    energies = rows
    for stage, bit in enumerate(bits):
        received = flip(energies, "walk", bit)
        if stage == 0:
            received, last, far[0] = tied(received, last, far[0])
            far_others = [flip(far[0], "tan", 1)]
            *first_slopes, first_last = slopes(far[0], far_others[0])
        if stage == len(bits) - 3:
            received, first_last, far[1] = tied(received, first_last, far[1])
            far_others.append(flip(far[1], "tan", 1))
            *far_slopes, far_last = slopes(far[1], far_others[1])
        if stage == len(bits) - 1:
            received, far_last = tied(received, far_last)
        energies = joined(energies, received)
    laplacian = joined(laplacian, more_laplacian)
    square = shape((feat, feat), F32)
    step = walk_size // 4
    tables = ((0, step), (step // 2, step // 2 + 2 * step),
              (2 * step, 3 * step), (step // 2 + step, step // 2 + 3 * step))
    grad_self, grad_spin = call(
        functools.partial(gradients_kernel, walkers, own, tables), (square, square), [whole()] * 18)(
            energies, *near, *near_others, *near_slopes, last, far[0], far_others[0], *first_slopes, first_last,
            far[1], far_others[1], *far_slopes, far_last)
    return laplacian, energy, grad_self, grad_spin


def solution(mesh):
    placed = (
        P("walk", "tan", None),
        P("walk", "tan", None),
        P("walk", None, "tan", None),
        P("walk", None),
        P("walk"),
        P(),
        P(),
        P(),
        P(),
        P("walk"),
    )
    return jax.shard_map(
        shards,
        mesh=mesh,
        in_specs=placed,
        out_specs=(P("walk", "tan", None), P("walk"), P(), P()),
        check_vma=False,
    )
```

```python
import functools

import jax
import jax.numpy as jnp
from jax import lax
from jax.experimental import pallas as pl
from jax.experimental.pallas import tpu as pltpu
from jax.sharding import PartitionSpec as P

F32 = jnp.float32
BF16 = jnp.bfloat16
MIB = 1024 * 1024
VMEM_LIMIT = 24 * MIB
HIGHEST = lax.Precision.HIGHEST
FIRST = ((0,), (0,))
LAST = ((1,), (1,))


def iota(shape, axis):
    return lax.broadcasted_iota(jnp.int32, shape, axis)


def dot(a, b, dims=((1,), (0,)), precision=None):
    return lax.dot_general(a, b, (dims, ((), ())), precision=precision, preferred_element_type=F32)


def two_terms(array):
    high = array.astype(BF16)
    return high, (array - high.astype(F32)).astype(BF16)


def three_terms(array):
    high = array.astype(BF16)
    middle, low = two_terms(array - high.astype(F32))
    return jnp.concatenate([high, middle, low], axis=0)


def first_slot(own):
    return lax.axis_index("tan") * own


def upper_row(slot_ref, w, count):
    return (slot_ref[pl.ds(w, 1), :] < count).astype(F32)


def upper_column(slot_ref, w, count, own):
    row = upper_row(slot_ref, w, count)
    place = iota((own, row.shape[1]), 1) == iota((own, row.shape[1]), 0) + first_slot(own)
    return jnp.sum(jnp.where(place, row, 0.0), axis=1, keepdims=True)


def own_places(electrons, own, wide):
    return (iota((electrons, wide), 0) == iota((electrons, wide), 1) % own + first_slot(own)).astype(BF16)


def pack_kernel(walkers, own, spin_ref, slot_far, values_far, lap_far, packed_ref, value_sums_ref, lines_ref,
                slot_ref, lap_ref, small_sems):
    rows, feat = lap_ref.shape
    electrons = slot_ref.shape[1]
    values_ref = packed_ref.at[pl.ds(0, rows)]
    near = [pltpu.make_async_copy(*ends, small_sems.at[i]) for i, ends in enumerate(
        ((slot_far, slot_ref), (values_far, values_ref), (lap_far, lap_ref)))]
    for copy in near:
        copy.start()
    near[0].wait()
    slots = jnp.zeros((2 * walkers, electrons), jnp.int32)
    for w in range(walkers):
        slots = jnp.where(iota(slots.shape, 0) // 2 == w, slot_ref[w:w + 1, :], slots)

    def column(shape):
        line = iota(shape, 0)
        count = jnp.zeros(shape, jnp.int32)
        for w in range(walkers):
            count = jnp.where(line // 2 == w, spin_ref[w], count)
        return line, count

    line, count = column(slots.shape)
    upper = (slots < count).astype(F32)
    chosen = jnp.where(line % 2 == 0, upper, 1.0 - upper).astype(BF16)
    tiled = dot(chosen, own_places(electrons, own, feat))
    line, count = column(tiled.shape)
    lane = iota(tiled.shape, 1)
    size = jnp.where(line % 2 == 0, count, electrons - count).astype(F32)
    groups = jnp.where(lane < rows, jnp.where(lane // own == line // 2, tiled, 0.0), size)
    groups = jnp.concatenate([groups, jnp.zeros((16 - 2 * walkers, feat), F32)], axis=0).astype(BF16)
    packed_ref[rows:, :] = groups
    lines_ref[...] = groups
    near[1].wait()
    near[2].wait()
    value_sums_ref[0] = dot(groups[:, :rows], values_ref[...])
    value_sums_ref[1] = dot(groups[:, :rows], lap_ref[...])


def sums_kernel(walkers, own, block, lines_ref, far_ref, out_ref, sent_ref, tangent_ref, mask_ref, sems):
    dirs = out_ref.shape[2]
    rows, feat = walkers * own, lines_ref.shape[1]
    repeat = mask_ref.shape[1] // 2
    steps, chunk = dirs // block, block * own

    def fetch(i):
        at = pl.ds(pl.multiple_of(i * chunk, chunk), chunk)
        return pltpu.make_async_copy(far_ref.at[at], tangent_ref.at[at], sems.at[i])

    for i in range(walkers * steps):
        fetch(i).start()
    spots = (iota((rows, feat), 0) % own == iota((rows, feat), 1) % own).astype(F32).astype(BF16)
    tiled = dot(lines_ref[:, :rows], spots)
    place = iota((repeat, feat), 1) // own == iota((repeat, feat), 0)
    for w in range(walkers):
        both = [jnp.where(place, tiled[2 * w + g:2 * w + g + 1], 0.0) for g in range(2)]
        mask_ref[w] = jnp.concatenate(both, axis=0).astype(BF16)

    @pl.loop(0, walkers * steps)
    def _(i):
        w, step = i // steps, i % steps
        mask = mask_ref[w]
        fetch(i).wait()
        for part in range(block // repeat):
            row = pl.multiple_of(i * chunk + part * repeat * own, repeat * own)
            sums = dot(mask, tangent_ref[pl.ds(row, repeat * own), :])
            at = pl.ds(pl.multiple_of(step * block + part * repeat, repeat), repeat)
            out_ref[w, 0, at, :] = sums[:repeat]
            out_ref[w, 1, at, :] = sums[repeat:]
        at = pl.ds(pl.multiple_of(step * block, block), block)
        sent_ref[w, :, at, :] = out_ref[w, :, at, :].astype(BF16)


def picked_rows(groups, mixed):
    lines = jnp.concatenate([groups, groups, groups], axis=0)
    return dot(lines, three_terms(mixed), FIRST)


def layer_kernel(values_ref, lap_ref, packed_ref, own_ref, other_ref, w_self_ref, w_spin_ref,
                 bias_ref, readout_ref, base_ref, curve_ref, weighted_ref):
    rows, feat = values_ref.shape
    lines = packed_ref[rows:, :]
    groups = lines[:, :rows]
    sizes = jnp.maximum(lines[:, rows:rows + 1].astype(F32), 1.0)
    means = ((own_ref[...] + other_ref[...]) / sizes).astype(BF16)
    preact = dot(values_ref[...], w_self_ref[...]) + picked_rows(groups, dot(means[0], w_spin_ref[...])) + bias_ref[...]
    lap_pre = dot(lap_ref[...], w_self_ref[...]) + picked_rows(groups, dot(means[1], w_spin_ref[...]))
    squash = jnp.tanh(preact)
    slopes = 1.0 - squash * squash
    base_ref[...] = slopes * lap_pre
    curve_ref[...] = -2.0 * squash * slopes
    weighted_ref[...] = slopes * readout_ref[...]


def change_kernel(own, block, piece, base, spin_ref, pot_ref, slot_ref, tangent_ref, own_ref, other_ref, w_self_ref,
                  w_spin_ref, readout_ref, base_ref, curve_ref, weighted_ref, before_ref, lap_ref, grad_ref,
                  mixed_ref, squares_ref, column_ref, terms_ref):
    walkers, feat = lap_ref.shape[0], w_self_ref.shape[0]
    dirs = own_ref.shape[2]
    electrons = slot_ref.shape[1]
    steps, part = dirs // block, 8
    halves = [slice(0, feat // 2), slice(feat // 2, feat)]
    grad_ref[...] = before_ref[...]

    @pl.loop(0, walkers)
    def _(n):
        w = base + n
        count = spin_ref[w]
        ups = count.astype(F32)
        mine = pl.ds(pl.multiple_of(w * own, own), own)
        for g, size in enumerate((ups, electrons - ups)):
            means = ((own_ref[w, g] + other_ref[w, g].astype(F32)) / size).astype(BF16)
            mixed_ref[g] = dot(means, w_spin_ref[...])
        column_ref[...] = jnp.broadcast_to(upper_column(slot_ref, w, count, own), (own, feat // 2))
        squares_ref[...] = jnp.zeros_like(squares_ref)

        @pl.loop(0, steps)
        def _(step):
            upper = column_ref[...] > 0.5
            weighted = [weighted_ref[mine, lanes] for lanes in halves]
            squares = [squares_ref[:, lanes] for lanes in halves]
            for c in range(block // piece):
                row = pl.multiple_of(((w * steps + step) * block + c * piece) * own, own)
                plain = dot(tangent_ref[pl.ds(row, piece * own), :], w_self_ref[...])
                for p in range(piece // part):
                    at = pl.multiple_of(step * block + c * piece + p * part, part)
                    mixed = mixed_ref[:, pl.ds(at, part), :]
                    for d in range(part):
                        row = (p * part + d) * own
                        terms = jnp.zeros((8, feat // 2), F32)
                        for h, lanes in enumerate(halves):
                            picked = jnp.where(upper, mixed[0, d:d + 1, lanes], mixed[1, d:d + 1, lanes])
                            change = plain[row:row + own, lanes] + picked
                            squares[h] = squares[h] + change * change
                            terms = terms + (change * weighted[h]).reshape(own // 8, 8, feat // 2).sum(axis=0)
                        terms_ref[pl.ds(pl.multiple_of(at * 8 + d * 8, 8), 8), :] = terms
            for lanes, total in zip(halves, squares):
                squares_ref[:, lanes] = total

        laplacian = base_ref[mine, :] + curve_ref[mine, :] * squares_ref[...]
        lap_ref[n] = laplacian
        summed = terms_ref[...].reshape(dirs, 8, feat // 2).sum(axis=1)
        spare = jnp.zeros((grad_ref.shape[1] - dirs, feat // 2), F32)
        summed = jnp.concatenate([summed, spare], axis=0)
        row = dot(jnp.ones((8, feat // 2), F32), summed, LAST, HIGHEST)
        share = jnp.sum(laplacian * readout_ref[...]) - jnp.where(lax.axis_index("tan") == 0, 2.0 * pot_ref[w], 0.0)
        row = jnp.where(iota(row.shape, 1) == dirs, share, row)
        grad_ref[...] = jnp.where(iota(row.shape, 0) == w, row, grad_ref[...])


def energy_kernel(dirs, walkers, own_ref, other_ref, out_ref):
    both = own_ref[...] + other_ref[...]
    place = iota(both.shape, 1)
    parts = jnp.where(place < dirs, both * both, jnp.where(place == dirs, both, 0.0))
    energy = -0.5 * jnp.sum(parts, axis=1, keepdims=True)
    lane = iota((1, 128), 1)
    row = jnp.zeros((1, 128), F32)
    for w in range(walkers):
        row = jnp.where(lane == w, energy[w:w + 1], row)
    out_ref[...] = row.reshape(1, 1, 128)


def pair(own_ref, other_ref, rows, r):
    values = jnp.concatenate([ref[r, 0:rows, :] for ref in (own_ref, other_ref)], axis=0)
    groups = jnp.concatenate([ref[r, rows:, 0:rows] for ref in (own_ref, other_ref)], axis=1)
    return values, groups


def slopes_kernel(rows, *refs):
    owns, others, weights, (slopes_ref, sums_ref, means_ref) = refs[0:2], refs[2:4], refs[4:8], refs[8:]
    w_self_ref, w_spin_ref, bias_ref, readout_ref = weights
    blocks, lines, _ = owns[0].shape
    group = lines - rows
    bunch = min(blocks, 8)

    for part, (own_ref, other_ref) in enumerate(zip(owns, others)):
        @pl.loop(0, blocks // bunch)
        def _(i):
            pairs = [pair(own_ref, other_ref, rows, i * bunch + k) for k in range(bunch)]
            means = []
            for k, (values, groups) in enumerate(pairs):
                sizes = jnp.maximum(own_ref[i * bunch + k, rows:, rows:rows + 1].astype(F32), 1.0)
                means.append(dot(groups, values) / sizes)
            means = jnp.concatenate(means, axis=0).astype(BF16)
            first = part * blocks + i * bunch
            at = pl.ds(pl.multiple_of(first * group, bunch * group), bunch * group)
            means_ref[at, :] = means
            mixed = dot(means, w_spin_ref[...])
            sums = []
            for k, (values, groups) in enumerate(pairs):
                preact = (dot(values, w_self_ref[...]) + picked_rows(groups, mixed[k * group:(k + 1) * group])
                          + bias_ref[...])
                squash = jnp.tanh(preact)
                slopes = ((1.0 - squash * squash) * readout_ref[...]).astype(BF16)
                slopes_ref[pl.ds(pl.multiple_of((first + k) * 2 * rows, 2 * rows), 2 * rows), :] = slopes
                sums.append(dot(groups, slopes))
            sums_ref[at, :] = jnp.concatenate(sums, axis=0)


def gradients_kernel(walkers, own, tables, energy_ref, *refs):
    self_ref, spin_ref = refs[-2:]
    rows = walkers * own
    blocks, lines, feat = refs[0].shape
    group, half = lines - rows, blocks // 2
    bunch = min(blocks, 8)
    everyone = energy_ref.shape[0] * walkers
    center = jnp.sum(jnp.sum(energy_ref[...], axis=0), axis=1, keepdims=True) / everyone
    line = iota((group, feat), 0) // 2
    self_ref[...] = jnp.zeros_like(self_ref)
    spin_ref[...] = jnp.zeros_like(spin_ref)
    for side, part in ((side, part) for side in range(2) for part in range(2)):
        owns, others, (slopes_ref, sums_ref, means_ref) = (
            refs[7 * side:7 * side + 2], refs[7 * side + 2:7 * side + 4], refs[7 * side + 4:7 * side + 7])
        own_ref, other_ref, (low_place, high_place) = owns[part], others[part], tables[side][part]

        @pl.loop(0, blocks // bunch)
        def _(i):
            first = part * blocks + i * bunch
            values, high, low, spreads = [], [], [], []
            for k in range(bunch):
                block = i * bunch + k
                row = energy_ref[block % half + jnp.where(block < half, low_place, high_place)] - center
                row_at = pl.multiple_of((first + k) * 2 * rows, 2 * rows)
                slopes = slopes_ref[pl.ds(row_at, 2 * rows), :].astype(F32)
                spread = jnp.zeros((group, feat), F32)
                for w in range(walkers):
                    spread = jnp.where(line == w, row[:, w:w + 1], spread)
                spreads.append(spread)
                for core in range(2):
                    for w in range(walkers):
                        at = core * rows + w * own
                        top, rest = two_terms(slopes[at:at + own] * row[:, w:w + 1])
                        high.append(top)
                        low.append(rest)
                values.append(pair(own_ref, other_ref, rows, block)[0])
            values = jnp.concatenate(values, axis=0)
            self_ref[...] += dot(values, jnp.concatenate(high, axis=0), FIRST) + dot(
                values, jnp.concatenate(low, axis=0), FIRST)
            at = pl.ds(pl.multiple_of(first * group, bunch * group), bunch * group)
            top, rest = two_terms(sums_ref[at, :] * jnp.concatenate(spreads, axis=0))
            means = means_ref[at, :]
            spin_ref[...] += dot(means, top, FIRST) + dot(means, rest, FIRST)


def whole(memory=pltpu.VMEM):
    return pl.BlockSpec(memory_space=memory)


def call(kernel, out_shape, in_specs, scratch=(), cost=None, limit=VMEM_LIMIT, out_specs=None):
    flops, moved = cost if cost is not None else (0, 0)
    return pl.pallas_call(
        kernel,
        out_shape=out_shape,
        in_specs=in_specs,
        out_specs=jax.tree.map(lambda _: whole(), out_shape) if out_specs is None else out_specs,
        scratch_shapes=scratch,
        cost_estimate=pl.CostEstimate(flops=flops, bytes_accessed=moved, transcendentals=0) if cost else None,
        compiler_params=pltpu.CompilerParams(vmem_limit_bytes=limit),
    )


def flip(array, axis, bit):
    size = lax.axis_size(axis)
    return lax.ppermute(array, axis, [(i, i ^ bit) for i in range(size)])


def tied(*arrays):
    return lax.optimization_barrier(arrays)


def shards(values, lap_in, tangent, slot_electron, spin_up, w_self, w_spin, bias, readout, potential):
    walk_size = lax.axis_size("walk")
    walkers, own, feat = values.shape
    dirs = tangent.shape[1]
    shape = jax.ShapeDtypeStruct
    smem = whole(pltpu.SMEM)
    flat = tangent.reshape(walkers * dirs * own, feat)
    values, lap_in = values.reshape(walkers * own, feat), lap_in.reshape(walkers * own, feat)
    bias, readout = bias.reshape(1, feat), readout.reshape(1, feat)
    bits = [1 << b for b in reversed(range(walk_size.bit_length() - 1))]

    small = (2, 16, feat)
    packed, value_sums, lines = call(
        functools.partial(pack_kernel, walkers, own),
        (shape((walkers * own + 16, feat), BF16), shape(small, F32), shape((16, feat), BF16)),
        [smem] + [whole(pltpu.HBM)] * 3,
        [pltpu.VMEM(slot_electron.shape, jnp.int32), pltpu.VMEM(lap_in.shape, BF16), pltpu.SemaphoreType.DMA((3,))],
        limit=63 * MIB)(spin_up, slot_electron, values, lap_in)
    other_value_sums = flip(value_sums, "tan", 1)
    gathered = packed.reshape((1,) + packed.shape)

    repeat, block, piece = feat // own, dirs // 2, dirs // 4
    sums, sent, held = call(
        functools.partial(sums_kernel, walkers, own, block),
        (shape((walkers, 2, dirs, feat), F32), shape((walkers, 2, dirs, feat), BF16), shape(flat.shape, BF16)),
        [whole(), whole(pltpu.HBM)],
        [pltpu.VMEM((walkers, 2 * repeat, feat), BF16), pltpu.SemaphoreType.DMA((walkers * dirs // block,))],
        (flat.size * 32, flat.size * 2), 36 * MIB)(lines, flat)
    received, sent, other_value_sums = tied(flip(gathered, "walk", bits[0]), sent, other_value_sums)
    gathered = jnp.concatenate([gathered, received], axis=0)
    other_sums = flip(sent, "tan", 1)
    for bit in bits[1:-3]:
        gathered = jnp.concatenate([gathered, flip(gathered, "walk", bit)], axis=0)
    received = flip(gathered, "walk", bits[-3])

    full = shape((walkers * own, feat), F32)
    base, curve, weighted = call(
        layer_kernel, (full, full, full), [whole()] * 9, cost=(4 * feat * feat * walkers * own, 4 << 20))(
            values, lap_in, packed, value_sums, other_value_sums, w_self, w_spin, bias, readout)

    counts = (1, walkers - 1)
    wide = -(-(dirs + 1) // 128) * 128

    def change(h, ups, before):
        return call(
            functools.partial(change_kernel, own, block, piece, sum(counts[:h])),
            (shape((counts[h], own, feat), F32), shape((8, wide), F32)),
            [smem, smem] + [whole()] * 11,
            [pltpu.VMEM((2, dirs, feat), F32), pltpu.VMEM((own, feat), F32), pltpu.VMEM((own, feat // 2), F32),
             pltpu.VMEM((dirs * 8, feat // 2), F32)],
            (flat.size * feat * counts[h] // 2, flat.size),
        )(ups, potential, slot_electron, held, sums, other_sums, w_self, w_spin, readout, base, curve, weighted, before)

    def joined(*arrays):
        return jnp.concatenate(arrays, axis=0)

    def across(arrays):
        return [flip(array, "tan", 1) for array in arrays]

    far_bits = bits[-2:]
    laplacian, partial = change(0, spin_up, jnp.zeros((8, wide), F32))
    received, late_spin_up, partial = tied(received, spin_up, partial)
    gathered = joined(gathered, received)
    middle = gathered.shape[0] // 2
    near = [gathered[:middle], gathered[middle:]]
    received = [flip(part, "walk", bit) for part, bit in zip(near, far_bits)]
    more_laplacian, more_partial = change(1, late_spin_up, partial)
    *received, more_partial = tied(*received, more_partial)
    near = [joined(*both) for both in zip(near, received)]
    near_others = across(near)
    rows = call(
        functools.partial(energy_kernel, dirs, walkers), shape((1, 1, 128), F32), [whole()] * 2)(
            more_partial, flip(more_partial, "tan", 1))
    energy = rows[0, 0, :walkers]
    *sent_near, _ = tied(*near, rows)
    far = [flip(part, "walk", bit) for part, bit in zip(sent_near, reversed(far_bits))]
    *near_others, more_laplacian, _ = tied(*near_others, more_laplacian, rows)

    blocks = walk_size // 2
    group_shape = (blocks * 16, feat)
    half = [((blocks * 2 * walkers * own, feat), BF16), (group_shape, F32), (group_shape, BF16)]
    weights = (w_self, w_spin, bias, readout)

    def slopes(*parts):
        return call(
            functools.partial(slopes_kernel, walkers * own), tuple(shape(*h) for h in half), [whole()] * 8,
            cost=(blocks * 8 * walkers * own * feat * feat, 8 << 20))(*parts, *weights)

    *near_slopes, last = slopes(*near, *near_others)
    energies = rows
    for stage, bit in enumerate(bits):
        received = flip(energies, "walk", bit)
        if stage == 0:
            received, last = tied(received, last)
        if stage == len(bits) - 2:
            received, *far = tied(received, *far)
            far_others = across(far)
            *far_slopes, far_last = slopes(*far, *far_others)
        if stage == len(bits) - 1:
            received, far_last = tied(received, far_last)
        energies = joined(energies, received)
    laplacian = joined(laplacian, more_laplacian)
    square = shape((feat, feat), F32)
    step = walk_size // 4
    tables = (((0, step), (step // 2, step // 2 + 2 * step)),
              ((2 * step, 3 * step), (step // 2 + step, step // 2 + 3 * step)))
    grad_self, grad_spin = call(
        functools.partial(gradients_kernel, walkers, own, tables), (square, square), [whole()] * 15)(
            energies, *near, *near_others, *near_slopes, last, *far, *far_others, *far_slopes, far_last)
    return laplacian, energy, grad_self, grad_spin


def solution(mesh):
    placed = (
        P("walk", "tan", None),
        P("walk", "tan", None),
        P("walk", None, "tan", None),
        P("walk", None),
        P("walk"),
        P(),
        P(),
        P(),
        P(),
        P("walk"),
    )
    return jax.shard_map(
        shards,
        mesh=mesh,
        in_specs=placed,
        out_specs=(P("walk", "tan", None), P("walk"), P(), P()),
        check_vma=False,
    )
```

```python
import functools

import jax
import jax.numpy as jnp
from jax import lax
from jax.experimental import pallas as pl
from jax.experimental.pallas import tpu as pltpu
from jax.sharding import PartitionSpec as P

F32 = jnp.float32
BF16 = jnp.bfloat16
MIB = 1024 * 1024
VMEM_LIMIT = 24 * MIB
HIGHEST = lax.Precision.HIGHEST
FIRST = ((0,), (0,))
LAST = ((1,), (1,))


def iota(shape, axis):
    return lax.broadcasted_iota(jnp.int32, shape, axis)


def dot(a, b, dims=((1,), (0,)), precision=None):
    return lax.dot_general(a, b, (dims, ((), ())), precision=precision, preferred_element_type=F32)


def two_terms(array):
    high = array.astype(BF16)
    return high, (array - high.astype(F32)).astype(BF16)


def three_terms(array):
    high = array.astype(BF16)
    middle, low = two_terms(array - high.astype(F32))
    return jnp.concatenate([high, middle, low], axis=0)


def first_slot(own):
    return lax.axis_index("tan") * own


def upper_row(slot_ref, w, count):
    return (slot_ref[pl.ds(w, 1), :] < count).astype(F32)


def upper_column(slot_ref, w, count, own):
    row = upper_row(slot_ref, w, count)
    place = iota((own, row.shape[1]), 1) == iota((own, row.shape[1]), 0) + first_slot(own)
    return jnp.sum(jnp.where(place, row, 0.0), axis=1, keepdims=True)


def own_places(electrons, own, wide):
    return (iota((electrons, wide), 0) == iota((electrons, wide), 1) % own + first_slot(own)).astype(BF16)


def pack_kernel(walkers, own, spin_ref, slot_far, values_far, lap_far, packed_ref, value_sums_ref, lines_ref,
                slot_ref, lap_ref, small_sems):
    rows, feat = lap_ref.shape
    electrons = slot_ref.shape[1]
    values_ref = packed_ref.at[pl.ds(0, rows)]
    near = [pltpu.make_async_copy(*ends, small_sems.at[i]) for i, ends in enumerate(
        ((slot_far, slot_ref), (values_far, values_ref), (lap_far, lap_ref)))]
    for copy in near:
        copy.start()
    near[0].wait()
    slots = jnp.zeros((2 * walkers, electrons), jnp.int32)
    for w in range(walkers):
        slots = jnp.where(iota(slots.shape, 0) // 2 == w, slot_ref[w:w + 1, :], slots)

    def column(shape):
        line = iota(shape, 0)
        count = jnp.zeros(shape, jnp.int32)
        for w in range(walkers):
            count = jnp.where(line // 2 == w, spin_ref[w], count)
        return line, count

    line, count = column(slots.shape)
    upper = (slots < count).astype(F32)
    chosen = jnp.where(line % 2 == 0, upper, 1.0 - upper).astype(BF16)
    tiled = dot(chosen, own_places(electrons, own, feat))
    line, count = column(tiled.shape)
    lane = iota(tiled.shape, 1)
    size = jnp.where(line % 2 == 0, count, electrons - count).astype(F32)
    groups = jnp.where(lane < rows, jnp.where(lane // own == line // 2, tiled, 0.0), size)
    groups = jnp.concatenate([groups, jnp.zeros((16 - 2 * walkers, feat), F32)], axis=0).astype(BF16)
    packed_ref[rows:, :] = groups
    lines_ref[...] = groups
    near[1].wait()
    near[2].wait()
    value_sums_ref[0] = dot(groups[:, :rows], values_ref[...])
    value_sums_ref[1] = dot(groups[:, :rows], lap_ref[...])


def sums_kernel(walkers, own, block, lines_ref, far_ref, out_ref, sent_ref, tangent_ref, mask_ref, sems):
    dirs = out_ref.shape[2]
    rows, feat = walkers * own, lines_ref.shape[1]
    repeat = mask_ref.shape[1] // 2
    steps, chunk = dirs // block, block * own

    def fetch(i):
        at = pl.ds(pl.multiple_of(i * chunk, chunk), chunk)
        return pltpu.make_async_copy(far_ref.at[at], tangent_ref.at[at], sems.at[i])

    for i in range(walkers * steps):
        fetch(i).start()
    spots = (iota((rows, feat), 0) % own == iota((rows, feat), 1) % own).astype(F32).astype(BF16)
    tiled = dot(lines_ref[:, :rows], spots)
    place = iota((repeat, feat), 1) // own == iota((repeat, feat), 0)
    for w in range(walkers):
        both = [jnp.where(place, tiled[2 * w + g:2 * w + g + 1], 0.0) for g in range(2)]
        mask_ref[w] = jnp.concatenate(both, axis=0).astype(BF16)

    @pl.loop(0, walkers * steps)
    def _(i):
        w, step = i // steps, i % steps
        mask = mask_ref[w]
        fetch(i).wait()
        for part in range(block // repeat):
            row = pl.multiple_of(i * chunk + part * repeat * own, repeat * own)
            sums = dot(mask, tangent_ref[pl.ds(row, repeat * own), :])
            at = pl.ds(pl.multiple_of(step * block + part * repeat, repeat), repeat)
            out_ref[w, 0, at, :] = sums[:repeat]
            out_ref[w, 1, at, :] = sums[repeat:]
        at = pl.ds(pl.multiple_of(step * block, block), block)
        sent_ref[w, :, at, :] = out_ref[w, :, at, :].astype(BF16)


def picked_rows(groups, mixed):
    lines = jnp.concatenate([groups, groups, groups], axis=0)
    return dot(lines, three_terms(mixed), FIRST)


def layer_kernel(values_ref, lap_ref, packed_ref, own_ref, other_ref, w_self_ref, w_spin_ref,
                 bias_ref, readout_ref, base_ref, curve_ref, weighted_ref):
    rows, feat = values_ref.shape
    lines = packed_ref[rows:, :]
    groups = lines[:, :rows]
    sizes = jnp.maximum(lines[:, rows:rows + 1].astype(F32), 1.0)
    means = ((own_ref[...] + other_ref[...]) / sizes).astype(BF16)
    preact = dot(values_ref[...], w_self_ref[...]) + picked_rows(groups, dot(means[0], w_spin_ref[...])) + bias_ref[...]
    lap_pre = dot(lap_ref[...], w_self_ref[...]) + picked_rows(groups, dot(means[1], w_spin_ref[...]))
    squash = jnp.tanh(preact)
    slopes = 1.0 - squash * squash
    base_ref[...] = slopes * lap_pre
    curve_ref[...] = -2.0 * squash * slopes
    weighted_ref[...] = slopes * readout_ref[...]


def change_kernel(own, block, piece, base, spin_ref, pot_ref, slot_ref, tangent_ref, own_ref, other_ref, w_self_ref,
                  w_spin_ref, readout_ref, base_ref, curve_ref, weighted_ref, before_ref, lap_ref, grad_ref,
                  mixed_ref, squares_ref, column_ref, terms_ref):
    walkers, feat = lap_ref.shape[0], w_self_ref.shape[0]
    dirs = own_ref.shape[2]
    electrons = slot_ref.shape[1]
    steps, part = dirs // block, 8
    halves = [slice(0, feat // 2), slice(feat // 2, feat)]
    grad_ref[...] = before_ref[...]

    @pl.loop(0, walkers)
    def _(n):
        w = base + n
        count = spin_ref[w]
        ups = count.astype(F32)
        mine = pl.ds(pl.multiple_of(w * own, own), own)
        for g, size in enumerate((ups, electrons - ups)):
            means = ((own_ref[w, g] + other_ref[w, g].astype(F32)) / size).astype(BF16)
            mixed_ref[g] = dot(means, w_spin_ref[...])
        column_ref[...] = jnp.broadcast_to(upper_column(slot_ref, w, count, own), (own, feat // 2))
        squares_ref[...] = jnp.zeros_like(squares_ref)

        @pl.loop(0, steps)
        def _(step):
            upper = column_ref[...] > 0.5
            weighted = [weighted_ref[mine, lanes] for lanes in halves]
            squares = [squares_ref[:, lanes] for lanes in halves]
            for c in range(block // piece):
                row = pl.multiple_of(((w * steps + step) * block + c * piece) * own, own)
                plain = dot(tangent_ref[pl.ds(row, piece * own), :], w_self_ref[...])
                for p in range(piece // part):
                    at = pl.multiple_of(step * block + c * piece + p * part, part)
                    mixed = mixed_ref[:, pl.ds(at, part), :]
                    for d in range(part):
                        row = (p * part + d) * own
                        terms = jnp.zeros((8, feat // 2), F32)
                        for h, lanes in enumerate(halves):
                            picked = jnp.where(upper, mixed[0, d:d + 1, lanes], mixed[1, d:d + 1, lanes])
                            change = plain[row:row + own, lanes] + picked
                            squares[h] = squares[h] + change * change
                            terms = terms + (change * weighted[h]).reshape(own // 8, 8, feat // 2).sum(axis=0)
                        terms_ref[pl.ds(pl.multiple_of(at * 8 + d * 8, 8), 8), :] = terms
            for lanes, total in zip(halves, squares):
                squares_ref[:, lanes] = total

        laplacian = base_ref[mine, :] + curve_ref[mine, :] * squares_ref[...]
        lap_ref[n] = laplacian
        summed = terms_ref[...].reshape(dirs, 8, feat // 2).sum(axis=1)
        spare = jnp.zeros((grad_ref.shape[1] - dirs, feat // 2), F32)
        summed = jnp.concatenate([summed, spare], axis=0)
        row = dot(jnp.ones((8, feat // 2), F32), summed, LAST, HIGHEST)
        share = jnp.sum(laplacian * readout_ref[...]) - jnp.where(lax.axis_index("tan") == 0, 2.0 * pot_ref[w], 0.0)
        row = jnp.where(iota(row.shape, 1) == dirs, share, row)
        grad_ref[...] = jnp.where(iota(row.shape, 0) == w, row, grad_ref[...])


def energy_kernel(dirs, walkers, own_ref, other_ref, out_ref):
    both = own_ref[...] + other_ref[...]
    place = iota(both.shape, 1)
    parts = jnp.where(place < dirs, both * both, jnp.where(place == dirs, both, 0.0))
    energy = -0.5 * jnp.sum(parts, axis=1, keepdims=True)
    lane = iota((1, 128), 1)
    row = jnp.zeros((1, 128), F32)
    for w in range(walkers):
        row = jnp.where(lane == w, energy[w:w + 1], row)
    out_ref[...] = row.reshape(1, 1, 128)


def pair(own_ref, other_ref, rows, r):
    values = jnp.concatenate([ref[r, 0:rows, :] for ref in (own_ref, other_ref)], axis=0)
    groups = jnp.concatenate([ref[r, rows:, 0:rows] for ref in (own_ref, other_ref)], axis=1)
    return values, groups


def slopes_kernel(rows, *refs):
    owns, others, weights, (slopes_ref, sums_ref, means_ref) = refs[0:2], refs[2:4], refs[4:8], refs[8:]
    w_self_ref, w_spin_ref, bias_ref, readout_ref = weights
    blocks, lines, _ = owns[0].shape
    group = lines - rows
    bunch = min(blocks, 8)

    for part, (own_ref, other_ref) in enumerate(zip(owns, others)):
        @pl.loop(0, blocks // bunch)
        def _(i):
            pairs = [pair(own_ref, other_ref, rows, i * bunch + k) for k in range(bunch)]
            means = []
            for k, (values, groups) in enumerate(pairs):
                sizes = jnp.maximum(own_ref[i * bunch + k, rows:, rows:rows + 1].astype(F32), 1.0)
                means.append(dot(groups, values) / sizes)
            means = jnp.concatenate(means, axis=0).astype(BF16)
            first = part * blocks + i * bunch
            at = pl.ds(pl.multiple_of(first * group, bunch * group), bunch * group)
            means_ref[at, :] = means
            mixed = dot(means, w_spin_ref[...])
            sums = []
            for k, (values, groups) in enumerate(pairs):
                preact = (dot(values, w_self_ref[...]) + picked_rows(groups, mixed[k * group:(k + 1) * group])
                          + bias_ref[...])
                squash = jnp.tanh(preact)
                slopes = ((1.0 - squash * squash) * readout_ref[...]).astype(BF16)
                slopes_ref[pl.ds(pl.multiple_of((first + k) * 2 * rows, 2 * rows), 2 * rows), :] = slopes
                sums.append(dot(groups, slopes))
            sums_ref[at, :] = jnp.concatenate(sums, axis=0)


def gradients_kernel(walkers, own, tables, energy_ref, *refs):
    self_ref, spin_ref = refs[-2:]
    rows = walkers * own
    blocks, lines, feat = refs[0].shape
    group, half = lines - rows, blocks // 2
    bunch = min(blocks, 8)
    everyone = energy_ref.shape[0] * walkers
    center = jnp.sum(jnp.sum(energy_ref[...], axis=0), axis=1, keepdims=True) / everyone
    line = iota((group, feat), 0) // 2
    self_ref[...] = jnp.zeros_like(self_ref)
    spin_ref[...] = jnp.zeros_like(spin_ref)
    for side, part in ((side, part) for side in range(2) for part in range(2)):
        owns, others, (slopes_ref, sums_ref, means_ref) = (
            refs[7 * side:7 * side + 2], refs[7 * side + 2:7 * side + 4], refs[7 * side + 4:7 * side + 7])
        own_ref, other_ref, (low_place, high_place) = owns[part], others[part], tables[side][part]

        @pl.loop(0, blocks // bunch)
        def _(i):
            first = part * blocks + i * bunch
            values, high, low, spreads = [], [], [], []
            for k in range(bunch):
                block = i * bunch + k
                row = energy_ref[block % half + jnp.where(block < half, low_place, high_place)] - center
                row_at = pl.multiple_of((first + k) * 2 * rows, 2 * rows)
                slopes = slopes_ref[pl.ds(row_at, 2 * rows), :].astype(F32)
                spread = jnp.zeros((group, feat), F32)
                for w in range(walkers):
                    spread = jnp.where(line == w, row[:, w:w + 1], spread)
                spreads.append(spread)
                for core in range(2):
                    for w in range(walkers):
                        at = core * rows + w * own
                        top, rest = two_terms(slopes[at:at + own] * row[:, w:w + 1])
                        high.append(top)
                        low.append(rest)
                values.append(pair(own_ref, other_ref, rows, block)[0])
            values = jnp.concatenate(values, axis=0)
            self_ref[...] += dot(values, jnp.concatenate(high, axis=0), FIRST) + dot(
                values, jnp.concatenate(low, axis=0), FIRST)
            at = pl.ds(pl.multiple_of(first * group, bunch * group), bunch * group)
            top, rest = two_terms(sums_ref[at, :] * jnp.concatenate(spreads, axis=0))
            means = means_ref[at, :]
            spin_ref[...] += dot(means, top, FIRST) + dot(means, rest, FIRST)


def whole(memory=pltpu.VMEM):
    return pl.BlockSpec(memory_space=memory)


def call(kernel, out_shape, in_specs, scratch=(), cost=None, limit=VMEM_LIMIT, out_specs=None):
    flops, moved = cost if cost is not None else (0, 0)
    return pl.pallas_call(
        kernel,
        out_shape=out_shape,
        in_specs=in_specs,
        out_specs=jax.tree.map(lambda _: whole(), out_shape) if out_specs is None else out_specs,
        scratch_shapes=scratch,
        cost_estimate=pl.CostEstimate(flops=flops, bytes_accessed=moved, transcendentals=0) if cost else None,
        compiler_params=pltpu.CompilerParams(vmem_limit_bytes=limit),
    )


def flip(array, axis, bit):
    size = lax.axis_size(axis)
    return lax.ppermute(array, axis, [(i, i ^ bit) for i in range(size)])


def tied(*arrays):
    return lax.optimization_barrier(arrays)


def shards(values, lap_in, tangent, slot_electron, spin_up, w_self, w_spin, bias, readout, potential):
    walk_size = lax.axis_size("walk")
    walkers, own, feat = values.shape
    dirs = tangent.shape[1]
    shape = jax.ShapeDtypeStruct
    smem = whole(pltpu.SMEM)
    flat = tangent.reshape(walkers * dirs * own, feat)
    values, lap_in = values.reshape(walkers * own, feat), lap_in.reshape(walkers * own, feat)
    bias, readout = bias.reshape(1, feat), readout.reshape(1, feat)
    bits = [1 << b for b in reversed(range(walk_size.bit_length() - 1))]

    small = (2, 16, feat)
    packed, value_sums, lines = call(
        functools.partial(pack_kernel, walkers, own),
        (shape((walkers * own + 16, feat), BF16), shape(small, F32), shape((16, feat), BF16)),
        [smem] + [whole(pltpu.HBM)] * 3,
        [pltpu.VMEM(slot_electron.shape, jnp.int32), pltpu.VMEM(lap_in.shape, BF16), pltpu.SemaphoreType.DMA((3,))],
        limit=63 * MIB)(spin_up, slot_electron, values, lap_in)
    other_value_sums = flip(value_sums, "tan", 1)
    gathered = packed.reshape((1,) + packed.shape)

    repeat, block, piece = feat // own, dirs // 2, dirs // 4
    sums, sent, held = call(
        functools.partial(sums_kernel, walkers, own, block),
        (shape((walkers, 2, dirs, feat), F32), shape((walkers, 2, dirs, feat), BF16), shape(flat.shape, BF16)),
        [whole(), whole(pltpu.HBM)],
        [pltpu.VMEM((walkers, 2 * repeat, feat), BF16), pltpu.SemaphoreType.DMA((walkers * dirs // block,))],
        (flat.size * 32, flat.size * 2), 36 * MIB)(lines, flat)
    received, sent, other_value_sums = tied(flip(gathered, "walk", bits[0]), sent, other_value_sums)
    gathered = jnp.concatenate([gathered, received], axis=0)
    other_sums = flip(sent, "tan", 1)
    for bit in bits[1:-3]:
        gathered = jnp.concatenate([gathered, flip(gathered, "walk", bit)], axis=0)
    received = flip(gathered, "walk", bits[-3])

    full = shape((walkers * own, feat), F32)
    base, curve, weighted = call(
        layer_kernel, (full, full, full), [whole()] * 9, cost=(4 * feat * feat * walkers * own, 4 << 20))(
            values, lap_in, packed, value_sums, other_value_sums, w_self, w_spin, bias, readout)

    counts = (1, walkers - 1)
    wide = -(-(dirs + 1) // 128) * 128

    def change(h, ups, before):
        return call(
            functools.partial(change_kernel, own, block, piece, sum(counts[:h])),
            (shape((counts[h], own, feat), F32), shape((8, wide), F32)),
            [smem, smem] + [whole()] * 11,
            [pltpu.VMEM((2, dirs, feat), F32), pltpu.VMEM((own, feat), F32), pltpu.VMEM((own, feat // 2), F32),
             pltpu.VMEM((dirs * 8, feat // 2), F32)],
            (flat.size * feat * counts[h] // 2, flat.size),
        )(ups, potential, slot_electron, held, sums, other_sums, w_self, w_spin, readout, base, curve, weighted, before)

    def joined(*arrays):
        return jnp.concatenate(arrays, axis=0)

    def across(arrays):
        return [flip(array, "tan", 1) for array in arrays]

    far_bits = bits[-2:]
    laplacian, partial = change(0, spin_up, jnp.zeros((8, wide), F32))
    received, late_spin_up, partial = tied(received, spin_up, partial)
    gathered = joined(gathered, received)
    middle = gathered.shape[0] // 2
    near = [gathered[:middle], gathered[middle:]]
    received = [flip(part, "walk", bit) for part, bit in zip(near, far_bits)]
    more_laplacian, more_partial = change(1, late_spin_up, partial)
    *received, more_partial = tied(*received, more_partial)
    near = [joined(*both) for both in zip(near, received)]
    far = [flip(part, "walk", bit) for part, bit in zip(near, reversed(far_bits))]
    near_others = across(near)
    rows = call(
        functools.partial(energy_kernel, dirs, walkers), shape((1, 1, 128), F32), [whole()] * 2)(
            more_partial, flip(more_partial, "tan", 1))
    energy = rows[0, 0, :walkers]
    *near_others, more_laplacian, _ = tied(*near_others, more_laplacian, rows)

    blocks = walk_size // 2
    group_shape = (blocks * 16, feat)
    half = [((blocks * 2 * walkers * own, feat), BF16), (group_shape, F32), (group_shape, BF16)]
    weights = (w_self, w_spin, bias, readout)

    def slopes(*parts):
        return call(
            functools.partial(slopes_kernel, walkers * own), tuple(shape(*h) for h in half), [whole()] * 8,
            cost=(blocks * 8 * walkers * own * feat * feat, 8 << 20))(*parts, *weights)

    *near_slopes, last = slopes(*near, *near_others)
    energies = rows
    for stage, bit in enumerate(bits):
        received = flip(energies, "walk", bit)
        if stage == 0:
            received, last = tied(received, last)
        if stage == len(bits) - 2:
            received, *far = tied(received, *far)
            far_others = across(far)
            *far_slopes, far_last = slopes(*far, *far_others)
        if stage == len(bits) - 1:
            received, far_last = tied(received, far_last)
        energies = joined(energies, received)
    laplacian = joined(laplacian, more_laplacian)
    square = shape((feat, feat), F32)
    step = walk_size // 4
    tables = (((0, step), (step // 2, step // 2 + 2 * step)),
              ((2 * step, 3 * step), (step // 2 + step, step // 2 + 3 * step)))
    grad_self, grad_spin = call(
        functools.partial(gradients_kernel, walkers, own, tables), (square, square), [whole()] * 15)(
            energies, *near, *near_others, *near_slopes, last, *far, *far_others, *far_slopes, far_last)
    return laplacian, energy, grad_self, grad_spin


def solution(mesh):
    placed = (
        P("walk", "tan", None),
        P("walk", "tan", None),
        P("walk", None, "tan", None),
        P("walk", None),
        P("walk"),
        P(),
        P(),
        P(),
        P(),
        P("walk"),
    )
    return jax.shard_map(
        shards,
        mesh=mesh,
        in_specs=placed,
        out_specs=(P("walk", "tan", None), P("walk"), P(), P()),
        check_vma=False,
    )
```
